32 devices in a mesh: fsdp: 8 (over y, x, core), seq: 4 (over z).
Axes of the slice: x: 2, y: 2, z: 4, core: 2. Of those that a mesh axis runs over, the one named last changes fastest.
Arguments:
- tokens: bfloat16 [2, 8, 1024, 2048], P(None, 'fsdp', 'seq'), may hold values from -6 to 6
- cotangent: bfloat16 [2, 8, 1024, 2048], P(None, 'fsdp', 'seq'), may hold values from -6 to 6
- attn_gain: bfloat16 [2048], P('fsdp'), may hold values from 0.5 to 1.5
- query_gain: bfloat16 [64], P('fsdp'), may hold values from 0.5 to 1.5
- key_gain: bfloat16 [64], P('fsdp'), may hold values from 0.5 to 1.5
- w_query: bfloat16 [2048, 2048], P('fsdp'), may hold values from -0.125 to 0.125
- w_key: bfloat16 [2048, 512], P('fsdp'), may hold values from -0.125 to 0.125
- w_value: bfloat16 [2048, 512], P('fsdp'), may hold values from -0.125 to 0.125
- w_out: bfloat16 [2048, 2048], P('fsdp'), may hold values from -1 to 1
- ffn_gain: bfloat16 [2048], P('fsdp'), may hold values from 0.5 to 1.5
- w_gate: bfloat16 [2048, 8192], P('fsdp'), may hold values from -0.125 to 0.125
- w_up: bfloat16 [2048, 8192], P('fsdp'), may hold values from -0.125 to 0.125
- w_down: bfloat16 [8192, 2048], P('fsdp'), may hold values from -0.0625 to 0.0625
Outputs:
- block_out: bfloat16 [2, 8, 1024, 2048], P(None, 'fsdp', 'seq')
- tokens_grad: bfloat16 [2, 8, 1024, 2048], P(None, 'fsdp', 'seq')
- attn_gain_grad: float32 [2048], P('fsdp')
- query_gain_grad: float32 [64], P('fsdp')
- key_gain_grad: float32 [64], P('fsdp')
- w_query_grad: float32 [2048, 2048], P('fsdp')
- w_key_grad: float32 [2048, 512], P('fsdp')
- w_value_grad: float32 [2048, 512], P('fsdp')
- w_out_grad: float32 [2048, 2048], P('fsdp')
- ffn_gain_grad: float32 [2048], P('fsdp')
- w_gate_grad: float32 [2048, 8192], P('fsdp')
- w_up_grad: float32 [2048, 8192], P('fsdp')
- w_down_grad: float32 [8192, 2048], P('fsdp')
The draws below stay inside these ranges and needn't reach their ends.
All inputs are finite; a program needn't handle non-finite values.
Results may differ from the reference program's by a relative error of at most 0.015.
Values may be sent and summed in bfloat16 or wider, within the bound.
No kernel may reach another device: no remote copies, remote signals or barrier semaphores. Data moves between devices by JAX's collectives and lax.ppermute only.
A program may use at most 800 MiB of HBM per device.

```python
import math
import jax
import jax.numpy as jnp
from jax import lax

D = 2048
HQ = 32
KVH = 8
HD = 64
FF = 8192
LENGTH = 1024
MICRO = 2
BATCH = 8


def shard_levels(key, dims, pieces, smallest, high):
    def one(position, blocks):
        steps = jax.random.uniform(jax.random.fold_in(jax.random.fold_in(key, 6), position), (blocks,), jnp.float32, smallest / len(pieces), high / len(pieces))
        return jnp.repeat(jnp.exp(steps), dims[position] // blocks).reshape((-1,) + (1,) * (len(dims) - position - 1))

    factor_of = one(*pieces[0])
    for cut in pieces[1:]:
        factor_of = factor_of * one(*cut)
    return factor_of


def centred(stream_key, shape, scale, limit, shards=(), kind=jnp.bfloat16):
    drawn = jax.random.normal(stream_key, shape, jnp.float32) * scale
    if len(shards) > 0:
        drawn = shard_levels(stream_key, shape, shards, -0.22, 0.18) * drawn
    return jnp.clip(drawn, min=-limit, max=limit).astype(kind)


def setup_inputs(seed: int = 0) -> dict:
    arg_keys = jax.random.split(jax.random.key(seed), 14)
    return {
        "tokens": centred(arg_keys[0], (MICRO, BATCH, LENGTH, D), 1.0, 6.0, ((1, 8), (2, 4))),
        "cotangent": centred(arg_keys[1], (MICRO, BATCH, LENGTH, D), 1.0, 6.0, ((1, 8), (2, 4))),
        "attn_gain": jnp.clip(1.0 + 0.1 * jax.random.normal(arg_keys[2], (D,), jnp.float32), 0.5, 1.5).astype(jnp.bfloat16),
        "query_gain": jnp.clip(1.0 + 0.1 * jax.random.normal(arg_keys[3], (HD,), jnp.float32), 0.5, 1.5).astype(jnp.bfloat16),
        "key_gain": jnp.clip(1.0 + 0.1 * jax.random.normal(arg_keys[4], (HD,), jnp.float32), 0.5, 1.5).astype(jnp.bfloat16),
        "w_query": centred(arg_keys[5], (D, HQ * HD), D ** -0.5, 0.125, ((0, 8),)),
        "w_key": centred(arg_keys[6], (D, KVH * HD), D ** -0.5, 0.125, ((0, 8),)),
        "w_value": centred(arg_keys[7], (D, KVH * HD), D ** -0.5, 0.125, ((0, 8),)),
        "w_out": centred(arg_keys[8], (HQ * HD, D), (HQ * HD // 64) ** -0.5, 1.0, ((0, 8),)),
        "ffn_gain": jnp.clip(1.0 + 0.1 * jax.random.normal(arg_keys[9], (D,), jnp.float32), 0.5, 1.5).astype(jnp.bfloat16),
        "w_gate": centred(arg_keys[10], (D, FF), D ** -0.5, 0.125, ((0, 8),)),
        "w_up": centred(arg_keys[11], (D, FF), D ** -0.5, 0.125, ((0, 8),)),
        "w_down": centred(arg_keys[12], (FF, D), FF ** -0.5, 0.0625, ((0, 8),)),
    }


@jax.custom_vjp
def low(v):
    return lax.optimization_barrier(v.astype(jnp.bfloat16)).astype(jnp.float32)

@jax.custom_vjp
def low_back(v):
    return v

def low_keep(v):
    return (low(v), None)

def low_pass(kept, grad):
    return (grad,)

def back_keep(v):
    return (v, None)

def back_low(kept, grad):
    return (low(grad),)
low.defvjp(low_keep, low_pass)
low_back.defvjp(back_keep, back_low)
EPSILON = 1e-05
THETA = 1000000.0
MASKED = -1e+30

def product(left_side, right_side):
    return jnp.dot(left_side, right_side, precision=lax.Precision.HIGHEST, preferred_element_type=jnp.float32)

def rms_norm(values, row_gain):
    inverse = lax.rsqrt(lax.optimization_barrier(jnp.mean(values * values, axis=-1, keepdims=True)) + EPSILON)
    return values * inverse * row_gain

def rope_tables(positions, head_width):
    half_width = head_width // 2
    frequency = THETA ** (-(jnp.arange(half_width).astype(jnp.float32) * 2.0 / head_width))
    angles = positions[:, None] * frequency[None, :]
    return (jnp.cos(angles)[:, None, :], jnp.sin(angles)[:, None, :])

def rotate(values, cosine_table, sine_table):
    half_width = values.shape[-1] // 2
    front_half = values[..., :half_width]
    back_half = values[..., half_width:]
    return jnp.concatenate([front_half * cosine_table - back_half * sine_table, back_half * cosine_table + front_half * sine_table], axis=-1)

def attention(queries, keys_all, values_all):
    length = queries.shape[0]
    block_size = min(512, length)
    score_scale = 1.0 / math.sqrt(HD)
    key_index = jnp.arange(length, dtype=jnp.int32)

    def one_block(block_index):
        first_row = block_index * block_size
        query_block = lax.dynamic_slice_in_dim(queries, first_row, block_size, 0)
        scores = jnp.einsum('qcgd,kcd->cgqk', query_block, keys_all, precision=lax.Precision.HIGHEST) * score_scale
        scores = low_back(scores)
        row_index = first_row + jnp.arange(block_size, dtype=jnp.int32)
        allowed = key_index[None, :] <= row_index[:, None]
        scores = jnp.where(allowed, scores, MASKED)
        top_score = lax.optimization_barrier(jnp.max(scores, axis=-1, keepdims=True))
        log_total = top_score + jnp.log(lax.optimization_barrier(jnp.sum(jnp.exp(scores - top_score), axis=-1, keepdims=True)))
        weights = low(jnp.exp(scores - log_total))
        return jnp.einsum('cgqk,kcd->qcgd', weights, values_all, precision=lax.Precision.HIGHEST)
    blocks = lax.map(jax.checkpoint(one_block), jnp.arange(length // block_size, dtype=jnp.int32))
    return blocks.reshape(length, -1)

def forward(inputs, attn_gain, query_gain, key_gain, w_query, w_key, w_value, w_out, ffn_gain, w_gate, w_up, w_down):
    positions = jnp.arange(LENGTH).astype(jnp.float32)
    cosine_table, sine_table = rope_tables(positions, HD)
    normed = low(rms_norm(inputs, attn_gain))
    query_raw = low_back(product(normed, w_query)).reshape(LENGTH, HQ, HD)
    key_raw = low_back(product(normed, w_key)).reshape(LENGTH, KVH, HD)
    values_all = low(low_back(product(normed, w_value))).reshape(LENGTH, KVH, HD)
    queries = low(low_back(rotate(rms_norm(query_raw, query_gain), cosine_table, sine_table)))
    keys_all = low(low_back(rotate(rms_norm(key_raw, key_gain), cosine_table, sine_table)))
    attended = low(low_back(attention(queries.reshape(LENGTH, KVH, HQ // KVH, HD), keys_all, values_all)))
    middle = inputs + low_back(product(attended, w_out))
    ffn_normed = low(rms_norm(middle, ffn_gain))
    gate_pre = low_back(product(ffn_normed, w_gate))
    up_pre = low_back(product(ffn_normed, w_up))
    hidden = low(jax.nn.silu(gate_pre) * up_pre)
    return middle + low_back(product(hidden, w_down))

def reference(tokens, cotangent, attn_gain, query_gain, key_gain, w_query, w_key, w_value, w_out, ffn_gain, w_gate, w_up, w_down):
    weights_all = tuple((weight_item.astype(jnp.float32) for weight_item in (attn_gain, query_gain, key_gain, w_query, w_key, w_value, w_out, ffn_gain, w_gate, w_up, w_down)))
    seq_inputs = tokens.reshape(MICRO * BATCH, LENGTH, D).astype(jnp.float32)
    seq_cotangents = cotangent.reshape(MICRO * BATCH, LENGTH, D).astype(jnp.float32)

    def one_sequence(running, seq_pair):
        inputs, grad_outputs = seq_pair
        outputs, pullback = jax.vjp(forward, inputs, *weights_all)
        gradients = pullback(grad_outputs)
        running = tuple((total_item + grad_item for total_item, grad_item in zip(running, gradients[1:])))
        return (running, (outputs.astype(jnp.bfloat16), gradients[0].astype(jnp.bfloat16)))
    empty_all = tuple((jnp.zeros_like(weight_item) for weight_item in weights_all))
    totals, (outputs, input_grads) = lax.scan(one_sequence, empty_all, (seq_inputs, seq_cotangents))
    return (outputs.reshape(tokens.shape), input_grads.reshape(tokens.shape), totals[0], totals[1], totals[2], totals[3], totals[4], totals[5], totals[6], totals[7], totals[8], totals[9], totals[10])
```

```python
import functools
import math

import jax
import jax.numpy as jnp
from jax import lax
from jax.experimental import pallas as pl
from jax.experimental.pallas import tpu as pltpu
from jax.sharding import PartitionSpec as P

D = 2048
HQ = 32
KVH = 8
HD = 64
FF = 8192
LENGTH = 1024
MICRO = 2

EPSILON = 1e-05
THETA = 1000000.0
GROUP = HQ // KVH
BLOCK = 128
SCALE = 1.0 / math.sqrt(HD)
LOG2E = math.log2(math.e)
VMEM_LIMIT = 48 * 1024 * 1024

F32 = jnp.float32
BF16 = jnp.bfloat16


def dot(left_side, right_side, left_dim, right_dim):
    return lax.dot_general(
        left_side,
        right_side,
        (((left_dim,), (right_dim,)), ((), ())),
        preferred_element_type=F32,
    )


def rms_fwd(values, row_gain):
    inverse = lax.rsqrt(jnp.mean(values * values, axis=-1, keepdims=True) + EPSILON)
    unit_rows = values * inverse
    return (unit_rows * row_gain, unit_rows, inverse)


def rms_back(grad_outputs, unit_rows, inverse, row_gain):
    scaled = grad_outputs * row_gain
    grad_inputs = inverse * (
        scaled - unit_rows * jnp.mean(scaled * unit_rows, axis=-1, keepdims=True)
    )
    grad_gain = jnp.sum(grad_outputs * unit_rows, axis=0)
    return (grad_inputs, grad_gain)


def head_rms_fwd(values, gains):
    inverse = lax.rsqrt(jnp.mean(values * values, axis=1, keepdims=True) + EPSILON)
    unit = values * inverse
    return (unit * gains, unit, inverse)


def rotate(values, cosine_table, sine_table):
    half_width = values.shape[1] // 2
    front_half = values[:, :half_width]
    back_half = values[:, half_width:]
    return jnp.concatenate(
        [
            front_half * cosine_table - back_half * sine_table,
            back_half * cosine_table + front_half * sine_table,
        ],
        axis=1,
    )


def block_masks(index, pieces, piece_rows, step_rows):
    key = lax.broadcasted_iota(jnp.int32, (BLOCK, GROUP * BLOCK), 0)
    query = lax.broadcasted_iota(jnp.int32, (BLOCK, GROUP * BLOCK), 1) & (BLOCK - 1)

    def place(row, piece):
        return (row // piece_rows) * step_rows + piece * piece_rows + (row & (piece_rows - 1))

    return [place(key, index ^ k) <= place(query, index) for k in range(pieces)]


def heads_beside(block, first, count):
    return jnp.concatenate(
        [block[h * HD : (h + 1) * HD, first : first + count] for h in range(GROUP)], axis=1
    )


def mask_tail(values, mask, first):
    tail = jnp.where(mask, values[first:], 0.0)
    if first == 0:
        return tail
    return jnp.concatenate([values[:first], tail], axis=0)


def attend_kernel(index_ref, q_ref, k_ref, v_ref, out_ref, lse_ref, *, pieces, piece_rows, step_rows):
    rows = q_ref.shape[1]
    masks = block_masks(index_ref[0], pieces, piece_rows, step_rows)
    queries = q_ref[...]
    for first in range(0, rows, BLOCK):
        count = first + BLOCK
        query_block = heads_beside(queries, first, BLOCK)
        total = None
        result = None
        for k in range(pieces):
            spot = pl.ds(k * rows, count)
            scores = dot(k_ref[:, spot], query_block, 0, 0)
            weights = mask_tail(jnp.exp2(scores * (SCALE * LOG2E)), masks[k], first)
            part = jnp.sum(weights, axis=0, keepdims=True)
            value = dot(v_ref[:, spot], weights.astype(BF16), 1, 0)
            total = part if total is None else total + part
            result = value if result is None else result + value
        result = result * (1.0 / total)
        log_total = jnp.log2(total)
        for h in range(GROUP):
            columns = slice(h * BLOCK, (h + 1) * BLOCK)
            out_ref[h * HD : (h + 1) * HD, first : first + BLOCK] = result[:, columns].astype(BF16)
            lse_ref[0, h : h + 1, first : first + BLOCK] = log_total[:, columns]


def attend_back_kernel(
    index_ref, q_ref, k_ref, v_ref, out_ref, lse_ref, grad_ref, dq_ref, dk_ref, dv_ref,
    *, pieces, piece_rows, step_rows
):
    rows = q_ref.shape[1]
    masks = block_masks(index_ref[0], pieces, piece_rows, step_rows)
    queries = q_ref[...]
    grads = grad_ref[...]
    results = out_ref[...]
    dk_ref[...] = jnp.zeros_like(dk_ref)
    dv_ref[...] = jnp.zeros_like(dv_ref)
    for first in range(0, rows, BLOCK):
        count = first + BLOCK
        query_block = heads_beside(queries, first, BLOCK)
        grad_block = heads_beside(grads, first, BLOCK)
        result_block = heads_beside(results, first, BLOCK)
        centre = jnp.sum(
            grad_block.astype(F32) * result_block.astype(F32), axis=0, keepdims=True
        )
        log_total = jnp.concatenate(
            [lse_ref[0, h : h + 1, first : first + BLOCK] for h in range(GROUP)], axis=1
        )
        dq = None
        for k in range(pieces):
            spot = pl.ds(k * rows, count)
            keys = k_ref[:, spot]
            scores = dot(keys, query_block, 0, 0)
            weights = mask_tail(
                jnp.exp2(scores * (SCALE * LOG2E) - log_total), masks[k], first
            )
            grad_weights = dot(v_ref[:, spot], grad_block, 0, 0)
            grad_scores = (weights * (grad_weights - centre)).astype(BF16)
            part = dot(keys, grad_scores, 1, 0)
            dq = part if dq is None else dq + part
            dk_ref[:, spot] += dot(query_block, grad_scores, 1, 1) * SCALE
            dv_ref[:, spot] += dot(grad_block, weights.astype(BF16), 1, 1)
        dq = (dq * SCALE).astype(BF16)
        for h in range(GROUP):
            columns = slice(h * BLOCK, (h + 1) * BLOCK)
            dq_ref[h * HD : (h + 1) * HD, first : first + BLOCK] = dq[:, columns]


def attention_specs(rows, total_rows):
    group_spec = pl.BlockSpec((GROUP * HD, rows), lambda i: (i, 0))
    pair_spec = pl.BlockSpec((HD, total_rows), lambda i: (i, 0))
    lse_spec = pl.BlockSpec((1, GROUP, rows), lambda i: (i, 0, 0))
    return group_spec, pair_spec, lse_spec


def attend(index, queries, keys, values, pieces, piece_rows, step_rows):
    rows, total_rows = queries.shape[1], keys.shape[1]
    group_spec, pair_spec, lse_spec = attention_specs(rows, total_rows)
    return pl.pallas_call(
        functools.partial(
            attend_kernel, pieces=pieces, piece_rows=piece_rows, step_rows=step_rows
        ),
        grid=(KVH,),
        in_specs=[pl.BlockSpec(memory_space=pltpu.SMEM), group_spec, pair_spec, pair_spec],
        out_specs=[group_spec, lse_spec],
        out_shape=[
            jax.ShapeDtypeStruct((HQ * HD, rows), BF16),
            jax.ShapeDtypeStruct((KVH, GROUP, rows), F32),
        ],
        compiler_params=pltpu.CompilerParams(vmem_limit_bytes=VMEM_LIMIT),
        cost_estimate=pl.CostEstimate(
            flops=4 * HQ * HD * rows * total_rows,
            bytes_accessed=8 * HQ * HD * rows,
            transcendentals=HQ * rows * total_rows,
        ),
        name="attend",
    )(index, queries, keys, values)


def attend_back(index, queries, keys, values, results, lse, grads, pieces, piece_rows, step_rows):
    rows, total_rows = queries.shape[1], keys.shape[1]
    group_spec, pair_spec, lse_spec = attention_specs(rows, total_rows)
    return pl.pallas_call(
        functools.partial(
            attend_back_kernel, pieces=pieces, piece_rows=piece_rows, step_rows=step_rows
        ),
        grid=(KVH,),
        in_specs=[
            pl.BlockSpec(memory_space=pltpu.SMEM),
            group_spec,
            pair_spec,
            pair_spec,
            group_spec,
            lse_spec,
            group_spec,
        ],
        out_specs=[group_spec, pair_spec, pair_spec],
        out_shape=[
            jax.ShapeDtypeStruct((HQ * HD, rows), BF16),
            jax.ShapeDtypeStruct((KVH * HD, total_rows), F32),
            jax.ShapeDtypeStruct((KVH * HD, total_rows), F32),
        ],
        compiler_params=pltpu.CompilerParams(vmem_limit_bytes=VMEM_LIMIT),
        cost_estimate=pl.CostEstimate(
            flops=10 * HQ * HD * rows * total_rows,
            bytes_accessed=16 * HQ * HD * rows,
            transcendentals=HQ * rows * total_rows,
        ),
        name="attend_back",
    )(index, queries, keys, values, results, lse, grads)


class Layout:
    def __init__(self, fsdp_devices, seq_devices, rows_dev):
        self.fsdp = fsdp_devices
        self.seq = seq_devices
        self.chips = fsdp_devices // 2
        self.share = 2 * seq_devices // (2 * MICRO)
        self.near = self.share // 2
        self.piece_rows = rows_dev // self.share
        self.step_rows = rows_dev
        self.rows = LENGTH // self.share

    def flat(self, f, z):
        return f * self.seq + z

    def moved(self, r):
        pairs = []
        for f in range(self.fsdp):
            for z in range(self.seq):
                slot = z ^ r
                micro, j = slot // self.share, slot % self.share
                target_f = (f // 2) * 2 + j % 2
                target_z = (2 * micro + f % 2) * self.near + j // 2
                pairs.append((self.flat(f, z), self.flat(target_f, target_z)))
        return pairs

    def across(self, k):
        pairs = []
        for f in range(self.fsdp):
            for z in range(self.seq):
                pairs.append((self.flat(f, z), self.flat(f ^ (k & 1), z ^ (k >> 1))))
        return pairs


def permute(value, pairs):
    return lax.ppermute(value, ("fsdp", "seq"), pairs)


def scatter_rows(layout, values, z, slot):
    parts = values.reshape(layout.seq, layout.piece_rows, values.shape[-1])
    result = jnp.zeros_like(parts)
    for r in range(layout.seq):
        sent = lax.dynamic_index_in_dim(parts, z ^ r, 0, keepdims=False)
        got = permute(sent, layout.moved(r))
        result = lax.dynamic_update_index_in_dim(result, got, slot ^ r, 0)
    return result.reshape(layout.rows, values.shape[-1])


def return_rows(layout, values, z, slot):
    parts = values.reshape(layout.seq, layout.piece_rows, values.shape[-1])
    result = jnp.zeros_like(parts)
    for r in range(layout.seq):
        sent = lax.dynamic_index_in_dim(parts, slot ^ r, 0, keepdims=False)
        got = permute(sent, [(b, a) for a, b in layout.moved(r)])
        result = lax.dynamic_update_index_in_dim(result, got, z ^ r, 0)
    return result.reshape(MICRO, layout.step_rows, values.shape[-1])


def line_sum(value, z, seq_devices):
    half = seq_devices // 2
    last = seq_devices - 1
    for s in range(half - 1):
        got = lax.ppermute(value, "seq", [(s, s + 1), (last - s, last - s - 1)])
        value = (value.astype(F32) + got.astype(F32)).astype(BF16)
    got = lax.ppermute(value, "seq", [(half - 1, half), (half, half - 1)])
    value = (value.astype(F32) + got.astype(F32)).astype(BF16)
    for s in reversed(range(half - 1)):
        got = lax.ppermute(value, "seq", [(s + 1, s), (last - s - 1, last - s)])
        value = jnp.where((z == s) | (z == last - s), got, value)
    return value


def body(
    tokens,
    cotangent,
    attn_gain,
    query_gain,
    key_gain,
    w_query,
    w_key,
    w_value,
    w_out,
    ffn_gain,
    w_gate,
    w_up,
    w_down,
):
    fsdp_devices = lax.axis_size("fsdp")
    seq_devices = lax.axis_size("seq")
    layout = Layout(fsdp_devices, seq_devices, tokens.shape[2])
    f = lax.axis_index("fsdp")
    z = lax.axis_index("seq")
    rows = layout.rows
    share = layout.share
    member = (z % layout.near) * 2 + f % 2
    slot = (z // layout.near // 2) * share + member

    w_attn = lax.all_gather(
        jnp.concatenate([w_query, w_key, w_value], axis=1), "fsdp", axis=0, tiled=True
    )
    gains = lax.all_gather(
        jnp.concatenate([attn_gain, ffn_gain, query_gain, key_gain]), "fsdp", axis=0, tiled=False
    ).astype(F32)
    wide, narrow = attn_gain.shape[0], query_gain.shape[0]
    full_attn_gain = gains[:, :wide].reshape(D)
    full_ffn_gain = gains[:, wide : 2 * wide].reshape(D)
    full_query_gain = gains[:, 2 * wide : 2 * wide + narrow].reshape(HD)
    full_key_gain = gains[:, 2 * wide + narrow :].reshape(HD)
    inputs_low = scatter_rows(layout, tokens[:, 0], z, slot)
    full_out = lax.all_gather(w_out, "fsdp", axis=0, tiled=True)
    gate_columns = lax.all_to_all(w_gate, "fsdp", split_axis=1, concat_axis=0, tiled=True)
    up_columns = lax.all_to_all(w_up, "fsdp", split_axis=1, concat_axis=0, tiled=True)
    grad_out_low = scatter_rows(layout, cotangent[:, 0], z, slot)

    row = jnp.arange(rows, dtype=jnp.int32)
    position = (
        (row // layout.piece_rows) * layout.step_rows
        + member * layout.piece_rows
        + row % layout.piece_rows
    ).astype(F32)
    frequency = THETA ** (-(jnp.arange(HD // 2).astype(F32) * 2.0 / HD))
    angles = frequency[:, None] * position[None, :]
    cosine_table, sine_table = jnp.cos(angles)[None], jnp.sin(angles)[None]
    head_gains = jnp.concatenate(
        [
            jnp.broadcast_to(full_query_gain[None, :, None], (HQ, HD, 1)),
            jnp.broadcast_to(full_key_gain[None, :, None], (KVH, HD, 1)),
        ]
    )

    inputs = inputs_low.astype(F32)
    normed, normed_unit, normed_inverse = rms_fwd(inputs, full_attn_gain)
    normed_low = normed.astype(BF16)
    raw = dot(w_attn, normed_low, 0, 1)
    pair_width = KVH * HD
    turned = HQ + KVH
    head_raw = raw[: turned * HD].reshape(turned, HD, rows)
    head_normed, head_unit, head_inverse = head_rms_fwd(head_raw, head_gains)
    heads_low = rotate(head_normed, cosine_table, sine_table).astype(BF16).reshape(turned * HD, rows)
    queries = heads_low[: HQ * HD]
    own_pair = jnp.concatenate([heads_low[HQ * HD :], raw[turned * HD :].astype(BF16)], axis=0)
    pair_pieces = [own_pair] + [permute(own_pair, layout.across(k)) for k in range(1, share)]
    keys = jnp.concatenate([piece[:pair_width] for piece in pair_pieces], axis=1)
    values = jnp.concatenate([piece[pair_width:] for piece in pair_pieces], axis=1)
    index = member.astype(jnp.int32).reshape(1)
    attended, log_totals = attend(
        index, queries, keys, values, share, layout.piece_rows, layout.step_rows
    )
    middle = inputs + dot(attended, full_out, 0, 0)
    ffn_normed, ffn_unit, ffn_inverse = rms_fwd(middle, full_ffn_gain)
    ffn_low = ffn_normed.astype(BF16)

    ffn_rows = lax.all_gather(ffn_low, "fsdp", axis=0, tiled=True)
    grad_out_rows = lax.all_gather(grad_out_low, "fsdp", axis=0, tiled=True)
    gate_pre = dot(ffn_rows, gate_columns, 1, 0)
    up_pre = dot(ffn_rows, up_columns, 1, 0)
    grad_hidden = dot(grad_out_rows, w_down, 1, 1)
    sigmoid_gate = jax.nn.sigmoid(gate_pre)
    silu_gate = gate_pre * sigmoid_gate
    hidden_low = (silu_gate * up_pre).astype(BF16)
    grad_gate_low = (
        grad_hidden * up_pre * sigmoid_gate * (1.0 + gate_pre * (1.0 - sigmoid_gate))
    ).astype(BF16)
    grad_up_low = (grad_hidden * silu_gate).astype(BF16)
    grad_ffn_part = dot(grad_gate_low, gate_columns, 1, 1) + dot(grad_up_low, up_columns, 1, 1)
    grad_ffn_normed = lax.psum_scatter(
        grad_ffn_part.astype(BF16), "fsdp", scatter_dimension=0, tiled=True
    ).astype(F32)
    out_part = dot(hidden_low, w_down, 1, 0)
    out_sum = lax.psum_scatter(
        out_part.astype(BF16), "fsdp", scatter_dimension=0, tiled=True
    ).astype(F32)
    block_out = return_rows(layout, (middle + out_sum).astype(BF16), z, slot)

    down_term = dot(hidden_low, grad_out_rows, 0, 0).astype(BF16)
    gate_term = dot(ffn_rows, grad_gate_low, 0, 0).astype(BF16)
    up_term = dot(ffn_rows, grad_up_low, 0, 0).astype(BF16)

    def summed(term, cuts):
        step = term.shape[0] // cuts
        return jnp.concatenate(
            [
                line_sum(term[i * step : (i + 1) * step], z, seq_devices)
                for i in range(cuts)
            ]
        ).astype(F32)

    w_down_grad = summed(down_term, 2)
    w_gate_grad = summed(
        lax.all_to_all(gate_term, "fsdp", split_axis=0, concat_axis=1, tiled=True), 2
    )
    w_up_grad = summed(
        lax.all_to_all(up_term, "fsdp", split_axis=0, concat_axis=1, tiled=True), 2
    )

    grad_middle_norm, ffn_gain_term = rms_back(
        grad_ffn_normed, ffn_unit, ffn_inverse, full_ffn_gain
    )
    grad_middle = grad_out_low.astype(F32) + grad_middle_norm
    grad_branch_low = grad_middle.astype(BF16)
    grad_attended = dot(full_out, grad_branch_low, 1, 1).astype(BF16)
    out_term = dot(attended, grad_branch_low, 1, 0).astype(BF16)
    grad_queries, grad_keys, grad_values = attend_back(
        index,
        queries,
        keys,
        values,
        attended,
        log_totals,
        grad_attended,
        share,
        layout.piece_rows,
        layout.step_rows,
    )
    grad_pair = jnp.concatenate([grad_keys[:, :rows], grad_values[:, :rows]], axis=0)
    for k in range(1, share):
        columns = slice(k * rows, (k + 1) * rows)
        sent = jnp.concatenate([grad_keys[:, columns], grad_values[:, columns]], axis=0)
        grad_pair = grad_pair + permute(sent.astype(BF16), layout.across(k)).astype(F32)
    grad_pair_low = grad_pair.astype(BF16)
    grad_turned = (
        jnp.concatenate([grad_queries, grad_pair_low[:pair_width]], axis=0)
        .astype(F32)
        .reshape(turned, HD, rows)
    )
    grad_head_normed = rotate(grad_turned, cosine_table, -sine_table)
    scaled = grad_head_normed * head_gains
    grad_head_raw = head_inverse * (
        scaled - head_unit * jnp.mean(scaled * head_unit, axis=1, keepdims=True)
    )
    head_gain_terms = jnp.sum(grad_head_normed * head_unit, axis=2)
    grad_raw = jnp.concatenate(
        [grad_head_raw.astype(BF16).reshape(turned * HD, rows), grad_pair_low[pair_width:]], axis=0
    )
    projection_term = dot(normed_low, grad_raw, 0, 1).astype(BF16)
    grad_normed = dot(grad_raw, w_attn, 0, 1)
    grad_input_norm, attn_gain_term = rms_back(
        grad_normed, normed_unit, normed_inverse, full_attn_gain
    )
    tokens_grad = return_rows(layout, (grad_middle + grad_input_norm).astype(BF16), z, slot)

    w_out_grad = line_sum(
        lax.psum_scatter(out_term, "fsdp", scatter_dimension=0, tiled=True), z, seq_devices
    ).astype(F32)
    attn_rows = line_sum(
        lax.psum_scatter(projection_term, "fsdp", scatter_dimension=0, tiled=True), z, seq_devices
    ).astype(F32)
    query_width = HQ * HD
    gain_sums = lax.psum(
        jnp.concatenate(
            [
                attn_gain_term,
                ffn_gain_term,
                jnp.sum(head_gain_terms[:HQ], axis=0),
                jnp.sum(head_gain_terms[HQ:], axis=0),
            ]
        ),
        ("fsdp", "seq"),
    )

    def own_share(vector):
        width = vector.shape[0] // fsdp_devices
        return lax.dynamic_slice_in_dim(vector, f * width, width, 0)

    return (
        block_out[:, None],
        tokens_grad[:, None],
        own_share(gain_sums[:D]),
        own_share(gain_sums[2 * D : 2 * D + HD]),
        own_share(gain_sums[2 * D + HD :]),
        attn_rows[:, :query_width],
        attn_rows[:, query_width : query_width + pair_width],
        attn_rows[:, query_width + pair_width :],
        w_out_grad,
        own_share(gain_sums[D : 2 * D]),
        w_gate_grad,
        w_up_grad,
        w_down_grad,
    )


def solution(mesh):
    activations = P(None, "fsdp", "seq", None)
    vector = P("fsdp")
    matrix = P("fsdp", None)
    specs = (
        (activations, activations)
        + (vector,) * 3
        + (matrix,) * 4
        + (vector,)
        + (matrix,) * 3
    )
    return jax.shard_map(body, mesh=mesh, in_specs=specs, out_specs=specs, check_vma=False)
```

```python
import functools
import math

import jax
import jax.numpy as jnp
from jax import lax
from jax.experimental import pallas as pl
from jax.experimental.pallas import tpu as pltpu
from jax.sharding import PartitionSpec as P

D = 2048
HQ = 32
KVH = 8
HD = 64
FF = 8192
LENGTH = 1024
MICRO = 2
HALVES = 2

EPSILON = 1e-05
THETA = 1000000.0
GROUP = HQ // KVH
BLOCK = 128
SCALE = 1.0 / math.sqrt(HD)
LOG2E = math.log2(math.e)
VMEM_LIMIT = 48 * 1024 * 1024

F32 = jnp.float32
BF16 = jnp.bfloat16


def dot(left_side, right_side, left_dim, right_dim):
    return lax.dot_general(
        left_side,
        right_side,
        (((left_dim,), (right_dim,)), ((), ())),
        preferred_element_type=F32,
    )


def rms_fwd(values, row_gain):
    inverse = lax.rsqrt(jnp.mean(values * values, axis=-1, keepdims=True) + EPSILON)
    unit_rows = values * inverse
    return (unit_rows * row_gain, unit_rows, inverse)


def rms_back(grad_outputs, unit_rows, inverse, row_gain):
    scaled = grad_outputs * row_gain
    grad_inputs = inverse * (
        scaled - unit_rows * jnp.mean(scaled * unit_rows, axis=-1, keepdims=True)
    )
    grad_gain = jnp.sum(grad_outputs * unit_rows, axis=0)
    return (grad_inputs, grad_gain)


def head_rms_fwd(values, gains):
    inverse = lax.rsqrt(jnp.mean(values * values, axis=1, keepdims=True) + EPSILON)
    unit = values * inverse
    return (unit * gains, unit, inverse)


def rotate(values, cosine_table, sine_table):
    half_width = values.shape[1] // 2
    front_half = values[:, :half_width]
    back_half = values[:, half_width:]
    return jnp.concatenate(
        [
            front_half * cosine_table - back_half * sine_table,
            back_half * cosine_table + front_half * sine_table,
        ],
        axis=1,
    )


def block_masks(index, pieces, piece_rows, step_rows):
    key = lax.broadcasted_iota(jnp.int32, (BLOCK, GROUP * BLOCK), 0)
    query = lax.broadcasted_iota(jnp.int32, (BLOCK, GROUP * BLOCK), 1) & (BLOCK - 1)

    def place(row, piece):
        return (row // piece_rows) * step_rows + piece * piece_rows + (row & (piece_rows - 1))

    return [place(key, index ^ k) <= place(query, index) for k in range(pieces)]


def heads_beside(block, first, count):
    return jnp.concatenate(
        [block[h * HD : (h + 1) * HD, first : first + count] for h in range(GROUP)], axis=1
    )


def mask_tail(values, mask, first):
    tail = jnp.where(mask, values[first:], 0.0)
    if first == 0:
        return tail
    return jnp.concatenate([values[:first], tail], axis=0)


def attend_kernel(index_ref, q_ref, k_ref, v_ref, out_ref, lse_ref, *, pieces, piece_rows, step_rows):
    rows = q_ref.shape[1]
    masks = block_masks(index_ref[0], pieces, piece_rows, step_rows)
    queries = q_ref[...]
    for first in range(0, rows, BLOCK):
        count = first + BLOCK
        query_block = heads_beside(queries, first, BLOCK)
        total = None
        result = None
        for k in range(pieces):
            spot = pl.ds(k * rows, count)
            scores = dot(k_ref[:, spot], query_block, 0, 0)
            weights = mask_tail(jnp.exp2(scores * (SCALE * LOG2E)), masks[k], first)
            part = jnp.sum(weights, axis=0, keepdims=True)
            value = dot(v_ref[:, spot], weights.astype(BF16), 1, 0)
            total = part if total is None else total + part
            result = value if result is None else result + value
        result = result * (1.0 / total)
        log_total = jnp.log2(total)
        for h in range(GROUP):
            columns = slice(h * BLOCK, (h + 1) * BLOCK)
            out_ref[h * HD : (h + 1) * HD, first : first + BLOCK] = result[:, columns].astype(BF16)
            lse_ref[0, h : h + 1, first : first + BLOCK] = log_total[:, columns]


def attend_back_kernel(
    index_ref, q_ref, k_ref, v_ref, out_ref, lse_ref, grad_ref, dq_ref, dk_ref, dv_ref,
    *, pieces, piece_rows, step_rows
):
    rows = q_ref.shape[1]
    masks = block_masks(index_ref[0], pieces, piece_rows, step_rows)
    queries = q_ref[...]
    grads = grad_ref[...]
    results = out_ref[...]
    dk_ref[...] = jnp.zeros_like(dk_ref)
    dv_ref[...] = jnp.zeros_like(dv_ref)
    for first in range(0, rows, BLOCK):
        count = first + BLOCK
        query_block = heads_beside(queries, first, BLOCK)
        grad_block = heads_beside(grads, first, BLOCK)
        result_block = heads_beside(results, first, BLOCK)
        centre = jnp.sum(
            grad_block.astype(F32) * result_block.astype(F32), axis=0, keepdims=True
        )
        log_total = jnp.concatenate(
            [lse_ref[0, h : h + 1, first : first + BLOCK] for h in range(GROUP)], axis=1
        )
        dq = None
        for k in range(pieces):
            spot = pl.ds(k * rows, count)
            keys = k_ref[:, spot]
            scores = dot(keys, query_block, 0, 0)
            weights = mask_tail(
                jnp.exp2(scores * (SCALE * LOG2E) - log_total), masks[k], first
            )
            grad_weights = dot(v_ref[:, spot], grad_block, 0, 0)
            grad_scores = (weights * (grad_weights - centre)).astype(BF16)
            part = dot(keys, grad_scores, 1, 0)
            dq = part if dq is None else dq + part
            dk_ref[:, spot] += dot(query_block, grad_scores, 1, 1) * SCALE
            dv_ref[:, spot] += dot(grad_block, weights.astype(BF16), 1, 1)
        dq = (dq * SCALE).astype(BF16)
        for h in range(GROUP):
            columns = slice(h * BLOCK, (h + 1) * BLOCK)
            dq_ref[h * HD : (h + 1) * HD, first : first + BLOCK] = dq[:, columns]


def attention_specs(rows, total_rows):
    group_spec = pl.BlockSpec((GROUP * HD, rows), lambda i: (i, 0))
    pair_spec = pl.BlockSpec((HD, total_rows), lambda i: (i, 0))
    lse_spec = pl.BlockSpec((1, GROUP, rows), lambda i: (i, 0, 0))
    return group_spec, pair_spec, lse_spec


def attend(index, queries, keys, values, pieces, piece_rows, step_rows):
    rows, total_rows = queries.shape[1], keys.shape[1]
    group_spec, pair_spec, lse_spec = attention_specs(rows, total_rows)
    return pl.pallas_call(
        functools.partial(
            attend_kernel, pieces=pieces, piece_rows=piece_rows, step_rows=step_rows
        ),
        grid=(KVH,),
        in_specs=[pl.BlockSpec(memory_space=pltpu.SMEM), group_spec, pair_spec, pair_spec],
        out_specs=[group_spec, lse_spec],
        out_shape=[
            jax.ShapeDtypeStruct((HQ * HD, rows), BF16),
            jax.ShapeDtypeStruct((KVH, GROUP, rows), F32),
        ],
        compiler_params=pltpu.CompilerParams(vmem_limit_bytes=VMEM_LIMIT),
        cost_estimate=pl.CostEstimate(
            flops=4 * HQ * HD * rows * total_rows,
            bytes_accessed=8 * HQ * HD * rows,
            transcendentals=HQ * rows * total_rows,
        ),
        name="attend",
    )(index, queries, keys, values)


def attend_back(index, queries, keys, values, results, lse, grads, pieces, piece_rows, step_rows):
    rows, total_rows = queries.shape[1], keys.shape[1]
    group_spec, pair_spec, lse_spec = attention_specs(rows, total_rows)
    return pl.pallas_call(
        functools.partial(
            attend_back_kernel, pieces=pieces, piece_rows=piece_rows, step_rows=step_rows
        ),
        grid=(KVH,),
        in_specs=[
            pl.BlockSpec(memory_space=pltpu.SMEM),
            group_spec,
            pair_spec,
            pair_spec,
            group_spec,
            lse_spec,
            group_spec,
        ],
        out_specs=[group_spec, pair_spec, pair_spec],
        out_shape=[
            jax.ShapeDtypeStruct((HQ * HD, rows), BF16),
            jax.ShapeDtypeStruct((KVH * HD, total_rows), F32),
            jax.ShapeDtypeStruct((KVH * HD, total_rows), F32),
        ],
        compiler_params=pltpu.CompilerParams(vmem_limit_bytes=VMEM_LIMIT),
        cost_estimate=pl.CostEstimate(
            flops=10 * HQ * HD * rows * total_rows,
            bytes_accessed=16 * HQ * HD * rows,
            transcendentals=HQ * rows * total_rows,
        ),
        name="attend_back",
    )(index, queries, keys, values, results, lse, grads)


def hidden_kernel(x_ref, c_ref, gate_ref, up_ref, down_ref, hidden_ref, grad_gate_ref, grad_up_ref):
    x = x_ref[...]
    gate = dot(x, gate_ref[...], 1, 0)
    up = dot(x, up_ref[...], 1, 0)
    grad_hidden = dot(c_ref[...], down_ref[...], 1, 1)
    sigmoid = 1.0 / (1.0 + jnp.exp(-gate))
    silu = gate * sigmoid
    hidden_ref[...] = (silu * up).astype(BF16)
    grad_up_ref[...] = (grad_hidden * silu).astype(BF16)
    grad_gate_ref[...] = (grad_hidden * up * sigmoid * (1.0 + gate * (1.0 - sigmoid))).astype(BF16)


def hidden_step(x, c, gate_w, up_w, w_down, half, width):
    count, depth = x.shape
    tile = min(512, count)
    rows = pl.BlockSpec((tile, depth), lambda i: (i, 0))
    columns = pl.BlockSpec((depth, width), lambda i: (0, 0))
    result = pl.BlockSpec((tile, width), lambda i: (i, 0))
    return pl.pallas_call(
        hidden_kernel,
        grid=(count // tile,),
        in_specs=[
            rows,
            rows,
            columns,
            columns,
            pl.BlockSpec((width, depth), lambda i: (half, 0)),
        ],
        out_specs=[result] * 3,
        out_shape=[jax.ShapeDtypeStruct((count, width), BF16)] * 3,
        compiler_params=pltpu.CompilerParams(vmem_limit_bytes=VMEM_LIMIT),
        cost_estimate=pl.CostEstimate(
            flops=6 * count * depth * width,
            bytes_accessed=4 * count * depth + 6 * count * width + 6 * depth * width,
            transcendentals=count * width,
        ),
        name="hidden_step",
    )(x, c, gate_w, up_w, w_down)


def pack_kernel(even_ref, first_ref, second_ref, result_ref):
    chosen = jnp.where(even_ref[0] > 0, first_ref[...], second_ref[...])
    width = result_ref.shape[-1]
    for h in range(HALVES):
        result_ref[0, h] = chosen[:, h * width : (h + 1) * width]


def pack_columns(even, first, second, parts):
    rows, columns = first.shape
    width = columns // parts
    block = pl.BlockSpec((rows, width), lambda i: (0, i))
    half = width // HALVES
    return pl.pallas_call(
        pack_kernel,
        grid=(parts,),
        in_specs=[pl.BlockSpec(memory_space=pltpu.SMEM), block, block],
        out_specs=pl.BlockSpec((1, HALVES, rows, half), lambda i: (i, 0, 0, 0)),
        out_shape=jax.ShapeDtypeStruct((parts, HALVES, rows, half), BF16),
        compiler_params=pltpu.CompilerParams(vmem_limit_bytes=VMEM_LIMIT),
        cost_estimate=pl.CostEstimate(
            flops=0, bytes_accessed=6 * rows * columns, transcendentals=0
        ),
        name="pack_columns",
    )(even.astype(jnp.int32).reshape(1), first, second)


def unpack_kernel(*refs):
    result_ref = refs[-1]
    width = refs[0].shape[-1]
    for h in range(HALVES):
        result_ref[:, h * width : (h + 1) * width] = refs[h][0].astype(F32)


def unpack_columns(pieces):
    parts, rows, half = pieces[0].shape
    return pl.pallas_call(
        unpack_kernel,
        grid=(parts,),
        in_specs=[pl.BlockSpec((1, rows, half), lambda i: (i, 0, 0))] * HALVES,
        out_specs=pl.BlockSpec((rows, HALVES * half), lambda i: (0, i)),
        out_shape=jax.ShapeDtypeStruct((rows, parts * HALVES * half), F32),
        compiler_params=pltpu.CompilerParams(vmem_limit_bytes=VMEM_LIMIT),
        cost_estimate=pl.CostEstimate(
            flops=0, bytes_accessed=6 * parts * rows * HALVES * half, transcendentals=0
        ),
        name="unpack_columns",
    )(*pieces)


def sum_kernel(*refs, right_dim):
    half = len(refs) // 2
    result_ref = refs[-1]
    total = None
    for left_ref, right_ref in zip(refs[:half], refs[half:-1]):
        part = dot(left_ref[...], right_ref[...], 1, right_dim)
        total = part if total is None else total + part
    result_ref[...] = total.astype(BF16)


def sum_of_products(lefts, rights, right_dim, name):
    count, width = lefts[0].shape
    depth = D
    tile = min(512, count)
    column = min(1024, depth)
    left = pl.BlockSpec((tile, width), lambda j, i: (i, 0))

    def right(block):
        if right_dim == 1:
            return pl.BlockSpec((column, width), lambda j, i: (j, 0))
        return pl.BlockSpec((width, column), lambda j, i: (block, j))

    return pl.pallas_call(
        functools.partial(sum_kernel, right_dim=right_dim),
        grid=(depth // column, count // tile),
        in_specs=[left] * len(lefts) + [right(block) for _, block in rights],
        out_specs=pl.BlockSpec((tile, column), lambda j, i: (i, j)),
        out_shape=jax.ShapeDtypeStruct((count, depth), BF16),
        compiler_params=pltpu.CompilerParams(vmem_limit_bytes=VMEM_LIMIT),
        cost_estimate=pl.CostEstimate(
            flops=2 * count * depth * width * len(lefts),
            bytes_accessed=2 * (count * width * len(lefts) * 2 + count * depth),
            transcendentals=0,
        ),
        name=name,
    )(*lefts, *[array for array, _ in rights])


class Layout:
    def __init__(self, fsdp_devices, seq_devices, rows_dev):
        self.fsdp = fsdp_devices
        self.seq = seq_devices
        self.chips = fsdp_devices // 2
        self.share = 2 * seq_devices // (2 * MICRO)
        self.near = self.share // 2
        self.piece_rows = rows_dev // self.share
        self.step_rows = rows_dev
        self.rows = LENGTH // self.share

    def flat(self, f, z):
        return f * self.seq + z

    def moved(self, r):
        pairs = []
        for f in range(self.fsdp):
            for z in range(self.seq):
                slot = z ^ r
                micro, j = slot // self.share, slot % self.share
                target_f = (f // 2) * 2 + j % 2
                target_z = (2 * micro + f % 2) * self.near + j // 2
                pairs.append((self.flat(f, z), self.flat(target_f, target_z)))
        return pairs

    def across(self, k):
        pairs = []
        for f in range(self.fsdp):
            for z in range(self.seq):
                pairs.append((self.flat(f, z), self.flat(f ^ (k & 1), z ^ (k >> 1))))
        return pairs


def permute(value, pairs):
    return lax.ppermute(value, ("fsdp", "seq"), pairs)


def scatter_rows(layout, values, z, slot):
    parts = values.reshape(layout.seq, layout.piece_rows, values.shape[-1])
    result = jnp.zeros_like(parts)
    for r in range(layout.seq):
        sent = lax.dynamic_index_in_dim(parts, z ^ r, 0, keepdims=False)
        got = permute(sent, layout.moved(r))
        result = lax.dynamic_update_index_in_dim(result, got, slot ^ r, 0)
    return result.reshape(layout.rows, values.shape[-1])


def return_rows(layout, values, z, slot):
    parts = values.reshape(layout.seq, layout.piece_rows, values.shape[-1])
    result = jnp.zeros_like(parts)
    for r in range(layout.seq):
        sent = lax.dynamic_index_in_dim(parts, slot ^ r, 0, keepdims=False)
        got = permute(sent, [(b, a) for a, b in layout.moved(r)])
        result = lax.dynamic_update_index_in_dim(result, got, z ^ r, 0)
    return result.reshape(MICRO, layout.step_rows, values.shape[-1])


class LinePipe:
    def __init__(self, z, seq_devices):
        self.z = z
        self.seq = seq_devices
        self.flying = []
        self.results = {}

    def advance(self, stage, value):
        half, last = self.seq // 2, self.seq - 1
        if stage < half - 1:
            s = stage
            got = lax.ppermute(value, "seq", [(s, s + 1), (last - s, last - s - 1)])
            return (value.astype(F32) + got.astype(F32)).astype(BF16)
        if stage == half - 1:
            got = lax.ppermute(value, "seq", [(half - 1, half), (half, half - 1)])
            return (value.astype(F32) + got.astype(F32)).astype(BF16)
        s = last - 1 - stage
        got = lax.ppermute(value, "seq", [(s + 1, s), (last - s - 1, last - s)])
        return jnp.where((self.z == s) | (self.z == last - s), got, value)

    def step(self, name=None, value=None, others=()):
        if name is not None:
            self.flying.append((name, 0, value))
        held, self.results, others = lax.optimization_barrier(
            ([entry[2] for entry in self.flying], self.results, others)
        )
        flying = []
        for (key, stage, _), operand in zip(self.flying, held):
            moved = self.advance(stage, operand)
            if stage == self.seq - 2:
                self.results[key] = moved
            else:
                flying.append((key, stage + 1, moved))
        self.flying = flying
        return others

    def finish(self):
        while self.flying:
            self.step()


def body(
    tokens,
    cotangent,
    attn_gain,
    query_gain,
    key_gain,
    w_query,
    w_key,
    w_value,
    w_out,
    ffn_gain,
    w_gate,
    w_up,
    w_down,
):
    fsdp_devices = lax.axis_size("fsdp")
    seq_devices = lax.axis_size("seq")
    layout = Layout(fsdp_devices, seq_devices, tokens.shape[2])
    f = lax.axis_index("fsdp")
    z = lax.axis_index("seq")
    rows = layout.rows
    share = layout.share
    member = (z % layout.near) * 2 + f % 2
    slot = (z // layout.near // 2) * share + member

    w_attn = lax.all_gather(
        jnp.concatenate([w_query, w_key, w_value], axis=1), "fsdp", axis=0, tiled=True
    )
    gains = lax.all_gather(
        jnp.concatenate([attn_gain, ffn_gain, query_gain, key_gain]), "fsdp", axis=0, tiled=False
    ).astype(F32)
    wide, narrow = attn_gain.shape[0], query_gain.shape[0]
    full_attn_gain = gains[:, :wide].reshape(D)
    full_ffn_gain = gains[:, wide : 2 * wide].reshape(D)
    full_query_gain = gains[:, 2 * wide : 2 * wide + narrow].reshape(HD)
    full_key_gain = gains[:, 2 * wide + narrow :].reshape(HD)
    inputs_low = scatter_rows(layout, tokens[:, 0], z, slot)
    grad_out_low = scatter_rows(layout, cotangent[:, 0], z, slot)
    full_out = lax.all_gather(w_out, "fsdp", axis=0, tiled=True)

    row = jnp.arange(rows, dtype=jnp.int32)
    position = (
        (row // layout.piece_rows) * layout.step_rows
        + member * layout.piece_rows
        + row % layout.piece_rows
    ).astype(F32)
    frequency = THETA ** (-(jnp.arange(HD // 2).astype(F32) * 2.0 / HD))
    angles = frequency[:, None] * position[None, :]
    cosine_table, sine_table = jnp.cos(angles)[None], jnp.sin(angles)[None]
    head_gains = jnp.concatenate(
        [
            jnp.broadcast_to(full_query_gain[None, :, None], (HQ, HD, 1)),
            jnp.broadcast_to(full_key_gain[None, :, None], (KVH, HD, 1)),
        ]
    )

    inputs = inputs_low.astype(F32)
    normed, normed_unit, normed_inverse = rms_fwd(inputs, full_attn_gain)
    even = z % 2 == 0
    hidden_dev = w_down.shape[0]
    half_width = hidden_dev // HALVES
    fetched = lax.all_to_all(
        pack_columns(even, w_gate, w_up, fsdp_devices),
        "fsdp",
        split_axis=0,
        concat_axis=0,
        tiled=True,
    )
    normed_low, grad_out_low, w_attn, fetched = lax.optimization_barrier(
        (normed.astype(BF16), grad_out_low, w_attn, fetched)
    )
    grad_out_rows = lax.all_gather(grad_out_low, "fsdp", axis=0, tiled=True)
    raw = dot(w_attn, normed_low, 0, 1)
    pair_width = KVH * HD
    turned = HQ + KVH
    head_raw = raw[: turned * HD].reshape(turned, HD, rows)
    head_normed, head_unit, head_inverse = head_rms_fwd(head_raw, head_gains)
    heads_low = rotate(head_normed, cosine_table, sine_table).astype(BF16).reshape(turned * HD, rows)
    queries = heads_low[: HQ * HD]
    own_pair = jnp.concatenate([heads_low[HQ * HD :], raw[turned * HD :].astype(BF16)], axis=0)
    pair_pieces = [own_pair] + [permute(own_pair, layout.across(k)) for k in range(1, share)]
    keys = jnp.concatenate([piece[:pair_width] for piece in pair_pieces], axis=1)
    values = jnp.concatenate([piece[pair_width:] for piece in pair_pieces], axis=1)
    index = member.astype(jnp.int32).reshape(1)
    fetched = [fetched[:, h].reshape(D, half_width) for h in range(HALVES)]
    swapped = [
        lax.ppermute(fetched[h], "seq", [(i, i ^ 1) for i in range(seq_devices)])
        for h in range(HALVES)
    ]
    attended, log_totals = attend(
        index, queries, keys, values, share, layout.piece_rows, layout.step_rows
    )
    attended, swapped[0] = lax.optimization_barrier((attended, swapped[0]))
    middle = inputs + dot(attended, full_out, 0, 0)
    ffn_normed, ffn_unit, ffn_inverse = rms_fwd(middle, full_ffn_gain)
    ffn_low = ffn_normed.astype(BF16)

    ffn_rows = lax.all_gather(ffn_low, "fsdp", axis=0, tiled=True)
    line = LinePipe(z, seq_devices)
    gate_w = [jnp.where(even, fetched[h], swapped[h]) for h in range(HALVES)]
    up_w = [jnp.where(even, swapped[h], fetched[h]) for h in range(HALVES)]

    def hidden_of(h):
        return hidden_step(
            ffn_rows, grad_out_rows, gate_w[h], up_w[h], w_down, h, half_width
        )

    def to_owners(term):
        return lax.all_to_all(
            term.reshape(fsdp_devices, wide, half_width),
            "fsdp",
            split_axis=0,
            concat_axis=0,
            tiled=True,
        )

    first = hidden_of(0)
    down_0 = dot(first[0], grad_out_rows, 0, 0).astype(BF16)
    first, ffn_rows = line.step("down0", down_0, (first, ffn_rows))
    gate_0 = to_owners(dot(ffn_rows, first[1], 0, 0).astype(BF16))
    up_0 = to_owners(dot(ffn_rows, first[2], 0, 0).astype(BF16))
    gate_0, up_0, ffn_rows = lax.optimization_barrier((gate_0, up_0, ffn_rows))
    second = hidden_of(1)
    second, first = line.step("gate0", gate_0, (second, first))
    grad_ffn_part = sum_of_products(
        [first[1], first[2], second[1], second[2]],
        [(gate_w[0], 0), (up_w[0], 0), (gate_w[1], 0), (up_w[1], 0)],
        1,
        "grad_ffn_normed",
    )
    grad_ffn_part, second, first = line.step("up0", up_0, (grad_ffn_part, second, first))
    grad_ffn_normed = lax.psum_scatter(
        grad_ffn_part, "fsdp", scatter_dimension=0, tiled=True
    )
    down_1 = dot(second[0], grad_out_rows, 0, 0).astype(BF16)
    gate_1 = to_owners(dot(ffn_rows, second[1], 0, 0).astype(BF16))
    up_1 = to_owners(dot(ffn_rows, second[2], 0, 0).astype(BF16))
    first, second, up_1, gate_1 = line.step("down1", down_1, (first, second, up_1, gate_1))
    out_part = sum_of_products(
        [first[0], second[0]], [(w_down, 0), (w_down, 1)], 0, "block_out"
    )
    out_sum = lax.psum_scatter(out_part, "fsdp", scatter_dimension=0, tiled=True)
    grad_ffn_normed, up_1 = line.step("gate1", gate_1, (grad_ffn_normed, up_1))
    grad_ffn_normed = grad_ffn_normed.astype(F32)

    grad_middle_norm, ffn_gain_term = rms_back(
        grad_ffn_normed, ffn_unit, ffn_inverse, full_ffn_gain
    )
    grad_middle = grad_out_low.astype(F32) + grad_middle_norm
    grad_branch_low = grad_middle.astype(BF16)
    grad_attended = dot(full_out, grad_branch_low, 1, 1).astype(BF16)
    out_term = dot(attended, grad_branch_low, 1, 0).astype(BF16)
    out_rows = lax.psum_scatter(out_term, "fsdp", scatter_dimension=0, tiled=True)
    grad_queries, grad_keys, grad_values = attend_back(
        index,
        queries,
        keys,
        values,
        attended,
        log_totals,
        grad_attended,
        share,
        layout.piece_rows,
        layout.step_rows,
    )
    grad_queries, grad_keys, grad_values = line.step(
        "up1", up_1, (grad_queries, grad_keys, grad_values)
    )
    grad_pair = jnp.concatenate([grad_keys[:, :rows], grad_values[:, :rows]], axis=0)
    for k in range(1, share):
        columns = slice(k * rows, (k + 1) * rows)
        sent = jnp.concatenate([grad_keys[:, columns], grad_values[:, columns]], axis=0)
        grad_pair = grad_pair + permute(sent.astype(BF16), layout.across(k)).astype(F32)
    grad_pair_low = grad_pair.astype(BF16)
    grad_turned = (
        jnp.concatenate([grad_queries, grad_pair_low[:pair_width]], axis=0)
        .astype(F32)
        .reshape(turned, HD, rows)
    )
    grad_head_normed = rotate(grad_turned, cosine_table, -sine_table)
    scaled = grad_head_normed * head_gains
    grad_head_raw = head_inverse * (
        scaled - head_unit * jnp.mean(scaled * head_unit, axis=1, keepdims=True)
    )
    head_gain_terms = jnp.sum(grad_head_normed * head_unit, axis=2)
    grad_raw = jnp.concatenate(
        [grad_head_raw.astype(BF16).reshape(turned * HD, rows), grad_pair_low[pair_width:]], axis=0
    )
    projection_term = dot(normed_low, grad_raw, 0, 1).astype(BF16)
    projection_term, grad_raw = lax.optimization_barrier((projection_term, grad_raw))
    projection_rows = lax.psum_scatter(
        projection_term, "fsdp", scatter_dimension=0, tiled=True
    )
    grad_raw, out_sum = line.step("out", out_rows, (grad_raw, out_sum))
    block_out = return_rows(layout, (middle + out_sum.astype(F32)).astype(BF16), z, slot)
    grad_normed = dot(grad_raw, w_attn, 0, 1)
    grad_input_norm, attn_gain_term = rms_back(
        grad_normed, normed_unit, normed_inverse, full_attn_gain
    )

    def column(vector):
        spread = vector.reshape(fsdp_devices, -1)
        return jnp.pad(spread, ((0, 0), (0, wide - spread.shape[1]))).reshape(D)

    gain_terms = jnp.stack(
        [
            attn_gain_term,
            ffn_gain_term,
            column(jnp.sum(head_gain_terms[:HQ], axis=0)),
            column(jnp.sum(head_gain_terms[HQ:], axis=0)),
        ],
        axis=1,
    )
    gain_terms = jnp.pad(gain_terms, ((0, 0), (0, 128 - gain_terms.shape[1]))).astype(BF16)
    gain_rows = lax.psum_scatter(gain_terms, "fsdp", scatter_dimension=0, tiled=True)
    tokens_grad_low, block_out, gain_rows = line.step(
        "attn",
        projection_rows,
        ((grad_middle + grad_input_norm).astype(BF16), block_out, gain_rows),
    )
    tokens_grad = return_rows(layout, tokens_grad_low, z, slot)
    line.step("gain", gain_rows)
    line.finish()

    w_down_grad = jnp.concatenate([line.results[f"down{h}"] for h in range(HALVES)]).astype(F32)
    w_gate_grad = unpack_columns([line.results[f"gate{h}"] for h in range(HALVES)])
    w_up_grad = unpack_columns([line.results[f"up{h}"] for h in range(HALVES)])
    w_out_grad = line.results["out"].astype(F32)
    attn_rows = line.results["attn"].astype(F32)
    gain_rows = line.results["gain"].astype(F32)
    query_width = HQ * HD

    return (
        block_out[:, None],
        tokens_grad[:, None],
        gain_rows[:, 0],
        gain_rows[:narrow, 2],
        gain_rows[:narrow, 3],
        attn_rows[:, :query_width],
        attn_rows[:, query_width : query_width + pair_width],
        attn_rows[:, query_width + pair_width :],
        w_out_grad,
        gain_rows[:, 1],
        w_gate_grad,
        w_up_grad,
        w_down_grad,
    )


def solution(mesh):
    activations = P(None, "fsdp", "seq", None)
    vector = P("fsdp")
    matrix = P("fsdp", None)
    specs = (
        (activations, activations)
        + (vector,) * 3
        + (matrix,) * 4
        + (vector,)
        + (matrix,) * 3
    )
    return jax.shard_map(body, mesh=mesh, in_specs=specs, out_specs=specs, check_vma=False)
```

```python
import functools
import math

import jax
import jax.numpy as jnp
from jax import lax
from jax.experimental import pallas as pl
from jax.experimental.pallas import tpu as pltpu
from jax.sharding import PartitionSpec as P

D = 2048
HQ = 32
KVH = 8
HD = 64
FF = 8192
LENGTH = 1024
MICRO = 2
HALVES = 2

EPSILON = 1e-05
THETA = 1000000.0
GROUP = HQ // KVH
BLOCK = 128
SCALE = 1.0 / math.sqrt(HD)
LOG2E = math.log2(math.e)
VMEM_LIMIT = 56 * 1024 * 1024

F32 = jnp.float32
BF16 = jnp.bfloat16


def dot(left_side, right_side, left_dim, right_dim):
    return lax.dot_general(
        left_side,
        right_side,
        (((left_dim,), (right_dim,)), ((), ())),
        preferred_element_type=F32,
    )


def rms_fwd(values, row_gain):
    inverse = lax.rsqrt(jnp.mean(values * values, axis=-1, keepdims=True) + EPSILON)
    unit_rows = values * inverse
    return (unit_rows * row_gain, unit_rows, inverse)


def rms_back(grad_outputs, unit_rows, inverse, row_gain):
    scaled = grad_outputs * row_gain
    grad_inputs = inverse * (
        scaled - unit_rows * jnp.mean(scaled * unit_rows, axis=-1, keepdims=True)
    )
    grad_gain = jnp.sum(grad_outputs * unit_rows, axis=0)
    return (grad_inputs, grad_gain)


def head_rms_fwd(values, gains):
    inverse = lax.rsqrt(jnp.mean(values * values, axis=1, keepdims=True) + EPSILON)
    unit = values * inverse
    return (unit * gains, unit, inverse)


def rotate(values, cosine_table, sine_table):
    half_width = values.shape[1] // 2
    front_half = values[:, :half_width]
    back_half = values[:, half_width:]
    return jnp.concatenate(
        [
            front_half * cosine_table - back_half * sine_table,
            back_half * cosine_table + front_half * sine_table,
        ],
        axis=1,
    )


def block_masks(index, pieces, piece_rows, step_rows):
    key = lax.broadcasted_iota(jnp.int32, (BLOCK, GROUP * BLOCK), 0)
    query = lax.broadcasted_iota(jnp.int32, (BLOCK, GROUP * BLOCK), 1) & (BLOCK - 1)

    def place(row, piece):
        return (row // piece_rows) * step_rows + piece * piece_rows + (row & (piece_rows - 1))

    return [place(key, index ^ k) <= place(query, index) for k in range(pieces)]


def heads_beside(block, first, count):
    return jnp.concatenate(
        [block[h * HD : (h + 1) * HD, first : first + count] for h in range(GROUP)], axis=1
    )


def mask_tail(values, mask, first):
    tail = jnp.where(mask, values[first:], 0.0)
    if first == 0:
        return tail
    return jnp.concatenate([values[:first], tail], axis=0)


def attend_kernel(index_ref, q_ref, k_ref, v_ref, out_ref, lse_ref, *, pieces, piece_rows, step_rows):
    rows = q_ref.shape[1]
    masks = block_masks(index_ref[0], pieces, piece_rows, step_rows)
    queries = q_ref[...]
    for first in range(0, rows, BLOCK):
        count = first + BLOCK
        query_block = heads_beside(queries, first, BLOCK)
        total = None
        result = None
        for k in range(pieces):
            spot = pl.ds(k * rows, count)
            scores = dot(k_ref[:, spot], query_block, 0, 0)
            weights = mask_tail(jnp.exp2(scores * (SCALE * LOG2E)), masks[k], first)
            part = jnp.sum(weights, axis=0, keepdims=True)
            value = dot(v_ref[:, spot], weights.astype(BF16), 1, 0)
            total = part if total is None else total + part
            result = value if result is None else result + value
        result = result * (1.0 / total)
        log_total = jnp.log2(total)
        for h in range(GROUP):
            columns = slice(h * BLOCK, (h + 1) * BLOCK)
            out_ref[h * HD : (h + 1) * HD, first : first + BLOCK] = result[:, columns].astype(BF16)
            lse_ref[0, h : h + 1, first : first + BLOCK] = log_total[:, columns]


def attend_back_kernel(
    index_ref, q_ref, k_ref, v_ref, out_ref, lse_ref, grad_ref, dq_ref, dk_ref, dv_ref,
    *, pieces, piece_rows, step_rows
):
    rows = q_ref.shape[1]
    masks = block_masks(index_ref[0], pieces, piece_rows, step_rows)
    queries = q_ref[...]
    grads = grad_ref[...]
    results = out_ref[...]
    dk_ref[...] = jnp.zeros_like(dk_ref)
    dv_ref[...] = jnp.zeros_like(dv_ref)
    for first in range(0, rows, BLOCK):
        count = first + BLOCK
        query_block = heads_beside(queries, first, BLOCK)
        grad_block = heads_beside(grads, first, BLOCK)
        result_block = heads_beside(results, first, BLOCK)
        centre = jnp.sum(
            grad_block.astype(F32) * result_block.astype(F32), axis=0, keepdims=True
        )
        log_total = jnp.concatenate(
            [lse_ref[0, h : h + 1, first : first + BLOCK] for h in range(GROUP)], axis=1
        )
        dq = None
        for k in range(pieces):
            spot = pl.ds(k * rows, count)
            keys = k_ref[:, spot]
            scores = dot(keys, query_block, 0, 0)
            weights = mask_tail(
                jnp.exp2(scores * (SCALE * LOG2E) - log_total), masks[k], first
            )
            grad_weights = dot(v_ref[:, spot], grad_block, 0, 0)
            grad_scores = (weights * (grad_weights - centre)).astype(BF16)
            part = dot(keys, grad_scores, 1, 0)
            dq = part if dq is None else dq + part
            dk_ref[:, spot] += dot(query_block, grad_scores, 1, 1) * SCALE
            dv_ref[:, spot] += dot(grad_block, weights.astype(BF16), 1, 1)
        dq = (dq * SCALE).astype(BF16)
        for h in range(GROUP):
            columns = slice(h * BLOCK, (h + 1) * BLOCK)
            dq_ref[h * HD : (h + 1) * HD, first : first + BLOCK] = dq[:, columns]


def attention_specs(rows, total_rows):
    group_spec = pl.BlockSpec((GROUP * HD, rows), lambda i: (i, 0))
    pair_spec = pl.BlockSpec((HD, total_rows), lambda i: (i, 0))
    lse_spec = pl.BlockSpec((1, GROUP, rows), lambda i: (i, 0, 0))
    return group_spec, pair_spec, lse_spec


def attend(index, queries, keys, values, pieces, piece_rows, step_rows):
    rows, total_rows = queries.shape[1], keys.shape[1]
    group_spec, pair_spec, lse_spec = attention_specs(rows, total_rows)
    return pl.pallas_call(
        functools.partial(
            attend_kernel, pieces=pieces, piece_rows=piece_rows, step_rows=step_rows
        ),
        grid=(KVH,),
        in_specs=[pl.BlockSpec(memory_space=pltpu.SMEM), group_spec, pair_spec, pair_spec],
        out_specs=[group_spec, lse_spec],
        out_shape=[
            jax.ShapeDtypeStruct((HQ * HD, rows), BF16),
            jax.ShapeDtypeStruct((KVH, GROUP, rows), F32),
        ],
        compiler_params=pltpu.CompilerParams(vmem_limit_bytes=VMEM_LIMIT),
        cost_estimate=pl.CostEstimate(
            flops=4 * HQ * HD * rows * total_rows,
            bytes_accessed=8 * HQ * HD * rows,
            transcendentals=HQ * rows * total_rows,
        ),
        name="attend",
    )(index, queries, keys, values)


def attend_back(index, queries, keys, values, results, lse, grads, pieces, piece_rows, step_rows):
    rows, total_rows = queries.shape[1], keys.shape[1]
    group_spec, pair_spec, lse_spec = attention_specs(rows, total_rows)
    return pl.pallas_call(
        functools.partial(
            attend_back_kernel, pieces=pieces, piece_rows=piece_rows, step_rows=step_rows
        ),
        grid=(KVH,),
        in_specs=[
            pl.BlockSpec(memory_space=pltpu.SMEM),
            group_spec,
            pair_spec,
            pair_spec,
            group_spec,
            lse_spec,
            group_spec,
        ],
        out_specs=[group_spec, pair_spec, pair_spec],
        out_shape=[
            jax.ShapeDtypeStruct((HQ * HD, rows), BF16),
            jax.ShapeDtypeStruct((KVH * HD, total_rows), F32),
            jax.ShapeDtypeStruct((KVH * HD, total_rows), F32),
        ],
        compiler_params=pltpu.CompilerParams(vmem_limit_bytes=VMEM_LIMIT),
        cost_estimate=pl.CostEstimate(
            flops=10 * HQ * HD * rows * total_rows,
            bytes_accessed=16 * HQ * HD * rows,
            transcendentals=HQ * rows * total_rows,
        ),
        name="attend_back",
    )(index, queries, keys, values, results, lse, grads)


def hidden_kernel(x_ref, c_ref, *refs):
    gate_refs, up_refs = refs[:HALVES], refs[HALVES : 2 * HALVES]
    down_ref = refs[2 * HALVES]
    hidden_ref, grad_gate_ref, grad_up_ref, hidden_t_ref, grad_gate_t_ref, grad_up_t_ref = refs[
        2 * HALVES + 1 :
    ]
    x = x_ref[...]
    c = c_ref[...]
    width = gate_refs[0].shape[1]
    for h in range(HALVES):
        part = slice(h * width, (h + 1) * width)
        gate = dot(x, gate_refs[h][...], 1, 0)
        up = dot(x, up_refs[h][...], 1, 0)
        grad_hidden = dot(c, down_ref[part, :], 1, 1)
        sigmoid = 1.0 / (1.0 + jnp.exp(-gate))
        silu = gate * sigmoid
        hidden = (silu * up).astype(BF16)
        grad_up = (grad_hidden * silu).astype(BF16)
        grad_gate = (grad_hidden * up * sigmoid * (1.0 + gate * (1.0 - sigmoid))).astype(BF16)
        hidden_ref[:, part] = hidden
        grad_gate_ref[:, part] = grad_gate
        grad_up_ref[:, part] = grad_up
        hidden_t_ref[part, :] = hidden.T
        grad_gate_t_ref[part, :] = grad_gate.T
        grad_up_t_ref[part, :] = grad_up.T


def hidden_step(x, c, gate_w, up_w, w_down):
    count, depth = x.shape
    width = w_down.shape[0]
    tile = min(512, count)
    rows = pl.BlockSpec((tile, depth), lambda i: (i, 0))
    once = pl.Buffered(1)
    columns = pl.BlockSpec((depth, width // HALVES), lambda i: (0, 0), pipeline_mode=once)
    result = pl.BlockSpec((tile, width), lambda i: (i, 0))
    turned = pl.BlockSpec((width, tile), lambda i: (0, i))
    return pl.pallas_call(
        hidden_kernel,
        grid=(count // tile,),
        in_specs=[rows, rows]
        + [columns] * (2 * HALVES)
        + [pl.BlockSpec((width, depth), lambda i: (0, 0), pipeline_mode=once)],
        out_specs=[result] * 3 + [turned] * 3,
        out_shape=[jax.ShapeDtypeStruct((count, width), BF16)] * 3
        + [jax.ShapeDtypeStruct((width, count), BF16)] * 3,
        compiler_params=pltpu.CompilerParams(vmem_limit_bytes=VMEM_LIMIT),
        cost_estimate=pl.CostEstimate(
            flops=6 * count * depth * width,
            bytes_accessed=4 * count * depth + 12 * count * width + 6 * depth * width,
            transcendentals=count * width,
        ),
        name="hidden_step",
    )(x, c, *gate_w, *up_w, w_down)


def rows_kernel(me_ref, *refs, chunks, starts, terms, right_dim):
    lefts, rights, result_ref = refs[: terms * chunks], refs[terms * chunks : -1], refs[-1]
    i = pl.program_id(1)
    for n in range(chunks):

        @pl.when((i >= starts[n]) & (i < starts[n + 1]))
        def _():
            total = None
            for t in range(terms):
                for h in range(len(rights) // terms):
                    right = rights[t * (len(rights) // terms) + h]
                    width = right.shape[1 - (1 - right_dim)]
                    left = lefts[t * chunks + n][:, h * width : (h + 1) * width]
                    part = dot(left, right[...], 1, right_dim)
                    total = part if total is None else total + part
            result_ref[...] = total.astype(BF16)


def rows_product(me, terms, right_dim, block_rows, name):
    chunks = len(terms[0][0])
    counts = [chunk.shape[0] // block_rows for chunk in terms[0][0]]
    starts = [sum(counts[:n]) for n in range(chunks + 1)]
    width = terms[0][0][0].shape[1]
    column = min(1024, D)

    def left_spec(n):
        first, last = starts[n], starts[n + 1] - 1
        return pl.BlockSpec(
            (block_rows, width),
            lambda j, i, me_ref: (jnp.clip(i, first, last) - first, 0),
        )

    def right_spec(array):
        if right_dim == 1:
            return pl.BlockSpec((column, array.shape[1]), lambda j, i, me_ref: (j, 0))
        return pl.BlockSpec((array.shape[0], column), lambda j, i, me_ref: (0, j))

    lefts = [chunk for left, _ in terms for chunk in left]
    rights = [piece for _, right in terms for piece in right]
    return pl.pallas_call(
        functools.partial(
            rows_kernel, chunks=chunks, starts=starts, terms=len(terms), right_dim=right_dim
        ),
        grid_spec=pltpu.PrefetchScalarGridSpec(
            num_scalar_prefetch=1,
            grid=(D // column, starts[-1]),
            in_specs=[left_spec(n) for _ in terms for n in range(chunks)]
            + [right_spec(piece) for piece in rights],
            out_specs=pl.BlockSpec((block_rows, column), lambda j, i, me_ref: (me_ref[0] ^ i, j)),
        ),
        out_shape=jax.ShapeDtypeStruct((starts[-1] * block_rows, D), BF16),
        compiler_params=pltpu.CompilerParams(vmem_limit_bytes=VMEM_LIMIT),
        cost_estimate=pl.CostEstimate(
            flops=2 * starts[-1] * block_rows * D * width * len(terms),
            bytes_accessed=2 * starts[-1] * block_rows * (2 * width * len(terms) + D),
            transcendentals=0,
        ),
        name=name,
    )(me, *lefts, *rights)


def weight_kernel(*refs, chunks, parts):
    result_ref = refs[-1]
    total = None
    for n in range(chunks):
        part = dot(refs[n][...], refs[chunks + n][...], 1, 0)
        total = part if total is None else total + part
    if parts == 0:
        result_ref[0] = total.astype(BF16)
        return
    wide = total.shape[1] // parts
    for p in range(parts):
        result_ref[0, p] = total[:, p * wide : (p + 1) * wide].T.astype(BF16)


def weight_product(lefts, rights, wide, name):
    chunks = len(lefts)
    half = lefts[0].shape[0] // HALVES
    column = min(1024, D)
    parts = column // wide if wide else 0
    if wide:
        out_spec = pl.BlockSpec((1, parts, wide, half), lambda i, j: (i, j, 0, 0))
        out_shape = jax.ShapeDtypeStruct((HALVES, D // wide, wide, half), BF16)
    else:
        out_spec = pl.BlockSpec((1, half, column), lambda i, j: (i, 0, j))
        out_shape = jax.ShapeDtypeStruct((HALVES, half, D), BF16)
    depth = sum(left.shape[1] for left in lefts)
    return pl.pallas_call(
        functools.partial(weight_kernel, chunks=chunks, parts=parts),
        grid=(HALVES, D // column),
        in_specs=[pl.BlockSpec((half, left.shape[1]), lambda i, j: (i, 0)) for left in lefts]
        + [pl.BlockSpec((right.shape[0], column), lambda i, j: (0, j)) for right in rights],
        out_specs=out_spec,
        out_shape=out_shape,
        compiler_params=pltpu.CompilerParams(vmem_limit_bytes=VMEM_LIMIT),
        cost_estimate=pl.CostEstimate(
            flops=2 * HALVES * half * depth * D,
            bytes_accessed=2 * depth * (2 * HALVES * half + 2 * D) + 2 * HALVES * half * D,
            transcendentals=0,
        ),
        name=name,
    )(*lefts, *rights)


def pack_kernel(even_ref, first_ref, second_ref, result_ref):
    chosen = jnp.where(even_ref[0] > 0, first_ref[...], second_ref[...])
    width = result_ref.shape[-1]
    for h in range(HALVES):
        result_ref[0, h] = chosen[:, h * width : (h + 1) * width]


def pack_columns(even, first, second, parts):
    rows, columns = first.shape
    width = columns // parts
    block = pl.BlockSpec((rows, width), lambda i: (0, i))
    half = width // HALVES
    return pl.pallas_call(
        pack_kernel,
        grid=(parts,),
        in_specs=[pl.BlockSpec(memory_space=pltpu.SMEM), block, block],
        out_specs=pl.BlockSpec((1, HALVES, rows, half), lambda i: (i, 0, 0, 0)),
        out_shape=jax.ShapeDtypeStruct((parts, HALVES, rows, half), BF16),
        compiler_params=pltpu.CompilerParams(vmem_limit_bytes=VMEM_LIMIT),
        cost_estimate=pl.CostEstimate(
            flops=0, bytes_accessed=6 * rows * columns, transcendentals=0
        ),
        name="pack_columns",
    )(even.astype(jnp.int32).reshape(1), first, second)


def unpack_kernel(*refs):
    result_ref = refs[-1]
    width = refs[0].shape[-1]
    for h in range(HALVES):
        result_ref[:, h * width : (h + 1) * width] = refs[h][0].astype(F32)


def unpack_columns(pieces):
    parts, rows, half = pieces[0].shape
    return pl.pallas_call(
        unpack_kernel,
        grid=(parts,),
        in_specs=[pl.BlockSpec((1, rows, half), lambda i: (i, 0, 0))] * HALVES,
        out_specs=pl.BlockSpec((rows, HALVES * half), lambda i: (0, i)),
        out_shape=jax.ShapeDtypeStruct((rows, parts * HALVES * half), F32),
        compiler_params=pltpu.CompilerParams(vmem_limit_bytes=VMEM_LIMIT),
        cost_estimate=pl.CostEstimate(
            flops=0, bytes_accessed=6 * parts * rows * HALVES * half, transcendentals=0
        ),
        name="unpack_columns",
    )(*pieces)


class Layout:
    def __init__(self, fsdp_devices, seq_devices, rows_dev):
        self.fsdp = fsdp_devices
        self.seq = seq_devices
        self.chips = fsdp_devices // 2
        self.share = 2 * seq_devices // (2 * MICRO)
        self.near = self.share // 2
        self.piece_rows = rows_dev // self.share
        self.step_rows = rows_dev
        self.rows = LENGTH // self.share

    def flat(self, f, z):
        return f * self.seq + z

    def moved(self, r):
        pairs = []
        for f in range(self.fsdp):
            for z in range(self.seq):
                slot = z ^ r
                micro, j = slot // self.share, slot % self.share
                target_f = (f // 2) * 2 + j % 2
                target_z = (2 * micro + f % 2) * self.near + j // 2
                pairs.append((self.flat(f, z), self.flat(target_f, target_z)))
        return pairs

    def other(self, k):
        return [
            (self.flat(f, z), self.flat(f ^ k, z))
            for f in range(self.fsdp)
            for z in range(self.seq)
        ]

    def across(self, k):
        pairs = []
        for f in range(self.fsdp):
            for z in range(self.seq):
                pairs.append((self.flat(f, z), self.flat(f ^ (k & 1), z ^ (k >> 1))))
        return pairs


def permute(value, pairs):
    return lax.ppermute(value, ("fsdp", "seq"), pairs)


def scatter_rows(layout, values, z, slot):
    parts = values.reshape(layout.seq, layout.piece_rows, values.shape[-1])
    result = jnp.zeros_like(parts)
    for r in range(layout.seq):
        sent = lax.dynamic_index_in_dim(parts, z ^ r, 0, keepdims=False)
        got = permute(sent, layout.moved(r))
        result = lax.dynamic_update_index_in_dim(result, got, slot ^ r, 0)
    return result.reshape(layout.rows, values.shape[-1])


def return_rows(layout, values, z, slot):
    parts = values.reshape(layout.seq, layout.piece_rows, values.shape[-1])
    result = jnp.zeros_like(parts)
    for r in range(layout.seq):
        sent = lax.dynamic_index_in_dim(parts, slot ^ r, 0, keepdims=False)
        got = permute(sent, [(b, a) for a, b in layout.moved(r)])
        result = lax.dynamic_update_index_in_dim(result, got, z ^ r, 0)
    return result.reshape(MICRO, layout.step_rows, values.shape[-1])


class RowGather:
    def __init__(self, layout, own):
        self.layout = layout
        self.own = {0: own}
        self.sibling = {0: self.move(own, 1)}
        chips = layout.chips
        for n in range(1, 3 if chips == 4 else chips):
            self.own[n] = self.move(own, 2 * n)

    def move(self, value, k):
        return permute(value, self.layout.other(k))

    def chunk(self, n):
        if n > 0 and n not in self.sibling:
            self.sibling[n] = self.move(self.own[n], 1)
        return jnp.concatenate([self.own[n], self.sibling[n]])

    def after(self, n, *values):
        chips = self.layout.chips
        if n + 1 < chips:
            waiting = {m: value for m, value in self.own.items() if m > n}
            siblings = {m: value for m, value in self.sibling.items() if m > n}
            waiting, siblings, values = lax.optimization_barrier((waiting, siblings, values))
            self.own.update(waiting)
            self.sibling.update(siblings)
            if chips == 4 and n == 0:
                cut = self.own[0].shape[0] // 2
                self.far = [self.move(self.own[2][:cut], 2), self.move(self.own[1][cut:], 4)]
            if chips == 4 and n == 1:
                self.far = lax.optimization_barrier((self.far, values))[0]
                self.own[3] = jnp.concatenate(self.far)
            for m in (n + 1, n + 2):
                if m in self.own and m not in self.sibling:
                    self.sibling[m] = self.move(self.own[m], 1)
        return values


def gather_small(layout, f, own):
    held = own[None]
    k = 1
    while k < layout.fsdp:
        got = permute(held, layout.other(k))
        upper = (f & k) > 0
        held = jnp.concatenate(
            [jnp.where(upper, got, held), jnp.where(upper, held, got)], axis=0
        )
        k *= 2
    return held


class LinePipe:
    def __init__(self, z, seq_devices):
        self.z = z
        self.seq = seq_devices
        self.flying = []
        self.results = {}
        self.then = {}

    def advance(self, stage, value):
        half, last = self.seq // 2, self.seq - 1
        if stage < half - 1:
            s = stage
            got = lax.ppermute(value, "seq", [(s, s + 1), (last - s, last - s - 1)])
            return (value.astype(F32) + got.astype(F32)).astype(BF16)
        if stage == half - 1:
            got = lax.ppermute(value, "seq", [(half - 1, half), (half, half - 1)])
            return (value.astype(F32) + got.astype(F32)).astype(BF16)
        s = last - 1 - stage
        got = lax.ppermute(value, "seq", [(s + 1, s), (last - s - 1, last - s)])
        return jnp.where((self.z == s) | (self.z == last - s), got, value)

    def step(self, name=None, value=None, others=(), then=None):
        if name is not None:
            self.flying.append((name, 0, value))
            self.then[name] = then
        held, self.results, others = lax.optimization_barrier(
            ([entry[2] for entry in self.flying], self.results, others)
        )
        flying = []
        for (key, stage, _), operand in zip(self.flying, held):
            moved = self.advance(stage, operand)
            if stage == self.seq - 2:
                then = self.then[key]
                self.results[key] = moved if then is None else then(moved)
            else:
                flying.append((key, stage + 1, moved))
        self.flying = flying
        return others

    def finish(self):
        while self.flying:
            self.step()


def body(
    tokens,
    cotangent,
    attn_gain,
    query_gain,
    key_gain,
    w_query,
    w_key,
    w_value,
    w_out,
    ffn_gain,
    w_gate,
    w_up,
    w_down,
):
    fsdp_devices = lax.axis_size("fsdp")
    seq_devices = lax.axis_size("seq")
    layout = Layout(fsdp_devices, seq_devices, tokens.shape[2])
    f = lax.axis_index("fsdp")
    z = lax.axis_index("seq")
    rows = layout.rows
    share = layout.share
    member = (z % layout.near) * 2 + f % 2
    slot = (z // layout.near // 2) * share + member

    w_attn = lax.all_gather(
        jnp.concatenate([w_query, w_key, w_value], axis=1), "fsdp", axis=0, tiled=True
    )
    gains = gather_small(
        layout, f, jnp.concatenate([attn_gain, ffn_gain, query_gain, key_gain])
    ).astype(F32)
    wide, narrow = attn_gain.shape[0], query_gain.shape[0]
    full_attn_gain = gains[:, :wide].reshape(D)
    full_ffn_gain = gains[:, wide : 2 * wide].reshape(D)
    full_query_gain = gains[:, 2 * wide : 2 * wide + narrow].reshape(HD)
    full_key_gain = gains[:, 2 * wide + narrow :].reshape(HD)
    inputs_low = scatter_rows(layout, tokens[:, 0], z, slot)
    grad_out_low = scatter_rows(layout, cotangent[:, 0], z, slot)
    full_out = lax.all_gather(w_out, "fsdp", axis=0, tiled=True)

    row = jnp.arange(rows, dtype=jnp.int32)
    position = (
        (row // layout.piece_rows) * layout.step_rows
        + member * layout.piece_rows
        + row % layout.piece_rows
    ).astype(F32)
    frequency = THETA ** (-(jnp.arange(HD // 2).astype(F32) * 2.0 / HD))
    angles = frequency[:, None] * position[None, :]
    cosine_table, sine_table = jnp.cos(angles)[None], jnp.sin(angles)[None]
    head_gains = jnp.concatenate(
        [
            jnp.broadcast_to(full_query_gain[None, :, None], (HQ, HD, 1)),
            jnp.broadcast_to(full_key_gain[None, :, None], (KVH, HD, 1)),
        ]
    )

    inputs = inputs_low.astype(F32)
    normed, normed_unit, normed_inverse = rms_fwd(inputs, full_attn_gain)
    even = z % 2 == 0
    hidden_dev = w_down.shape[0]
    half_width = hidden_dev // HALVES
    fetched = lax.all_to_all(
        pack_columns(even, w_gate, w_up, fsdp_devices),
        "fsdp",
        split_axis=0,
        concat_axis=0,
        tiled=True,
    )
    normed_low, grad_out_low, w_attn, fetched = lax.optimization_barrier(
        (normed.astype(BF16), grad_out_low, w_attn, fetched)
    )
    grad_out_gather = RowGather(layout, grad_out_low)
    raw = dot(w_attn, normed_low, 0, 1)
    pair_width = KVH * HD
    turned = HQ + KVH
    head_raw = raw[: turned * HD].reshape(turned, HD, rows)
    head_normed, head_unit, head_inverse = head_rms_fwd(head_raw, head_gains)
    heads_low = rotate(head_normed, cosine_table, sine_table).astype(BF16).reshape(turned * HD, rows)
    queries = heads_low[: HQ * HD]
    own_pair = jnp.concatenate([heads_low[HQ * HD :], raw[turned * HD :].astype(BF16)], axis=0)
    pair_pieces = [own_pair] + [permute(own_pair, layout.across(k)) for k in range(1, share)]
    keys = jnp.concatenate([piece[:pair_width] for piece in pair_pieces], axis=1)
    values = jnp.concatenate([piece[pair_width:] for piece in pair_pieces], axis=1)
    index = member.astype(jnp.int32).reshape(1)
    fetched = [fetched[:, h].reshape(D, half_width) for h in range(HALVES)]
    swapped = [
        lax.ppermute(fetched[h], "seq", [(i, i ^ 1) for i in range(seq_devices)])
        for h in range(HALVES)
    ]
    attended, log_totals = attend(
        index, queries, keys, values, share, layout.piece_rows, layout.step_rows
    )
    attended, swapped[0] = lax.optimization_barrier((attended, swapped[0]))
    attended = grad_out_gather.after(0, attended)[0]
    middle = inputs + dot(attended, full_out, 0, 0)
    ffn_normed, ffn_unit, ffn_inverse = rms_fwd(middle, full_ffn_gain)
    ffn_low = ffn_normed.astype(BF16)

    ffn_gather = RowGather(layout, ffn_low)
    line = LinePipe(z, seq_devices)
    gate_w = [jnp.where(even, fetched[h], swapped[h]) for h in range(HALVES)]
    up_w = [jnp.where(even, swapped[h], fetched[h]) for h in range(HALVES)]
    worked = []
    ffn_chunks = []
    grad_out_chunks = []
    for n in range(layout.chips):
        ffn_chunks.append(ffn_gather.chunk(n))
        grad_out_chunks.append(grad_out_gather.chunk(n))
        step = hidden_step(ffn_chunks[n], grad_out_chunks[n], gate_w, up_w, w_down)
        if n > 0:
            step = grad_out_gather.after(n, *step)
        worked.append(ffn_gather.after(n, *step))
    hiddens, grad_gates, grad_ups, hiddens_t, grad_gates_t, grad_ups_t = zip(*worked)
    me = f.astype(jnp.int32).reshape(1)

    def to_owners(term):
        return lax.all_to_all(term, "fsdp", split_axis=0, concat_axis=0, tiled=True)

    down_term = weight_product(hiddens_t, grad_out_chunks, 0, "w_down_grad")
    grad_gates, grad_ups = line.step("down0", down_term[0], (grad_gates, grad_ups))
    grad_ffn_part = rows_product(
        me, [(grad_gates, gate_w), (grad_ups, up_w)], 1, rows, "grad_ffn_normed"
    )
    grad_ffn_part, grad_gates_t = line.step("down1", down_term[1], (grad_ffn_part, grad_gates_t))
    grad_ffn_normed = lax.psum_scatter(
        grad_ffn_part, "fsdp", scatter_dimension=0, tiled=True
    )
    gate_term = weight_product(grad_gates_t, ffn_chunks, wide, "w_gate_grad")
    hiddens, grad_ups_t = line.step("gate0", gate_term[0], (hiddens, grad_ups_t), to_owners)
    up_term = weight_product(grad_ups_t, ffn_chunks, wide, "w_up_grad")
    hiddens, up_term = line.step("gate1", gate_term[1], (hiddens, up_term), to_owners)
    out_part = rows_product(me, [(hiddens, [w_down])], 0, rows, "block_out")
    out_part, grad_ffn_normed = line.step("up0", up_term[0], (out_part, grad_ffn_normed), to_owners)
    out_sum = lax.psum_scatter(out_part, "fsdp", scatter_dimension=0, tiled=True)
    grad_ffn_normed = grad_ffn_normed.astype(F32)

    grad_middle_norm, ffn_gain_term = rms_back(
        grad_ffn_normed, ffn_unit, ffn_inverse, full_ffn_gain
    )
    grad_middle = grad_out_low.astype(F32) + grad_middle_norm
    grad_branch_low = grad_middle.astype(BF16)
    grad_attended = dot(full_out, grad_branch_low, 1, 1).astype(BF16)
    out_term = dot(attended, grad_branch_low, 1, 0).astype(BF16)
    out_rows = lax.psum_scatter(out_term, "fsdp", scatter_dimension=0, tiled=True)
    grad_queries, grad_keys, grad_values = attend_back(
        index,
        queries,
        keys,
        values,
        attended,
        log_totals,
        grad_attended,
        share,
        layout.piece_rows,
        layout.step_rows,
    )
    grad_queries, grad_keys, grad_values = line.step(
        "up1", up_term[1], (grad_queries, grad_keys, grad_values), to_owners
    )
    grad_pair = jnp.concatenate([grad_keys[:, :rows], grad_values[:, :rows]], axis=0)
    for k in range(1, share):
        columns = slice(k * rows, (k + 1) * rows)
        sent = jnp.concatenate([grad_keys[:, columns], grad_values[:, columns]], axis=0)
        grad_pair = grad_pair + permute(sent.astype(BF16), layout.across(k)).astype(F32)
    grad_pair_low = grad_pair.astype(BF16)
    grad_turned = (
        jnp.concatenate([grad_queries, grad_pair_low[:pair_width]], axis=0)
        .astype(F32)
        .reshape(turned, HD, rows)
    )
    grad_head_normed = rotate(grad_turned, cosine_table, -sine_table)
    scaled = grad_head_normed * head_gains
    grad_head_raw = head_inverse * (
        scaled - head_unit * jnp.mean(scaled * head_unit, axis=1, keepdims=True)
    )
    head_gain_terms = jnp.sum(grad_head_normed * head_unit, axis=2)
    grad_raw = jnp.concatenate(
        [grad_head_raw.astype(BF16).reshape(turned * HD, rows), grad_pair_low[pair_width:]], axis=0
    )
    projection_term = dot(normed_low, grad_raw, 0, 1).astype(BF16)
    projection_term, grad_raw = lax.optimization_barrier((projection_term, grad_raw))
    projection_rows = lax.psum_scatter(
        projection_term, "fsdp", scatter_dimension=0, tiled=True
    )
    grad_raw, out_sum = line.step("out", out_rows, (grad_raw, out_sum))
    block_out = return_rows(layout, (middle + out_sum.astype(F32)).astype(BF16), z, slot)
    grad_normed = dot(grad_raw, w_attn, 0, 1)
    grad_input_norm, attn_gain_term = rms_back(
        grad_normed, normed_unit, normed_inverse, full_attn_gain
    )

    def column(vector):
        spread = vector.reshape(fsdp_devices, -1)
        return jnp.pad(spread, ((0, 0), (0, wide - spread.shape[1]))).reshape(D)

    gain_terms = jnp.stack(
        [
            attn_gain_term,
            ffn_gain_term,
            column(jnp.sum(head_gain_terms[:HQ], axis=0)),
            column(jnp.sum(head_gain_terms[HQ:], axis=0)),
        ],
        axis=1,
    )
    gain_terms = jnp.pad(gain_terms, ((0, 0), (0, 128 - gain_terms.shape[1]))).astype(BF16)
    projection_rows, gain_terms = lax.optimization_barrier((projection_rows, gain_terms))
    gain_rows = lax.psum_scatter(gain_terms, "fsdp", scatter_dimension=0, tiled=True)
    tokens_grad = return_rows(layout, (grad_middle + grad_input_norm).astype(BF16), z, slot)
    line.step("attn", projection_rows)
    line.step("gain", gain_rows)
    line.finish()

    w_down_grad = jnp.concatenate([line.results[f"down{h}"] for h in range(HALVES)]).astype(F32)
    w_gate_grad = unpack_columns([line.results[f"gate{h}"] for h in range(HALVES)])
    w_up_grad = unpack_columns([line.results[f"up{h}"] for h in range(HALVES)])
    w_out_grad = line.results["out"].astype(F32)
    attn_rows = line.results["attn"].astype(F32)
    gain_rows = line.results["gain"].astype(F32)
    query_width = HQ * HD

    return (
        block_out[:, None],
        tokens_grad[:, None],
        gain_rows[:, 0],
        gain_rows[:narrow, 2],
        gain_rows[:narrow, 3],
        attn_rows[:, :query_width],
        attn_rows[:, query_width : query_width + pair_width],
        attn_rows[:, query_width + pair_width :],
        w_out_grad,
        gain_rows[:, 1],
        w_gate_grad,
        w_up_grad,
        w_down_grad,
    )


def solution(mesh):
    activations = P(None, "fsdp", "seq", None)
    vector = P("fsdp")
    matrix = P("fsdp", None)
    specs = (
        (activations, activations)
        + (vector,) * 3
        + (matrix,) * 4
        + (vector,)
        + (matrix,) * 3
    )
    return jax.shard_map(body, mesh=mesh, in_specs=specs, out_specs=specs, check_vma=False)
```

```python
import functools
import math

import jax
import jax.numpy as jnp
from jax import lax
from jax.experimental import pallas as pl
from jax.experimental.pallas import tpu as pltpu
from jax.sharding import PartitionSpec as P

D = 2048
HQ = 32
KVH = 8
HD = 64
FF = 8192
LENGTH = 1024
MICRO = 2
HALVES = 2

EPSILON = 1e-05
THETA = 1000000.0
GROUP = HQ // KVH
BLOCK = 128
SCALE = 1.0 / math.sqrt(HD)
LOG2E = math.log2(math.e)
VMEM_LIMIT = 56 * 1024 * 1024

F32 = jnp.float32
BF16 = jnp.bfloat16


def dot(left_side, right_side, left_dim, right_dim):
    return lax.dot_general(
        left_side,
        right_side,
        (((left_dim,), (right_dim,)), ((), ())),
        preferred_element_type=F32,
    )


def rms_fwd(values, row_gain):
    inverse = lax.rsqrt(jnp.mean(values * values, axis=-1, keepdims=True) + EPSILON)
    unit_rows = values * inverse
    return (unit_rows * row_gain, unit_rows, inverse)


def rms_back(grad_outputs, unit_rows, inverse, row_gain):
    scaled = grad_outputs * row_gain
    grad_inputs = inverse * (
        scaled - unit_rows * jnp.mean(scaled * unit_rows, axis=-1, keepdims=True)
    )
    grad_gain = jnp.sum(grad_outputs * unit_rows, axis=0)
    return (grad_inputs, grad_gain)


def head_rms_fwd(values, gains):
    inverse = lax.rsqrt(jnp.mean(values * values, axis=1, keepdims=True) + EPSILON)
    unit = values * inverse
    return (unit * gains, unit, inverse)


def rotate(values, cosine_table, sine_table):
    half_width = values.shape[1] // 2
    front_half = values[:, :half_width]
    back_half = values[:, half_width:]
    return jnp.concatenate(
        [
            front_half * cosine_table - back_half * sine_table,
            back_half * cosine_table + front_half * sine_table,
        ],
        axis=1,
    )


def block_masks(index, pieces, piece_rows, step_rows):
    key = lax.broadcasted_iota(jnp.int32, (BLOCK, GROUP * BLOCK), 0)
    query = lax.broadcasted_iota(jnp.int32, (BLOCK, GROUP * BLOCK), 1) & (BLOCK - 1)

    def place(row, piece):
        return (row // piece_rows) * step_rows + piece * piece_rows + (row & (piece_rows - 1))

    return [place(key, index ^ k) <= place(query, index) for k in range(pieces)]


def heads_beside(block, first, count):
    return jnp.concatenate(
        [block[h * HD : (h + 1) * HD, first : first + count] for h in range(GROUP)], axis=1
    )


def mask_tail(values, mask, first):
    tail = jnp.where(mask, values[first:], 0.0)
    if first == 0:
        return tail
    return jnp.concatenate([values[:first], tail], axis=0)


def attend_kernel(index_ref, q_ref, k_ref, v_ref, out_ref, lse_ref, *, pieces, piece_rows, step_rows):
    rows = q_ref.shape[1]
    masks = block_masks(index_ref[0], pieces, piece_rows, step_rows)
    queries = q_ref[...]
    for first in range(0, rows, BLOCK):
        count = first + BLOCK
        query_block = heads_beside(queries, first, BLOCK)
        total = None
        result = None
        for k in range(pieces):
            spot = pl.ds(k * rows, count)
            scores = dot(k_ref[:, spot], query_block, 0, 0)
            weights = mask_tail(jnp.exp2(scores * (SCALE * LOG2E)), masks[k], first)
            part = jnp.sum(weights, axis=0, keepdims=True)
            value = dot(v_ref[:, spot], weights.astype(BF16), 1, 0)
            total = part if total is None else total + part
            result = value if result is None else result + value
        result = result * (1.0 / total)
        log_total = jnp.log2(total)
        for h in range(GROUP):
            columns = slice(h * BLOCK, (h + 1) * BLOCK)
            out_ref[h * HD : (h + 1) * HD, first : first + BLOCK] = result[:, columns].astype(BF16)
            lse_ref[0, h : h + 1, first : first + BLOCK] = log_total[:, columns]


def attend_back_kernel(
    index_ref, q_ref, k_ref, v_ref, out_ref, lse_ref, grad_ref, dq_ref, dk_ref, dv_ref,
    *, pieces, piece_rows, step_rows
):
    rows = q_ref.shape[1]
    masks = block_masks(index_ref[0], pieces, piece_rows, step_rows)
    queries = q_ref[...]
    grads = grad_ref[...]
    results = out_ref[...]
    dk_ref[...] = jnp.zeros_like(dk_ref)
    dv_ref[...] = jnp.zeros_like(dv_ref)
    for first in range(0, rows, BLOCK):
        count = first + BLOCK
        query_block = heads_beside(queries, first, BLOCK)
        grad_block = heads_beside(grads, first, BLOCK)
        result_block = heads_beside(results, first, BLOCK)
        centre = jnp.sum(
            grad_block.astype(F32) * result_block.astype(F32), axis=0, keepdims=True
        )
        log_total = jnp.concatenate(
            [lse_ref[0, h : h + 1, first : first + BLOCK] for h in range(GROUP)], axis=1
        )
        dq = None
        for k in range(pieces):
            spot = pl.ds(k * rows, count)
            keys = k_ref[:, spot]
            scores = dot(keys, query_block, 0, 0)
            weights = mask_tail(
                jnp.exp2(scores * (SCALE * LOG2E) - log_total), masks[k], first
            )
            grad_weights = dot(v_ref[:, spot], grad_block, 0, 0)
            grad_scores = (weights * (grad_weights - centre)).astype(BF16)
            part = dot(keys, grad_scores, 1, 0)
            dq = part if dq is None else dq + part
            dk_ref[:, spot] += dot(query_block, grad_scores, 1, 1) * SCALE
            dv_ref[:, spot] += dot(grad_block, weights.astype(BF16), 1, 1)
        dq = (dq * SCALE).astype(BF16)
        for h in range(GROUP):
            columns = slice(h * BLOCK, (h + 1) * BLOCK)
            dq_ref[h * HD : (h + 1) * HD, first : first + BLOCK] = dq[:, columns]


def attention_specs(rows, total_rows):
    group_spec = pl.BlockSpec((GROUP * HD, rows), lambda i: (i, 0))
    pair_spec = pl.BlockSpec((HD, total_rows), lambda i: (i, 0))
    lse_spec = pl.BlockSpec((1, GROUP, rows), lambda i: (i, 0, 0))
    return group_spec, pair_spec, lse_spec


def attend(index, queries, keys, values, pieces, piece_rows, step_rows):
    rows, total_rows = queries.shape[1], keys.shape[1]
    group_spec, pair_spec, lse_spec = attention_specs(rows, total_rows)
    return pl.pallas_call(
        functools.partial(
            attend_kernel, pieces=pieces, piece_rows=piece_rows, step_rows=step_rows
        ),
        grid=(KVH,),
        in_specs=[pl.BlockSpec(memory_space=pltpu.SMEM), group_spec, pair_spec, pair_spec],
        out_specs=[group_spec, lse_spec],
        out_shape=[
            jax.ShapeDtypeStruct((HQ * HD, rows), BF16),
            jax.ShapeDtypeStruct((KVH, GROUP, rows), F32),
        ],
        compiler_params=pltpu.CompilerParams(vmem_limit_bytes=VMEM_LIMIT),
        cost_estimate=pl.CostEstimate(
            flops=4 * HQ * HD * rows * total_rows,
            bytes_accessed=8 * HQ * HD * rows,
            transcendentals=HQ * rows * total_rows,
        ),
        name="attend",
    )(index, queries, keys, values)


def attend_back(index, queries, keys, values, results, lse, grads, pieces, piece_rows, step_rows):
    rows, total_rows = queries.shape[1], keys.shape[1]
    group_spec, pair_spec, lse_spec = attention_specs(rows, total_rows)
    return pl.pallas_call(
        functools.partial(
            attend_back_kernel, pieces=pieces, piece_rows=piece_rows, step_rows=step_rows
        ),
        grid=(KVH,),
        in_specs=[
            pl.BlockSpec(memory_space=pltpu.SMEM),
            group_spec,
            pair_spec,
            pair_spec,
            group_spec,
            lse_spec,
            group_spec,
        ],
        out_specs=[group_spec, pair_spec, pair_spec],
        out_shape=[
            jax.ShapeDtypeStruct((HQ * HD, rows), BF16),
            jax.ShapeDtypeStruct((KVH * HD, total_rows), F32),
            jax.ShapeDtypeStruct((KVH * HD, total_rows), F32),
        ],
        compiler_params=pltpu.CompilerParams(vmem_limit_bytes=VMEM_LIMIT),
        cost_estimate=pl.CostEstimate(
            flops=10 * HQ * HD * rows * total_rows,
            bytes_accessed=16 * HQ * HD * rows,
            transcendentals=HQ * rows * total_rows,
        ),
        name="attend_back",
    )(index, queries, keys, values, results, lse, grads)


def hidden_kernel(x_ref, c_ref, weight_ref, down_ref, *refs):
    hidden_ref, grads_ref, hidden_t_ref, grads_t_ref = refs[-4:]
    x = x_ref[...]
    c = c_ref[...]
    units = down_ref.shape[0]
    half = units // HALVES
    for h in range(HALVES):
        part = slice(h * half, (h + 1) * half)
        up_part = slice(units + h * half, units + (h + 1) * half)
        gate = dot(x, weight_ref[:, part], 1, 0)
        up = dot(x, weight_ref[:, up_part], 1, 0)
        grad_hidden = dot(c, down_ref[part, :], 1, 1)
        sigmoid = 1.0 / (1.0 + jnp.exp(-gate))
        silu = gate * sigmoid
        hidden = (silu * up).astype(BF16)
        grad_up = (grad_hidden * silu).astype(BF16)
        grad_gate = (grad_hidden * up * sigmoid * (1.0 + gate * (1.0 - sigmoid))).astype(BF16)
        hidden_ref[:, part] = hidden
        grads_ref[:, part] = grad_gate
        grads_ref[:, up_part] = grad_up
        hidden_t_ref[part, :] = hidden.T
        grads_t_ref[part, :] = grad_gate.T
        grads_t_ref[up_part, :] = grad_up.T


def hidden_step(n, rows, x, c, weights, w_down, so_far):
    count, depth = x.shape
    units = w_down.shape[0]
    tile = min(512, rows)
    first = n * (rows // tile)
    once = pl.Buffered(1)
    read = pl.BlockSpec((tile, depth), lambda i: (first + i, 0))
    widths = (units, 2 * units)
    shapes = [(count, width) for width in widths] + [(width, count) for width in widths]
    flops = 6 * rows * depth * units
    return pl.pallas_call(
        hidden_kernel,
        grid=(rows // tile,),
        in_specs=[
            read,
            read,
            pl.BlockSpec((depth, 2 * units), lambda i: (0, 0), pipeline_mode=once),
            pl.BlockSpec((units, depth), lambda i: (0, 0), pipeline_mode=once),
        ]
        + [pl.BlockSpec(memory_space=pl.ANY)] * len(so_far),
        out_specs=[pl.BlockSpec((tile, width), lambda i: (first + i, 0)) for width in widths]
        + [pl.BlockSpec((width, tile), lambda i: (0, first + i)) for width in widths],
        out_shape=[jax.ShapeDtypeStruct(shape, BF16) for shape in shapes],
        input_output_aliases={4 + k: k for k in range(len(so_far))},
        compiler_params=pltpu.CompilerParams(vmem_limit_bytes=VMEM_LIMIT),
        cost_estimate=pl.CostEstimate(
            flops=flops,
            bytes_accessed=4 * rows * depth + 12 * rows * units + 6 * depth * units,
            transcendentals=rows * units,
        ),
        name="hidden_step",
    )(x, c, weights, w_down, *so_far)


def rows_kernel(me_ref, left_ref, right_ref, result_ref, *, right_dim):
    result_ref[...] = dot(left_ref[...], right_ref[...], 1, right_dim).astype(BF16)


def rows_product(me, left, right, right_dim, block_rows, name):
    count, width = left.shape
    return pl.pallas_call(
        functools.partial(rows_kernel, right_dim=right_dim),
        grid_spec=pltpu.PrefetchScalarGridSpec(
            num_scalar_prefetch=1,
            grid=(count // block_rows,),
            in_specs=[
                pl.BlockSpec((block_rows, width), lambda i, me_ref: (i, 0)),
                pl.BlockSpec(
                    right.shape, lambda i, me_ref: (0, 0), pipeline_mode=pl.Buffered(1)
                ),
            ],
            out_specs=pl.BlockSpec((block_rows, D), lambda i, me_ref: (me_ref[0] ^ i, 0)),
        ),
        out_shape=jax.ShapeDtypeStruct((count, D), BF16),
        compiler_params=pltpu.CompilerParams(vmem_limit_bytes=VMEM_LIMIT),
        cost_estimate=pl.CostEstimate(
            flops=2 * count * D * width,
            bytes_accessed=2 * (count * width + count * D + D * width),
            transcendentals=0,
        ),
        name=name,
    )(me, left, right)


def weight_kernel(left_ref, right_ref, *result_refs, parts):
    total = dot(left_ref[...], right_ref[...], 1, 0)
    if parts:
        wide = total.shape[1] // parts
        pieces = [total[:, p * wide : (p + 1) * wide].T.astype(BF16) for p in range(parts)]
    else:
        pieces = [total.astype(BF16)]
    for h, result_ref in enumerate(result_refs):

        @pl.when(pl.program_id(0) == h)
        def _():
            for p, piece in enumerate(pieces):
                if parts:
                    result_ref[p] = piece
                else:
                    result_ref[...] = piece


def weight_product(left, right, first, units, wide, name):
    depth = left.shape[1]
    half = units // HALVES
    column = min(1024, D)
    steps = D // column
    parts = column // wide if wide else 0
    block = first // half

    def place(h):
        return lambda i, j: jnp.where(i < h, 0, jnp.where(i == h, j, steps - 1))

    if wide:
        out_specs = [
            pl.BlockSpec((parts, wide, half), lambda i, j, at=place(h): (at(i, j), 0, 0))
            for h in range(HALVES)
        ]
        out_shape = [jax.ShapeDtypeStruct((D // wide, wide, half), BF16)] * HALVES
    else:
        out_specs = [
            pl.BlockSpec((half, column), lambda i, j, at=place(h): (0, at(i, j)))
            for h in range(HALVES)
        ]
        out_shape = [jax.ShapeDtypeStruct((half, D), BF16)] * HALVES
    return pl.pallas_call(
        functools.partial(weight_kernel, parts=parts),
        grid=(HALVES, steps),
        in_specs=[
            pl.BlockSpec((half, depth), lambda i, j: (block + i, 0)),
            pl.BlockSpec((depth, column), lambda i, j: (0, j)),
        ],
        out_specs=out_specs,
        out_shape=out_shape,
        compiler_params=pltpu.CompilerParams(vmem_limit_bytes=VMEM_LIMIT),
        cost_estimate=pl.CostEstimate(
            flops=2 * units * depth * D,
            bytes_accessed=2 * depth * (units + HALVES * D) + 2 * units * D,
            transcendentals=0,
        ),
        name=name,
    )(left, right)


def merge_kernel(even_ref, *refs):
    result_ref = refs[-1]
    half = result_ref.shape[1] // (2 * HALVES)
    for h in range(HALVES):
        mine, theirs = refs[h][...], refs[HALVES + h][...]
        gate = jnp.where(even_ref[0] > 0, mine, theirs)
        up = jnp.where(even_ref[0] > 0, theirs, mine)
        result_ref[:, h * half : (h + 1) * half] = gate
        result_ref[:, (HALVES + h) * half : (HALVES + h + 1) * half] = up


def merge_columns(even, mine, theirs):
    rows, half = mine[0].shape
    tile = min(256, rows)
    return pl.pallas_call(
        merge_kernel,
        grid=(rows // tile,),
        in_specs=[pl.BlockSpec(memory_space=pltpu.SMEM)]
        + [pl.BlockSpec((tile, half), lambda i: (i, 0))] * (2 * HALVES),
        out_specs=pl.BlockSpec((tile, 2 * HALVES * half), lambda i: (i, 0)),
        out_shape=jax.ShapeDtypeStruct((rows, 2 * HALVES * half), BF16),
        compiler_params=pltpu.CompilerParams(vmem_limit_bytes=VMEM_LIMIT),
        cost_estimate=pl.CostEstimate(
            flops=0, bytes_accessed=8 * rows * HALVES * half, transcendentals=0
        ),
        name="merge_columns",
    )(even.astype(jnp.int32).reshape(1), *mine, *theirs)


def pack_kernel(even_ref, first_ref, second_ref, result_ref):
    chosen = jnp.where(even_ref[0] > 0, first_ref[...], second_ref[...])
    width = result_ref.shape[-1]
    for h in range(HALVES):
        result_ref[0, h] = chosen[:, h * width : (h + 1) * width]


def pack_columns(even, first, second, parts):
    rows, columns = first.shape
    width = columns // parts
    block = pl.BlockSpec((rows, width), lambda i: (0, i))
    half = width // HALVES
    return pl.pallas_call(
        pack_kernel,
        grid=(parts,),
        in_specs=[pl.BlockSpec(memory_space=pltpu.SMEM), block, block],
        out_specs=pl.BlockSpec((1, HALVES, rows, half), lambda i: (i, 0, 0, 0)),
        out_shape=jax.ShapeDtypeStruct((parts, HALVES, rows, half), BF16),
        compiler_params=pltpu.CompilerParams(vmem_limit_bytes=VMEM_LIMIT),
        cost_estimate=pl.CostEstimate(
            flops=0, bytes_accessed=6 * rows * columns, transcendentals=0
        ),
        name="pack_columns",
    )(even.astype(jnp.int32).reshape(1), first, second)


def unpack_kernel(outer_ref, *refs):
    result_ref = refs[-1]
    width = refs[0].shape[-1]
    for h in range(HALVES):
        chosen = jnp.where(outer_ref[0] > 0, refs[2 * h][0], refs[2 * h + 1][0])
        result_ref[:, h * width : (h + 1) * width] = chosen.astype(F32)


def unpack_columns(outer, pieces):
    arrays = [array for pair in pieces for array in pair]
    parts, rows, half = arrays[0].shape
    return pl.pallas_call(
        unpack_kernel,
        grid=(parts,),
        in_specs=[pl.BlockSpec(memory_space=pltpu.SMEM)]
        + [pl.BlockSpec((1, rows, half), lambda i: (i, 0, 0))] * len(arrays),
        out_specs=pl.BlockSpec((rows, HALVES * half), lambda i: (0, i)),
        out_shape=jax.ShapeDtypeStruct((rows, parts * HALVES * half), F32),
        compiler_params=pltpu.CompilerParams(vmem_limit_bytes=VMEM_LIMIT),
        cost_estimate=pl.CostEstimate(
            flops=0, bytes_accessed=8 * parts * rows * HALVES * half, transcendentals=0
        ),
        name="unpack_columns",
    )(outer.astype(jnp.int32).reshape(1), *arrays)


class Layout:
    def __init__(self, fsdp_devices, seq_devices, rows_dev):
        self.fsdp = fsdp_devices
        self.seq = seq_devices
        self.chips = fsdp_devices // 2
        self.share = 2 * seq_devices // (2 * MICRO)
        self.near = self.share // 2
        self.piece_rows = rows_dev // self.share
        self.step_rows = rows_dev
        self.rows = LENGTH // self.share

    def flat(self, f, z):
        return f * self.seq + z

    def moved(self, r):
        pairs = []
        for f in range(self.fsdp):
            for z in range(self.seq):
                slot = z ^ r
                micro, j = slot // self.share, slot % self.share
                target_f = (f // 2) * 2 + j % 2
                target_z = (2 * micro + f % 2) * self.near + j // 2
                pairs.append((self.flat(f, z), self.flat(target_f, target_z)))
        return pairs

    def other(self, k):
        return [
            (self.flat(f, z), self.flat(f ^ k, z))
            for f in range(self.fsdp)
            for z in range(self.seq)
        ]

    def across(self, k):
        pairs = []
        for f in range(self.fsdp):
            for z in range(self.seq):
                pairs.append((self.flat(f, z), self.flat(f ^ (k & 1), z ^ (k >> 1))))
        return pairs


def permute(value, pairs):
    return lax.ppermute(value, ("fsdp", "seq"), pairs)


def scatter_rows(layout, values, z, slot):
    parts = values.reshape(layout.seq, layout.piece_rows, values.shape[-1])
    result = jnp.zeros_like(parts)
    for r in range(layout.seq):
        sent = lax.dynamic_index_in_dim(parts, z ^ r, 0, keepdims=False)
        got = permute(sent, layout.moved(r))
        result = lax.dynamic_update_index_in_dim(result, got, slot ^ r, 0)
    return result.reshape(layout.rows, values.shape[-1])


def return_rows(layout, values, f):
    width = values.shape[-1]
    parts = values.reshape(layout.seq, layout.piece_rows, width)
    parts = lax.all_to_all(parts, "seq", split_axis=0, concat_axis=0, tiled=True)
    parts = parts.reshape(MICRO, 2, layout.near, layout.piece_rows, width)
    core = f % 2
    kept = lax.dynamic_index_in_dim(parts, core, 1, keepdims=False)
    sent = lax.dynamic_index_in_dim(parts, 1 - core, 1, keepdims=False)
    got = permute(sent, layout.other(1))
    both = jnp.stack(
        [jnp.where(core == 0, kept, got), jnp.where(core == 0, got, kept)], axis=2
    )
    return both.reshape(MICRO, layout.step_rows, width)


class RowGather:
    def __init__(self, layout, own):
        self.layout = layout
        self.own = {0: own}
        self.sibling = {0: self.move(own, 1)}
        self.whole = jnp.zeros((layout.fsdp * own.shape[0], own.shape[1]), own.dtype)
        chips = layout.chips
        for n in range(1, 3 if chips == 4 else chips):
            self.own[n] = self.move(own, 2 * n)

    def move(self, value, k):
        return permute(value, self.layout.other(k))

    def chunk(self, n):
        if n not in self.sibling:
            self.sibling[n] = self.move(self.own[n], 1)
        count = self.own[n].shape[0]
        for k, piece in enumerate((self.own[n], self.sibling[n])):
            self.whole = lax.dynamic_update_slice(self.whole, piece, ((2 * n + k) * count, 0))
        return self.whole

    def after(self, n, *values):
        chips = self.layout.chips
        if n + 1 < chips:
            waiting = {m: value for m, value in self.own.items() if m > n}
            siblings = {m: value for m, value in self.sibling.items() if m > n}
            waiting, siblings, self.whole, values = lax.optimization_barrier(
                (waiting, siblings, self.whole, values)
            )
            self.own.update(waiting)
            self.sibling.update(siblings)
            if chips == 4 and n == 0:
                cut = self.own[0].shape[0] // 2
                self.far = [self.move(self.own[2][:cut], 2), self.move(self.own[1][cut:], 4)]
            if chips == 4 and n == 1:
                self.far = lax.optimization_barrier((self.far, values))[0]
                self.own[3] = jnp.concatenate(self.far)
            for m in (n + 1, n + 2):
                if m in self.own and m not in self.sibling:
                    self.sibling[m] = self.move(self.own[m], 1)
        return values


def gather_small(layout, f, own):
    held = own[None]
    k = 1
    while k < layout.fsdp:
        got = permute(held, layout.other(k))
        upper = (f & k) > 0
        held = jnp.concatenate(
            [jnp.where(upper, got, held), jnp.where(upper, held, got)], axis=0
        )
        k *= 2
    return held


class LinePipe:
    def __init__(self, z, seq_devices):
        self.seq = seq_devices
        self.z = z
        self.outer = (z == 0) | (z == seq_devices - 1)
        self.flying = []
        self.results = {}

    def send(self, stage, value):
        half, last = self.seq // 2, self.seq - 1
        if stage < half - 1:
            pairs = [(stage, stage + 1), (last - stage, last - stage - 1)]
        elif stage == half - 1:
            pairs = [(half - 1, half), (half, half - 1)]
        else:
            s = last - 1 - stage
            pairs = [(s + 1, s), (last - s - 1, last - s)]
        return lax.ppermute(value, "seq", pairs)

    def join(self, stage, value, got):
        if stage < self.seq // 2:
            return value + got
        s = self.seq - 2 - stage
        return jnp.where((self.z == s) | (self.z == self.seq - 1 - s), got, value)

    def step(self, name=None, value=None, others=()):
        arrived = [entry[3] for entry in self.flying]
        arrived, self.results, value, others = lax.optimization_barrier(
            (arrived, self.results, value, others)
        )
        flying = []
        if name is not None:
            flying.append((name, 0, value, self.send(0, value)))
        for (key, stage, held, _), got in zip(self.flying, arrived):
            if stage == self.seq - 2:
                self.results[key] = (got, held)
                continue
            held = self.join(stage, held, got)
            flying.append((key, stage + 1, held, self.send(stage + 1, held)))
        self.flying = flying
        return others

    def finish(self):
        while self.flying:
            self.step()

    def result(self, name):
        got, held = self.results[name]
        return jnp.where(self.outer, got, held)


def body(
    tokens,
    cotangent,
    attn_gain,
    query_gain,
    key_gain,
    w_query,
    w_key,
    w_value,
    w_out,
    ffn_gain,
    w_gate,
    w_up,
    w_down,
):
    fsdp_devices = lax.axis_size("fsdp")
    seq_devices = lax.axis_size("seq")
    layout = Layout(fsdp_devices, seq_devices, tokens.shape[2])
    f = lax.axis_index("fsdp")
    z = lax.axis_index("seq")
    rows = layout.rows
    share = layout.share
    member = (z % layout.near) * 2 + f % 2
    slot = (z // layout.near // 2) * share + member

    w_attn = lax.all_gather(
        jnp.concatenate([w_query, w_key, w_value], axis=1), "fsdp", axis=0, tiled=True
    )
    gains = gather_small(
        layout, f, jnp.concatenate([attn_gain, ffn_gain, query_gain, key_gain])
    ).astype(F32)
    wide, narrow = attn_gain.shape[0], query_gain.shape[0]
    even = z % 2 == 0
    hidden_dev = w_down.shape[0]
    half_width = hidden_dev // HALVES
    gains, gate_rows, up_rows = lax.optimization_barrier((gains, w_gate, w_up))
    fetched = lax.all_to_all(
        pack_columns(even, gate_rows, up_rows, fsdp_devices),
        "fsdp",
        split_axis=0,
        concat_axis=0,
        tiled=True,
    )
    fetched = [fetched[:, h].reshape(D, half_width) for h in range(HALVES)]
    swapped = [
        lax.ppermute(fetched[h], "seq", [(i, i ^ 1) for i in range(seq_devices)])
        for h in range(HALVES)
    ]
    full_attn_gain = gains[:, :wide].reshape(D)
    full_ffn_gain = gains[:, wide : 2 * wide].reshape(D)
    full_query_gain = gains[:, 2 * wide : 2 * wide + narrow].reshape(HD)
    full_key_gain = gains[:, 2 * wide + narrow :].reshape(HD)
    inputs_low = scatter_rows(layout, tokens[:, 0], z, slot)
    grad_out_low = scatter_rows(layout, cotangent[:, 0], z, slot)
    full_out = lax.all_gather(w_out, "fsdp", axis=0, tiled=True)

    row = jnp.arange(rows, dtype=jnp.int32)
    position = (
        (row // layout.piece_rows) * layout.step_rows
        + member * layout.piece_rows
        + row % layout.piece_rows
    ).astype(F32)
    frequency = THETA ** (-(jnp.arange(HD // 2).astype(F32) * 2.0 / HD))
    angles = frequency[:, None] * position[None, :]
    cosine_table, sine_table = jnp.cos(angles)[None], jnp.sin(angles)[None]
    head_gains = jnp.concatenate(
        [
            jnp.broadcast_to(full_query_gain[None, :, None], (HQ, HD, 1)),
            jnp.broadcast_to(full_key_gain[None, :, None], (KVH, HD, 1)),
        ]
    )

    inputs = inputs_low.astype(F32)
    normed, normed_unit, normed_inverse = rms_fwd(inputs, full_attn_gain)
    normed_low, grad_out_low, w_attn = lax.optimization_barrier(
        (normed.astype(BF16), grad_out_low, w_attn)
    )
    grad_out_gather = RowGather(layout, grad_out_low)
    raw = dot(w_attn, normed_low, 0, 1)
    pair_width = KVH * HD
    turned = HQ + KVH
    head_raw = raw[: turned * HD].reshape(turned, HD, rows)
    head_normed, head_unit, head_inverse = head_rms_fwd(head_raw, head_gains)
    heads_low = rotate(head_normed, cosine_table, sine_table).astype(BF16).reshape(turned * HD, rows)
    queries = heads_low[: HQ * HD]
    own_pair = jnp.concatenate([heads_low[HQ * HD :], raw[turned * HD :].astype(BF16)], axis=0)
    pair_pieces = [own_pair] + [permute(own_pair, layout.across(k)) for k in range(1, share)]
    keys = jnp.concatenate([piece[:pair_width] for piece in pair_pieces], axis=1)
    values = jnp.concatenate([piece[pair_width:] for piece in pair_pieces], axis=1)
    index = member.astype(jnp.int32).reshape(1)
    attended, log_totals = attend(
        index, queries, keys, values, share, layout.piece_rows, layout.step_rows
    )
    attended, swapped[0] = lax.optimization_barrier((attended, swapped[0]))
    attended = grad_out_gather.after(0, attended)[0]
    middle = inputs + dot(attended, full_out, 0, 0)
    ffn_normed, ffn_unit, ffn_inverse = rms_fwd(middle, full_ffn_gain)
    ffn_low = ffn_normed.astype(BF16)

    ffn_gather = RowGather(layout, ffn_low)
    line = LinePipe(z, seq_devices)
    weights = merge_columns(even, fetched, swapped)
    worked = ()
    for n in range(layout.chips):
        ffn_rows = ffn_gather.chunk(n)
        grad_out_rows = grad_out_gather.chunk(n)
        worked = hidden_step(n, 2 * rows, ffn_rows, grad_out_rows, weights, w_down, worked)
        if n > 0:
            worked = grad_out_gather.after(n, *worked)
        worked = ffn_gather.after(n, *worked)
    hidden, grads, hidden_t, grads_t = worked
    me = f.astype(jnp.int32).reshape(1)

    def to_owners(terms):
        return [
            lax.all_to_all(term, "fsdp", split_axis=0, concat_axis=0, tiled=True)
            for term in terms
        ]

    down_term = weight_product(hidden_t, grad_out_rows, 0, hidden_dev, 0, "w_down_grad")
    (grads,) = line.step("down0", down_term[0], (grads,))
    grad_ffn_part = rows_product(me, grads, weights, 1, rows, "grad_ffn_normed")
    grad_ffn_part, grads_t = line.step("down1", down_term[1], (grad_ffn_part, grads_t))
    grad_ffn_normed = lax.psum_scatter(
        grad_ffn_part, "fsdp", scatter_dimension=0, tiled=True
    )
    gate_term = to_owners(
        weight_product(grads_t, ffn_rows, 0, hidden_dev, wide, "w_gate_grad")
    )
    up_term = weight_product(grads_t, ffn_rows, hidden_dev, hidden_dev, wide, "w_up_grad")
    hidden, up_term = line.step("gate0", gate_term[0], (hidden, up_term))
    up_term = to_owners(up_term)
    out_part = rows_product(me, hidden, w_down, 0, rows, "block_out")
    out_part, grad_ffn_normed = line.step("gate1", gate_term[1], (out_part, grad_ffn_normed))
    out_sum = lax.psum_scatter(out_part, "fsdp", scatter_dimension=0, tiled=True)
    grad_ffn_normed = grad_ffn_normed.astype(F32)

    grad_middle_norm, ffn_gain_term = rms_back(
        grad_ffn_normed, ffn_unit, ffn_inverse, full_ffn_gain
    )
    grad_middle = grad_out_low.astype(F32) + grad_middle_norm
    grad_branch_low = grad_middle.astype(BF16)
    grad_attended = dot(full_out, grad_branch_low, 1, 1).astype(BF16)
    out_term = dot(attended, grad_branch_low, 1, 0).astype(BF16)
    out_rows = lax.psum_scatter(out_term, "fsdp", scatter_dimension=0, tiled=True)
    (grad_attended,) = line.step("up0", up_term[0], (grad_attended,))
    grad_queries, grad_keys, grad_values = attend_back(
        index,
        queries,
        keys,
        values,
        attended,
        log_totals,
        grad_attended,
        share,
        layout.piece_rows,
        layout.step_rows,
    )
    grad_queries, grad_keys, grad_values = line.step(
        "up1", up_term[1], (grad_queries, grad_keys, grad_values)
    )
    grad_pair = jnp.concatenate([grad_keys[:, :rows], grad_values[:, :rows]], axis=0)
    for k in range(1, share):
        columns = slice(k * rows, (k + 1) * rows)
        sent = jnp.concatenate([grad_keys[:, columns], grad_values[:, columns]], axis=0)
        grad_pair = grad_pair + permute(sent.astype(BF16), layout.across(k)).astype(F32)
    grad_pair_low = grad_pair.astype(BF16)
    grad_turned = (
        jnp.concatenate([grad_queries, grad_pair_low[:pair_width]], axis=0)
        .astype(F32)
        .reshape(turned, HD, rows)
    )
    grad_head_normed = rotate(grad_turned, cosine_table, -sine_table)
    scaled = grad_head_normed * head_gains
    grad_head_raw = head_inverse * (
        scaled - head_unit * jnp.mean(scaled * head_unit, axis=1, keepdims=True)
    )
    head_gain_terms = jnp.sum(grad_head_normed * head_unit, axis=2)
    grad_raw = jnp.concatenate(
        [grad_head_raw.astype(BF16).reshape(turned * HD, rows), grad_pair_low[pair_width:]], axis=0
    )
    projection_term = dot(normed_low, grad_raw, 0, 1).astype(BF16)
    projection_term, grad_raw = lax.optimization_barrier((projection_term, grad_raw))
    projection_rows = lax.psum_scatter(
        projection_term, "fsdp", scatter_dimension=0, tiled=True
    )
    grad_raw, out_sum = line.step("out", out_rows, (grad_raw, out_sum))
    block_out = return_rows(layout, (middle + out_sum.astype(F32)).astype(BF16), f)
    grad_normed = dot(grad_raw, w_attn, 0, 1)
    grad_input_norm, attn_gain_term = rms_back(
        grad_normed, normed_unit, normed_inverse, full_attn_gain
    )

    def column(vector):
        spread = vector.reshape(fsdp_devices, -1)
        return jnp.pad(spread, ((0, 0), (0, wide - spread.shape[1]))).reshape(D)

    gain_terms = jnp.stack(
        [
            attn_gain_term,
            ffn_gain_term,
            column(jnp.sum(head_gain_terms[:HQ], axis=0)),
            column(jnp.sum(head_gain_terms[HQ:], axis=0)),
        ],
        axis=1,
    )
    gain_terms = jnp.pad(gain_terms, ((0, 0), (0, 128 - gain_terms.shape[1]))).astype(BF16)
    projection_rows, gain_terms = lax.optimization_barrier((projection_rows, gain_terms))
    gain_rows = lax.psum_scatter(gain_terms, "fsdp", scatter_dimension=0, tiled=True)
    tokens_grad = return_rows(layout, (grad_middle + grad_input_norm).astype(BF16), f)
    line.step("attn", projection_rows)
    line.step("gain", gain_rows)
    line.finish()

    w_down_grad = jnp.concatenate([line.result(f"down{h}") for h in range(HALVES)]).astype(F32)
    w_gate_grad = unpack_columns(line.outer, [line.results[f"gate{h}"] for h in range(HALVES)])
    w_up_grad = unpack_columns(line.outer, [line.results[f"up{h}"] for h in range(HALVES)])
    w_out_grad = line.result("out").astype(F32)
    attn_rows = line.result("attn").astype(F32)
    gain_rows = line.result("gain").astype(F32)
    query_width = HQ * HD

    return (
        block_out[:, None],
        tokens_grad[:, None],
        gain_rows[:, 0],
        gain_rows[:narrow, 2],
        gain_rows[:narrow, 3],
        attn_rows[:, :query_width],
        attn_rows[:, query_width : query_width + pair_width],
        attn_rows[:, query_width + pair_width :],
        w_out_grad,
        gain_rows[:, 1],
        w_gate_grad,
        w_up_grad,
        w_down_grad,
    )


def solution(mesh):
    activations = P(None, "fsdp", "seq", None)
    vector = P("fsdp")
    matrix = P("fsdp", None)
    specs = (
        (activations, activations)
        + (vector,) * 3
        + (matrix,) * 4
        + (vector,)
        + (matrix,) * 3
    )
    return jax.shard_map(body, mesh=mesh, in_specs=specs, out_specs=specs, check_vma=False)
```

```python
import functools
import math

import jax
import jax.numpy as jnp
from jax import lax
from jax.experimental import pallas as pl
from jax.experimental.pallas import tpu as pltpu
from jax.sharding import PartitionSpec as P

D = 2048
HQ = 32
KVH = 8
HD = 64
FF = 8192
LENGTH = 1024
MICRO = 2
HALVES = 2
SWAPS = 4

EPSILON = 1e-05
THETA = 1000000.0
GROUP = HQ // KVH
BLOCK = 128
SCALE = 1.0 / math.sqrt(HD)
LOG2E = math.log2(math.e)
VMEM_LIMIT = 56 * 1024 * 1024

F32 = jnp.float32
BF16 = jnp.bfloat16


def dot(left_side, right_side, left_dim, right_dim):
    return lax.dot_general(
        left_side,
        right_side,
        (((left_dim,), (right_dim,)), ((), ())),
        preferred_element_type=F32,
    )


def rms_fwd(values, row_gain):
    inverse = lax.rsqrt(jnp.mean(values * values, axis=-1, keepdims=True) + EPSILON)
    unit_rows = values * inverse
    return (unit_rows * row_gain, unit_rows, inverse)


def rms_back(grad_outputs, unit_rows, inverse, row_gain):
    scaled = grad_outputs * row_gain
    grad_inputs = inverse * (
        scaled - unit_rows * jnp.mean(scaled * unit_rows, axis=-1, keepdims=True)
    )
    grad_gain = jnp.sum(grad_outputs * unit_rows, axis=0)
    return (grad_inputs, grad_gain)


def head_rms_fwd(values, gains):
    inverse = lax.rsqrt(jnp.mean(values * values, axis=1, keepdims=True) + EPSILON)
    unit = values * inverse
    return (unit * gains, unit, inverse)


def rotate(values, cosine_table, sine_table):
    half_width = values.shape[1] // 2
    front_half = values[:, :half_width]
    back_half = values[:, half_width:]
    return jnp.concatenate(
        [
            front_half * cosine_table - back_half * sine_table,
            back_half * cosine_table + front_half * sine_table,
        ],
        axis=1,
    )


def block_masks(index, pieces, piece_rows, step_rows):
    key = lax.broadcasted_iota(jnp.int32, (BLOCK, GROUP * BLOCK), 0)
    query = lax.broadcasted_iota(jnp.int32, (BLOCK, GROUP * BLOCK), 1) & (BLOCK - 1)

    def place(row, piece):
        return (row // piece_rows) * step_rows + piece * piece_rows + (row & (piece_rows - 1))

    return [place(key, index ^ k) <= place(query, index) for k in range(pieces)]


def heads_beside(block, first, count):
    return jnp.concatenate(
        [block[h * HD : (h + 1) * HD, first : first + count] for h in range(GROUP)], axis=1
    )


def mask_tail(values, mask, first):
    tail = jnp.where(mask, values[first:], 0.0)
    if first == 0:
        return tail
    return jnp.concatenate([values[:first], tail], axis=0)


def attend_kernel(index_ref, q_ref, k_ref, v_ref, out_ref, lse_ref, *, pieces, piece_rows, step_rows):
    rows = q_ref.shape[1]
    masks = block_masks(index_ref[0], pieces, piece_rows, step_rows)
    queries = q_ref[...]
    for first in range(0, rows, BLOCK):
        count = first + BLOCK
        query_block = heads_beside(queries, first, BLOCK)
        total = None
        result = None
        for k in range(pieces):
            spot = pl.ds(k * rows, count)
            scores = dot(k_ref[:, spot], query_block, 0, 0)
            weights = mask_tail(jnp.exp2(scores * (SCALE * LOG2E)), masks[k], first)
            part = jnp.sum(weights, axis=0, keepdims=True)
            value = dot(v_ref[:, spot], weights.astype(BF16), 1, 0)
            total = part if total is None else total + part
            result = value if result is None else result + value
        result = result * (1.0 / total)
        log_total = jnp.log2(total)
        for h in range(GROUP):
            columns = slice(h * BLOCK, (h + 1) * BLOCK)
            out_ref[h * HD : (h + 1) * HD, first : first + BLOCK] = result[:, columns].astype(BF16)
            lse_ref[0, h : h + 1, first : first + BLOCK] = log_total[:, columns]


def attend_back_kernel(
    index_ref, q_ref, k_ref, v_ref, out_ref, lse_ref, grad_ref, dq_ref, dk_ref, dv_ref,
    *, pieces, piece_rows, step_rows
):
    rows = q_ref.shape[1]
    masks = block_masks(index_ref[0], pieces, piece_rows, step_rows)
    queries = q_ref[...]
    grads = grad_ref[...]
    results = out_ref[...]
    dk_ref[...] = jnp.zeros_like(dk_ref)
    dv_ref[...] = jnp.zeros_like(dv_ref)
    for first in range(0, rows, BLOCK):
        count = first + BLOCK
        query_block = heads_beside(queries, first, BLOCK)
        grad_block = heads_beside(grads, first, BLOCK)
        result_block = heads_beside(results, first, BLOCK)
        centre = jnp.sum(
            grad_block.astype(F32) * result_block.astype(F32), axis=0, keepdims=True
        )
        log_total = jnp.concatenate(
            [lse_ref[0, h : h + 1, first : first + BLOCK] for h in range(GROUP)], axis=1
        )
        dq = None
        for k in range(pieces):
            spot = pl.ds(k * rows, count)
            keys = k_ref[:, spot]
            scores = dot(keys, query_block, 0, 0)
            weights = mask_tail(
                jnp.exp2(scores * (SCALE * LOG2E) - log_total), masks[k], first
            )
            grad_weights = dot(v_ref[:, spot], grad_block, 0, 0)
            grad_scores = (weights * (grad_weights - centre)).astype(BF16)
            part = dot(keys, grad_scores, 1, 0)
            dq = part if dq is None else dq + part
            dk_ref[:, spot] += dot(query_block, grad_scores, 1, 1) * SCALE
            dv_ref[:, spot] += dot(grad_block, weights.astype(BF16), 1, 1)
        dq = (dq * SCALE).astype(BF16)
        for h in range(GROUP):
            columns = slice(h * BLOCK, (h + 1) * BLOCK)
            dq_ref[h * HD : (h + 1) * HD, first : first + BLOCK] = dq[:, columns]


def attention_specs(rows, total_rows):
    group_spec = pl.BlockSpec((GROUP * HD, rows), lambda i: (i, 0))
    pair_spec = pl.BlockSpec((HD, total_rows), lambda i: (i, 0))
    lse_spec = pl.BlockSpec((1, GROUP, rows), lambda i: (i, 0, 0))
    return group_spec, pair_spec, lse_spec


def attend(index, queries, keys, values, pieces, piece_rows, step_rows):
    rows, total_rows = queries.shape[1], keys.shape[1]
    group_spec, pair_spec, lse_spec = attention_specs(rows, total_rows)
    return pl.pallas_call(
        functools.partial(
            attend_kernel, pieces=pieces, piece_rows=piece_rows, step_rows=step_rows
        ),
        grid=(KVH,),
        in_specs=[pl.BlockSpec(memory_space=pltpu.SMEM), group_spec, pair_spec, pair_spec],
        out_specs=[group_spec, lse_spec],
        out_shape=[
            jax.ShapeDtypeStruct((HQ * HD, rows), BF16),
            jax.ShapeDtypeStruct((KVH, GROUP, rows), F32),
        ],
        compiler_params=pltpu.CompilerParams(vmem_limit_bytes=VMEM_LIMIT),
        cost_estimate=pl.CostEstimate(
            flops=4 * HQ * HD * rows * total_rows,
            bytes_accessed=8 * HQ * HD * rows,
            transcendentals=HQ * rows * total_rows,
        ),
        name="attend",
    )(index, queries, keys, values)


def attend_back(index, queries, keys, values, results, lse, grads, pieces, piece_rows, step_rows):
    rows, total_rows = queries.shape[1], keys.shape[1]
    group_spec, pair_spec, lse_spec = attention_specs(rows, total_rows)
    return pl.pallas_call(
        functools.partial(
            attend_back_kernel, pieces=pieces, piece_rows=piece_rows, step_rows=step_rows
        ),
        grid=(KVH,),
        in_specs=[
            pl.BlockSpec(memory_space=pltpu.SMEM),
            group_spec,
            pair_spec,
            pair_spec,
            group_spec,
            lse_spec,
            group_spec,
        ],
        out_specs=[group_spec, pair_spec, pair_spec],
        out_shape=[
            jax.ShapeDtypeStruct((HQ * HD, rows), BF16),
            jax.ShapeDtypeStruct((KVH * HD, total_rows), F32),
            jax.ShapeDtypeStruct((KVH * HD, total_rows), F32),
        ],
        compiler_params=pltpu.CompilerParams(vmem_limit_bytes=VMEM_LIMIT),
        cost_estimate=pl.CostEstimate(
            flops=10 * HQ * HD * rows * total_rows,
            bytes_accessed=16 * HQ * HD * rows,
            transcendentals=HQ * rows * total_rows,
        ),
        name="attend_back",
    )(index, queries, keys, values, results, lse, grads)


def hidden_kernel(own_x_ref, own_c_ref, other_x_ref, other_c_ref, weight_ref, down_ref, *refs):
    hidden_ref, grads_ref, hidden_t_ref, grads_t_ref, all_x_ref, all_c_ref = refs[-6:]
    units = down_ref.shape[0]
    half = units // HALVES

    def work(x_ref, c_ref):
        x = x_ref[...]
        c = c_ref[...]
        all_x_ref[...] = x
        all_c_ref[...] = c
        for h in range(HALVES):
            part = slice(h * half, (h + 1) * half)
            up_part = slice(units + h * half, units + (h + 1) * half)
            gate = dot(x, weight_ref[:, part], 1, 0)
            up = dot(x, weight_ref[:, up_part], 1, 0)
            grad_hidden = dot(c, down_ref[part, :], 1, 1)
            sigmoid = 0.5 * jnp.tanh(0.5 * gate) + 0.5
            silu = gate * sigmoid
            hidden = (silu * up).astype(BF16)
            grad_up = (grad_hidden * silu).astype(BF16)
            grad_gate = (grad_hidden * up * (sigmoid + silu * (1.0 - sigmoid))).astype(BF16)
            hidden_ref[:, part] = hidden
            grads_ref[:, part] = grad_gate
            grads_ref[:, up_part] = grad_up
            hidden_t_ref[part, :] = hidden.T
            grads_t_ref[part, :] = grad_gate.T
            grads_t_ref[up_part, :] = grad_up.T

    pl.when(pl.program_id(0) == 0)(lambda: work(own_x_ref, own_c_ref))
    pl.when(pl.program_id(0) == 1)(lambda: work(other_x_ref, other_c_ref))


def hidden_step(n, count, rows, pieces, weights, w_down, so_far):
    depth = w_down.shape[1]
    units = w_down.shape[0]
    once = pl.Buffered(1)
    read = [
        pl.BlockSpec((rows, depth), lambda i, block=block: (block, 0), pipeline_mode=once)
        for _, block in pieces
    ]
    widths = (units, 2 * units)
    upright = [(count, width) for width in widths]
    turned = [(width, count) for width in widths]
    whole = [(count, depth)] * 2
    flops = 12 * rows * depth * units
    return pl.pallas_call(
        hidden_kernel,
        grid=(2,),
        in_specs=read
        + [
            pl.BlockSpec((depth, 2 * units), lambda i: (0, 0), pipeline_mode=once),
            pl.BlockSpec((units, depth), lambda i: (0, 0), pipeline_mode=once),
        ]
        + [pl.BlockSpec(memory_space=pl.ANY)] * len(so_far),
        out_specs=[pl.BlockSpec((rows, shape[1]), lambda i: (2 * n + i, 0)) for shape in upright]
        + [pl.BlockSpec((shape[0], rows), lambda i: (0, 2 * n + i)) for shape in turned]
        + [pl.BlockSpec((rows, shape[1]), lambda i: (2 * n + i, 0)) for shape in whole],
        out_shape=[jax.ShapeDtypeStruct(shape, BF16) for shape in upright + turned + whole],
        input_output_aliases={6 + k: k for k in range(len(so_far))},
        compiler_params=pltpu.CompilerParams(vmem_limit_bytes=VMEM_LIMIT),
        cost_estimate=pl.CostEstimate(
            flops=flops,
            bytes_accessed=16 * rows * depth + 24 * rows * units + 6 * depth * units,
            transcendentals=2 * rows * units,
        ),
        name="hidden_step",
    )(*[array for array, _ in pieces], weights, w_down, *so_far)


def rows_kernel(me_ref, left_ref, right_ref, result_ref, *, right_dim):
    result_ref[...] = dot(left_ref[...], right_ref[...], 1, right_dim).astype(BF16)


def rows_product(me, left, right, right_dim, block_rows, name):
    count, width = left.shape
    return pl.pallas_call(
        functools.partial(rows_kernel, right_dim=right_dim),
        grid_spec=pltpu.PrefetchScalarGridSpec(
            num_scalar_prefetch=1,
            grid=(count // block_rows,),
            in_specs=[
                pl.BlockSpec((block_rows, width), lambda i, me_ref: (i, 0)),
                pl.BlockSpec(
                    right.shape, lambda i, me_ref: (0, 0), pipeline_mode=pl.Buffered(1)
                ),
            ],
            out_specs=pl.BlockSpec((block_rows, D), lambda i, me_ref: (me_ref[0] ^ i, 0)),
        ),
        out_shape=jax.ShapeDtypeStruct((count, D), BF16),
        compiler_params=pltpu.CompilerParams(vmem_limit_bytes=VMEM_LIMIT),
        cost_estimate=pl.CostEstimate(
            flops=2 * count * D * width,
            bytes_accessed=2 * (count * width + count * D + D * width),
            transcendentals=0,
        ),
        name=name,
    )(me, left, right)


def weight_kernel(left_ref, right_ref, *result_refs, parts):
    total = dot(left_ref[...], right_ref[...], 1, 0)
    half = total.shape[0] // HALVES
    for h, result_ref in enumerate(result_refs):
        piece = total[h * half : (h + 1) * half]
        if parts == 0:
            result_ref[...] = piece.astype(BF16)
            continue
        wide = piece.shape[1] // parts
        for p in range(parts):
            result_ref[p] = piece[:, p * wide : (p + 1) * wide].astype(BF16).T


def weight_product(left, right, first, units, wide, name):
    depth = left.shape[1]
    half = units // HALVES
    column = min(512, D)
    parts = column // wide if wide else 0
    block = first // units
    if wide:
        out_spec = pl.BlockSpec((parts, wide, half), lambda j: (j, 0, 0))
        out_shape = jax.ShapeDtypeStruct((D // wide, wide, half), BF16)
    else:
        out_spec = pl.BlockSpec((half, column), lambda j: (0, j))
        out_shape = jax.ShapeDtypeStruct((half, D), BF16)
    return pl.pallas_call(
        functools.partial(weight_kernel, parts=parts),
        grid=(D // column,),
        in_specs=[
            pl.BlockSpec((units, depth), lambda j: (block, 0), pipeline_mode=pl.Buffered(1)),
            pl.BlockSpec((depth, column), lambda j: (0, j)),
        ],
        out_specs=[out_spec] * HALVES,
        out_shape=[out_shape] * HALVES,
        compiler_params=pltpu.CompilerParams(vmem_limit_bytes=VMEM_LIMIT),
        cost_estimate=pl.CostEstimate(
            flops=2 * units * depth * D,
            bytes_accessed=2 * depth * (units + D) + 2 * units * D,
            transcendentals=0,
        ),
        name=name,
    )(left, right)


def merge_kernel(even_ref, *refs):
    result_ref = refs[-1]
    piece = result_ref.shape[1] // (2 * SWAPS)
    for h in range(SWAPS):
        mine, theirs = refs[h][...], refs[SWAPS + h][...]
        gate = jnp.where(even_ref[0] > 0, mine, theirs)
        up = jnp.where(even_ref[0] > 0, theirs, mine)
        result_ref[:, h * piece : (h + 1) * piece] = gate
        result_ref[:, (SWAPS + h) * piece : (SWAPS + h + 1) * piece] = up


def merge_columns(even, mine, theirs):
    rows, piece = mine[0].shape
    tile = min(256, rows)
    return pl.pallas_call(
        merge_kernel,
        grid=(rows // tile,),
        in_specs=[pl.BlockSpec(memory_space=pltpu.SMEM)]
        + [pl.BlockSpec((tile, piece), lambda i: (i, 0))] * (2 * SWAPS),
        out_specs=pl.BlockSpec((tile, 2 * SWAPS * piece), lambda i: (i, 0)),
        out_shape=jax.ShapeDtypeStruct((rows, 2 * SWAPS * piece), BF16),
        compiler_params=pltpu.CompilerParams(vmem_limit_bytes=VMEM_LIMIT),
        cost_estimate=pl.CostEstimate(
            flops=0, bytes_accessed=8 * rows * SWAPS * piece, transcendentals=0
        ),
        name="merge_columns",
    )(even.astype(jnp.int32).reshape(1), *mine, *theirs)


def pack_kernel(even_ref, first_ref, second_ref, result_ref):
    chosen = jnp.where(even_ref[0] > 0, first_ref[...], second_ref[...])
    width = result_ref.shape[-1]
    for h in range(SWAPS):
        result_ref[0, h] = chosen[:, h * width : (h + 1) * width]


def pack_columns(even, first, second, parts):
    rows, columns = first.shape
    width = columns // parts
    block = pl.BlockSpec((rows, width), lambda i: (0, i))
    piece = width // SWAPS
    return pl.pallas_call(
        pack_kernel,
        grid=(parts,),
        in_specs=[pl.BlockSpec(memory_space=pltpu.SMEM), block, block],
        out_specs=pl.BlockSpec((1, SWAPS, rows, piece), lambda i: (i, 0, 0, 0)),
        out_shape=jax.ShapeDtypeStruct((parts, SWAPS, rows, piece), BF16),
        compiler_params=pltpu.CompilerParams(vmem_limit_bytes=VMEM_LIMIT),
        cost_estimate=pl.CostEstimate(
            flops=0, bytes_accessed=6 * rows * columns, transcendentals=0
        ),
        name="pack_columns",
    )(even.astype(jnp.int32).reshape(1), first, second)


def unpack_kernel(*refs):
    result_ref = refs[-1]
    width = refs[0].shape[-1]
    for h in range(HALVES):
        result_ref[:, h * width : (h + 1) * width] = refs[h][0].astype(F32)


def unpack_columns(pieces):
    parts, rows, half = pieces[0].shape
    return pl.pallas_call(
        unpack_kernel,
        grid=(parts,),
        in_specs=[pl.BlockSpec((1, rows, half), lambda i: (i, 0, 0))] * HALVES,
        out_specs=pl.BlockSpec((rows, HALVES * half), lambda i: (0, i)),
        out_shape=jax.ShapeDtypeStruct((rows, parts * HALVES * half), F32),
        compiler_params=pltpu.CompilerParams(vmem_limit_bytes=VMEM_LIMIT),
        cost_estimate=pl.CostEstimate(
            flops=0, bytes_accessed=6 * parts * rows * HALVES * half, transcendentals=0
        ),
        name="unpack_columns",
    )(*pieces)


class Layout:
    def __init__(self, fsdp_devices, seq_devices, rows_dev):
        self.fsdp = fsdp_devices
        self.seq = seq_devices
        self.chips = fsdp_devices // 2
        self.share = 2 * seq_devices // (2 * MICRO)
        self.near = self.share // 2
        self.piece_rows = rows_dev // self.share
        self.step_rows = rows_dev
        self.rows = LENGTH // self.share

    def flat(self, f, z):
        return f * self.seq + z

    def moved(self, r):
        pairs = []
        for f in range(self.fsdp):
            for z in range(self.seq):
                slot = z ^ r
                micro, j = slot // self.share, slot % self.share
                target_f = (f // 2) * 2 + j % 2
                target_z = (2 * micro + f % 2) * self.near + j // 2
                pairs.append((self.flat(f, z), self.flat(target_f, target_z)))
        return pairs

    def other(self, k):
        return [
            (self.flat(f, z), self.flat(f ^ k, z))
            for f in range(self.fsdp)
            for z in range(self.seq)
        ]

    def across(self, k):
        pairs = []
        for f in range(self.fsdp):
            for z in range(self.seq):
                pairs.append((self.flat(f, z), self.flat(f ^ (k & 1), z ^ (k >> 1))))
        return pairs


def permute(value, pairs):
    return lax.ppermute(value, ("fsdp", "seq"), pairs)


def scatter_rows(layout, values, z, slot):
    parts = values.reshape(layout.seq, layout.piece_rows, values.shape[-1])
    result = jnp.zeros_like(parts)
    for r in range(layout.seq):
        sent = lax.dynamic_index_in_dim(parts, z ^ r, 0, keepdims=False)
        got = permute(sent, layout.moved(r))
        result = lax.dynamic_update_index_in_dim(result, got, slot ^ r, 0)
    return result.reshape(layout.rows, values.shape[-1])


def return_rows(layout, values, f):
    width = values.shape[-1]
    parts = values.reshape(layout.seq, layout.piece_rows, width)
    parts = lax.all_to_all(parts, "seq", split_axis=0, concat_axis=0, tiled=True)
    parts = parts.reshape(MICRO, 2, layout.near, layout.piece_rows, width)
    core = f % 2
    kept = lax.dynamic_index_in_dim(parts, core, 1, keepdims=False)
    sent = lax.dynamic_index_in_dim(parts, 1 - core, 1, keepdims=False)
    got = permute(sent, layout.other(1))
    both = jnp.stack(
        [jnp.where(core == 0, kept, got), jnp.where(core == 0, got, kept)], axis=2
    )
    return both.reshape(MICRO, layout.step_rows, width)


class RowGather:
    def __init__(self, layout, first, second):
        self.layout = layout
        self.rows = first.shape[0]
        both = jnp.concatenate([first, second])
        self.own = {0: [both]}
        self.sibling = {0: [self.move(both, 1)]}
        chips = layout.chips
        for n in range(1, 3 if chips == 4 else chips):
            self.own[n] = [self.move(both, 2 * n)]

    def move(self, value, k):
        return permute(value, self.layout.other(k))

    def chunk(self, n):
        pieces = []
        for arrays in (self.own[n], self.sibling[n]):
            pieces += [(arrays[0], 0), (arrays[-1], len(arrays) % 2)]
        return pieces

    def after(self, n, *values):
        chips = self.layout.chips
        if n + 1 < chips:
            waiting = {m: value for m, value in self.own.items() if m > n}
            siblings = {m: value for m, value in self.sibling.items() if m > n}
            waiting, siblings, values = lax.optimization_barrier((waiting, siblings, values))
            self.own.update(waiting)
            self.sibling.update(siblings)
            if chips == 4 and n == 0:
                far = [self.move(self.own[2][0][: self.rows], 2)]
                far += [self.move(self.own[1][0][self.rows :], 4)]
                self.far = far
            if chips == 4 and n == 1:
                self.own[3] = lax.optimization_barrier((self.far, values))[0]
            for m in (n + 1, n + 2):
                if m in self.own and m not in self.sibling:
                    self.sibling[m] = [self.move(value, 1) for value in self.own[m]]
        return values


def gather_small(layout, f, own):
    held = own[None]
    k = 1
    while k < layout.fsdp:
        got = permute(held, layout.other(k))
        upper = (f & k) > 0
        held = jnp.concatenate(
            [jnp.where(upper, got, held), jnp.where(upper, held, got)], axis=0
        )
        k *= 2
    return held


def sum_small(layout, value):
    k = 1
    while k < layout.fsdp:
        value = value + permute(value, layout.other(k))
        k *= 2
    return value


class LinePipe:
    def __init__(self, z, seq_devices):
        self.seq = seq_devices
        self.z = z
        self.outer = (z == 0) | (z == seq_devices - 1)
        self.flying = []
        self.results = {}
        self.then = {}
        self.age = {}

    def send(self, stage, value):
        half, last = self.seq // 2, self.seq - 1
        if stage < half - 1:
            pairs = [(stage, stage + 1), (last - stage, last - stage - 1)]
        elif stage == half - 1:
            pairs = [(half - 1, half), (half, half - 1)]
        else:
            s = last - 1 - stage
            pairs = [(s + 1, s), (last - s - 1, last - s)]
        return lax.ppermute(value, "seq", pairs)

    def join(self, stage, value, got):
        if stage < self.seq // 2:
            return value + got
        s = self.seq - 2 - stage
        return jnp.where((self.z == s) | (self.z == self.seq - 1 - s), got, value)

    def step(self, name=None, value=None, others=(), then=None):
        arrived = [entry[3] for entry in self.flying]
        old = {key: self.results[key] for key in self.results if self.age.get(key, 0) <= 0}
        arrived, old, value, others = lax.optimization_barrier((arrived, old, value, others))
        self.results.update(old)
        self.age = {key: age - 1 for key, age in self.age.items()}
        flying = []
        if name is not None:
            self.then[name] = then
            flying.append((name, 0, value, self.send(0, value)))
        for (key, stage, held, _), got in zip(self.flying, arrived):
            if stage == self.seq - 2:
                chosen = jnp.where(self.outer, got, held)
                self.results[key] = chosen
                if self.then[key] is not None:
                    self.results[key] = self.then[key](chosen)
                    self.age[key] = 1
                continue
            held = self.join(stage, held, got)
            flying.append((key, stage + 1, held, self.send(stage + 1, held)))
        self.flying = flying
        return others

    def landed(self, names):
        return all(name in self.results for name in names)

    def finish(self):
        while self.flying:
            self.step()


def body(
    tokens,
    cotangent,
    attn_gain,
    query_gain,
    key_gain,
    w_query,
    w_key,
    w_value,
    w_out,
    ffn_gain,
    w_gate,
    w_up,
    w_down,
):
    fsdp_devices = lax.axis_size("fsdp")
    seq_devices = lax.axis_size("seq")
    layout = Layout(fsdp_devices, seq_devices, tokens.shape[2])
    f = lax.axis_index("fsdp")
    z = lax.axis_index("seq")
    rows = layout.rows
    share = layout.share
    member = (z % layout.near) * 2 + f % 2
    slot = (z // layout.near // 2) * share + member

    w_attn = lax.all_gather(
        jnp.concatenate([w_query, w_key, w_value], axis=1), "fsdp", axis=0, tiled=True
    )
    gains = gather_small(
        layout, f, jnp.concatenate([attn_gain, ffn_gain, query_gain, key_gain])
    ).astype(F32)
    wide, narrow = attn_gain.shape[0], query_gain.shape[0]
    even = z % 2 == 0
    hidden_dev = w_down.shape[0]
    gains, gate_rows, up_rows = lax.optimization_barrier((gains, w_gate, w_up))
    fetched = lax.all_to_all(
        pack_columns(even, gate_rows, up_rows, fsdp_devices),
        "fsdp",
        split_axis=0,
        concat_axis=0,
        tiled=True,
    )
    full_attn_gain = gains[:, :wide].reshape(D)
    full_ffn_gain = gains[:, wide : 2 * wide].reshape(D)
    full_query_gain = gains[:, 2 * wide : 2 * wide + narrow].reshape(HD)
    full_key_gain = gains[:, 2 * wide + narrow :].reshape(HD)
    inputs_low = scatter_rows(layout, tokens[:, 0], z, slot)
    grad_out_low = scatter_rows(layout, cotangent[:, 0], z, slot)
    full_out = lax.all_gather(w_out, "fsdp", axis=0, tiled=True)

    row = jnp.arange(rows, dtype=jnp.int32)
    position = (
        (row // layout.piece_rows) * layout.step_rows
        + member * layout.piece_rows
        + row % layout.piece_rows
    ).astype(F32)
    frequency = THETA ** (-(jnp.arange(HD // 2).astype(F32) * 2.0 / HD))
    angles = frequency[:, None] * position[None, :]
    cosine_table, sine_table = jnp.cos(angles)[None], jnp.sin(angles)[None]
    head_gains = jnp.concatenate(
        [
            jnp.broadcast_to(full_query_gain[None, :, None], (HQ, HD, 1)),
            jnp.broadcast_to(full_key_gain[None, :, None], (KVH, HD, 1)),
        ]
    )

    inputs = inputs_low.astype(F32)
    normed, normed_unit, normed_inverse = rms_fwd(inputs, full_attn_gain)
    normed_low, grad_out_low, w_attn, fetched = lax.optimization_barrier(
        (normed.astype(BF16), grad_out_low, w_attn, fetched)
    )
    fetched = [fetched[:, h].reshape(D, hidden_dev // SWAPS) for h in range(SWAPS)]
    swapped = [
        lax.ppermute(piece, "seq", [(i, i ^ 1) for i in range(seq_devices)]) for piece in fetched
    ]
    raw = dot(w_attn, normed_low, 0, 1)
    pair_width = KVH * HD
    turned = HQ + KVH
    head_raw = raw[: turned * HD].reshape(turned, HD, rows)
    head_normed, head_unit, head_inverse = head_rms_fwd(head_raw, head_gains)
    heads_low = rotate(head_normed, cosine_table, sine_table).astype(BF16).reshape(turned * HD, rows)
    queries = heads_low[: HQ * HD]
    own_pair = jnp.concatenate([heads_low[HQ * HD :], raw[turned * HD :].astype(BF16)], axis=0)
    pair_pieces = [own_pair] + [permute(own_pair, layout.across(k)) for k in range(1, share)]
    keys = jnp.concatenate([piece[:pair_width] for piece in pair_pieces], axis=1)
    values = jnp.concatenate([piece[pair_width:] for piece in pair_pieces], axis=1)
    index = member.astype(jnp.int32).reshape(1)
    attended, log_totals = attend(
        index, queries, keys, values, share, layout.piece_rows, layout.step_rows
    )
    attended, swapped[:2] = lax.optimization_barrier((attended, swapped[:2]))
    middle = inputs + dot(attended, full_out, 0, 0)
    ffn_normed, ffn_unit, ffn_inverse = rms_fwd(middle, full_ffn_gain)
    ffn_low = ffn_normed.astype(BF16)

    gather = RowGather(layout, ffn_low, grad_out_low)
    line = LinePipe(z, seq_devices)
    weights = merge_columns(even, fetched, swapped)
    worked = ()
    for n in range(layout.chips):
        worked = hidden_step(n, fsdp_devices * rows, rows, gather.chunk(n), weights, w_down, worked)
        worked = gather.after(n, *worked)
    hidden, grads, hidden_t, grads_t, ffn_rows, grad_out_rows = worked
    me = f.astype(jnp.int32).reshape(1)

    def to_owners(term):
        return lax.all_to_all(term, "fsdp", split_axis=0, concat_axis=0, tiled=True)

    down_term = weight_product(hidden_t, grad_out_rows, 0, hidden_dev, 0, "w_down_grad")
    (grads,) = line.step("down0", down_term[0], (grads,))
    grad_ffn_part = rows_product(me, grads, weights, 1, rows, "grad_ffn_normed")
    grad_ffn_part, grads_t = line.step("down1", down_term[1], (grad_ffn_part, grads_t))
    grad_ffn_normed = lax.psum_scatter(
        grad_ffn_part, "fsdp", scatter_dimension=0, tiled=True
    )
    gate_term = weight_product(grads_t, ffn_rows, 0, hidden_dev, wide, "w_gate_grad")
    up_term = weight_product(grads_t, ffn_rows, hidden_dev, hidden_dev, wide, "w_up_grad")
    hidden, up_term = line.step("gate0", gate_term[0], (hidden, up_term), to_owners)
    out_part = rows_product(me, hidden, w_down, 0, rows, "block_out")
    out_part, grad_ffn_normed = line.step(
        "gate1", gate_term[1], (out_part, grad_ffn_normed), to_owners
    )
    out_sum = lax.psum_scatter(out_part, "fsdp", scatter_dimension=0, tiled=True)
    grad_ffn_normed = grad_ffn_normed.astype(F32)

    grad_middle_norm, ffn_gain_term = rms_back(
        grad_ffn_normed, ffn_unit, ffn_inverse, full_ffn_gain
    )
    grad_middle = grad_out_low.astype(F32) + grad_middle_norm
    grad_branch_low = grad_middle.astype(BF16)
    grad_attended = dot(full_out, grad_branch_low, 1, 1).astype(BF16)
    out_term = dot(attended, grad_branch_low, 1, 0).astype(BF16)
    out_rows = lax.psum_scatter(out_term, "fsdp", scatter_dimension=0, tiled=True)
    (grad_attended,) = line.step("up0", up_term[0], (grad_attended,), to_owners)
    grad_queries, grad_keys, grad_values = attend_back(
        index,
        queries,
        keys,
        values,
        attended,
        log_totals,
        grad_attended,
        share,
        layout.piece_rows,
        layout.step_rows,
    )
    grad_queries, grad_keys, grad_values = line.step(
        "up1", up_term[1], (grad_queries, grad_keys, grad_values), to_owners
    )
    grad_pair = jnp.concatenate([grad_keys[:, :rows], grad_values[:, :rows]], axis=0)
    for k in range(1, share):
        columns = slice(k * rows, (k + 1) * rows)
        sent = jnp.concatenate([grad_keys[:, columns], grad_values[:, columns]], axis=0)
        grad_pair = grad_pair + permute(sent.astype(BF16), layout.across(k)).astype(F32)
    grad_pair_low = grad_pair.astype(BF16)
    grad_turned = (
        jnp.concatenate([grad_queries, grad_pair_low[:pair_width]], axis=0)
        .astype(F32)
        .reshape(turned, HD, rows)
    )
    grad_head_normed = rotate(grad_turned, cosine_table, -sine_table)
    scaled = grad_head_normed * head_gains
    grad_head_raw = head_inverse * (
        scaled - head_unit * jnp.mean(scaled * head_unit, axis=1, keepdims=True)
    )
    head_gain_terms = jnp.sum(grad_head_normed * head_unit, axis=2)
    grad_raw = jnp.concatenate(
        [grad_head_raw.astype(BF16).reshape(turned * HD, rows), grad_pair_low[pair_width:]], axis=0
    )
    projection_term = dot(normed_low, grad_raw, 0, 1).astype(BF16)
    projection_term, grad_raw = lax.optimization_barrier((projection_term, grad_raw))
    projection_rows = lax.psum_scatter(
        projection_term, "fsdp", scatter_dimension=0, tiled=True
    )
    grad_raw, out_sum = line.step("out", out_rows, (grad_raw, out_sum))
    block_out = return_rows(layout, (middle + out_sum.astype(F32)).astype(BF16), f)
    grad_normed = dot(grad_raw, w_attn, 0, 1)
    grad_input_norm, attn_gain_term = rms_back(
        grad_normed, normed_unit, normed_inverse, full_attn_gain
    )

    tokens_grad = return_rows(layout, (grad_middle + grad_input_norm).astype(BF16), f)
    gain_terms = sum_small(
        layout,
        jnp.concatenate(
            [
                attn_gain_term,
                ffn_gain_term,
                jnp.sum(head_gain_terms[:HQ], axis=0),
                jnp.sum(head_gain_terms[HQ:], axis=0),
            ]
        )[None],
    )[0]

    def own_share(first, count):
        share_of = count // fsdp_devices
        vector = lax.dynamic_slice_in_dim(gain_terms, first + f * share_of, share_of, 0)
        return jnp.pad(vector, (0, wide - share_of))

    gain_columns = jnp.stack(
        [own_share(0, D), own_share(D, D), own_share(2 * D, HD), own_share(2 * D + HD, HD)],
        axis=1,
    )
    gain_columns = jnp.pad(gain_columns, ((0, 0), (0, 128 - gain_columns.shape[1]))).astype(BF16)

    middle_column = projection_rows.shape[1] // 2
    line.step("attn0", projection_rows[:, :middle_column])
    (gain_columns,) = line.step(
        "attn1",
        jnp.concatenate([projection_rows[:, middle_column:], gain_columns], axis=1),
        (gain_columns,),
    )
    while not line.landed([f"{name}{h}" for name in ("down", "gate", "up") for h in range(HALVES)]):
        line.step()
    w_gate_grad = unpack_columns([line.results[f"gate{h}"] for h in range(HALVES)])
    w_up_grad = unpack_columns([line.results[f"up{h}"] for h in range(HALVES)])
    w_down_grad = jnp.concatenate([line.results[f"down{h}"] for h in range(HALVES)]).astype(F32)
    w_gate_grad, w_up_grad, w_down_grad = line.step(
        others=(w_gate_grad, w_up_grad, w_down_grad)
    )
    line.finish()

    attn_rows = jnp.concatenate([line.results["attn0"], line.results["attn1"]], axis=1).astype(F32)
    w_out_grad = line.results["out"].astype(F32)
    gain_rows = attn_rows[:, attn_rows.shape[1] - 128 :]
    query_width = HQ * HD

    return (
        block_out[:, None],
        tokens_grad[:, None],
        gain_rows[:, 0],
        gain_rows[:narrow, 2],
        gain_rows[:narrow, 3],
        attn_rows[:, :query_width],
        attn_rows[:, query_width : query_width + pair_width],
        attn_rows[:, query_width + pair_width : query_width + 2 * pair_width],
        w_out_grad,
        gain_rows[:, 1],
        w_gate_grad,
        w_up_grad,
        w_down_grad,
    )


def solution(mesh):
    activations = P(None, "fsdp", "seq", None)
    vector = P("fsdp")
    matrix = P("fsdp", None)
    specs = (
        (activations, activations)
        + (vector,) * 3
        + (matrix,) * 4
        + (vector,)
        + (matrix,) * 3
    )
    return jax.shard_map(body, mesh=mesh, in_specs=specs, out_specs=specs, check_vma=False)
```

```python
import functools
import math

import jax
import jax.numpy as jnp
from jax import lax
from jax.experimental import pallas as pl
from jax.experimental.pallas import tpu as pltpu
from jax.sharding import PartitionSpec as P

D = 2048
HQ = 32
KVH = 8
HD = 64
FF = 8192
LENGTH = 1024
MICRO = 2
HALVES = 2

EPSILON = 1e-05
THETA = 1000000.0
GROUP = HQ // KVH
BLOCK = 128
SCALE = 1.0 / math.sqrt(HD)
LOG2E = math.log2(math.e)
VMEM_LIMIT = 56 * 1024 * 1024

F32 = jnp.float32
BF16 = jnp.bfloat16


def dot(left_side, right_side, left_dim, right_dim):
    return lax.dot_general(
        left_side,
        right_side,
        (((left_dim,), (right_dim,)), ((), ())),
        preferred_element_type=F32,
    )


def rms_fwd(values, row_gain):
    inverse = lax.rsqrt(jnp.mean(values * values, axis=-1, keepdims=True) + EPSILON)
    unit_rows = values * inverse
    return (unit_rows * row_gain, unit_rows, inverse)


def rms_back(grad_outputs, unit_rows, inverse, row_gain):
    scaled = grad_outputs * row_gain
    grad_inputs = inverse * (
        scaled - unit_rows * jnp.mean(scaled * unit_rows, axis=-1, keepdims=True)
    )
    grad_gain = jnp.sum(grad_outputs * unit_rows, axis=0)
    return (grad_inputs, grad_gain)


def head_rms_fwd(values, gains):
    inverse = lax.rsqrt(jnp.mean(values * values, axis=1, keepdims=True) + EPSILON)
    unit = values * inverse
    return (unit * gains, unit, inverse)


def rotate(values, cosine_table, sine_table):
    half_width = values.shape[1] // 2
    front_half = values[:, :half_width]
    back_half = values[:, half_width:]
    return jnp.concatenate(
        [
            front_half * cosine_table - back_half * sine_table,
            back_half * cosine_table + front_half * sine_table,
        ],
        axis=1,
    )


def block_masks(index, pieces, piece_rows, step_rows):
    key = lax.broadcasted_iota(jnp.int32, (BLOCK, GROUP * BLOCK), 0)
    query = lax.broadcasted_iota(jnp.int32, (BLOCK, GROUP * BLOCK), 1) & (BLOCK - 1)

    def place(row, piece):
        return (row // piece_rows) * step_rows + piece * piece_rows + (row & (piece_rows - 1))

    return [place(key, index ^ k) <= place(query, index) for k in range(pieces)]


def heads_beside(block, first, count):
    return jnp.concatenate(
        [block[h * HD : (h + 1) * HD, first : first + count] for h in range(GROUP)], axis=1
    )


def mask_tail(values, mask, first):
    tail = jnp.where(mask, values[first:], 0.0)
    if first == 0:
        return tail
    return jnp.concatenate([values[:first], tail], axis=0)


def attend_kernel(index_ref, q_ref, k_ref, v_ref, out_ref, lse_ref, *, pieces, piece_rows, step_rows):
    rows = q_ref.shape[1]
    masks = block_masks(index_ref[0], pieces, piece_rows, step_rows)
    queries = q_ref[...]
    for first in range(0, rows, BLOCK):
        count = first + BLOCK
        query_block = heads_beside(queries, first, BLOCK)
        total = None
        result = None
        for k in range(pieces):
            spot = pl.ds(k * rows, count)
            scores = dot(k_ref[:, spot], query_block, 0, 0)
            weights = mask_tail(jnp.exp2(scores * (SCALE * LOG2E)), masks[k], first)
            part = jnp.sum(weights, axis=0, keepdims=True)
            value = dot(v_ref[:, spot], weights.astype(BF16), 1, 0)
            total = part if total is None else total + part
            result = value if result is None else result + value
        result = result * (1.0 / total)
        log_total = jnp.log2(total)
        for h in range(GROUP):
            columns = slice(h * BLOCK, (h + 1) * BLOCK)
            out_ref[h * HD : (h + 1) * HD, first : first + BLOCK] = result[:, columns].astype(BF16)
            lse_ref[0, h : h + 1, first : first + BLOCK] = log_total[:, columns]


def attend_back_kernel(
    index_ref, q_ref, k_ref, v_ref, out_ref, lse_ref, grad_ref, dq_ref, dk_ref, dv_ref,
    *, pieces, piece_rows, step_rows
):
    rows = q_ref.shape[1]
    masks = block_masks(index_ref[0], pieces, piece_rows, step_rows)
    queries = q_ref[...]
    grads = grad_ref[...]
    results = out_ref[...]
    dk_ref[...] = jnp.zeros_like(dk_ref)
    dv_ref[...] = jnp.zeros_like(dv_ref)
    for first in range(0, rows, BLOCK):
        count = first + BLOCK
        query_block = heads_beside(queries, first, BLOCK)
        grad_block = heads_beside(grads, first, BLOCK)
        result_block = heads_beside(results, first, BLOCK)
        centre = jnp.sum(
            grad_block.astype(F32) * result_block.astype(F32), axis=0, keepdims=True
        )
        log_total = jnp.concatenate(
            [lse_ref[0, h : h + 1, first : first + BLOCK] for h in range(GROUP)], axis=1
        )
        dq = None
        for k in range(pieces):
            spot = pl.ds(k * rows, count)
            keys = k_ref[:, spot]
            scores = dot(keys, query_block, 0, 0)
            weights = mask_tail(
                jnp.exp2(scores * (SCALE * LOG2E) - log_total), masks[k], first
            )
            grad_weights = dot(v_ref[:, spot], grad_block, 0, 0)
            grad_scores = (weights * (grad_weights - centre)).astype(BF16)
            part = dot(keys, grad_scores, 1, 0)
            dq = part if dq is None else dq + part
            dk_ref[:, spot] += dot(query_block, grad_scores, 1, 1) * SCALE
            dv_ref[:, spot] += dot(grad_block, weights.astype(BF16), 1, 1)
        dq = (dq * SCALE).astype(BF16)
        for h in range(GROUP):
            columns = slice(h * BLOCK, (h + 1) * BLOCK)
            dq_ref[h * HD : (h + 1) * HD, first : first + BLOCK] = dq[:, columns]


def attention_specs(rows, total_rows):
    group_spec = pl.BlockSpec((GROUP * HD, rows), lambda i: (i, 0))
    pair_spec = pl.BlockSpec((HD, total_rows), lambda i: (i, 0))
    lse_spec = pl.BlockSpec((1, GROUP, rows), lambda i: (i, 0, 0))
    return group_spec, pair_spec, lse_spec


def attend(index, queries, keys, values, pieces, piece_rows, step_rows):
    rows, total_rows = queries.shape[1], keys.shape[1]
    group_spec, pair_spec, lse_spec = attention_specs(rows, total_rows)
    return pl.pallas_call(
        functools.partial(
            attend_kernel, pieces=pieces, piece_rows=piece_rows, step_rows=step_rows
        ),
        grid=(KVH,),
        in_specs=[pl.BlockSpec(memory_space=pltpu.SMEM), group_spec, pair_spec, pair_spec],
        out_specs=[group_spec, lse_spec],
        out_shape=[
            jax.ShapeDtypeStruct((HQ * HD, rows), BF16),
            jax.ShapeDtypeStruct((KVH, GROUP, rows), F32),
        ],
        compiler_params=pltpu.CompilerParams(vmem_limit_bytes=VMEM_LIMIT),
        cost_estimate=pl.CostEstimate(
            flops=4 * HQ * HD * rows * total_rows,
            bytes_accessed=8 * HQ * HD * rows,
            transcendentals=HQ * rows * total_rows,
        ),
        name="attend",
    )(index, queries, keys, values)


def attend_back(index, queries, keys, values, results, lse, grads, pieces, piece_rows, step_rows):
    rows, total_rows = queries.shape[1], keys.shape[1]
    group_spec, pair_spec, lse_spec = attention_specs(rows, total_rows)
    return pl.pallas_call(
        functools.partial(
            attend_back_kernel, pieces=pieces, piece_rows=piece_rows, step_rows=step_rows
        ),
        grid=(KVH,),
        in_specs=[
            pl.BlockSpec(memory_space=pltpu.SMEM),
            group_spec,
            pair_spec,
            pair_spec,
            group_spec,
            lse_spec,
            group_spec,
        ],
        out_specs=[group_spec, pair_spec, pair_spec],
        out_shape=[
            jax.ShapeDtypeStruct((HQ * HD, rows), BF16),
            jax.ShapeDtypeStruct((KVH * HD, total_rows), F32),
            jax.ShapeDtypeStruct((KVH * HD, total_rows), F32),
        ],
        compiler_params=pltpu.CompilerParams(vmem_limit_bytes=VMEM_LIMIT),
        cost_estimate=pl.CostEstimate(
            flops=10 * HQ * HD * rows * total_rows,
            bytes_accessed=16 * HQ * HD * rows,
            transcendentals=HQ * rows * total_rows,
        ),
        name="attend_back",
    )(index, queries, keys, values, results, lse, grads)


def hidden_kernel(
    own_x_ref, own_c_ref, other_x_ref, other_c_ref, gate_ref, up_ref, down_ref, *refs
):
    hidden_ref, grads_ref, hidden_t_ref, grads_t_ref, all_x_ref, all_c_ref = refs[-6:]
    units = down_ref.shape[0]
    half = units // HALVES

    def work(x_ref, c_ref):
        x = x_ref[...]
        c = c_ref[...]
        all_x_ref[...] = x
        all_c_ref[...] = c
        for h in range(HALVES):
            part = slice(h * half, (h + 1) * half)
            up_part = slice(units + h * half, units + (h + 1) * half)
            gate = dot(x, gate_ref[:, part], 1, 0)
            up = dot(x, up_ref[:, part], 1, 0)
            grad_hidden = dot(c, down_ref[part, :], 1, 1)
            sigmoid = 0.5 * jnp.tanh(0.5 * gate) + 0.5
            silu = gate * sigmoid
            hidden = (silu * up).astype(BF16)
            grad_up = (grad_hidden * silu).astype(BF16)
            grad_gate = (grad_hidden * up * (sigmoid + silu * (1.0 - sigmoid))).astype(BF16)
            hidden_ref[:, part] = hidden
            grads_ref[:, part] = grad_gate
            grads_ref[:, up_part] = grad_up
            hidden_t_ref[part, :] = hidden.T
            grads_t_ref[part, :] = grad_gate.T
            grads_t_ref[up_part, :] = grad_up.T

    pl.when(pl.program_id(0) == 0)(lambda: work(own_x_ref, own_c_ref))
    pl.when(pl.program_id(0) == 1)(lambda: work(other_x_ref, other_c_ref))


def hidden_step(n, count, rows, pieces, gate_w, up_w, w_down, so_far):
    depth = w_down.shape[1]
    units = w_down.shape[0]
    once = pl.Buffered(1)
    read = [
        pl.BlockSpec((rows, depth), lambda i, block=block: (block, 0), pipeline_mode=once)
        for _, block in pieces
    ]
    widths = (units, 2 * units)
    upright = [(count, width) for width in widths]
    turned = [(width, count) for width in widths]
    whole = [(count, depth)] * 2
    flops = 12 * rows * depth * units
    return pl.pallas_call(
        hidden_kernel,
        grid=(2,),
        in_specs=read
        + [
            pl.BlockSpec((depth, units), lambda i: (0, 0), pipeline_mode=once),
            pl.BlockSpec((depth, units), lambda i: (0, 0), pipeline_mode=once),
            pl.BlockSpec((units, depth), lambda i: (0, 0), pipeline_mode=once),
        ]
        + [pl.BlockSpec(memory_space=pl.ANY)] * len(so_far),
        out_specs=[pl.BlockSpec((rows, shape[1]), lambda i: (2 * n + i, 0)) for shape in upright]
        + [pl.BlockSpec((shape[0], rows), lambda i: (0, 2 * n + i)) for shape in turned]
        + [pl.BlockSpec((rows, shape[1]), lambda i: (2 * n + i, 0)) for shape in whole],
        out_shape=[jax.ShapeDtypeStruct(shape, BF16) for shape in upright + turned + whole],
        input_output_aliases={7 + k: k for k in range(len(so_far))},
        compiler_params=pltpu.CompilerParams(vmem_limit_bytes=VMEM_LIMIT),
        cost_estimate=pl.CostEstimate(
            flops=flops,
            bytes_accessed=16 * rows * depth + 24 * rows * units + 6 * depth * units,
            transcendentals=2 * rows * units,
        ),
        name="hidden_step",
    )(*[array for array, _ in pieces], gate_w, up_w, w_down, *so_far)


def rows_kernel(me_ref, left_ref, *refs, right_dim):
    result_ref = refs[-1]
    total = None
    first = 0
    for right_ref in refs[:-1]:
        width = right_ref.shape[right_dim]
        part = dot(left_ref[:, first : first + width], right_ref[...], 1, right_dim)
        total = part if total is None else total + part
        first += width
    result_ref[...] = total.astype(BF16)


def rows_product(me, left, rights, right_dim, block_rows, name):
    count, width = left.shape
    return pl.pallas_call(
        functools.partial(rows_kernel, right_dim=right_dim),
        grid_spec=pltpu.PrefetchScalarGridSpec(
            num_scalar_prefetch=1,
            grid=(count // block_rows,),
            in_specs=[pl.BlockSpec((block_rows, width), lambda i, me_ref: (i, 0))]
            + [
                pl.BlockSpec(
                    right.shape, lambda i, me_ref: (0, 0), pipeline_mode=pl.Buffered(1)
                )
                for right in rights
            ],
            out_specs=pl.BlockSpec((block_rows, D), lambda i, me_ref: (me_ref[0] ^ i, 0)),
        ),
        out_shape=jax.ShapeDtypeStruct((count, D), BF16),
        compiler_params=pltpu.CompilerParams(vmem_limit_bytes=VMEM_LIMIT),
        cost_estimate=pl.CostEstimate(
            flops=2 * count * D * width,
            bytes_accessed=2 * (count * width + count * D + D * width),
            transcendentals=0,
        ),
        name=name,
    )(me, left, *rights)


def weight_kernel(left_ref, right_ref, *result_refs, parts):
    total = dot(left_ref[...], right_ref[...], 1, 0)
    half = total.shape[0] // HALVES
    for h, result_ref in enumerate(result_refs):
        piece = total[h * half : (h + 1) * half]
        if parts == 0:
            result_ref[...] = piece.astype(BF16)
            continue
        wide = piece.shape[1] // parts
        for p in range(parts):
            result_ref[p] = piece[:, p * wide : (p + 1) * wide].astype(BF16).T


def weight_product(left, right, first, units, wide, name):
    depth = left.shape[1]
    half = units // HALVES
    column = min(512, D)
    parts = column // wide if wide else 0
    block = first // units
    if wide:
        out_spec = pl.BlockSpec((parts, wide, half), lambda j: (j, 0, 0))
        out_shape = jax.ShapeDtypeStruct((D // wide, wide, half), BF16)
    else:
        out_spec = pl.BlockSpec((half, column), lambda j: (0, j))
        out_shape = jax.ShapeDtypeStruct((half, D), BF16)
    return pl.pallas_call(
        functools.partial(weight_kernel, parts=parts),
        grid=(D // column,),
        in_specs=[
            pl.BlockSpec((units, depth), lambda j: (block, 0), pipeline_mode=pl.Buffered(1)),
            pl.BlockSpec((depth, column), lambda j: (0, j)),
        ],
        out_specs=[out_spec] * HALVES,
        out_shape=[out_shape] * HALVES,
        compiler_params=pltpu.CompilerParams(vmem_limit_bytes=VMEM_LIMIT),
        cost_estimate=pl.CostEstimate(
            flops=2 * units * depth * D,
            bytes_accessed=2 * depth * (units + D) + 2 * units * D,
            transcendentals=0,
        ),
        name=name,
    )(left, right)


def pack_kernel(matrix_ref, result_ref):
    result_ref[0] = matrix_ref[...]


def pack_columns(matrix, parts):
    rows, columns = matrix.shape
    width = columns // parts
    return pl.pallas_call(
        pack_kernel,
        grid=(parts,),
        in_specs=[pl.BlockSpec((rows, width), lambda i: (0, i))],
        out_specs=pl.BlockSpec((1, rows, width), lambda i: (i, 0, 0)),
        out_shape=jax.ShapeDtypeStruct((parts, rows, width), BF16),
        compiler_params=pltpu.CompilerParams(vmem_limit_bytes=VMEM_LIMIT),
        cost_estimate=pl.CostEstimate(
            flops=0, bytes_accessed=4 * rows * columns, transcendentals=0
        ),
        name="pack_columns",
    )(matrix)


def unpack_kernel(*refs):
    result_ref = refs[-1]
    width = refs[0].shape[-1]
    for h in range(HALVES):
        result_ref[:, h * width : (h + 1) * width] = refs[h][0].astype(F32)


def unpack_columns(pieces):
    parts, rows, half = pieces[0].shape
    return pl.pallas_call(
        unpack_kernel,
        grid=(parts,),
        in_specs=[pl.BlockSpec((1, rows, half), lambda i: (i, 0, 0))] * HALVES,
        out_specs=pl.BlockSpec((rows, HALVES * half), lambda i: (0, i)),
        out_shape=jax.ShapeDtypeStruct((rows, parts * HALVES * half), F32),
        compiler_params=pltpu.CompilerParams(vmem_limit_bytes=VMEM_LIMIT),
        cost_estimate=pl.CostEstimate(
            flops=0, bytes_accessed=6 * parts * rows * HALVES * half, transcendentals=0
        ),
        name="unpack_columns",
    )(*pieces)


class Layout:
    def __init__(self, fsdp_devices, seq_devices, rows_dev):
        self.fsdp = fsdp_devices
        self.seq = seq_devices
        self.chips = fsdp_devices // 2
        self.share = 2 * seq_devices // (2 * MICRO)
        self.near = self.share // 2
        self.piece_rows = rows_dev // self.share
        self.step_rows = rows_dev
        self.rows = LENGTH // self.share

    def flat(self, f, z):
        return f * self.seq + z

    def moved(self, r):
        pairs = []
        for f in range(self.fsdp):
            for z in range(self.seq):
                slot = z ^ r
                micro, j = slot // self.share, slot % self.share
                target_f = (f // 2) * 2 + j % 2
                target_z = (2 * micro + f % 2) * self.near + j // 2
                pairs.append((self.flat(f, z), self.flat(target_f, target_z)))
        return pairs

    def other(self, k):
        return [
            (self.flat(f, z), self.flat(f ^ k, z))
            for f in range(self.fsdp)
            for z in range(self.seq)
        ]

    def across(self, k):
        pairs = []
        for f in range(self.fsdp):
            for z in range(self.seq):
                pairs.append((self.flat(f, z), self.flat(f ^ (k & 1), z ^ (k >> 1))))
        return pairs


def permute(value, pairs):
    return lax.ppermute(value, ("fsdp", "seq"), pairs)


def scatter_rows(layout, values, z, slot):
    parts = values.reshape(layout.seq, layout.piece_rows, values.shape[-1])
    result = jnp.zeros_like(parts)
    for r in range(layout.seq):
        sent = lax.dynamic_index_in_dim(parts, z ^ r, 0, keepdims=False)
        got = permute(sent, layout.moved(r))
        result = lax.dynamic_update_index_in_dim(result, got, slot ^ r, 0)
    return result.reshape(layout.rows, values.shape[-1])


def return_rows(layout, values, f):
    width = values.shape[-1]
    parts = values.reshape(layout.seq, layout.piece_rows, width)
    parts = lax.all_to_all(parts, "seq", split_axis=0, concat_axis=0, tiled=True)
    parts = parts.reshape(MICRO, 2, layout.near, layout.piece_rows, width)
    core = f % 2
    kept = lax.dynamic_index_in_dim(parts, core, 1, keepdims=False)
    sent = lax.dynamic_index_in_dim(parts, 1 - core, 1, keepdims=False)
    got = permute(sent, layout.other(1))
    both = jnp.stack(
        [jnp.where(core == 0, kept, got), jnp.where(core == 0, got, kept)], axis=2
    )
    return both.reshape(MICRO, layout.step_rows, width)


class RowGather:
    def __init__(self, layout, first, second):
        self.layout = layout
        self.rows = first.shape[0]
        both = jnp.concatenate([first, second])
        self.own = {0: [both]}
        self.sibling = {0: [self.move(both, 1)]}
        chips = layout.chips
        for n in range(1, 3 if chips == 4 else chips):
            self.own[n] = [self.move(both, 2 * n)]

    def move(self, value, k):
        return permute(value, self.layout.other(k))

    def chunk(self, n):
        pieces = []
        for arrays in (self.own[n], self.sibling[n]):
            pieces += [(arrays[0], 0), (arrays[-1], len(arrays) % 2)]
        return pieces

    def after(self, n, *values):
        chips = self.layout.chips
        if n + 1 < chips:
            waiting = {m: value for m, value in self.own.items() if m > n}
            siblings = {m: value for m, value in self.sibling.items() if m > n}
            waiting, siblings, values = lax.optimization_barrier((waiting, siblings, values))
            self.own.update(waiting)
            self.sibling.update(siblings)
            if chips == 4 and n == 0:
                far = [self.move(self.own[2][0][: self.rows], 2)]
                far += [self.move(self.own[1][0][self.rows :], 4)]
                self.far = far
            if chips == 4 and n == 1:
                self.own[3] = lax.optimization_barrier((self.far, values))[0]
            for m in (n + 1, n + 2):
                if m in self.own and m not in self.sibling:
                    self.sibling[m] = [self.move(value, 1) for value in self.own[m]]
        return values


def gather_small(layout, f, own):
    held = own[None]
    k = 1
    while k < layout.fsdp:
        got = permute(held, layout.other(k))
        upper = (f & k) > 0
        held = jnp.concatenate(
            [jnp.where(upper, got, held), jnp.where(upper, held, got)], axis=0
        )
        k *= 2
    return held


def sum_small(layout, value):
    k = 1
    while k < layout.fsdp:
        value = value + permute(value, layout.other(k))
        k *= 2
    return value


class LinePipe:
    def __init__(self, z, seq_devices):
        self.seq = seq_devices
        self.z = z
        self.outer = (z == 0) | (z == seq_devices - 1)
        self.flying = []
        self.results = {}
        self.then = {}
        self.age = {}

    def send(self, stage, value):
        half, last = self.seq // 2, self.seq - 1
        if stage < half - 1:
            pairs = [(stage, stage + 1), (last - stage, last - stage - 1)]
        elif stage == half - 1:
            pairs = [(half - 1, half), (half, half - 1)]
        else:
            s = last - 1 - stage
            pairs = [(s + 1, s), (last - s - 1, last - s)]
        return lax.ppermute(value, "seq", pairs)

    def join(self, stage, value, got):
        if stage < self.seq // 2:
            return value + got
        s = self.seq - 2 - stage
        return jnp.where((self.z == s) | (self.z == self.seq - 1 - s), got, value)

    def step(self, name=None, value=None, others=(), then=None):
        arrived = [entry[3] for entry in self.flying]
        old = {key: self.results[key] for key in self.results if self.age.get(key, 0) <= 0}
        arrived, old, value, others = lax.optimization_barrier((arrived, old, value, others))
        self.results.update(old)
        self.age = {key: age - 1 for key, age in self.age.items()}
        flying = []
        if name is not None:
            self.then[name] = then
            flying.append((name, 0, value, self.send(0, value)))
        for (key, stage, held, _), got in zip(self.flying, arrived):
            if stage == self.seq - 2:
                chosen = jnp.where(self.outer, got, held)
                self.results[key] = chosen
                if self.then[key] is not None:
                    self.results[key] = self.then[key](chosen)
                    self.age[key] = 1
                continue
            held = self.join(stage, held, got)
            flying.append((key, stage + 1, held, self.send(stage + 1, held)))
        self.flying = flying
        return others

    def landed(self, names):
        return all(name in self.results for name in names)

    def finish(self):
        while self.flying:
            self.step()


def body(
    tokens,
    cotangent,
    attn_gain,
    query_gain,
    key_gain,
    w_query,
    w_key,
    w_value,
    w_out,
    ffn_gain,
    w_gate,
    w_up,
    w_down,
):
    fsdp_devices = lax.axis_size("fsdp")
    seq_devices = lax.axis_size("seq")
    layout = Layout(fsdp_devices, seq_devices, tokens.shape[2])
    f = lax.axis_index("fsdp")
    z = lax.axis_index("seq")
    rows = layout.rows
    share = layout.share
    member = (z % layout.near) * 2 + f % 2
    slot = (z // layout.near // 2) * share + member

    w_attn = lax.all_gather(
        jnp.concatenate([w_query, w_key, w_value], axis=1), "fsdp", axis=0, tiled=True
    )
    gains = gather_small(
        layout, f, jnp.concatenate([attn_gain, ffn_gain, query_gain, key_gain])
    ).astype(F32)
    wide, narrow = attn_gain.shape[0], query_gain.shape[0]
    hidden_dev = w_down.shape[0]

    def own_columns(matrix):
        return lax.all_to_all(
            pack_columns(matrix, fsdp_devices), "fsdp", split_axis=0, concat_axis=0, tiled=True
        ).reshape(D, hidden_dev)

    gains, gate_rows = lax.optimization_barrier((gains, w_gate))
    gate_w = own_columns(gate_rows)
    full_attn_gain = gains[:, :wide].reshape(D)
    full_ffn_gain = gains[:, wide : 2 * wide].reshape(D)
    full_query_gain = gains[:, 2 * wide : 2 * wide + narrow].reshape(HD)
    full_key_gain = gains[:, 2 * wide + narrow :].reshape(HD)
    inputs_low = scatter_rows(layout, tokens[:, 0], z, slot)
    grad_out_low = scatter_rows(layout, cotangent[:, 0], z, slot)
    full_out = lax.all_gather(w_out, "fsdp", axis=0, tiled=True)

    row = jnp.arange(rows, dtype=jnp.int32)
    position = (
        (row // layout.piece_rows) * layout.step_rows
        + member * layout.piece_rows
        + row % layout.piece_rows
    ).astype(F32)
    frequency = THETA ** (-(jnp.arange(HD // 2).astype(F32) * 2.0 / HD))
    angles = frequency[:, None] * position[None, :]
    cosine_table, sine_table = jnp.cos(angles)[None], jnp.sin(angles)[None]
    head_gains = jnp.concatenate(
        [
            jnp.broadcast_to(full_query_gain[None, :, None], (HQ, HD, 1)),
            jnp.broadcast_to(full_key_gain[None, :, None], (KVH, HD, 1)),
        ]
    )

    inputs = inputs_low.astype(F32)
    normed, normed_unit, normed_inverse = rms_fwd(inputs, full_attn_gain)
    normed_low, grad_out_low, w_attn, gate_w, up_rows = lax.optimization_barrier(
        (normed.astype(BF16), grad_out_low, w_attn, gate_w, w_up)
    )
    up_w = own_columns(up_rows)
    raw = dot(w_attn, normed_low, 0, 1)
    pair_width = KVH * HD
    turned = HQ + KVH
    head_raw = raw[: turned * HD].reshape(turned, HD, rows)
    head_normed, head_unit, head_inverse = head_rms_fwd(head_raw, head_gains)
    heads_low = rotate(head_normed, cosine_table, sine_table).astype(BF16).reshape(turned * HD, rows)
    queries = heads_low[: HQ * HD]
    own_pair = jnp.concatenate([heads_low[HQ * HD :], raw[turned * HD :].astype(BF16)], axis=0)
    pair_pieces = [own_pair] + [permute(own_pair, layout.across(k)) for k in range(1, share)]
    keys = jnp.concatenate([piece[:pair_width] for piece in pair_pieces], axis=1)
    values = jnp.concatenate([piece[pair_width:] for piece in pair_pieces], axis=1)
    index = member.astype(jnp.int32).reshape(1)
    attended, log_totals = attend(
        index, queries, keys, values, share, layout.piece_rows, layout.step_rows
    )
    middle = inputs + dot(attended, full_out, 0, 0)
    ffn_normed, ffn_unit, ffn_inverse = rms_fwd(middle, full_ffn_gain)
    ffn_low, up_w = lax.optimization_barrier((ffn_normed.astype(BF16), up_w))

    gather = RowGather(layout, ffn_low, grad_out_low)
    line = LinePipe(z, seq_devices)
    worked = ()
    for n in range(layout.chips):
        worked = hidden_step(
            n, fsdp_devices * rows, rows, gather.chunk(n), gate_w, up_w, w_down, worked
        )
        worked = gather.after(n, *worked)
    hidden, grads, hidden_t, grads_t, ffn_rows, grad_out_rows = worked
    me = f.astype(jnp.int32).reshape(1)

    def to_owners(term):
        return lax.all_to_all(term, "fsdp", split_axis=0, concat_axis=0, tiled=True)

    grad_ffn_part = rows_product(me, grads, [gate_w, up_w], 1, rows, "grad_ffn_normed")
    grad_ffn_part, hidden_t, grads_t = lax.optimization_barrier(
        (grad_ffn_part, hidden_t, grads_t)
    )
    grad_ffn_normed = lax.psum_scatter(
        grad_ffn_part, "fsdp", scatter_dimension=0, tiled=True
    )
    down_term = weight_product(hidden_t, grad_out_rows, 0, hidden_dev, 0, "w_down_grad")
    (grads_t,) = line.step("down0", down_term[0], (grads_t,))
    gate_term = weight_product(grads_t, ffn_rows, 0, hidden_dev, wide, "w_gate_grad")
    gate_term, grads_t = lax.optimization_barrier((gate_term, grads_t))
    gate_term = [to_owners(term) for term in gate_term]
    up_term = weight_product(grads_t, ffn_rows, hidden_dev, hidden_dev, wide, "w_up_grad")
    hidden, up_term = line.step("down1", down_term[1], (hidden, up_term))
    out_part = rows_product(me, hidden, [w_down], 0, rows, "block_out")
    out_part, grad_ffn_normed, gate_term[1] = line.step(
        "gate0", gate_term[0], (out_part, grad_ffn_normed, gate_term[1])
    )
    out_sum = lax.psum_scatter(out_part, "fsdp", scatter_dimension=0, tiled=True)
    up_term = [to_owners(term) for term in up_term]
    grad_ffn_normed = grad_ffn_normed.astype(F32)

    grad_middle_norm, ffn_gain_term = rms_back(
        grad_ffn_normed, ffn_unit, ffn_inverse, full_ffn_gain
    )
    grad_middle = grad_out_low.astype(F32) + grad_middle_norm
    grad_branch_low = grad_middle.astype(BF16)
    grad_attended = dot(full_out, grad_branch_low, 1, 1).astype(BF16)
    out_term = dot(attended, grad_branch_low, 1, 0).astype(BF16)
    out_rows = lax.psum_scatter(out_term, "fsdp", scatter_dimension=0, tiled=True)
    (grad_attended,) = line.step("gate1", gate_term[1], (grad_attended,))
    grad_queries, grad_keys, grad_values = attend_back(
        index,
        queries,
        keys,
        values,
        attended,
        log_totals,
        grad_attended,
        share,
        layout.piece_rows,
        layout.step_rows,
    )
    grad_queries, grad_keys, grad_values = line.step(
        "up0", up_term[0], (grad_queries, grad_keys, grad_values)
    )
    grad_pair = jnp.concatenate([grad_keys[:, :rows], grad_values[:, :rows]], axis=0)
    for k in range(1, share):
        columns = slice(k * rows, (k + 1) * rows)
        sent = jnp.concatenate([grad_keys[:, columns], grad_values[:, columns]], axis=0)
        grad_pair = grad_pair + permute(sent.astype(BF16), layout.across(k)).astype(F32)
    grad_pair_low = grad_pair.astype(BF16)
    grad_turned = (
        jnp.concatenate([grad_queries, grad_pair_low[:pair_width]], axis=0)
        .astype(F32)
        .reshape(turned, HD, rows)
    )
    grad_head_normed = rotate(grad_turned, cosine_table, -sine_table)
    scaled = grad_head_normed * head_gains
    grad_head_raw = head_inverse * (
        scaled - head_unit * jnp.mean(scaled * head_unit, axis=1, keepdims=True)
    )
    head_gain_terms = jnp.sum(grad_head_normed * head_unit, axis=2)
    grad_raw = jnp.concatenate(
        [grad_head_raw.astype(BF16).reshape(turned * HD, rows), grad_pair_low[pair_width:]], axis=0
    )
    projection_term = dot(normed_low, grad_raw, 0, 1).astype(BF16)
    projection_term, grad_raw = lax.optimization_barrier((projection_term, grad_raw))
    projection_rows = lax.psum_scatter(
        projection_term, "fsdp", scatter_dimension=0, tiled=True
    )
    grad_raw, out_sum = line.step("up1", up_term[1], (grad_raw, out_sum))
    block_out = return_rows(layout, (middle + out_sum.astype(F32)).astype(BF16), f)
    grad_normed = dot(grad_raw, w_attn, 0, 1)
    grad_input_norm, attn_gain_term = rms_back(
        grad_normed, normed_unit, normed_inverse, full_attn_gain
    )

    tokens_grad = return_rows(layout, (grad_middle + grad_input_norm).astype(BF16), f)
    gain_terms = sum_small(
        layout,
        jnp.concatenate(
            [
                attn_gain_term,
                ffn_gain_term,
                jnp.sum(head_gain_terms[:HQ], axis=0),
                jnp.sum(head_gain_terms[HQ:], axis=0),
            ]
        )[None],
    )[0]

    def own_share(first, count):
        share_of = count // fsdp_devices
        vector = lax.dynamic_slice_in_dim(gain_terms, first + f * share_of, share_of, 0)
        return jnp.pad(vector, (0, wide - share_of))

    gain_columns = jnp.stack(
        [own_share(0, D), own_share(D, D), own_share(2 * D, HD), own_share(2 * D + HD, HD)],
        axis=1,
    )
    gain_columns = jnp.pad(gain_columns, ((0, 0), (0, 128 - gain_columns.shape[1]))).astype(BF16)

    line.step("out", out_rows)
    middle_column = projection_rows.shape[1] // 2
    tokens_grad, block_out = line.step(
        "attn0", projection_rows[:, :middle_column], (tokens_grad, block_out)
    )
    (gain_columns,) = line.step(
        "attn1",
        jnp.concatenate([projection_rows[:, middle_column:], gain_columns], axis=1),
        (gain_columns,),
    )
    while not line.landed([f"{name}{h}" for name in ("down", "gate", "up") for h in range(HALVES)]):
        line.step()
    w_gate_grad = unpack_columns([line.results[f"gate{h}"] for h in range(HALVES)])
    w_up_grad = unpack_columns([line.results[f"up{h}"] for h in range(HALVES)])
    w_down_grad = jnp.concatenate([line.results[f"down{h}"] for h in range(HALVES)]).astype(F32)
    w_gate_grad, w_up_grad, w_down_grad = line.step(
        others=(w_gate_grad, w_up_grad, w_down_grad)
    )
    line.finish()

    attn_rows = jnp.concatenate([line.results["attn0"], line.results["attn1"]], axis=1).astype(F32)
    w_out_grad = line.results["out"].astype(F32)
    gain_rows = attn_rows[:, attn_rows.shape[1] - 128 :]
    query_width = HQ * HD

    return (
        block_out[:, None],
        tokens_grad[:, None],
        gain_rows[:, 0],
        gain_rows[:narrow, 2],
        gain_rows[:narrow, 3],
        attn_rows[:, :query_width],
        attn_rows[:, query_width : query_width + pair_width],
        attn_rows[:, query_width + pair_width : query_width + 2 * pair_width],
        w_out_grad,
        gain_rows[:, 1],
        w_gate_grad,
        w_up_grad,
        w_down_grad,
    )


def solution(mesh):
    activations = P(None, "fsdp", "seq", None)
    vector = P("fsdp")
    matrix = P("fsdp", None)
    specs = (
        (activations, activations)
        + (vector,) * 3
        + (matrix,) * 4
        + (vector,)
        + (matrix,) * 3
    )
    return jax.shard_map(body, mesh=mesh, in_specs=specs, out_specs=specs, check_vma=False)
```

```python
import functools
import math

import jax
import jax.numpy as jnp
from jax import lax
from jax.experimental import pallas as pl
from jax.experimental.pallas import tpu as pltpu
from jax.sharding import PartitionSpec as P

D = 2048
HQ = 32
KVH = 8
HD = 64
FF = 8192
LENGTH = 1024
MICRO = 2
HALVES = 2
SWAPS = 2

EPSILON = 1e-05
THETA = 1000000.0
GROUP = HQ // KVH
BLOCK = 128
SCALE = 1.0 / math.sqrt(HD)
LOG2E = math.log2(math.e)
VMEM_LIMIT = 56 * 1024 * 1024

F32 = jnp.float32
BF16 = jnp.bfloat16


def dot(left_side, right_side, left_dim, right_dim):
    return lax.dot_general(
        left_side,
        right_side,
        (((left_dim,), (right_dim,)), ((), ())),
        preferred_element_type=F32,
    )


def rms_fwd(values, row_gain):
    inverse = lax.rsqrt(jnp.mean(values * values, axis=-1, keepdims=True) + EPSILON)
    unit_rows = values * inverse
    return (unit_rows * row_gain, unit_rows, inverse)


def rms_back(grad_outputs, unit_rows, inverse, row_gain):
    scaled = grad_outputs * row_gain
    grad_inputs = inverse * (
        scaled - unit_rows * jnp.mean(scaled * unit_rows, axis=-1, keepdims=True)
    )
    grad_gain = jnp.sum(grad_outputs * unit_rows, axis=0)
    return (grad_inputs, grad_gain)


def head_rms_fwd(values, gains):
    inverse = lax.rsqrt(jnp.mean(values * values, axis=1, keepdims=True) + EPSILON)
    unit = values * inverse
    return (unit * gains, unit, inverse)


def rotate(values, cosine_table, sine_table):
    half_width = values.shape[1] // 2
    front_half = values[:, :half_width]
    back_half = values[:, half_width:]
    return jnp.concatenate(
        [
            front_half * cosine_table - back_half * sine_table,
            back_half * cosine_table + front_half * sine_table,
        ],
        axis=1,
    )


def block_masks(index, pieces, piece_rows, step_rows):
    key = lax.broadcasted_iota(jnp.int32, (BLOCK, GROUP * BLOCK), 0)
    query = lax.broadcasted_iota(jnp.int32, (BLOCK, GROUP * BLOCK), 1) & (BLOCK - 1)

    def place(row, piece):
        return (row // piece_rows) * step_rows + piece * piece_rows + (row & (piece_rows - 1))

    return [place(key, index ^ k) <= place(query, index) for k in range(pieces)]


def heads_beside(block, first, count):
    return jnp.concatenate(
        [block[h * HD : (h + 1) * HD, first : first + count] for h in range(GROUP)], axis=1
    )


def mask_tail(values, mask, first):
    tail = jnp.where(mask, values[first:], 0.0)
    if first == 0:
        return tail
    return jnp.concatenate([values[:first], tail], axis=0)


def attend_kernel(index_ref, q_ref, k_ref, v_ref, out_ref, lse_ref, *, pieces, piece_rows, step_rows):
    rows = q_ref.shape[1]
    masks = block_masks(index_ref[0], pieces, piece_rows, step_rows)
    queries = q_ref[...]
    for first in range(0, rows, BLOCK):
        count = first + BLOCK
        query_block = heads_beside(queries, first, BLOCK)
        total = None
        result = None
        for k in range(pieces):
            spot = pl.ds(k * rows, count)
            scores = dot(k_ref[:, spot], query_block, 0, 0)
            weights = mask_tail(jnp.exp2(scores * (SCALE * LOG2E)), masks[k], first)
            part = jnp.sum(weights, axis=0, keepdims=True)
            value = dot(v_ref[:, spot], weights.astype(BF16), 1, 0)
            total = part if total is None else total + part
            result = value if result is None else result + value
        result = result * (1.0 / total)
        log_total = jnp.log2(total)
        for h in range(GROUP):
            columns = slice(h * BLOCK, (h + 1) * BLOCK)
            out_ref[h * HD : (h + 1) * HD, first : first + BLOCK] = result[:, columns].astype(BF16)
            lse_ref[0, h : h + 1, first : first + BLOCK] = log_total[:, columns]


def attend_back_kernel(
    index_ref, q_ref, k_ref, v_ref, out_ref, lse_ref, grad_ref, dq_ref, dk_ref, dv_ref,
    *, pieces, piece_rows, step_rows
):
    rows = q_ref.shape[1]
    masks = block_masks(index_ref[0], pieces, piece_rows, step_rows)
    queries = q_ref[...]
    grads = grad_ref[...]
    results = out_ref[...]
    dk_ref[...] = jnp.zeros_like(dk_ref)
    dv_ref[...] = jnp.zeros_like(dv_ref)
    for first in range(0, rows, BLOCK):
        count = first + BLOCK
        query_block = heads_beside(queries, first, BLOCK)
        grad_block = heads_beside(grads, first, BLOCK)
        result_block = heads_beside(results, first, BLOCK)
        centre = jnp.sum(
            grad_block.astype(F32) * result_block.astype(F32), axis=0, keepdims=True
        )
        log_total = jnp.concatenate(
            [lse_ref[0, h : h + 1, first : first + BLOCK] for h in range(GROUP)], axis=1
        )
        dq = None
        for k in range(pieces):
            spot = pl.ds(k * rows, count)
            keys = k_ref[:, spot]
            scores = dot(keys, query_block, 0, 0)
            weights = mask_tail(
                jnp.exp2(scores * (SCALE * LOG2E) - log_total), masks[k], first
            )
            grad_weights = dot(v_ref[:, spot], grad_block, 0, 0)
            grad_scores = (weights * (grad_weights - centre)).astype(BF16)
            part = dot(keys, grad_scores, 1, 0)
            dq = part if dq is None else dq + part
            dk_ref[:, spot] += dot(query_block, grad_scores, 1, 1) * SCALE
            dv_ref[:, spot] += dot(grad_block, weights.astype(BF16), 1, 1)
        dq = (dq * SCALE).astype(BF16)
        for h in range(GROUP):
            columns = slice(h * BLOCK, (h + 1) * BLOCK)
            dq_ref[h * HD : (h + 1) * HD, first : first + BLOCK] = dq[:, columns]


def attention_specs(rows, total_rows):
    group_spec = pl.BlockSpec((GROUP * HD, rows), lambda i: (i, 0))
    pair_spec = pl.BlockSpec((HD, total_rows), lambda i: (i, 0))
    lse_spec = pl.BlockSpec((1, GROUP, rows), lambda i: (i, 0, 0))
    return group_spec, pair_spec, lse_spec


def attend(index, queries, keys, values, pieces, piece_rows, step_rows):
    rows, total_rows = queries.shape[1], keys.shape[1]
    group_spec, pair_spec, lse_spec = attention_specs(rows, total_rows)
    return pl.pallas_call(
        functools.partial(
            attend_kernel, pieces=pieces, piece_rows=piece_rows, step_rows=step_rows
        ),
        grid=(KVH,),
        in_specs=[pl.BlockSpec(memory_space=pltpu.SMEM), group_spec, pair_spec, pair_spec],
        out_specs=[group_spec, lse_spec],
        out_shape=[
            jax.ShapeDtypeStruct((HQ * HD, rows), BF16),
            jax.ShapeDtypeStruct((KVH, GROUP, rows), F32),
        ],
        compiler_params=pltpu.CompilerParams(vmem_limit_bytes=VMEM_LIMIT),
        cost_estimate=pl.CostEstimate(
            flops=4 * HQ * HD * rows * total_rows,
            bytes_accessed=8 * HQ * HD * rows,
            transcendentals=HQ * rows * total_rows,
        ),
        name="attend",
    )(index, queries, keys, values)


def attend_back(index, queries, keys, values, results, lse, grads, pieces, piece_rows, step_rows):
    rows, total_rows = queries.shape[1], keys.shape[1]
    group_spec, pair_spec, lse_spec = attention_specs(rows, total_rows)
    return pl.pallas_call(
        functools.partial(
            attend_back_kernel, pieces=pieces, piece_rows=piece_rows, step_rows=step_rows
        ),
        grid=(KVH,),
        in_specs=[
            pl.BlockSpec(memory_space=pltpu.SMEM),
            group_spec,
            pair_spec,
            pair_spec,
            group_spec,
            lse_spec,
            group_spec,
        ],
        out_specs=[group_spec, pair_spec, pair_spec],
        out_shape=[
            jax.ShapeDtypeStruct((HQ * HD, rows), BF16),
            jax.ShapeDtypeStruct((KVH * HD, total_rows), F32),
            jax.ShapeDtypeStruct((KVH * HD, total_rows), F32),
        ],
        compiler_params=pltpu.CompilerParams(vmem_limit_bytes=VMEM_LIMIT),
        cost_estimate=pl.CostEstimate(
            flops=10 * HQ * HD * rows * total_rows,
            bytes_accessed=16 * HQ * HD * rows,
            transcendentals=HQ * rows * total_rows,
        ),
        name="attend_back",
    )(index, queries, keys, values, results, lse, grads)


def hidden_kernel(own_x_ref, own_c_ref, other_x_ref, other_c_ref, weight_ref, down_ref, *refs):
    hidden_ref, grads_ref, hidden_t_ref, grads_t_ref, all_x_ref, all_c_ref = refs[-6:]
    units = down_ref.shape[0]
    half = units // HALVES

    def work(x_ref, c_ref):
        x = x_ref[...]
        c = c_ref[...]
        all_x_ref[...] = x
        all_c_ref[...] = c
        for h in range(HALVES):
            part = slice(h * half, (h + 1) * half)
            up_part = slice(units + h * half, units + (h + 1) * half)
            gate = dot(x, weight_ref[:, part], 1, 0)
            up = dot(x, weight_ref[:, up_part], 1, 0)
            grad_hidden = dot(c, down_ref[part, :], 1, 1)
            sigmoid = 0.5 * jnp.tanh(0.5 * gate) + 0.5
            silu = gate * sigmoid
            hidden = (silu * up).astype(BF16)
            grad_up = (grad_hidden * silu).astype(BF16)
            grad_gate = (grad_hidden * up * (sigmoid + silu * (1.0 - sigmoid))).astype(BF16)
            hidden_ref[:, part] = hidden
            grads_ref[:, part] = grad_gate
            grads_ref[:, up_part] = grad_up
            hidden_t_ref[part, :] = hidden.T
            grads_t_ref[part, :] = grad_gate.T
            grads_t_ref[up_part, :] = grad_up.T

    pl.when(pl.program_id(0) == 0)(lambda: work(own_x_ref, own_c_ref))
    pl.when(pl.program_id(0) == 1)(lambda: work(other_x_ref, other_c_ref))


def hidden_step(n, count, rows, pieces, weights, w_down, so_far):
    depth = w_down.shape[1]
    units = w_down.shape[0]
    once = pl.Buffered(1)
    read = [
        pl.BlockSpec((rows, depth), lambda i, block=block: (block, 0), pipeline_mode=once)
        for _, block in pieces
    ]
    widths = (units, 2 * units)
    upright = [(count, width) for width in widths]
    turned = [(width, count) for width in widths]
    whole = [(count, depth)] * 2
    flops = 12 * rows * depth * units
    return pl.pallas_call(
        hidden_kernel,
        grid=(2,),
        in_specs=read
        + [
            pl.BlockSpec((depth, 2 * units), lambda i: (0, 0), pipeline_mode=once),
            pl.BlockSpec((units, depth), lambda i: (0, 0), pipeline_mode=once),
        ]
        + [pl.BlockSpec(memory_space=pl.ANY)] * len(so_far),
        out_specs=[pl.BlockSpec((rows, shape[1]), lambda i: (2 * n + i, 0)) for shape in upright]
        + [pl.BlockSpec((shape[0], rows), lambda i: (0, 2 * n + i)) for shape in turned]
        + [pl.BlockSpec((rows, shape[1]), lambda i: (2 * n + i, 0)) for shape in whole],
        out_shape=[jax.ShapeDtypeStruct(shape, BF16) for shape in upright + turned + whole],
        input_output_aliases={6 + k: k for k in range(len(so_far))},
        compiler_params=pltpu.CompilerParams(vmem_limit_bytes=VMEM_LIMIT),
        cost_estimate=pl.CostEstimate(
            flops=flops,
            bytes_accessed=16 * rows * depth + 24 * rows * units + 6 * depth * units,
            transcendentals=2 * rows * units,
        ),
        name="hidden_step",
    )(*[array for array, _ in pieces], weights, w_down, *so_far)


def rows_kernel(me_ref, left_ref, right_ref, result_ref, *, right_dim):
    result_ref[...] = dot(left_ref[...], right_ref[...], 1, right_dim).astype(BF16)


def rows_product(me, left, right, right_dim, block_rows, name):
    count, width = left.shape
    return pl.pallas_call(
        functools.partial(rows_kernel, right_dim=right_dim),
        grid_spec=pltpu.PrefetchScalarGridSpec(
            num_scalar_prefetch=1,
            grid=(count // block_rows,),
            in_specs=[
                pl.BlockSpec((block_rows, width), lambda i, me_ref: (i, 0)),
                pl.BlockSpec(
                    right.shape, lambda i, me_ref: (0, 0), pipeline_mode=pl.Buffered(1)
                ),
            ],
            out_specs=pl.BlockSpec((block_rows, D), lambda i, me_ref: (me_ref[0] ^ i, 0)),
        ),
        out_shape=jax.ShapeDtypeStruct((count, D), BF16),
        compiler_params=pltpu.CompilerParams(vmem_limit_bytes=VMEM_LIMIT),
        cost_estimate=pl.CostEstimate(
            flops=2 * count * D * width,
            bytes_accessed=2 * (count * width + count * D + D * width),
            transcendentals=0,
        ),
        name=name,
    )(me, left, right)


def weight_kernel(left_ref, right_ref, *result_refs, parts):
    total = dot(left_ref[...], right_ref[...], 1, 0)
    half = total.shape[0] // HALVES
    for h, result_ref in enumerate(result_refs):
        piece = total[h * half : (h + 1) * half]
        if parts == 0:
            result_ref[...] = piece.astype(BF16)
            continue
        wide = piece.shape[1] // parts
        for p in range(parts):
            result_ref[p] = piece[:, p * wide : (p + 1) * wide].astype(BF16).T


def weight_product(left, right, first, units, wide, name):
    depth = left.shape[1]
    half = units // HALVES
    column = min(512, D)
    parts = column // wide if wide else 0
    block = first // units
    if wide:
        out_spec = pl.BlockSpec((parts, wide, half), lambda j: (j, 0, 0))
        out_shape = jax.ShapeDtypeStruct((D // wide, wide, half), BF16)
    else:
        out_spec = pl.BlockSpec((half, column), lambda j: (0, j))
        out_shape = jax.ShapeDtypeStruct((half, D), BF16)
    return pl.pallas_call(
        functools.partial(weight_kernel, parts=parts),
        grid=(D // column,),
        in_specs=[
            pl.BlockSpec((units, depth), lambda j: (block, 0), pipeline_mode=pl.Buffered(1)),
            pl.BlockSpec((depth, column), lambda j: (0, j)),
        ],
        out_specs=[out_spec] * HALVES,
        out_shape=[out_shape] * HALVES,
        compiler_params=pltpu.CompilerParams(vmem_limit_bytes=VMEM_LIMIT),
        cost_estimate=pl.CostEstimate(
            flops=2 * units * depth * D,
            bytes_accessed=2 * depth * (units + D) + 2 * units * D,
            transcendentals=0,
        ),
        name=name,
    )(left, right)


def merge_kernel(even_ref, *refs):
    result_ref = refs[-1]
    piece = result_ref.shape[1] // (2 * SWAPS)
    for h in range(SWAPS):
        mine, theirs = refs[h][...], refs[SWAPS + h][...]
        gate = jnp.where(even_ref[0] > 0, mine, theirs)
        up = jnp.where(even_ref[0] > 0, theirs, mine)
        result_ref[:, h * piece : (h + 1) * piece] = gate
        result_ref[:, (SWAPS + h) * piece : (SWAPS + h + 1) * piece] = up


def merge_columns(even, mine, theirs):
    rows, piece = mine[0].shape
    tile = min(256, rows)
    return pl.pallas_call(
        merge_kernel,
        grid=(rows // tile,),
        in_specs=[pl.BlockSpec(memory_space=pltpu.SMEM)]
        + [pl.BlockSpec((tile, piece), lambda i: (i, 0))] * (2 * SWAPS),
        out_specs=pl.BlockSpec((tile, 2 * SWAPS * piece), lambda i: (i, 0)),
        out_shape=jax.ShapeDtypeStruct((rows, 2 * SWAPS * piece), BF16),
        compiler_params=pltpu.CompilerParams(vmem_limit_bytes=VMEM_LIMIT),
        cost_estimate=pl.CostEstimate(
            flops=0, bytes_accessed=8 * rows * SWAPS * piece, transcendentals=0
        ),
        name="merge_columns",
    )(even.astype(jnp.int32).reshape(1), *mine, *theirs)


def pack_kernel(even_ref, first_ref, second_ref, result_ref):
    chosen = jnp.where(even_ref[0] > 0, first_ref[...], second_ref[...])
    width = result_ref.shape[-1]
    for h in range(SWAPS):
        result_ref[0, h] = chosen[:, h * width : (h + 1) * width]


def pack_columns(even, first, second, parts):
    rows, columns = first.shape
    width = columns // parts
    block = pl.BlockSpec((rows, width), lambda i: (0, i))
    piece = width // SWAPS
    return pl.pallas_call(
        pack_kernel,
        grid=(parts,),
        in_specs=[pl.BlockSpec(memory_space=pltpu.SMEM), block, block],
        out_specs=pl.BlockSpec((1, SWAPS, rows, piece), lambda i: (i, 0, 0, 0)),
        out_shape=jax.ShapeDtypeStruct((parts, SWAPS, rows, piece), BF16),
        compiler_params=pltpu.CompilerParams(vmem_limit_bytes=VMEM_LIMIT),
        cost_estimate=pl.CostEstimate(
            flops=0, bytes_accessed=6 * rows * columns, transcendentals=0
        ),
        name="pack_columns",
    )(even.astype(jnp.int32).reshape(1), first, second)


def unpack_kernel(*refs):
    result_ref = refs[-1]
    width = refs[0].shape[-1]
    for h in range(HALVES):
        result_ref[:, h * width : (h + 1) * width] = refs[h][0].astype(F32)


def unpack_columns(pieces):
    parts, rows, half = pieces[0].shape
    return pl.pallas_call(
        unpack_kernel,
        grid=(parts,),
        in_specs=[pl.BlockSpec((1, rows, half), lambda i: (i, 0, 0))] * HALVES,
        out_specs=pl.BlockSpec((rows, HALVES * half), lambda i: (0, i)),
        out_shape=jax.ShapeDtypeStruct((rows, parts * HALVES * half), F32),
        compiler_params=pltpu.CompilerParams(vmem_limit_bytes=VMEM_LIMIT),
        cost_estimate=pl.CostEstimate(
            flops=0, bytes_accessed=6 * parts * rows * HALVES * half, transcendentals=0
        ),
        name="unpack_columns",
    )(*pieces)


class Layout:
    def __init__(self, fsdp_devices, seq_devices, rows_dev):
        self.fsdp = fsdp_devices
        self.seq = seq_devices
        self.chips = fsdp_devices // 2
        self.share = 2 * seq_devices // (2 * MICRO)
        self.near = self.share // 2
        self.piece_rows = rows_dev // self.share
        self.step_rows = rows_dev
        self.rows = LENGTH // self.share

    def flat(self, f, z):
        return f * self.seq + z

    def moved(self, r):
        pairs = []
        for f in range(self.fsdp):
            for z in range(self.seq):
                slot = z ^ r
                micro, j = slot // self.share, slot % self.share
                target_f = (f // 2) * 2 + j % 2
                target_z = (2 * micro + f % 2) * self.near + j // 2
                pairs.append((self.flat(f, z), self.flat(target_f, target_z)))
        return pairs

    def other(self, k):
        return [
            (self.flat(f, z), self.flat(f ^ k, z))
            for f in range(self.fsdp)
            for z in range(self.seq)
        ]

    def across(self, k):
        pairs = []
        for f in range(self.fsdp):
            for z in range(self.seq):
                pairs.append((self.flat(f, z), self.flat(f ^ (k & 1), z ^ (k >> 1))))
        return pairs


def permute(value, pairs):
    return lax.ppermute(value, ("fsdp", "seq"), pairs)


def scatter_rows(layout, values, z, slot):
    parts = values.reshape(layout.seq, layout.piece_rows, values.shape[-1])
    result = jnp.zeros_like(parts)
    for r in range(layout.seq):
        sent = lax.dynamic_index_in_dim(parts, z ^ r, 0, keepdims=False)
        got = permute(sent, layout.moved(r))
        result = lax.dynamic_update_index_in_dim(result, got, slot ^ r, 0)
    return result.reshape(layout.rows, values.shape[-1])


def return_rows(layout, values, f):
    width = values.shape[-1]
    parts = values.reshape(layout.seq, layout.piece_rows, width)
    parts = lax.all_to_all(parts, "seq", split_axis=0, concat_axis=0, tiled=True)
    parts = parts.reshape(MICRO, 2, layout.near, layout.piece_rows, width)
    core = f % 2
    kept = lax.dynamic_index_in_dim(parts, core, 1, keepdims=False)
    sent = lax.dynamic_index_in_dim(parts, 1 - core, 1, keepdims=False)
    got = permute(sent, layout.other(1))
    both = jnp.stack(
        [jnp.where(core == 0, kept, got), jnp.where(core == 0, got, kept)], axis=2
    )
    return both.reshape(MICRO, layout.step_rows, width)


class RowGather:
    def __init__(self, layout, own):
        self.layout = layout
        self.own = {0: own}
        self.sibling = {0: self.move(own, 1)}
        chips = layout.chips
        for n in range(1, 3 if chips == 4 else chips):
            self.own[n] = self.move(own, 2 * n)

    def move(self, value, k):
        return permute(value, self.layout.other(k))

    def after(self, n, *values):
        chips = self.layout.chips
        if n + 1 < chips:
            waiting = {m: value for m, value in self.own.items() if m > n}
            siblings = {m: value for m, value in self.sibling.items() if m > n}
            waiting, siblings, values = lax.optimization_barrier((waiting, siblings, values))
            self.own.update(waiting)
            self.sibling.update(siblings)
            if chips == 4 and n == 0:
                cut = self.own[0].shape[0] // 2
                self.far = [self.move(self.own[2][:cut], 2), self.move(self.own[1][cut:], 4)]
            if chips == 4 and n == 1:
                self.far = lax.optimization_barrier((self.far, values))[0]
                self.own[3] = jnp.concatenate(self.far)
            for m in (n + 1, n + 2):
                if m in self.own and m not in self.sibling:
                    self.sibling[m] = self.move(self.own[m], 1)
        return values


def gather_small(layout, f, own):
    held = own[None]
    k = 1
    while k < layout.fsdp:
        got = permute(held, layout.other(k))
        upper = (f & k) > 0
        held = jnp.concatenate(
            [jnp.where(upper, got, held), jnp.where(upper, held, got)], axis=0
        )
        k *= 2
    return held


def sum_small(layout, value):
    k = 1
    while k < layout.fsdp:
        value = value + permute(value, layout.other(k))
        k *= 2
    return value


class LinePipe:
    def __init__(self, z, seq_devices):
        self.seq = seq_devices
        self.z = z
        self.outer = (z == 0) | (z == seq_devices - 1)
        self.flying = []
        self.results = {}
        self.then = {}
        self.age = {}

    def send(self, stage, value):
        half, last = self.seq // 2, self.seq - 1
        if stage < half - 1:
            pairs = [(stage, stage + 1), (last - stage, last - stage - 1)]
        elif stage == half - 1:
            pairs = [(half - 1, half), (half, half - 1)]
        else:
            s = last - 1 - stage
            pairs = [(s + 1, s), (last - s - 1, last - s)]
        return lax.ppermute(value, "seq", pairs)

    def join(self, stage, value, got):
        if stage < self.seq // 2:
            return value + got
        s = self.seq - 2 - stage
        return jnp.where((self.z == s) | (self.z == self.seq - 1 - s), got, value)

    def step(self, name=None, value=None, others=(), then=None):
        arrived = [entry[3] for entry in self.flying]
        old = {key: self.results[key] for key in self.results if self.age.get(key, 0) <= 0}
        arrived, old, value, others = lax.optimization_barrier((arrived, old, value, others))
        self.results.update(old)
        self.age = {key: age - 1 for key, age in self.age.items()}
        flying = []
        if name is not None:
            self.then[name] = then
            flying.append((name, 0, value, self.send(0, value)))
        for (key, stage, held, _), got in zip(self.flying, arrived):
            if stage == self.seq - 2:
                chosen = jnp.where(self.outer, got, held)
                self.results[key] = chosen
                if self.then[key] is not None:
                    self.results[key] = self.then[key](chosen)
                    self.age[key] = 1
                continue
            held = self.join(stage, held, got)
            flying.append((key, stage + 1, held, self.send(stage + 1, held)))
        self.flying = flying
        return others

    def landed(self, names):
        return all(name in self.results for name in names)

    def finish(self):
        while self.flying:
            self.step()


def body(
    tokens,
    cotangent,
    attn_gain,
    query_gain,
    key_gain,
    w_query,
    w_key,
    w_value,
    w_out,
    ffn_gain,
    w_gate,
    w_up,
    w_down,
):
    fsdp_devices = lax.axis_size("fsdp")
    seq_devices = lax.axis_size("seq")
    layout = Layout(fsdp_devices, seq_devices, tokens.shape[2])
    f = lax.axis_index("fsdp")
    z = lax.axis_index("seq")
    rows = layout.rows
    share = layout.share
    member = (z % layout.near) * 2 + f % 2
    slot = (z // layout.near // 2) * share + member

    w_attn = lax.all_gather(
        jnp.concatenate([w_query, w_key, w_value], axis=1), "fsdp", axis=0, tiled=True
    )
    gains = gather_small(
        layout, f, jnp.concatenate([attn_gain, ffn_gain, query_gain, key_gain])
    ).astype(F32)
    wide, narrow = attn_gain.shape[0], query_gain.shape[0]
    even = z % 2 == 0
    hidden_dev = w_down.shape[0]
    gains, gate_rows, up_rows = lax.optimization_barrier((gains, w_gate, w_up))
    fetched = lax.all_to_all(
        pack_columns(even, gate_rows, up_rows, fsdp_devices),
        "fsdp",
        split_axis=0,
        concat_axis=0,
        tiled=True,
    )
    full_attn_gain = gains[:, :wide].reshape(D)
    full_ffn_gain = gains[:, wide : 2 * wide].reshape(D)
    full_query_gain = gains[:, 2 * wide : 2 * wide + narrow].reshape(HD)
    full_key_gain = gains[:, 2 * wide + narrow :].reshape(HD)
    inputs_low = scatter_rows(layout, tokens[:, 0], z, slot)
    grad_out_low = scatter_rows(layout, cotangent[:, 0], z, slot)
    full_out = lax.all_gather(w_out, "fsdp", axis=0, tiled=True)

    row = jnp.arange(rows, dtype=jnp.int32)
    position = (
        (row // layout.piece_rows) * layout.step_rows
        + member * layout.piece_rows
        + row % layout.piece_rows
    ).astype(F32)
    frequency = THETA ** (-(jnp.arange(HD // 2).astype(F32) * 2.0 / HD))
    angles = frequency[:, None] * position[None, :]
    cosine_table, sine_table = jnp.cos(angles)[None], jnp.sin(angles)[None]
    head_gains = jnp.concatenate(
        [
            jnp.broadcast_to(full_query_gain[None, :, None], (HQ, HD, 1)),
            jnp.broadcast_to(full_key_gain[None, :, None], (KVH, HD, 1)),
        ]
    )

    inputs = inputs_low.astype(F32)
    normed, normed_unit, normed_inverse = rms_fwd(inputs, full_attn_gain)
    fetched = [fetched[:, h].reshape(D, hidden_dev // SWAPS) for h in range(SWAPS)]
    swapped = [
        lax.ppermute(piece, "seq", [(i, i ^ 1) for i in range(seq_devices)]) for piece in fetched
    ]
    normed_low, grad_out_low, w_attn = lax.optimization_barrier(
        (normed.astype(BF16), grad_out_low, w_attn)
    )
    grad_out_gather = RowGather(layout, grad_out_low)
    raw = dot(w_attn, normed_low, 0, 1)
    pair_width = KVH * HD
    turned = HQ + KVH
    head_raw = raw[: turned * HD].reshape(turned, HD, rows)
    head_normed, head_unit, head_inverse = head_rms_fwd(head_raw, head_gains)
    heads_low = rotate(head_normed, cosine_table, sine_table).astype(BF16).reshape(turned * HD, rows)
    queries = heads_low[: HQ * HD]
    own_pair = jnp.concatenate([heads_low[HQ * HD :], raw[turned * HD :].astype(BF16)], axis=0)
    pair_pieces = [own_pair] + [permute(own_pair, layout.across(k)) for k in range(1, share)]
    keys = jnp.concatenate([piece[:pair_width] for piece in pair_pieces], axis=1)
    values = jnp.concatenate([piece[pair_width:] for piece in pair_pieces], axis=1)
    index = member.astype(jnp.int32).reshape(1)
    attended, log_totals = attend(
        index, queries, keys, values, share, layout.piece_rows, layout.step_rows
    )
    attended, swapped[0], grad_out_gather.own = lax.optimization_barrier(
        (attended, swapped[0], grad_out_gather.own)
    )
    middle = inputs + dot(attended, full_out, 0, 0)
    ffn_normed, ffn_unit, ffn_inverse = rms_fwd(middle, full_ffn_gain)
    ffn_low = ffn_normed.astype(BF16)

    ffn_gather = RowGather(layout, ffn_low)
    line = LinePipe(z, seq_devices)
    weights = merge_columns(even, fetched, swapped)
    worked = ()
    for n in range(layout.chips):
        pieces = [
            (side[n], 0)
            for side in (
                ffn_gather.own,
                grad_out_gather.own,
                ffn_gather.sibling,
                grad_out_gather.sibling,
            )
        ]
        worked = hidden_step(n, fsdp_devices * rows, rows, pieces, weights, w_down, worked)
        worked = ffn_gather.after(n, *worked)
        worked = grad_out_gather.after(n, *worked)
    hidden, grads, hidden_t, grads_t, ffn_rows, grad_out_rows = worked
    me = f.astype(jnp.int32).reshape(1)

    def to_owners(term):
        return lax.all_to_all(term, "fsdp", split_axis=0, concat_axis=0, tiled=True)

    down_term = weight_product(hidden_t, grad_out_rows, 0, hidden_dev, 0, "w_down_grad")
    (grads,) = line.step("down0", down_term[0], (grads,))
    grad_ffn_part = rows_product(me, grads, weights, 1, rows, "grad_ffn_normed")
    grad_ffn_part, grads_t = line.step("down1", down_term[1], (grad_ffn_part, grads_t))
    grad_ffn_normed = lax.psum_scatter(
        grad_ffn_part, "fsdp", scatter_dimension=0, tiled=True
    )
    gate_term = weight_product(grads_t, ffn_rows, 0, hidden_dev, wide, "w_gate_grad")
    gate_term, grads_t = lax.optimization_barrier((gate_term, grads_t))
    up_term = weight_product(grads_t, ffn_rows, hidden_dev, hidden_dev, wide, "w_up_grad")
    hidden, up_term = line.step("gate0", gate_term[0], (hidden, up_term), to_owners)
    out_part = rows_product(me, hidden, w_down, 0, rows, "block_out")
    out_part, grad_ffn_normed = line.step(
        "gate1", gate_term[1], (out_part, grad_ffn_normed), to_owners
    )
    out_sum = lax.psum_scatter(out_part, "fsdp", scatter_dimension=0, tiled=True)
    grad_ffn_normed = grad_ffn_normed.astype(F32)

    grad_middle_norm, ffn_gain_term = rms_back(
        grad_ffn_normed, ffn_unit, ffn_inverse, full_ffn_gain
    )
    grad_middle = grad_out_low.astype(F32) + grad_middle_norm
    grad_branch_low = grad_middle.astype(BF16)
    grad_attended = dot(full_out, grad_branch_low, 1, 1).astype(BF16)
    out_term = dot(attended, grad_branch_low, 1, 0).astype(BF16)
    out_rows = lax.psum_scatter(out_term, "fsdp", scatter_dimension=0, tiled=True)
    (grad_attended,) = line.step("up0", up_term[0], (grad_attended,), to_owners)
    grad_queries, grad_keys, grad_values = attend_back(
        index,
        queries,
        keys,
        values,
        attended,
        log_totals,
        grad_attended,
        share,
        layout.piece_rows,
        layout.step_rows,
    )
    grad_queries, grad_keys, grad_values = line.step(
        "up1", up_term[1], (grad_queries, grad_keys, grad_values), to_owners
    )
    grad_pair = jnp.concatenate([grad_keys[:, :rows], grad_values[:, :rows]], axis=0)
    for k in range(1, share):
        columns = slice(k * rows, (k + 1) * rows)
        sent = jnp.concatenate([grad_keys[:, columns], grad_values[:, columns]], axis=0)
        grad_pair = grad_pair + permute(sent.astype(BF16), layout.across(k)).astype(F32)
    grad_pair_low = grad_pair.astype(BF16)
    grad_turned = (
        jnp.concatenate([grad_queries, grad_pair_low[:pair_width]], axis=0)
        .astype(F32)
        .reshape(turned, HD, rows)
    )
    grad_head_normed = rotate(grad_turned, cosine_table, -sine_table)
    scaled = grad_head_normed * head_gains
    grad_head_raw = head_inverse * (
        scaled - head_unit * jnp.mean(scaled * head_unit, axis=1, keepdims=True)
    )
    head_gain_terms = jnp.sum(grad_head_normed * head_unit, axis=2)
    grad_raw = jnp.concatenate(
        [grad_head_raw.astype(BF16).reshape(turned * HD, rows), grad_pair_low[pair_width:]], axis=0
    )
    projection_term = dot(normed_low, grad_raw, 0, 1).astype(BF16)
    projection_term, grad_raw = lax.optimization_barrier((projection_term, grad_raw))
    projection_rows = lax.psum_scatter(
        projection_term, "fsdp", scatter_dimension=0, tiled=True
    )
    grad_raw, out_sum = line.step(others=(grad_raw, out_sum))
    block_out = return_rows(layout, (middle + out_sum.astype(F32)).astype(BF16), f)
    grad_normed = dot(grad_raw, w_attn, 0, 1)
    grad_input_norm, attn_gain_term = rms_back(
        grad_normed, normed_unit, normed_inverse, full_attn_gain
    )

    tokens_grad = return_rows(layout, (grad_middle + grad_input_norm).astype(BF16), f)
    gain_terms = sum_small(
        layout,
        jnp.concatenate(
            [
                attn_gain_term,
                ffn_gain_term,
                jnp.sum(head_gain_terms[:HQ], axis=0),
                jnp.sum(head_gain_terms[HQ:], axis=0),
            ]
        )[None],
    )[0]

    def own_share(first, count):
        share_of = count // fsdp_devices
        vector = lax.dynamic_slice_in_dim(gain_terms, first + f * share_of, share_of, 0)
        return jnp.pad(vector, (0, wide - share_of))

    gain_columns = jnp.stack(
        [own_share(0, D), own_share(D, D), own_share(2 * D, HD), own_share(2 * D + HD, HD)],
        axis=1,
    )
    gain_columns = jnp.pad(gain_columns, ((0, 0), (0, 128 - gain_columns.shape[1]))).astype(BF16)

    attn_rows = lax.psum(
        jnp.concatenate([out_rows, projection_rows, gain_columns], axis=1), "seq"
    )

    line.finish()
    w_gate_grad = unpack_columns([line.results[f"gate{h}"] for h in range(HALVES)])
    w_up_grad = unpack_columns([line.results[f"up{h}"] for h in range(HALVES)])
    w_down_grad = jnp.concatenate([line.results[f"down{h}"] for h in range(HALVES)]).astype(F32)

    attn_rows = attn_rows.astype(F32)
    w_out_grad, attn_rows = attn_rows[:, :D], attn_rows[:, D:]
    gain_rows = attn_rows[:, attn_rows.shape[1] - 128 :]
    query_width = HQ * HD

    return (
        block_out[:, None],
        tokens_grad[:, None],
        gain_rows[:, 0],
        gain_rows[:narrow, 2],
        gain_rows[:narrow, 3],
        attn_rows[:, :query_width],
        attn_rows[:, query_width : query_width + pair_width],
        attn_rows[:, query_width + pair_width : query_width + 2 * pair_width],
        w_out_grad,
        gain_rows[:, 1],
        w_gate_grad,
        w_up_grad,
        w_down_grad,
    )


def solution(mesh):
    activations = P(None, "fsdp", "seq", None)
    vector = P("fsdp")
    matrix = P("fsdp", None)
    specs = (
        (activations, activations)
        + (vector,) * 3
        + (matrix,) * 4
        + (vector,)
        + (matrix,) * 3
    )
    return jax.shard_map(body, mesh=mesh, in_specs=specs, out_specs=specs, check_vma=False)
```

```python
import functools
import math

import jax
import jax.numpy as jnp
from jax import lax
from jax.experimental import pallas as pl
from jax.experimental.pallas import tpu as pltpu
from jax.sharding import PartitionSpec as P

D = 2048
HQ = 32
KVH = 8
HD = 64
FF = 8192
LENGTH = 1024
MICRO = 2
HALVES = 2
SWAPS = 2

EPSILON = 1e-05
THETA = 1000000.0
GROUP = HQ // KVH
BLOCK = 128
SCALE = 1.0 / math.sqrt(HD)
LOG2E = math.log2(math.e)
VMEM_LIMIT = 56 * 1024 * 1024

F32 = jnp.float32
BF16 = jnp.bfloat16


def dot(left_side, right_side, left_dim, right_dim):
    return lax.dot_general(
        left_side,
        right_side,
        (((left_dim,), (right_dim,)), ((), ())),
        preferred_element_type=F32,
    )


def rms_fwd(values, row_gain):
    inverse = lax.rsqrt(jnp.mean(values * values, axis=-1, keepdims=True) + EPSILON)
    unit_rows = values * inverse
    return (unit_rows * row_gain, unit_rows, inverse)


def rms_back(grad_outputs, unit_rows, inverse, row_gain):
    scaled = grad_outputs * row_gain
    grad_inputs = inverse * (
        scaled - unit_rows * jnp.mean(scaled * unit_rows, axis=-1, keepdims=True)
    )
    grad_gain = jnp.sum(grad_outputs * unit_rows, axis=0)
    return (grad_inputs, grad_gain)


def head_rms_fwd(values, gains):
    inverse = lax.rsqrt(jnp.mean(values * values, axis=1, keepdims=True) + EPSILON)
    unit = values * inverse
    return (unit * gains, unit, inverse)


def rotate(values, cosine_table, sine_table):
    half_width = values.shape[1] // 2
    front_half = values[:, :half_width]
    back_half = values[:, half_width:]
    return jnp.concatenate(
        [
            front_half * cosine_table - back_half * sine_table,
            back_half * cosine_table + front_half * sine_table,
        ],
        axis=1,
    )


def block_masks(index, pieces, piece_rows, step_rows):
    key = lax.broadcasted_iota(jnp.int32, (BLOCK, GROUP * BLOCK), 0)
    query = lax.broadcasted_iota(jnp.int32, (BLOCK, GROUP * BLOCK), 1) & (BLOCK - 1)

    def place(row, piece):
        return (row // piece_rows) * step_rows + piece * piece_rows + (row & (piece_rows - 1))

    return [place(key, index ^ k) <= place(query, index) for k in range(pieces)]


def heads_beside(block, first, count):
    return jnp.concatenate(
        [block[h * HD : (h + 1) * HD, first : first + count] for h in range(GROUP)], axis=1
    )


def mask_tail(values, mask, first):
    tail = jnp.where(mask, values[first:], 0.0)
    if first == 0:
        return tail
    return jnp.concatenate([values[:first], tail], axis=0)


def attend_kernel(index_ref, q_ref, k_ref, v_ref, out_ref, lse_ref, *, pieces, piece_rows, step_rows):
    rows = q_ref.shape[1]
    masks = block_masks(index_ref[0], pieces, piece_rows, step_rows)
    queries = q_ref[...]
    for first in range(0, rows, BLOCK):
        count = first + BLOCK
        query_block = heads_beside(queries, first, BLOCK)
        total = None
        result = None
        for k in range(pieces):
            spot = pl.ds(k * rows, count)
            scores = dot(k_ref[:, spot], query_block, 0, 0)
            weights = mask_tail(jnp.exp2(scores * (SCALE * LOG2E)), masks[k], first)
            part = jnp.sum(weights, axis=0, keepdims=True)
            value = dot(v_ref[:, spot], weights.astype(BF16), 1, 0)
            total = part if total is None else total + part
            result = value if result is None else result + value
        result = result * (1.0 / total)
        log_total = jnp.log2(total)
        for h in range(GROUP):
            columns = slice(h * BLOCK, (h + 1) * BLOCK)
            out_ref[h * HD : (h + 1) * HD, first : first + BLOCK] = result[:, columns].astype(BF16)
            lse_ref[0, h : h + 1, first : first + BLOCK] = log_total[:, columns]


def attend_back_kernel(
    index_ref, q_ref, k_ref, v_ref, out_ref, lse_ref, grad_ref, dq_ref, dk_ref, dv_ref,
    *, pieces, piece_rows, step_rows
):
    rows = q_ref.shape[1]
    masks = block_masks(index_ref[0], pieces, piece_rows, step_rows)
    queries = q_ref[...]
    grads = grad_ref[...]
    results = out_ref[...]
    dk_ref[...] = jnp.zeros_like(dk_ref)
    dv_ref[...] = jnp.zeros_like(dv_ref)
    for first in range(0, rows, BLOCK):
        count = first + BLOCK
        query_block = heads_beside(queries, first, BLOCK)
        grad_block = heads_beside(grads, first, BLOCK)
        result_block = heads_beside(results, first, BLOCK)
        centre = jnp.sum(
            grad_block.astype(F32) * result_block.astype(F32), axis=0, keepdims=True
        )
        log_total = jnp.concatenate(
            [lse_ref[0, h : h + 1, first : first + BLOCK] for h in range(GROUP)], axis=1
        )
        dq = None
        for k in range(pieces):
            spot = pl.ds(k * rows, count)
            keys = k_ref[:, spot]
            scores = dot(keys, query_block, 0, 0)
            weights = mask_tail(
                jnp.exp2(scores * (SCALE * LOG2E) - log_total), masks[k], first
            )
            grad_weights = dot(v_ref[:, spot], grad_block, 0, 0)
            grad_scores = (weights * (grad_weights - centre)).astype(BF16)
            part = dot(keys, grad_scores, 1, 0)
            dq = part if dq is None else dq + part
            dk_ref[:, spot] += dot(query_block, grad_scores, 1, 1) * SCALE
            dv_ref[:, spot] += dot(grad_block, weights.astype(BF16), 1, 1)
        dq = (dq * SCALE).astype(BF16)
        for h in range(GROUP):
            columns = slice(h * BLOCK, (h + 1) * BLOCK)
            dq_ref[h * HD : (h + 1) * HD, first : first + BLOCK] = dq[:, columns]


def attention_specs(rows, total_rows):
    group_spec = pl.BlockSpec((GROUP * HD, rows), lambda i: (i, 0))
    pair_spec = pl.BlockSpec((HD, total_rows), lambda i: (i, 0))
    lse_spec = pl.BlockSpec((1, GROUP, rows), lambda i: (i, 0, 0))
    return group_spec, pair_spec, lse_spec


def attend(index, queries, keys, values, pieces, piece_rows, step_rows):
    rows, total_rows = queries.shape[1], keys.shape[1]
    group_spec, pair_spec, lse_spec = attention_specs(rows, total_rows)
    return pl.pallas_call(
        functools.partial(
            attend_kernel, pieces=pieces, piece_rows=piece_rows, step_rows=step_rows
        ),
        grid=(KVH,),
        in_specs=[pl.BlockSpec(memory_space=pltpu.SMEM), group_spec, pair_spec, pair_spec],
        out_specs=[group_spec, lse_spec],
        out_shape=[
            jax.ShapeDtypeStruct((HQ * HD, rows), BF16),
            jax.ShapeDtypeStruct((KVH, GROUP, rows), F32),
        ],
        compiler_params=pltpu.CompilerParams(vmem_limit_bytes=VMEM_LIMIT),
        cost_estimate=pl.CostEstimate(
            flops=4 * HQ * HD * rows * total_rows,
            bytes_accessed=8 * HQ * HD * rows,
            transcendentals=HQ * rows * total_rows,
        ),
        name="attend",
    )(index, queries, keys, values)


def attend_back(index, queries, keys, values, results, lse, grads, pieces, piece_rows, step_rows):
    rows, total_rows = queries.shape[1], keys.shape[1]
    group_spec, pair_spec, lse_spec = attention_specs(rows, total_rows)
    return pl.pallas_call(
        functools.partial(
            attend_back_kernel, pieces=pieces, piece_rows=piece_rows, step_rows=step_rows
        ),
        grid=(KVH,),
        in_specs=[
            pl.BlockSpec(memory_space=pltpu.SMEM),
            group_spec,
            pair_spec,
            pair_spec,
            group_spec,
            lse_spec,
            group_spec,
        ],
        out_specs=[group_spec, pair_spec, pair_spec],
        out_shape=[
            jax.ShapeDtypeStruct((HQ * HD, rows), BF16),
            jax.ShapeDtypeStruct((KVH * HD, total_rows), F32),
            jax.ShapeDtypeStruct((KVH * HD, total_rows), F32),
        ],
        compiler_params=pltpu.CompilerParams(vmem_limit_bytes=VMEM_LIMIT),
        cost_estimate=pl.CostEstimate(
            flops=10 * HQ * HD * rows * total_rows,
            bytes_accessed=16 * HQ * HD * rows,
            transcendentals=HQ * rows * total_rows,
        ),
        name="attend_back",
    )(index, queries, keys, values, results, lse, grads)


def hidden_kernel(own_x_ref, own_c_ref, other_x_ref, other_c_ref, weight_ref, down_ref, *refs):
    hidden_ref, grads_ref, hidden_t_ref, grads_t_ref, all_x_ref, all_c_ref = refs[-6:]
    units = down_ref.shape[0]
    half = units // HALVES

    def work(x_ref, c_ref):
        x = x_ref[...]
        c = c_ref[...]
        all_x_ref[...] = x
        all_c_ref[...] = c
        for h in range(HALVES):
            part = slice(h * half, (h + 1) * half)
            up_part = slice(units + h * half, units + (h + 1) * half)
            gate = dot(x, weight_ref[:, part], 1, 0)
            up = dot(x, weight_ref[:, up_part], 1, 0)
            grad_hidden = dot(c, down_ref[part, :], 1, 1)
            sigmoid = 0.5 * jnp.tanh(0.5 * gate) + 0.5
            silu = gate * sigmoid
            hidden = (silu * up).astype(BF16)
            grad_up = (grad_hidden * silu).astype(BF16)
            grad_gate = (grad_hidden * up * (sigmoid + silu * (1.0 - sigmoid))).astype(BF16)
            hidden_ref[:, part] = hidden
            grads_ref[:, part] = grad_gate
            grads_ref[:, up_part] = grad_up
            hidden_t_ref[part, :] = hidden.T
            grads_t_ref[part, :] = grad_gate.T
            grads_t_ref[up_part, :] = grad_up.T

    pl.when(pl.program_id(0) == 0)(lambda: work(own_x_ref, own_c_ref))
    pl.when(pl.program_id(0) == 1)(lambda: work(other_x_ref, other_c_ref))


def hidden_step(n, count, rows, pieces, weights, w_down, so_far):
    depth = w_down.shape[1]
    units = w_down.shape[0]
    once = pl.Buffered(1)
    read = [
        pl.BlockSpec((rows, depth), lambda i, block=block: (block, 0), pipeline_mode=once)
        for _, block in pieces
    ]
    widths = (units, 2 * units)
    upright = [(count, width) for width in widths]
    turned = [(width, count) for width in widths]
    whole = [(count, depth)] * 2
    flops = 12 * rows * depth * units
    return pl.pallas_call(
        hidden_kernel,
        grid=(2,),
        in_specs=read
        + [
            pl.BlockSpec((depth, 2 * units), lambda i: (0, 0), pipeline_mode=once),
            pl.BlockSpec((units, depth), lambda i: (0, 0), pipeline_mode=once),
        ]
        + [pl.BlockSpec(memory_space=pl.ANY)] * len(so_far),
        out_specs=[pl.BlockSpec((rows, shape[1]), lambda i: (2 * n + i, 0)) for shape in upright]
        + [pl.BlockSpec((shape[0], rows), lambda i: (0, 2 * n + i)) for shape in turned]
        + [pl.BlockSpec((rows, shape[1]), lambda i: (2 * n + i, 0)) for shape in whole],
        out_shape=[jax.ShapeDtypeStruct(shape, BF16) for shape in upright + turned + whole],
        input_output_aliases={6 + k: k for k in range(len(so_far))},
        compiler_params=pltpu.CompilerParams(vmem_limit_bytes=VMEM_LIMIT),
        cost_estimate=pl.CostEstimate(
            flops=flops,
            bytes_accessed=16 * rows * depth + 24 * rows * units + 6 * depth * units,
            transcendentals=2 * rows * units,
        ),
        name="hidden_step",
    )(*[array for array, _ in pieces], weights, w_down, *so_far)


def rows_kernel(me_ref, left_ref, right_ref, result_ref, *, right_dim):
    result_ref[...] = dot(left_ref[...], right_ref[...], 1, right_dim).astype(BF16)


def rows_product(me, left, right, right_dim, block_rows, name):
    count, width = left.shape
    return pl.pallas_call(
        functools.partial(rows_kernel, right_dim=right_dim),
        grid_spec=pltpu.PrefetchScalarGridSpec(
            num_scalar_prefetch=1,
            grid=(count // block_rows,),
            in_specs=[
                pl.BlockSpec((block_rows, width), lambda i, me_ref: (i, 0)),
                pl.BlockSpec(
                    right.shape, lambda i, me_ref: (0, 0), pipeline_mode=pl.Buffered(1)
                ),
            ],
            out_specs=pl.BlockSpec((block_rows, D), lambda i, me_ref: (me_ref[0] ^ i, 0)),
        ),
        out_shape=jax.ShapeDtypeStruct((count, D), BF16),
        compiler_params=pltpu.CompilerParams(vmem_limit_bytes=VMEM_LIMIT),
        cost_estimate=pl.CostEstimate(
            flops=2 * count * D * width,
            bytes_accessed=2 * (count * width + count * D + D * width),
            transcendentals=0,
        ),
        name=name,
    )(me, left, right)


def out_kernel(me_ref, hidden_ref, down_ref, *refs):
    refs[-1][...] = dot(hidden_ref[...], down_ref[...], 1, 0).astype(BF16)


def out_step(n, me, hidden, w_down, rows, so_far):
    count, units = hidden.shape
    return pl.pallas_call(
        out_kernel,
        grid_spec=pltpu.PrefetchScalarGridSpec(
            num_scalar_prefetch=1,
            grid=(2,),
            in_specs=[
                pl.BlockSpec((rows, units), lambda i, me_ref: (2 * n + i, 0)),
                pl.BlockSpec((units, D), lambda i, me_ref: (0, 0), pipeline_mode=pl.Buffered(1)),
            ]
            + [pl.BlockSpec(memory_space=pl.ANY)] * len(so_far),
            out_specs=pl.BlockSpec((rows, D), lambda i, me_ref: (me_ref[0] ^ (2 * n + i), 0)),
        ),
        out_shape=jax.ShapeDtypeStruct((count, D), BF16),
        input_output_aliases={3: 0} if so_far else {},
        compiler_params=pltpu.CompilerParams(vmem_limit_bytes=VMEM_LIMIT),
        cost_estimate=pl.CostEstimate(
            flops=4 * rows * D * units,
            bytes_accessed=4 * rows * (units + D) + 2 * units * D,
            transcendentals=0,
        ),
        name="block_out",
    )(me, hidden, w_down, *so_far)


def weight_kernel(left_ref, right_ref, *result_refs, parts):
    total = dot(left_ref[...], right_ref[...], 1, 0)
    half = total.shape[0] // HALVES
    for h, result_ref in enumerate(result_refs):
        piece = total[h * half : (h + 1) * half]
        if parts == 0:
            result_ref[...] = piece.astype(BF16)
            continue
        wide = piece.shape[1] // parts
        for p in range(parts):
            result_ref[p] = piece[:, p * wide : (p + 1) * wide].astype(BF16).T


def weight_product(left, right, first, units, wide, name):
    depth = left.shape[1]
    half = units // HALVES
    column = min(512, D)
    parts = column // wide if wide else 0
    block = first // units
    if wide:
        out_spec = pl.BlockSpec((parts, wide, half), lambda j: (j, 0, 0))
        out_shape = jax.ShapeDtypeStruct((D // wide, wide, half), BF16)
    else:
        out_spec = pl.BlockSpec((half, column), lambda j: (0, j))
        out_shape = jax.ShapeDtypeStruct((half, D), BF16)
    return pl.pallas_call(
        functools.partial(weight_kernel, parts=parts),
        grid=(D // column,),
        in_specs=[
            pl.BlockSpec((units, depth), lambda j: (block, 0), pipeline_mode=pl.Buffered(1)),
            pl.BlockSpec((depth, column), lambda j: (0, j)),
        ],
        out_specs=[out_spec] * HALVES,
        out_shape=[out_shape] * HALVES,
        compiler_params=pltpu.CompilerParams(vmem_limit_bytes=VMEM_LIMIT),
        cost_estimate=pl.CostEstimate(
            flops=2 * units * depth * D,
            bytes_accessed=2 * depth * (units + D) + 2 * units * D,
            transcendentals=0,
        ),
        name=name,
    )(left, right)


def merge_kernel(even_ref, *refs):
    result_ref = refs[-1]
    piece = result_ref.shape[1] // (2 * SWAPS)
    for h in range(SWAPS):
        mine, theirs = refs[h][...], refs[SWAPS + h][...]
        gate = jnp.where(even_ref[0] > 0, mine, theirs)
        up = jnp.where(even_ref[0] > 0, theirs, mine)
        result_ref[:, h * piece : (h + 1) * piece] = gate
        result_ref[:, (SWAPS + h) * piece : (SWAPS + h + 1) * piece] = up


def merge_columns(even, mine, theirs):
    rows, piece = mine[0].shape
    tile = min(256, rows)
    return pl.pallas_call(
        merge_kernel,
        grid=(rows // tile,),
        in_specs=[pl.BlockSpec(memory_space=pltpu.SMEM)]
        + [pl.BlockSpec((tile, piece), lambda i: (i, 0))] * (2 * SWAPS),
        out_specs=pl.BlockSpec((tile, 2 * SWAPS * piece), lambda i: (i, 0)),
        out_shape=jax.ShapeDtypeStruct((rows, 2 * SWAPS * piece), BF16),
        compiler_params=pltpu.CompilerParams(vmem_limit_bytes=VMEM_LIMIT),
        cost_estimate=pl.CostEstimate(
            flops=0, bytes_accessed=8 * rows * SWAPS * piece, transcendentals=0
        ),
        name="merge_columns",
    )(even.astype(jnp.int32).reshape(1), *mine, *theirs)


def pack_kernel(even_ref, first_ref, second_ref, result_ref):
    chosen = jnp.where(even_ref[0] > 0, first_ref[...], second_ref[...])
    width = result_ref.shape[-1]
    for h in range(SWAPS):
        result_ref[0, h] = chosen[:, h * width : (h + 1) * width]


def pack_columns(even, first, second, parts):
    rows, columns = first.shape
    width = columns // parts
    block = pl.BlockSpec((rows, width), lambda i: (0, i))
    piece = width // SWAPS
    return pl.pallas_call(
        pack_kernel,
        grid=(parts,),
        in_specs=[pl.BlockSpec(memory_space=pltpu.SMEM), block, block],
        out_specs=pl.BlockSpec((1, SWAPS, rows, piece), lambda i: (i, 0, 0, 0)),
        out_shape=jax.ShapeDtypeStruct((parts, SWAPS, rows, piece), BF16),
        compiler_params=pltpu.CompilerParams(vmem_limit_bytes=VMEM_LIMIT),
        cost_estimate=pl.CostEstimate(
            flops=0, bytes_accessed=6 * rows * columns, transcendentals=0
        ),
        name="pack_columns",
    )(even.astype(jnp.int32).reshape(1), first, second)


def unpack_kernel(*refs):
    result_ref = refs[-1]
    width = refs[0].shape[-1]
    for h in range(HALVES):
        result_ref[:, h * width : (h + 1) * width] = refs[h][0].astype(F32)


def unpack_columns(pieces):
    parts, rows, half = pieces[0].shape
    return pl.pallas_call(
        unpack_kernel,
        grid=(parts,),
        in_specs=[pl.BlockSpec((1, rows, half), lambda i: (i, 0, 0))] * HALVES,
        out_specs=pl.BlockSpec((rows, HALVES * half), lambda i: (0, i)),
        out_shape=jax.ShapeDtypeStruct((rows, parts * HALVES * half), F32),
        compiler_params=pltpu.CompilerParams(vmem_limit_bytes=VMEM_LIMIT),
        cost_estimate=pl.CostEstimate(
            flops=0, bytes_accessed=6 * parts * rows * HALVES * half, transcendentals=0
        ),
        name="unpack_columns",
    )(*pieces)


class Layout:
    def __init__(self, fsdp_devices, seq_devices, rows_dev):
        self.fsdp = fsdp_devices
        self.seq = seq_devices
        self.chips = fsdp_devices // 2
        self.share = 2 * seq_devices // (2 * MICRO)
        self.near = self.share // 2
        self.piece_rows = rows_dev // self.share
        self.step_rows = rows_dev
        self.rows = LENGTH // self.share

    def flat(self, f, z):
        return f * self.seq + z

    def moved(self, r):
        pairs = []
        for f in range(self.fsdp):
            for z in range(self.seq):
                slot = z ^ r
                micro, j = slot // self.share, slot % self.share
                target_f = (f // 2) * 2 + j % 2
                target_z = (2 * micro + f % 2) * self.near + j // 2
                pairs.append((self.flat(f, z), self.flat(target_f, target_z)))
        return pairs

    def other(self, k):
        return [
            (self.flat(f, z), self.flat(f ^ k, z))
            for f in range(self.fsdp)
            for z in range(self.seq)
        ]

    def across(self, k):
        pairs = []
        for f in range(self.fsdp):
            for z in range(self.seq):
                pairs.append((self.flat(f, z), self.flat(f ^ (k & 1), z ^ (k >> 1))))
        return pairs


def permute(value, pairs):
    return lax.ppermute(value, ("fsdp", "seq"), pairs)


def scatter_rows(layout, values, z, slot):
    parts = values.reshape(layout.seq, layout.piece_rows, values.shape[-1])
    result = jnp.zeros_like(parts)
    for r in range(layout.seq):
        sent = lax.dynamic_index_in_dim(parts, z ^ r, 0, keepdims=False)
        got = permute(sent, layout.moved(r))
        result = lax.dynamic_update_index_in_dim(result, got, slot ^ r, 0)
    return result.reshape(layout.rows, values.shape[-1])


def return_rows(layout, values, f):
    width = values.shape[-1]
    parts = values.reshape(layout.seq, layout.piece_rows, width)
    parts = lax.all_to_all(parts, "seq", split_axis=0, concat_axis=0, tiled=True)
    parts = parts.reshape(MICRO, 2, layout.near, layout.piece_rows, width)
    core = f % 2
    kept = lax.dynamic_index_in_dim(parts, core, 1, keepdims=False)
    sent = lax.dynamic_index_in_dim(parts, 1 - core, 1, keepdims=False)
    got = permute(sent, layout.other(1))
    both = jnp.stack(
        [jnp.where(core == 0, kept, got), jnp.where(core == 0, got, kept)], axis=2
    )
    return both.reshape(MICRO, layout.step_rows, width)


class RowGather:
    def __init__(self, layout, own):
        self.layout = layout
        self.own = {0: own}
        self.sibling = {0: self.move(own, 1)}
        chips = layout.chips
        for n in range(1, 3 if chips == 4 else chips):
            self.own[n] = self.move(own, 2 * n)

    def move(self, value, k):
        return permute(value, self.layout.other(k))

    def after(self, n, *values):
        chips = self.layout.chips
        if n + 1 < chips:
            waiting = {m: value for m, value in self.own.items() if m > n}
            siblings = {m: value for m, value in self.sibling.items() if m > n}
            waiting, siblings, values = lax.optimization_barrier((waiting, siblings, values))
            self.own.update(waiting)
            self.sibling.update(siblings)
            if chips == 4 and n == 0:
                cut = self.own[0].shape[0] // 2
                self.far = [self.move(self.own[2][:cut], 2), self.move(self.own[1][cut:], 4)]
            if chips == 4 and n == 1:
                self.far = lax.optimization_barrier((self.far, values))[0]
                self.own[3] = jnp.concatenate(self.far)
            for m in (n + 1, n + 2):
                if m in self.own and m not in self.sibling:
                    self.sibling[m] = self.move(self.own[m], 1)
        return values


def gather_small(layout, f, own):
    held = own[None]
    k = 1
    while k < layout.fsdp:
        got = permute(held, layout.other(k))
        upper = (f & k) > 0
        held = jnp.concatenate(
            [jnp.where(upper, got, held), jnp.where(upper, held, got)], axis=0
        )
        k *= 2
    return held


def sum_small(layout, value):
    k = 1
    while k < layout.fsdp:
        value = value + permute(value, layout.other(k))
        k *= 2
    return value


class LinePipe:
    def __init__(self, z, seq_devices):
        self.seq = seq_devices
        self.z = z
        self.outer = (z == 0) | (z == seq_devices - 1)
        self.flying = []
        self.results = {}
        self.then = {}
        self.age = {}

    def send(self, stage, value):
        half, last = self.seq // 2, self.seq - 1
        if stage < half - 1:
            pairs = [(stage, stage + 1), (last - stage, last - stage - 1)]
        elif stage == half - 1:
            pairs = [(half - 1, half), (half, half - 1)]
        else:
            s = last - 1 - stage
            pairs = [(s + 1, s), (last - s - 1, last - s)]
        return lax.ppermute(value, "seq", pairs)

    def join(self, stage, value, got):
        if stage < self.seq // 2:
            return value + got
        s = self.seq - 2 - stage
        return jnp.where((self.z == s) | (self.z == self.seq - 1 - s), got, value)

    def step(self, name=None, value=None, others=(), then=None):
        arrived = [entry[3] for entry in self.flying]
        old = {key: self.results[key] for key in self.results if self.age.get(key, 0) <= 0}
        arrived, old, value, others = lax.optimization_barrier((arrived, old, value, others))
        self.results.update(old)
        self.age = {key: age - 1 for key, age in self.age.items()}
        flying = []
        if name is not None:
            self.then[name] = then
            flying.append((name, 0, value, self.send(0, value)))
        for (key, stage, held, _), got in zip(self.flying, arrived):
            if stage == self.seq - 2:
                chosen = jnp.where(self.outer, got, held)
                self.results[key] = chosen
                if self.then[key] is not None:
                    self.results[key] = self.then[key](chosen)
                    self.age[key] = 1
                continue
            held = self.join(stage, held, got)
            flying.append((key, stage + 1, held, self.send(stage + 1, held)))
        self.flying = flying
        return others

    def landed(self, names):
        return all(name in self.results for name in names)

    def finish(self):
        while self.flying:
            self.step()


def body(
    tokens,
    cotangent,
    attn_gain,
    query_gain,
    key_gain,
    w_query,
    w_key,
    w_value,
    w_out,
    ffn_gain,
    w_gate,
    w_up,
    w_down,
):
    fsdp_devices = lax.axis_size("fsdp")
    seq_devices = lax.axis_size("seq")
    layout = Layout(fsdp_devices, seq_devices, tokens.shape[2])
    f = lax.axis_index("fsdp")
    z = lax.axis_index("seq")
    rows = layout.rows
    share = layout.share
    member = (z % layout.near) * 2 + f % 2
    slot = (z // layout.near // 2) * share + member

    w_attn = lax.all_gather(
        jnp.concatenate([w_query, w_key, w_value], axis=1), "fsdp", axis=0, tiled=True
    )
    gains = gather_small(
        layout, f, jnp.concatenate([attn_gain, ffn_gain, query_gain, key_gain])
    ).astype(F32)
    wide, narrow = attn_gain.shape[0], query_gain.shape[0]
    even = z % 2 == 0
    hidden_dev = w_down.shape[0]
    gains, gate_rows, up_rows = lax.optimization_barrier((gains, w_gate, w_up))
    fetched = lax.all_to_all(
        pack_columns(even, gate_rows, up_rows, fsdp_devices),
        "fsdp",
        split_axis=0,
        concat_axis=0,
        tiled=True,
    )
    full_attn_gain = gains[:, :wide].reshape(D)
    full_ffn_gain = gains[:, wide : 2 * wide].reshape(D)
    full_query_gain = gains[:, 2 * wide : 2 * wide + narrow].reshape(HD)
    full_key_gain = gains[:, 2 * wide + narrow :].reshape(HD)
    inputs_low = scatter_rows(layout, tokens[:, 0], z, slot)
    grad_out_low = scatter_rows(layout, cotangent[:, 0], z, slot)
    full_out = lax.all_gather(w_out, "fsdp", axis=0, tiled=True)

    row = jnp.arange(rows, dtype=jnp.int32)
    position = (
        (row // layout.piece_rows) * layout.step_rows
        + member * layout.piece_rows
        + row % layout.piece_rows
    ).astype(F32)
    frequency = THETA ** (-(jnp.arange(HD // 2).astype(F32) * 2.0 / HD))
    angles = frequency[:, None] * position[None, :]
    cosine_table, sine_table = jnp.cos(angles)[None], jnp.sin(angles)[None]
    head_gains = jnp.concatenate(
        [
            jnp.broadcast_to(full_query_gain[None, :, None], (HQ, HD, 1)),
            jnp.broadcast_to(full_key_gain[None, :, None], (KVH, HD, 1)),
        ]
    )

    inputs = inputs_low.astype(F32)
    normed, normed_unit, normed_inverse = rms_fwd(inputs, full_attn_gain)
    fetched = [fetched[:, h].reshape(D, hidden_dev // SWAPS) for h in range(SWAPS)]
    swapped = [
        lax.ppermute(piece, "seq", [(i, i ^ 1) for i in range(seq_devices)]) for piece in fetched
    ]
    normed_low, grad_out_low, w_attn = lax.optimization_barrier(
        (normed.astype(BF16), grad_out_low, w_attn)
    )
    grad_out_gather = RowGather(layout, grad_out_low)
    raw = dot(w_attn, normed_low, 0, 1)
    pair_width = KVH * HD
    turned = HQ + KVH
    head_raw = raw[: turned * HD].reshape(turned, HD, rows)
    head_normed, head_unit, head_inverse = head_rms_fwd(head_raw, head_gains)
    heads_low = rotate(head_normed, cosine_table, sine_table).astype(BF16).reshape(turned * HD, rows)
    queries = heads_low[: HQ * HD]
    own_pair = jnp.concatenate([heads_low[HQ * HD :], raw[turned * HD :].astype(BF16)], axis=0)
    pair_pieces = [own_pair] + [permute(own_pair, layout.across(k)) for k in range(1, share)]
    keys = jnp.concatenate([piece[:pair_width] for piece in pair_pieces], axis=1)
    values = jnp.concatenate([piece[pair_width:] for piece in pair_pieces], axis=1)
    index = member.astype(jnp.int32).reshape(1)
    attended, log_totals = attend(
        index, queries, keys, values, share, layout.piece_rows, layout.step_rows
    )
    attended, swapped[0], grad_out_gather.own = lax.optimization_barrier(
        (attended, swapped[0], grad_out_gather.own)
    )
    middle = inputs + dot(attended, full_out, 0, 0)
    ffn_normed, ffn_unit, ffn_inverse = rms_fwd(middle, full_ffn_gain)
    ffn_low = ffn_normed.astype(BF16)

    ffn_gather = RowGather(layout, ffn_low)
    line = LinePipe(z, seq_devices)
    weights = merge_columns(even, fetched, swapped)
    worked = ()
    out_part = ()
    me = f.astype(jnp.int32).reshape(1)
    for n in range(layout.chips):
        pieces = [
            (side[n], 0)
            for side in (
                ffn_gather.own,
                grad_out_gather.own,
                ffn_gather.sibling,
                grad_out_gather.sibling,
            )
        ]
        worked = hidden_step(n, fsdp_devices * rows, rows, pieces, weights, w_down, worked)
        out_part = out_step(n, me, worked[0], w_down, rows, out_part)
        *worked, out_part = lax.optimization_barrier((*worked, out_part))
        out_part = (out_part,)
        worked = ffn_gather.after(n, *worked)
        worked = grad_out_gather.after(n, *worked)
    hidden, grads, hidden_t, grads_t, ffn_rows, grad_out_rows = worked
    out_sum = lax.psum_scatter(out_part[0], "fsdp", scatter_dimension=0, tiled=True)

    def to_owners(term):
        return lax.all_to_all(term, "fsdp", split_axis=0, concat_axis=0, tiled=True)

    gate_term = weight_product(grads_t, ffn_rows, 0, hidden_dev, wide, "w_gate_grad")
    (grads,) = line.step("gate0", gate_term[0], (grads,), to_owners)
    grad_ffn_part = rows_product(me, grads, weights, 1, rows, "grad_ffn_normed")
    grad_ffn_part, grads_t = line.step(
        "gate1", gate_term[1], (grad_ffn_part, grads_t), to_owners
    )
    grad_ffn_normed = lax.psum_scatter(
        grad_ffn_part, "fsdp", scatter_dimension=0, tiled=True
    )
    up_term = weight_product(grads_t, ffn_rows, hidden_dev, hidden_dev, wide, "w_up_grad")
    (hidden_t,) = line.step("up0", up_term[0], (hidden_t,), to_owners)
    down_term = weight_product(hidden_t, grad_out_rows, 0, hidden_dev, 0, "w_down_grad")
    down_term, grad_ffn_normed, out_sum = line.step(
        "up1", up_term[1], (down_term, grad_ffn_normed, out_sum), to_owners
    )
    block_out = return_rows(layout, (middle + out_sum.astype(F32)).astype(BF16), f)
    grad_ffn_normed = grad_ffn_normed.astype(F32)

    grad_middle_norm, ffn_gain_term = rms_back(
        grad_ffn_normed, ffn_unit, ffn_inverse, full_ffn_gain
    )
    grad_middle = grad_out_low.astype(F32) + grad_middle_norm
    grad_branch_low = grad_middle.astype(BF16)
    grad_attended = dot(full_out, grad_branch_low, 1, 1).astype(BF16)
    out_term = dot(attended, grad_branch_low, 1, 0).astype(BF16)
    out_rows = lax.psum_scatter(out_term, "fsdp", scatter_dimension=0, tiled=True)
    (grad_attended,) = line.step("down0", down_term[0], (grad_attended,))
    grad_queries, grad_keys, grad_values = attend_back(
        index,
        queries,
        keys,
        values,
        attended,
        log_totals,
        grad_attended,
        share,
        layout.piece_rows,
        layout.step_rows,
    )
    grad_queries, grad_keys, grad_values = line.step(
        "down1", down_term[1], (grad_queries, grad_keys, grad_values)
    )
    grad_pair = jnp.concatenate([grad_keys[:, :rows], grad_values[:, :rows]], axis=0)
    for k in range(1, share):
        columns = slice(k * rows, (k + 1) * rows)
        sent = jnp.concatenate([grad_keys[:, columns], grad_values[:, columns]], axis=0)
        grad_pair = grad_pair + permute(sent.astype(BF16), layout.across(k)).astype(F32)
    grad_pair_low = grad_pair.astype(BF16)
    grad_turned = (
        jnp.concatenate([grad_queries, grad_pair_low[:pair_width]], axis=0)
        .astype(F32)
        .reshape(turned, HD, rows)
    )
    grad_head_normed = rotate(grad_turned, cosine_table, -sine_table)
    scaled = grad_head_normed * head_gains
    grad_head_raw = head_inverse * (
        scaled - head_unit * jnp.mean(scaled * head_unit, axis=1, keepdims=True)
    )
    head_gain_terms = jnp.sum(grad_head_normed * head_unit, axis=2)
    grad_raw = jnp.concatenate(
        [grad_head_raw.astype(BF16).reshape(turned * HD, rows), grad_pair_low[pair_width:]], axis=0
    )
    projection_term = dot(normed_low, grad_raw, 0, 1).astype(BF16)
    projection_term, grad_raw = lax.optimization_barrier((projection_term, grad_raw))
    projection_rows = lax.psum_scatter(
        projection_term, "fsdp", scatter_dimension=0, tiled=True
    )
    grad_raw, block_out = line.step("out", out_rows, (grad_raw, block_out))
    grad_normed = dot(grad_raw, w_attn, 0, 1)
    grad_input_norm, attn_gain_term = rms_back(
        grad_normed, normed_unit, normed_inverse, full_attn_gain
    )

    tokens_grad = return_rows(layout, (grad_middle + grad_input_norm).astype(BF16), f)
    gain_terms = sum_small(
        layout,
        jnp.concatenate(
            [
                attn_gain_term,
                ffn_gain_term,
                jnp.sum(head_gain_terms[:HQ], axis=0),
                jnp.sum(head_gain_terms[HQ:], axis=0),
            ]
        )[None],
    )[0]

    def own_share(first, count):
        share_of = count // fsdp_devices
        vector = lax.dynamic_slice_in_dim(gain_terms, first + f * share_of, share_of, 0)
        return jnp.pad(vector, (0, wide - share_of))

    gain_columns = jnp.stack(
        [own_share(0, D), own_share(D, D), own_share(2 * D, HD), own_share(2 * D + HD, HD)],
        axis=1,
    )
    gain_columns = jnp.pad(gain_columns, ((0, 0), (0, 128 - gain_columns.shape[1]))).astype(BF16)

    attn_rows = lax.psum(
        jnp.concatenate([projection_rows, gain_columns], axis=1), "seq"
    )

    (tokens_grad,) = line.step(others=(tokens_grad,))
    line.finish()
    w_gate_grad = unpack_columns([line.results[f"gate{h}"] for h in range(HALVES)])
    w_up_grad = unpack_columns([line.results[f"up{h}"] for h in range(HALVES)])
    w_down_grad = jnp.concatenate([line.results[f"down{h}"] for h in range(HALVES)]).astype(F32)

    attn_rows = attn_rows.astype(F32)
    w_out_grad = line.results["out"].astype(F32)
    gain_rows = attn_rows[:, attn_rows.shape[1] - 128 :]
    query_width = HQ * HD

    return (
        block_out[:, None],
        tokens_grad[:, None],
        gain_rows[:, 0],
        gain_rows[:narrow, 2],
        gain_rows[:narrow, 3],
        attn_rows[:, :query_width],
        attn_rows[:, query_width : query_width + pair_width],
        attn_rows[:, query_width + pair_width : query_width + 2 * pair_width],
        w_out_grad,
        gain_rows[:, 1],
        w_gate_grad,
        w_up_grad,
        w_down_grad,
    )


def solution(mesh):
    activations = P(None, "fsdp", "seq", None)
    vector = P("fsdp")
    matrix = P("fsdp", None)
    specs = (
        (activations, activations)
        + (vector,) * 3
        + (matrix,) * 4
        + (vector,)
        + (matrix,) * 3
    )
    return jax.shard_map(body, mesh=mesh, in_specs=specs, out_specs=specs, check_vma=False)
```

```python
import functools
import math

import jax
import jax.numpy as jnp
from jax import lax
from jax.experimental import pallas as pl
from jax.experimental.pallas import tpu as pltpu
from jax.sharding import PartitionSpec as P

D = 2048
HQ = 32
KVH = 8
HD = 64
FF = 8192
LENGTH = 1024
MICRO = 2
HALVES = 2
SWAPS = 2

EPSILON = 1e-05
THETA = 1000000.0
GROUP = HQ // KVH
BLOCK = 128
SCALE = 1.0 / math.sqrt(HD)
LOG2E = math.log2(math.e)
VMEM_LIMIT = 56 * 1024 * 1024

F32 = jnp.float32
BF16 = jnp.bfloat16


def dot(left_side, right_side, left_dim, right_dim):
    return lax.dot_general(
        left_side,
        right_side,
        (((left_dim,), (right_dim,)), ((), ())),
        preferred_element_type=F32,
    )


def rms_fwd(values, row_gain):
    inverse = lax.rsqrt(jnp.mean(values * values, axis=-1, keepdims=True) + EPSILON)
    unit_rows = values * inverse
    return (unit_rows * row_gain, unit_rows, inverse)


def rms_back(grad_outputs, unit_rows, inverse, row_gain):
    scaled = grad_outputs * row_gain
    grad_inputs = inverse * (
        scaled - unit_rows * jnp.mean(scaled * unit_rows, axis=-1, keepdims=True)
    )
    grad_gain = jnp.sum(grad_outputs * unit_rows, axis=0)
    return (grad_inputs, grad_gain)


def head_rms_fwd(values, gains):
    inverse = lax.rsqrt(jnp.mean(values * values, axis=1, keepdims=True) + EPSILON)
    unit = values * inverse
    return (unit * gains, unit, inverse)


def rotate(values, cosine_table, sine_table):
    half_width = values.shape[1] // 2
    front_half = values[:, :half_width]
    back_half = values[:, half_width:]
    return jnp.concatenate(
        [
            front_half * cosine_table - back_half * sine_table,
            back_half * cosine_table + front_half * sine_table,
        ],
        axis=1,
    )


def block_masks(index, pieces, piece_rows, step_rows):
    key = lax.broadcasted_iota(jnp.int32, (BLOCK, GROUP * BLOCK), 0)
    query = lax.broadcasted_iota(jnp.int32, (BLOCK, GROUP * BLOCK), 1) & (BLOCK - 1)

    def place(row, piece):
        return (row // piece_rows) * step_rows + piece * piece_rows + (row & (piece_rows - 1))

    return [place(key, index ^ k) <= place(query, index) for k in range(pieces)]


def heads_beside(block, first, count):
    return jnp.concatenate(
        [block[h * HD : (h + 1) * HD, first : first + count] for h in range(GROUP)], axis=1
    )


def mask_tail(values, mask, first):
    tail = jnp.where(mask, values[first:], 0.0)
    if first == 0:
        return tail
    return jnp.concatenate([values[:first], tail], axis=0)


def attend_kernel(index_ref, q_ref, k_ref, v_ref, out_ref, lse_ref, *, pieces, piece_rows, step_rows):
    rows = q_ref.shape[1]
    masks = block_masks(index_ref[0], pieces, piece_rows, step_rows)
    queries = q_ref[...]
    for first in range(0, rows, BLOCK):
        count = first + BLOCK
        query_block = heads_beside(queries, first, BLOCK)
        total = None
        result = None
        for k in range(pieces):
            spot = pl.ds(k * rows, count)
            scores = dot(k_ref[:, spot], query_block, 0, 0)
            weights = mask_tail(jnp.exp2(scores * (SCALE * LOG2E)), masks[k], first)
            part = jnp.sum(weights, axis=0, keepdims=True)
            value = dot(v_ref[:, spot], weights.astype(BF16), 1, 0)
            total = part if total is None else total + part
            result = value if result is None else result + value
        result = result * (1.0 / total)
        log_total = jnp.log2(total)
        for h in range(GROUP):
            columns = slice(h * BLOCK, (h + 1) * BLOCK)
            out_ref[h * HD : (h + 1) * HD, first : first + BLOCK] = result[:, columns].astype(BF16)
            lse_ref[0, h : h + 1, first : first + BLOCK] = log_total[:, columns]


def attend_back_kernel(
    index_ref, q_ref, k_ref, v_ref, out_ref, lse_ref, grad_ref, dq_ref, dk_ref, dv_ref,
    *, pieces, piece_rows, step_rows
):
    rows = q_ref.shape[1]
    masks = block_masks(index_ref[0], pieces, piece_rows, step_rows)
    queries = q_ref[...]
    grads = grad_ref[...]
    results = out_ref[...]
    dk_ref[...] = jnp.zeros_like(dk_ref)
    dv_ref[...] = jnp.zeros_like(dv_ref)
    for first in range(0, rows, BLOCK):
        count = first + BLOCK
        query_block = heads_beside(queries, first, BLOCK)
        grad_block = heads_beside(grads, first, BLOCK)
        result_block = heads_beside(results, first, BLOCK)
        centre = jnp.sum(
            grad_block.astype(F32) * result_block.astype(F32), axis=0, keepdims=True
        )
        log_total = jnp.concatenate(
            [lse_ref[0, h : h + 1, first : first + BLOCK] for h in range(GROUP)], axis=1
        )
        dq = None
        for k in range(pieces):
            spot = pl.ds(k * rows, count)
            keys = k_ref[:, spot]
            scores = dot(keys, query_block, 0, 0)
            weights = mask_tail(
                jnp.exp2(scores * (SCALE * LOG2E) - log_total), masks[k], first
            )
            grad_weights = dot(v_ref[:, spot], grad_block, 0, 0)
            grad_scores = (weights * (grad_weights - centre)).astype(BF16)
            part = dot(keys, grad_scores, 1, 0)
            dq = part if dq is None else dq + part
            dk_ref[:, spot] += dot(query_block, grad_scores, 1, 1) * SCALE
            dv_ref[:, spot] += dot(grad_block, weights.astype(BF16), 1, 1)
        dq = (dq * SCALE).astype(BF16)
        for h in range(GROUP):
            columns = slice(h * BLOCK, (h + 1) * BLOCK)
            dq_ref[h * HD : (h + 1) * HD, first : first + BLOCK] = dq[:, columns]


def attention_specs(rows, total_rows):
    group_spec = pl.BlockSpec((GROUP * HD, rows), lambda i: (i, 0))
    pair_spec = pl.BlockSpec((HD, total_rows), lambda i: (i, 0))
    lse_spec = pl.BlockSpec((1, GROUP, rows), lambda i: (i, 0, 0))
    return group_spec, pair_spec, lse_spec


def attend(index, queries, keys, values, pieces, piece_rows, step_rows):
    rows, total_rows = queries.shape[1], keys.shape[1]
    group_spec, pair_spec, lse_spec = attention_specs(rows, total_rows)
    return pl.pallas_call(
        functools.partial(
            attend_kernel, pieces=pieces, piece_rows=piece_rows, step_rows=step_rows
        ),
        grid=(KVH,),
        in_specs=[pl.BlockSpec(memory_space=pltpu.SMEM), group_spec, pair_spec, pair_spec],
        out_specs=[group_spec, lse_spec],
        out_shape=[
            jax.ShapeDtypeStruct((HQ * HD, rows), BF16),
            jax.ShapeDtypeStruct((KVH, GROUP, rows), F32),
        ],
        compiler_params=pltpu.CompilerParams(vmem_limit_bytes=VMEM_LIMIT),
        cost_estimate=pl.CostEstimate(
            flops=4 * HQ * HD * rows * total_rows,
            bytes_accessed=8 * HQ * HD * rows,
            transcendentals=HQ * rows * total_rows,
        ),
        name="attend",
    )(index, queries, keys, values)


def attend_back(index, queries, keys, values, results, lse, grads, pieces, piece_rows, step_rows):
    rows, total_rows = queries.shape[1], keys.shape[1]
    group_spec, pair_spec, lse_spec = attention_specs(rows, total_rows)
    return pl.pallas_call(
        functools.partial(
            attend_back_kernel, pieces=pieces, piece_rows=piece_rows, step_rows=step_rows
        ),
        grid=(KVH,),
        in_specs=[
            pl.BlockSpec(memory_space=pltpu.SMEM),
            group_spec,
            pair_spec,
            pair_spec,
            group_spec,
            lse_spec,
            group_spec,
        ],
        out_specs=[group_spec, pair_spec, pair_spec],
        out_shape=[
            jax.ShapeDtypeStruct((HQ * HD, rows), BF16),
            jax.ShapeDtypeStruct((KVH * HD, total_rows), F32),
            jax.ShapeDtypeStruct((KVH * HD, total_rows), F32),
        ],
        compiler_params=pltpu.CompilerParams(vmem_limit_bytes=VMEM_LIMIT),
        cost_estimate=pl.CostEstimate(
            flops=10 * HQ * HD * rows * total_rows,
            bytes_accessed=16 * HQ * HD * rows,
            transcendentals=HQ * rows * total_rows,
        ),
        name="attend_back",
    )(index, queries, keys, values, results, lse, grads)


def hidden_kernel(
    me_ref,
    own_x_ref,
    own_c_ref,
    other_x_ref,
    other_c_ref,
    weight_ref,
    down_ref,
    *refs,
    handed,
):
    refs = refs[handed:]
    out_ref, hidden_t_ref, grads_t_ref, all_x_ref, all_c_ref, own_grad_ref, other_grad_ref = refs[:7]
    hidden_ref, grads_ref = refs[7:]
    units = down_ref.shape[0]
    half = units // HALVES
    depth = down_ref.shape[1]
    column = min(512, depth)

    def work(x_ref, c_ref, grad_ref):
        x = x_ref[...]
        c = c_ref[...]
        all_x_ref[...] = x
        all_c_ref[...] = c
        for h in range(HALVES):
            part = slice(h * half, (h + 1) * half)
            up_part = slice(units + h * half, units + (h + 1) * half)
            gate = dot(x, weight_ref[:, part], 1, 0)
            up = dot(x, weight_ref[:, up_part], 1, 0)
            grad_hidden = dot(c, down_ref[part, :], 1, 1)
            sigmoid = 0.5 * jnp.tanh(0.5 * gate) + 0.5
            silu = gate * sigmoid
            hidden = (silu * up).astype(BF16)
            grad_up = (grad_hidden * silu).astype(BF16)
            grad_gate = (grad_hidden * up * (sigmoid + silu * (1.0 - sigmoid))).astype(BF16)
            hidden_ref[:, part] = hidden
            grads_ref[:, part] = grad_gate
            grads_ref[:, up_part] = grad_up
            hidden_t_ref[part, :] = hidden.T
            grads_t_ref[part, :] = grad_gate.T
            grads_t_ref[up_part, :] = grad_up.T
        for first in range(0, depth, column):
            columns = slice(first, first + column)
            out_ref[:, columns] = dot(hidden_ref[...], down_ref[:, columns], 1, 0).astype(BF16)
            grad_ref[:, columns] = dot(grads_ref[...], weight_ref[columns, :], 1, 1).astype(BF16)

    pl.when(pl.program_id(0) == 0)(lambda: work(own_x_ref, own_c_ref, own_grad_ref))
    pl.when(pl.program_id(0) == 1)(lambda: work(other_x_ref, other_c_ref, other_grad_ref))


def hidden_step(n, me, count, rows, pieces, weights, w_down, so_far):
    depth = w_down.shape[1]
    units = w_down.shape[0]
    once = pl.Buffered(1)
    read = [
        pl.BlockSpec((rows, depth), lambda i, me_ref, block=block: (block, 0), pipeline_mode=once)
        for _, block in pieces
    ]
    row_block = pl.BlockSpec((rows, depth), lambda i, me_ref: (2 * n + i, 0))
    part = pl.BlockSpec((rows, depth), lambda i, me_ref: (0, 0))
    shapes = [(count, depth), (units, count), (2 * units, count), (count, depth), (count, depth)]
    shapes += [(rows, depth)] * 2
    return pl.pallas_call(
        functools.partial(hidden_kernel, handed=len(so_far)),
        grid_spec=pltpu.PrefetchScalarGridSpec(
            num_scalar_prefetch=1,
            grid=(2,),
            in_specs=read
            + [
                pl.BlockSpec((depth, 2 * units), lambda i, me_ref: (0, 0), pipeline_mode=once),
                pl.BlockSpec((units, depth), lambda i, me_ref: (0, 0), pipeline_mode=once),
            ]
            + [pl.BlockSpec(memory_space=pl.ANY)] * len(so_far),
            out_specs=[
                pl.BlockSpec((rows, depth), lambda i, me_ref: (me_ref[0] ^ (2 * n + i), 0)),
                pl.BlockSpec((units, rows), lambda i, me_ref: (0, 2 * n + i)),
                pl.BlockSpec((2 * units, rows), lambda i, me_ref: (0, 2 * n + i)),
                row_block,
                row_block,
                part,
                part,
            ],
            scratch_shapes=[
                pltpu.VMEM((rows, units), BF16),
                pltpu.VMEM((rows, 2 * units), BF16),
            ],
        ),
        out_shape=[jax.ShapeDtypeStruct(shape, BF16) for shape in shapes],
        input_output_aliases={7 + k: k for k in range(len(so_far))},
        compiler_params=pltpu.CompilerParams(vmem_limit_bytes=VMEM_LIMIT),
        cost_estimate=pl.CostEstimate(
            flops=24 * rows * depth * units,
            bytes_accessed=24 * rows * depth + 12 * rows * units + 6 * depth * units,
            transcendentals=2 * rows * units,
        ),
        name="hidden_step",
    )(me, *[array for array, _ in pieces], weights, w_down, *so_far)


def weight_kernel(left_ref, right_ref, *result_refs, parts):
    total = dot(left_ref[...], right_ref[...], 1, 0)
    half = total.shape[0] // HALVES
    for h, result_ref in enumerate(result_refs):
        piece = total[h * half : (h + 1) * half]
        if parts == 0:
            result_ref[0] = piece.astype(BF16)
            continue
        wide = piece.shape[1] // parts
        for p in range(parts):
            result_ref[p] = piece[:, p * wide : (p + 1) * wide].astype(BF16).T


def weight_product(left, right, first, units, wide, name):
    depth = left.shape[1]
    half = units // HALVES
    column = min(512, D)
    parts = column // wide if wide else 0
    block = first // units
    if wide:
        out_spec = pl.BlockSpec((parts, wide, half), lambda j: (j, 0, 0))
        out_shape = jax.ShapeDtypeStruct((D // wide, wide, half), BF16)
    else:
        out_spec = pl.BlockSpec((1, half, column), lambda j: (j, 0, 0))
        out_shape = jax.ShapeDtypeStruct((D // column, half, column), BF16)
    return pl.pallas_call(
        functools.partial(weight_kernel, parts=parts),
        grid=(D // column,),
        in_specs=[
            pl.BlockSpec((units, depth), lambda j: (block, 0), pipeline_mode=pl.Buffered(1)),
            pl.BlockSpec((depth, column), lambda j: (0, j)),
        ],
        out_specs=[out_spec] * HALVES,
        out_shape=[out_shape] * HALVES,
        compiler_params=pltpu.CompilerParams(vmem_limit_bytes=VMEM_LIMIT),
        cost_estimate=pl.CostEstimate(
            flops=2 * units * depth * D,
            bytes_accessed=2 * depth * (units + D) + 2 * units * D,
            transcendentals=0,
        ),
        name=name,
    )(left, right)


def merge_kernel(even_ref, *refs):
    result_ref = refs[-1]
    piece = result_ref.shape[1] // (2 * SWAPS)
    for h in range(SWAPS):
        mine, theirs = refs[h][...], refs[SWAPS + h][...]
        gate = jnp.where(even_ref[0] > 0, mine, theirs)
        up = jnp.where(even_ref[0] > 0, theirs, mine)
        result_ref[:, h * piece : (h + 1) * piece] = gate
        result_ref[:, (SWAPS + h) * piece : (SWAPS + h + 1) * piece] = up


def merge_columns(even, mine, theirs):
    rows, piece = mine[0].shape
    tile = min(256, rows)
    return pl.pallas_call(
        merge_kernel,
        grid=(rows // tile,),
        in_specs=[pl.BlockSpec(memory_space=pltpu.SMEM)]
        + [pl.BlockSpec((tile, piece), lambda i: (i, 0))] * (2 * SWAPS),
        out_specs=pl.BlockSpec((tile, 2 * SWAPS * piece), lambda i: (i, 0)),
        out_shape=jax.ShapeDtypeStruct((rows, 2 * SWAPS * piece), BF16),
        compiler_params=pltpu.CompilerParams(vmem_limit_bytes=VMEM_LIMIT),
        cost_estimate=pl.CostEstimate(
            flops=0, bytes_accessed=8 * rows * SWAPS * piece, transcendentals=0
        ),
        name="merge_columns",
    )(even.astype(jnp.int32).reshape(1), *mine, *theirs)


def pack_kernel(even_ref, first_ref, second_ref, result_ref):
    chosen = jnp.where(even_ref[0] > 0, first_ref[...], second_ref[...])
    width = result_ref.shape[-1]
    for h in range(SWAPS):
        result_ref[0, h] = chosen[:, h * width : (h + 1) * width]


def pack_columns(even, first, second, parts):
    rows, columns = first.shape
    width = columns // parts
    block = pl.BlockSpec((rows, width), lambda i: (0, i))
    piece = width // SWAPS
    return pl.pallas_call(
        pack_kernel,
        grid=(parts,),
        in_specs=[pl.BlockSpec(memory_space=pltpu.SMEM), block, block],
        out_specs=pl.BlockSpec((1, SWAPS, rows, piece), lambda i: (i, 0, 0, 0)),
        out_shape=jax.ShapeDtypeStruct((parts, SWAPS, rows, piece), BF16),
        compiler_params=pltpu.CompilerParams(vmem_limit_bytes=VMEM_LIMIT),
        cost_estimate=pl.CostEstimate(
            flops=0, bytes_accessed=6 * rows * columns, transcendentals=0
        ),
        name="pack_columns",
    )(even.astype(jnp.int32).reshape(1), first, second)


def unpack_kernel(stacked_ref, result_ref):
    width = stacked_ref.shape[-1]
    for h in range(HALVES):
        result_ref[:, h * width : (h + 1) * width] = stacked_ref[0, h].astype(F32)


def unpack_columns(stacked):
    parts, _, rows, half = stacked.shape
    return pl.pallas_call(
        unpack_kernel,
        grid=(parts,),
        in_specs=[pl.BlockSpec((1, HALVES, rows, half), lambda i: (i, 0, 0, 0))],
        out_specs=pl.BlockSpec((rows, HALVES * half), lambda i: (0, i)),
        out_shape=jax.ShapeDtypeStruct((rows, parts * HALVES * half), F32),
        compiler_params=pltpu.CompilerParams(vmem_limit_bytes=VMEM_LIMIT),
        cost_estimate=pl.CostEstimate(
            flops=0, bytes_accessed=6 * parts * rows * HALVES * half, transcendentals=0
        ),
        name="unpack_columns",
    )(stacked)


def unpack_rows_kernel(*refs):
    result_ref = refs[-1]
    height = refs[0].shape[1]
    for h in range(HALVES):
        result_ref[h * height : (h + 1) * height, :] = refs[h][0].astype(F32)


def unpack_rows(pieces):
    blocks, half, column = pieces[0].shape
    return pl.pallas_call(
        unpack_rows_kernel,
        grid=(blocks,),
        in_specs=[pl.BlockSpec((1, half, column), lambda i: (i, 0, 0))] * HALVES,
        out_specs=pl.BlockSpec((HALVES * half, column), lambda i: (0, i)),
        out_shape=jax.ShapeDtypeStruct((HALVES * half, blocks * column), F32),
        compiler_params=pltpu.CompilerParams(vmem_limit_bytes=VMEM_LIMIT),
        cost_estimate=pl.CostEstimate(
            flops=0, bytes_accessed=6 * blocks * HALVES * half * column, transcendentals=0
        ),
        name="unpack_rows",
    )(*pieces)


class Layout:
    def __init__(self, fsdp_devices, seq_devices, rows_dev):
        self.fsdp = fsdp_devices
        self.seq = seq_devices
        self.chips = fsdp_devices // 2
        self.share = 2 * seq_devices // (2 * MICRO)
        self.near = self.share // 2
        self.piece_rows = rows_dev // self.share
        self.step_rows = rows_dev
        self.rows = LENGTH // self.share

    def flat(self, f, z):
        return f * self.seq + z

    def moved(self, r):
        pairs = []
        for f in range(self.fsdp):
            for z in range(self.seq):
                slot = z ^ r
                micro, j = slot // self.share, slot % self.share
                target_f = (f // 2) * 2 + j % 2
                target_z = (2 * micro + f % 2) * self.near + j // 2
                pairs.append((self.flat(f, z), self.flat(target_f, target_z)))
        return pairs

    def other(self, k):
        return [
            (self.flat(f, z), self.flat(f ^ k, z))
            for f in range(self.fsdp)
            for z in range(self.seq)
        ]

    def across(self, k):
        pairs = []
        for f in range(self.fsdp):
            for z in range(self.seq):
                pairs.append((self.flat(f, z), self.flat(f ^ (k & 1), z ^ (k >> 1))))
        return pairs


def permute(value, pairs):
    return lax.ppermute(value, ("fsdp", "seq"), pairs)


def scatter_rows(layout, values, z, slot):
    parts = values.reshape(layout.seq, layout.piece_rows, values.shape[-1])
    result = jnp.zeros_like(parts)
    for r in range(layout.seq):
        sent = lax.dynamic_index_in_dim(parts, z ^ r, 0, keepdims=False)
        got = permute(sent, layout.moved(r))
        result = lax.dynamic_update_index_in_dim(result, got, slot ^ r, 0)
    return result.reshape(layout.rows, values.shape[-1])


def return_rows(layout, values, f):
    width = values.shape[-1]
    parts = values.reshape(layout.seq, layout.piece_rows, width)
    parts = lax.all_to_all(parts, "seq", split_axis=0, concat_axis=0, tiled=True)
    parts = parts.reshape(MICRO, 2, layout.near, layout.piece_rows, width)
    core = f % 2
    kept = lax.dynamic_index_in_dim(parts, core, 1, keepdims=False)
    sent = lax.dynamic_index_in_dim(parts, 1 - core, 1, keepdims=False)
    got = permute(sent, layout.other(1))
    both = jnp.stack(
        [jnp.where(core == 0, kept, got), jnp.where(core == 0, got, kept)], axis=2
    )
    return both.reshape(MICRO, layout.step_rows, width)


class RowGather:
    def __init__(self, layout, own):
        self.layout = layout
        self.own = {0: own}
        self.sibling = {0: self.move(own, 1)}
        chips = layout.chips
        for n in range(1, 3 if chips == 4 else chips):
            self.own[n] = self.move(own, 2 * n)

    def move(self, value, k):
        return permute(value, self.layout.other(k))

    def after(self, n, *values):
        chips = self.layout.chips
        if n + 1 < chips:
            waiting = {m: value for m, value in self.own.items() if m > n}
            siblings = {m: value for m, value in self.sibling.items() if m > n}
            waiting, siblings, values = lax.optimization_barrier((waiting, siblings, values))
            self.own.update(waiting)
            self.sibling.update(siblings)
            if chips == 4 and n == 0:
                cut = self.own[0].shape[0] // 2
                self.far = [self.move(self.own[2][:cut], 2), self.move(self.own[1][cut:], 4)]
            if chips == 4 and n == 1:
                self.far = lax.optimization_barrier((self.far, values))[0]
                self.own[3] = jnp.concatenate(self.far)
            for m in (n + 1, n + 2):
                if m in self.own and m not in self.sibling:
                    self.sibling[m] = self.move(self.own[m], 1)
        return values


def gather_small(layout, f, own):
    held = own[None]
    k = 1
    while k < layout.fsdp:
        got = permute(held, layout.other(k))
        upper = (f & k) > 0
        held = jnp.concatenate(
            [jnp.where(upper, got, held), jnp.where(upper, held, got)], axis=0
        )
        k *= 2
    return held


def sum_small(layout, value):
    k = 1
    while k < layout.fsdp:
        value = value + permute(value, layout.other(k))
        k *= 2
    return value


class LinePipe:
    def __init__(self, z, seq_devices):
        self.seq = seq_devices
        self.z = z
        self.outer = (z == 0) | (z == seq_devices - 1)
        self.flying = []
        self.results = {}

    def send(self, stage, value):
        half, last = self.seq // 2, self.seq - 1
        if stage < half - 1:
            pairs = [(stage, stage + 1), (last - stage, last - stage - 1)]
        elif stage == half - 1:
            pairs = [(half - 1, half), (half, half - 1)]
        else:
            s = last - 1 - stage
            pairs = [(s + 1, s), (last - s - 1, last - s)]
        return lax.ppermute(value, "seq", pairs)

    def join(self, stage, value, got):
        if stage < self.seq // 2:
            return value + got
        s = self.seq - 2 - stage
        return jnp.where((self.z == s) | (self.z == self.seq - 1 - s), got, value)

    def step(self, name=None, value=None, others=()):
        arrived = [entry[3] for entry in self.flying]
        arrived, self.results, value, others = lax.optimization_barrier(
            (arrived, self.results, value, others)
        )
        flying = []
        if name is not None:
            flying.append((name, 0, value, self.send(0, value)))
        for (key, stage, held, _), got in zip(self.flying, arrived):
            if stage == self.seq - 2:
                self.results[key] = jnp.where(self.outer, got, held)
                continue
            held = self.join(stage, held, got)
            flying.append((key, stage + 1, held, self.send(stage + 1, held)))
        self.flying = flying
        return others


class PairPipe:
    def __init__(self, z):
        self.outer = (z == 0) | (z == 3)
        self.entered = self.halved = self.summed = None
        self.side = self.across = None
        self.results = {}

    @property
    def flying(self):
        return self.entered or self.halved or self.summed

    def step(self, name=None, value=None, others=()):
        side, across, self.results, value, others = lax.optimization_barrier(
            (self.side, self.across, self.results, value, others)
        )
        entered, halved, summed = self.entered, self.halved, self.summed
        total = halved[1] + across if halved else None
        inward, outward = [(0, 1), (3, 2)], [(1, 0), (2, 3)]
        self.side = self.across = None
        self.entered = self.halved = self.summed = None
        sent = value if total is None else total
        pairs = inward if total is None else outward
        if value is not None and total is not None:
            sent = jnp.where(self.outer, value, total)
            pairs = inward + outward
        if sent is not None:
            self.side = lax.ppermute(sent, "seq", pairs)
        if entered:
            joined = entered[1] + side
            self.across = lax.ppermute(joined, "seq", [(1, 2), (2, 1)])
            self.halved = (entered[0], joined)
        if summed:
            self.results[summed[0]] = jnp.where(self.outer, side, summed[1])
        if halved:
            self.summed = (halved[0], sent)
        if name is not None:
            self.entered = (name, value)
        return others


def body(
    tokens,
    cotangent,
    attn_gain,
    query_gain,
    key_gain,
    w_query,
    w_key,
    w_value,
    w_out,
    ffn_gain,
    w_gate,
    w_up,
    w_down,
):
    fsdp_devices = lax.axis_size("fsdp")
    seq_devices = lax.axis_size("seq")
    layout = Layout(fsdp_devices, seq_devices, tokens.shape[2])
    f = lax.axis_index("fsdp")
    z = lax.axis_index("seq")
    rows = layout.rows
    share = layout.share
    member = (z % layout.near) * 2 + f % 2
    slot = (z // layout.near // 2) * share + member

    w_attn = lax.all_gather(
        jnp.concatenate([w_query, w_key, w_value], axis=1), "fsdp", axis=0, tiled=True
    )
    gains = gather_small(
        layout, f, jnp.concatenate([attn_gain, ffn_gain, query_gain, key_gain])
    ).astype(F32)
    wide, narrow = attn_gain.shape[0], query_gain.shape[0]
    even = z % 2 == 0
    hidden_dev = w_down.shape[0]
    gains, gate_rows, up_rows = lax.optimization_barrier((gains, w_gate, w_up))
    fetched = lax.all_to_all(
        pack_columns(even, gate_rows, up_rows, fsdp_devices),
        "fsdp",
        split_axis=0,
        concat_axis=0,
        tiled=True,
    )
    full_attn_gain = gains[:, :wide].reshape(D)
    full_ffn_gain = gains[:, wide : 2 * wide].reshape(D)
    full_query_gain = gains[:, 2 * wide : 2 * wide + narrow].reshape(HD)
    full_key_gain = gains[:, 2 * wide + narrow :].reshape(HD)
    inputs_low = scatter_rows(layout, tokens[:, 0], z, slot)
    grad_out_low = scatter_rows(layout, cotangent[:, 0], z, slot)
    full_out = lax.all_gather(w_out, "fsdp", axis=0, tiled=True)

    row = jnp.arange(rows, dtype=jnp.int32)
    position = (
        (row // layout.piece_rows) * layout.step_rows
        + member * layout.piece_rows
        + row % layout.piece_rows
    ).astype(F32)
    frequency = THETA ** (-(jnp.arange(HD // 2).astype(F32) * 2.0 / HD))
    angles = frequency[:, None] * position[None, :]
    cosine_table, sine_table = jnp.cos(angles)[None], jnp.sin(angles)[None]
    head_gains = jnp.concatenate(
        [
            jnp.broadcast_to(full_query_gain[None, :, None], (HQ, HD, 1)),
            jnp.broadcast_to(full_key_gain[None, :, None], (KVH, HD, 1)),
        ]
    )

    inputs = inputs_low.astype(F32)
    normed, normed_unit, normed_inverse = rms_fwd(inputs, full_attn_gain)
    fetched = [fetched[:, h].reshape(D, hidden_dev // SWAPS) for h in range(SWAPS)]
    swapped = [
        lax.ppermute(piece, "seq", [(i, i ^ 1) for i in range(seq_devices)]) for piece in fetched
    ]
    normed_low, grad_out_low, w_attn = lax.optimization_barrier(
        (normed.astype(BF16), grad_out_low, w_attn)
    )
    grad_out_gather = RowGather(layout, grad_out_low)
    raw = dot(w_attn, normed_low, 0, 1)
    normed_all = lax.all_gather(
        lax.optimization_barrier((normed_low, full_out))[0], "seq", axis=0, tiled=True
    )
    pair_width = KVH * HD
    turned = HQ + KVH
    head_raw = raw[: turned * HD].reshape(turned, HD, rows)
    head_normed, head_unit, head_inverse = head_rms_fwd(head_raw, head_gains)
    heads_low = rotate(head_normed, cosine_table, sine_table).astype(BF16).reshape(turned * HD, rows)
    queries = heads_low[: HQ * HD]
    own_pair = jnp.concatenate([heads_low[HQ * HD :], raw[turned * HD :].astype(BF16)], axis=0)
    pair_pieces = [own_pair] + [permute(own_pair, layout.across(k)) for k in range(1, share)]
    keys = jnp.concatenate([piece[:pair_width] for piece in pair_pieces], axis=1)
    values = jnp.concatenate([piece[pair_width:] for piece in pair_pieces], axis=1)
    index = member.astype(jnp.int32).reshape(1)
    attended, log_totals = attend(
        index, queries, keys, values, share, layout.piece_rows, layout.step_rows
    )
    attended, swapped[0], grad_out_gather.own = lax.optimization_barrier(
        (attended, swapped[0], grad_out_gather.own)
    )
    middle = inputs + dot(attended, full_out, 0, 0)
    ffn_normed, ffn_unit, ffn_inverse = rms_fwd(middle, full_ffn_gain)
    ffn_low = ffn_normed.astype(BF16)

    ffn_gather = RowGather(layout, ffn_low)
    line = PairPipe(z) if seq_devices == 4 else LinePipe(z, seq_devices)
    weights = merge_columns(even, fetched, swapped)
    worked = ()
    grad_ffn_parts = []
    me = f.astype(jnp.int32).reshape(1)
    for n in range(layout.chips):
        pieces = [
            (side[n], 0)
            for side in (
                ffn_gather.own,
                grad_out_gather.own,
                ffn_gather.sibling,
                grad_out_gather.sibling,
            )
        ]
        *worked, own_grad, other_grad = hidden_step(
            n, me, fsdp_devices * rows, rows, pieces, weights, w_down, worked
        )
        worked = ffn_gather.after(n, *worked)
        worked = grad_out_gather.after(n, *worked)
        if grad_ffn_parts:
            worked, grad_ffn_parts[-1] = lax.optimization_barrier((worked, grad_ffn_parts[-1]))
            if n > 1:
                grad_ffn_parts[-1] = permute(grad_ffn_parts[-1], layout.other(2 * n - 2))
        grad_ffn_parts.append(own_grad + permute(other_grad, layout.other(1)))
        if n == layout.chips - 2:
            worked, normed_all = lax.optimization_barrier((worked, normed_all))
    grad_ffn_parts[-1] = permute(grad_ffn_parts[-1], layout.other(2 * layout.chips - 2))
    out_part, hidden_t, grads_t, ffn_rows, grad_out_rows = worked
    out_sum = lax.psum_scatter(out_part, "fsdp", scatter_dimension=0, tiled=True)

    waiting = {}
    finished = {}
    names = {}
    tied = []

    def to_owners(name):
        terms = [
            line.results[f"{name}{h}"].reshape(fsdp_devices, wide, -1) for h in range(HALVES)
        ]
        return lax.all_to_all(
            jnp.stack(terms, axis=1), "fsdp", split_axis=0, concat_axis=0, tiled=True
        )

    def advance(name=None, value=None, others=()):
        if name is not None:
            names[name] = value.shape
            value = value.reshape(-1, value.shape[-1])
        ties = {key: finished[key] for key in tied}
        ties, others = line.step(name, value, (ties, others))
        finished.update(ties)
        tied.clear()
        for key in ("gate", "up"):
            if key not in finished and all(f"{key}{h}" in line.results for h in range(HALVES)):
                waiting.setdefault(key, functools.partial(to_owners, key))
        if waiting:
            key = next(iter(waiting))
            finished[key] = waiting.pop(key)()
            tied.append(key)
        return others

    gate_term = weight_product(grads_t, ffn_rows, 0, hidden_dev, wide, "w_gate_grad")
    grads_t, grad_ffn_parts[:-1] = advance(
        "gate0", gate_term[0], (grads_t, grad_ffn_parts[:-1])
    )
    up_term = weight_product(grads_t, ffn_rows, hidden_dev, hidden_dev, wide, "w_up_grad")
    up_term, grad_ffn_parts = lax.optimization_barrier((up_term, grad_ffn_parts))
    grad_ffn_normed = sum(part.astype(F32) for part in grad_ffn_parts)

    grad_middle_norm, ffn_gain_term = rms_back(
        grad_ffn_normed, ffn_unit, ffn_inverse, full_ffn_gain
    )
    grad_middle = grad_out_low.astype(F32) + grad_middle_norm
    grad_branch_low = grad_middle.astype(BF16)
    (grad_branch_low,) = advance("gate1", gate_term[1], (grad_branch_low,))
    grad_attended = dot(full_out, grad_branch_low, 1, 1).astype(BF16)
    grad_queries, grad_keys, grad_values = attend_back(
        index,
        queries,
        keys,
        values,
        attended,
        log_totals,
        grad_attended,
        share,
        layout.piece_rows,
        layout.step_rows,
    )
    grad_queries, grad_keys, grad_values, grad_branch_low = advance(
        "up0", up_term[0], (grad_queries, grad_keys, grad_values, grad_branch_low)
    )
    grad_pair = jnp.concatenate([grad_keys[:, :rows], grad_values[:, :rows]], axis=0)
    for k in range(1, share):
        columns = slice(k * rows, (k + 1) * rows)
        sent = jnp.concatenate([grad_keys[:, columns], grad_values[:, columns]], axis=0)
        grad_pair = grad_pair + permute(sent.astype(BF16), layout.across(k)).astype(F32)
    grad_pair_low = grad_pair.astype(BF16)
    grad_turned = (
        jnp.concatenate([grad_queries, grad_pair_low[:pair_width]], axis=0)
        .astype(F32)
        .reshape(turned, HD, rows)
    )
    grad_head_normed = rotate(grad_turned, cosine_table, -sine_table)
    scaled = grad_head_normed * head_gains
    grad_head_raw = head_inverse * (
        scaled - head_unit * jnp.mean(scaled * head_unit, axis=1, keepdims=True)
    )
    head_gain_terms = jnp.sum(grad_head_normed * head_unit, axis=2)
    grad_raw = jnp.concatenate(
        [grad_head_raw.astype(BF16).reshape(turned * HD, rows), grad_pair_low[pair_width:]], axis=0
    )
    raw_share = grad_raw.shape[0] // seq_devices
    raw_all = lax.all_to_all(
        grad_raw.reshape(seq_devices, raw_share, rows), "seq", split_axis=0, concat_axis=0, tiled=True
    )
    out_term = dot(attended, grad_branch_low, 1, 0).astype(BF16)
    out_rows = lax.psum_scatter(out_term, "fsdp", scatter_dimension=0, tiled=True)
    down_term = weight_product(hidden_t, grad_out_rows, 0, hidden_dev, 0, "w_down_grad")
    down_term, raw_all, grad_raw, out_sum = advance(
        "up1", up_term[1], (down_term, raw_all, grad_raw, out_sum)
    )
    projection_term = lax.dot_general(
        normed_all.reshape(seq_devices, rows, D),
        raw_all,
        (((0, 1), (0, 2)), ((), ())),
        preferred_element_type=F32,
    ).astype(BF16)
    projection_rows = lax.psum_scatter(
        projection_term, "fsdp", scatter_dimension=0, tiled=True
    )
    waiting["block_out"] = lambda: return_rows(
        layout, (middle + out_sum.astype(F32)).astype(BF16), f
    )
    grad_normed = dot(grad_raw, w_attn, 0, 1)
    grad_input_norm, attn_gain_term = rms_back(
        grad_normed, normed_unit, normed_inverse, full_attn_gain
    )

    tokens_grad_low = (grad_middle + grad_input_norm).astype(BF16)
    gain_terms = sum_small(
        layout,
        jnp.concatenate(
            [
                attn_gain_term,
                ffn_gain_term,
                jnp.sum(head_gain_terms[:HQ], axis=0),
                jnp.sum(head_gain_terms[HQ:], axis=0),
            ]
        )[None],
    )[0]

    def own_share(first, count):
        share_of = count // fsdp_devices
        vector = lax.dynamic_slice_in_dim(gain_terms, first + f * share_of, share_of, 0)
        return jnp.pad(vector, (0, wide - share_of))

    gain_columns = jnp.stack(
        [own_share(0, D), own_share(D, D), own_share(2 * D, HD), own_share(2 * D + HD, HD)],
        axis=1,
    )
    gain_columns = jnp.pad(gain_columns, ((0, 0), (0, 128 - gain_columns.shape[1]))).astype(BF16)

    tokens_grad_low, projection_rows = advance(
        "down0", down_term[0], (tokens_grad_low, projection_rows)
    )
    waiting["tokens_grad"] = lambda: return_rows(layout, tokens_grad_low, f)
    attn_rows = lax.all_gather(projection_rows, "seq", axis=0, tiled=True)
    out_rows, attn_rows = lax.optimization_barrier((out_rows, attn_rows))
    out_rows = lax.psum(jnp.concatenate([out_rows, gain_columns], axis=1), "seq")
    advance("down1", down_term[1])
    while line.flying or waiting:
        advance()

    w_gate_grad = unpack_columns(finished["gate"])
    w_up_grad = unpack_columns(finished["up"])
    w_down_grad = unpack_rows(
        [line.results[f"down{h}"].reshape(names[f"down{h}"]) for h in range(HALVES)]
    )
    block_out, tokens_grad = finished["block_out"], finished["tokens_grad"]
    attn_rows = (
        attn_rows.reshape(seq_devices, wide, raw_share)
        .transpose(1, 0, 2)
        .reshape(wide, seq_devices * raw_share)
        .astype(F32)
    )
    out_rows = out_rows.astype(F32)
    w_out_grad, gain_rows = out_rows[:, :D], out_rows[:, D:]
    query_width = HQ * HD

    return (
        block_out[:, None],
        tokens_grad[:, None],
        gain_rows[:, 0],
        gain_rows[:narrow, 2],
        gain_rows[:narrow, 3],
        attn_rows[:, :query_width],
        attn_rows[:, query_width : query_width + pair_width],
        attn_rows[:, query_width + pair_width : query_width + 2 * pair_width],
        w_out_grad,
        gain_rows[:, 1],
        w_gate_grad,
        w_up_grad,
        w_down_grad,
    )


def solution(mesh):
    activations = P(None, "fsdp", "seq", None)
    vector = P("fsdp")
    matrix = P("fsdp", None)
    specs = (
        (activations, activations)
        + (vector,) * 3
        + (matrix,) * 4
        + (vector,)
        + (matrix,) * 3
    )
    return jax.shard_map(body, mesh=mesh, in_specs=specs, out_specs=specs, check_vma=False)
```

```python
import functools
import math

import jax
import jax.numpy as jnp
from jax import lax
from jax.experimental import pallas as pl
from jax.experimental.pallas import tpu as pltpu
from jax.sharding import PartitionSpec as P

D = 2048
HQ = 32
KVH = 8
HD = 64
FF = 8192
LENGTH = 1024
MICRO = 2
HALVES = 2
SWAPS = 2

EPSILON = 1e-05
THETA = 1000000.0
GROUP = HQ // KVH
BLOCK = 128
SCALE = 1.0 / math.sqrt(HD)
LOG2E = math.log2(math.e)
VMEM_LIMIT = 56 * 1024 * 1024

F32 = jnp.float32
BF16 = jnp.bfloat16


def dot(left_side, right_side, left_dim, right_dim):
    return lax.dot_general(
        left_side,
        right_side,
        (((left_dim,), (right_dim,)), ((), ())),
        preferred_element_type=F32,
    )


def rms_fwd(values, row_gain):
    inverse = lax.rsqrt(jnp.mean(values * values, axis=-1, keepdims=True) + EPSILON)
    unit_rows = values * inverse
    return (unit_rows * row_gain, unit_rows, inverse)


def rms_back(grad_outputs, unit_rows, inverse, row_gain):
    scaled = grad_outputs * row_gain
    grad_inputs = inverse * (
        scaled - unit_rows * jnp.mean(scaled * unit_rows, axis=-1, keepdims=True)
    )
    grad_gain = jnp.sum(grad_outputs * unit_rows, axis=0)
    return (grad_inputs, grad_gain)


def head_rms_fwd(values, gains):
    inverse = lax.rsqrt(jnp.mean(values * values, axis=1, keepdims=True) + EPSILON)
    unit = values * inverse
    return (unit * gains, unit, inverse)


def rotate(values, cosine_table, sine_table):
    half_width = values.shape[1] // 2
    front_half = values[:, :half_width]
    back_half = values[:, half_width:]
    return jnp.concatenate(
        [
            front_half * cosine_table - back_half * sine_table,
            back_half * cosine_table + front_half * sine_table,
        ],
        axis=1,
    )


def block_masks(index, pieces, piece_rows, step_rows):
    key = lax.broadcasted_iota(jnp.int32, (BLOCK, GROUP * BLOCK), 0)
    query = lax.broadcasted_iota(jnp.int32, (BLOCK, GROUP * BLOCK), 1) & (BLOCK - 1)

    def place(row, piece):
        return (row // piece_rows) * step_rows + piece * piece_rows + (row & (piece_rows - 1))

    return [place(key, index ^ k) <= place(query, index) for k in range(pieces)]


def heads_beside(block, first, count):
    return jnp.concatenate(
        [block[h * HD : (h + 1) * HD, first : first + count] for h in range(GROUP)], axis=1
    )


def mask_tail(values, mask, first):
    tail = jnp.where(mask, values[first:], 0.0)
    if first == 0:
        return tail
    return jnp.concatenate([values[:first], tail], axis=0)


def attend_kernel(index_ref, q_ref, k_ref, v_ref, out_ref, lse_ref, *, pieces, piece_rows, step_rows):
    rows = q_ref.shape[1]
    masks = block_masks(index_ref[0], pieces, piece_rows, step_rows)
    queries = q_ref[...]
    for first in range(0, rows, BLOCK):
        count = first + BLOCK
        query_block = heads_beside(queries, first, BLOCK)
        total = None
        result = None
        for k in range(pieces):
            spot = pl.ds(k * rows, count)
            scores = dot(k_ref[:, spot], query_block, 0, 0)
            weights = mask_tail(jnp.exp2(scores * (SCALE * LOG2E)), masks[k], first)
            part = jnp.sum(weights, axis=0, keepdims=True)
            value = dot(v_ref[:, spot], weights.astype(BF16), 1, 0)
            total = part if total is None else total + part
            result = value if result is None else result + value
        result = result * (1.0 / total)
        log_total = jnp.log2(total)
        for h in range(GROUP):
            columns = slice(h * BLOCK, (h + 1) * BLOCK)
            out_ref[h * HD : (h + 1) * HD, first : first + BLOCK] = result[:, columns].astype(BF16)
            lse_ref[0, h : h + 1, first : first + BLOCK] = log_total[:, columns]


def attend_back_kernel(
    index_ref, q_ref, k_ref, v_ref, out_ref, lse_ref, grad_ref, dq_ref, dk_ref, dv_ref,
    *, pieces, piece_rows, step_rows
):
    rows = q_ref.shape[1]
    masks = block_masks(index_ref[0], pieces, piece_rows, step_rows)
    queries = q_ref[...]
    grads = grad_ref[...]
    results = out_ref[...]
    dk_ref[...] = jnp.zeros_like(dk_ref)
    dv_ref[...] = jnp.zeros_like(dv_ref)
    for first in range(0, rows, BLOCK):
        count = first + BLOCK
        query_block = heads_beside(queries, first, BLOCK)
        grad_block = heads_beside(grads, first, BLOCK)
        result_block = heads_beside(results, first, BLOCK)
        centre = jnp.sum(
            grad_block.astype(F32) * result_block.astype(F32), axis=0, keepdims=True
        )
        log_total = jnp.concatenate(
            [lse_ref[0, h : h + 1, first : first + BLOCK] for h in range(GROUP)], axis=1
        )
        dq = None
        for k in range(pieces):
            spot = pl.ds(k * rows, count)
            keys = k_ref[:, spot]
            scores = dot(keys, query_block, 0, 0)
            weights = mask_tail(
                jnp.exp2(scores * (SCALE * LOG2E) - log_total), masks[k], first
            )
            grad_weights = dot(v_ref[:, spot], grad_block, 0, 0)
            grad_scores = (weights * (grad_weights - centre)).astype(BF16)
            part = dot(keys, grad_scores, 1, 0)
            dq = part if dq is None else dq + part
            dk_ref[:, spot] += dot(query_block, grad_scores, 1, 1) * SCALE
            dv_ref[:, spot] += dot(grad_block, weights.astype(BF16), 1, 1)
        dq = (dq * SCALE).astype(BF16)
        for h in range(GROUP):
            columns = slice(h * BLOCK, (h + 1) * BLOCK)
            dq_ref[h * HD : (h + 1) * HD, first : first + BLOCK] = dq[:, columns]


def attention_specs(rows, total_rows):
    group_spec = pl.BlockSpec((GROUP * HD, rows), lambda i: (i, 0))
    pair_spec = pl.BlockSpec((HD, total_rows), lambda i: (i, 0))
    lse_spec = pl.BlockSpec((1, GROUP, rows), lambda i: (i, 0, 0))
    return group_spec, pair_spec, lse_spec


def attend(index, queries, keys, values, pieces, piece_rows, step_rows):
    rows, total_rows = queries.shape[1], keys.shape[1]
    group_spec, pair_spec, lse_spec = attention_specs(rows, total_rows)
    return pl.pallas_call(
        functools.partial(
            attend_kernel, pieces=pieces, piece_rows=piece_rows, step_rows=step_rows
        ),
        grid=(KVH,),
        in_specs=[pl.BlockSpec(memory_space=pltpu.SMEM), group_spec, pair_spec, pair_spec],
        out_specs=[group_spec, lse_spec],
        out_shape=[
            jax.ShapeDtypeStruct((HQ * HD, rows), BF16),
            jax.ShapeDtypeStruct((KVH, GROUP, rows), F32),
        ],
        compiler_params=pltpu.CompilerParams(vmem_limit_bytes=VMEM_LIMIT),
        cost_estimate=pl.CostEstimate(
            flops=4 * HQ * HD * rows * total_rows,
            bytes_accessed=8 * HQ * HD * rows,
            transcendentals=HQ * rows * total_rows,
        ),
        name="attend",
    )(index, queries, keys, values)


def attend_back(index, queries, keys, values, results, lse, grads, pieces, piece_rows, step_rows):
    rows, total_rows = queries.shape[1], keys.shape[1]
    group_spec, pair_spec, lse_spec = attention_specs(rows, total_rows)
    return pl.pallas_call(
        functools.partial(
            attend_back_kernel, pieces=pieces, piece_rows=piece_rows, step_rows=step_rows
        ),
        grid=(KVH,),
        in_specs=[
            pl.BlockSpec(memory_space=pltpu.SMEM),
            group_spec,
            pair_spec,
            pair_spec,
            group_spec,
            lse_spec,
            group_spec,
        ],
        out_specs=[group_spec, pair_spec, pair_spec],
        out_shape=[
            jax.ShapeDtypeStruct((HQ * HD, rows), BF16),
            jax.ShapeDtypeStruct((KVH * HD, total_rows), F32),
            jax.ShapeDtypeStruct((KVH * HD, total_rows), F32),
        ],
        compiler_params=pltpu.CompilerParams(vmem_limit_bytes=VMEM_LIMIT),
        cost_estimate=pl.CostEstimate(
            flops=10 * HQ * HD * rows * total_rows,
            bytes_accessed=16 * HQ * HD * rows,
            transcendentals=HQ * rows * total_rows,
        ),
        name="attend_back",
    )(index, queries, keys, values, results, lse, grads)


def hidden_kernel(own_x_ref, own_c_ref, other_x_ref, other_c_ref, weight_ref, down_ref, *refs):
    hidden_ref, grads_ref, hidden_t_ref, grads_t_ref, all_x_ref, all_c_ref = refs[-6:]
    units = down_ref.shape[0]
    half = units // HALVES

    def work(x_ref, c_ref):
        x = x_ref[...]
        c = c_ref[...]
        all_x_ref[...] = x
        all_c_ref[...] = c
        for h in range(HALVES):
            part = slice(h * half, (h + 1) * half)
            up_part = slice(units + h * half, units + (h + 1) * half)
            gate = dot(x, weight_ref[:, part], 1, 0)
            up = dot(x, weight_ref[:, up_part], 1, 0)
            grad_hidden = dot(c, down_ref[part, :], 1, 1)
            sigmoid = 0.5 * jnp.tanh(0.5 * gate) + 0.5
            silu = gate * sigmoid
            hidden = (silu * up).astype(BF16)
            grad_up = (grad_hidden * silu).astype(BF16)
            grad_gate = (grad_hidden * up * (sigmoid + silu * (1.0 - sigmoid))).astype(BF16)
            hidden_ref[:, part] = hidden
            grads_ref[:, part] = grad_gate
            grads_ref[:, up_part] = grad_up
            hidden_t_ref[part, :] = hidden.T
            grads_t_ref[part, :] = grad_gate.T
            grads_t_ref[up_part, :] = grad_up.T

    pl.when(pl.program_id(0) == 0)(lambda: work(own_x_ref, own_c_ref))
    pl.when(pl.program_id(0) == 1)(lambda: work(other_x_ref, other_c_ref))


def hidden_step(n, count, rows, pieces, weights, w_down, so_far):
    depth = w_down.shape[1]
    units = w_down.shape[0]
    once = pl.Buffered(1)
    read = [
        pl.BlockSpec((rows, depth), lambda i, block=block: (block, 0), pipeline_mode=once)
        for _, block in pieces
    ]
    widths = (units, 2 * units)
    upright = [(count, width) for width in widths]
    turned = [(width, count) for width in widths]
    whole = [(count, depth)] * 2
    flops = 12 * rows * depth * units
    return pl.pallas_call(
        hidden_kernel,
        grid=(2,),
        in_specs=read
        + [
            pl.BlockSpec((depth, 2 * units), lambda i: (0, 0), pipeline_mode=once),
            pl.BlockSpec((units, depth), lambda i: (0, 0), pipeline_mode=once),
        ]
        + [pl.BlockSpec(memory_space=pl.ANY)] * len(so_far),
        out_specs=[pl.BlockSpec((rows, shape[1]), lambda i: (2 * n + i, 0)) for shape in upright]
        + [pl.BlockSpec((shape[0], rows), lambda i: (0, 2 * n + i)) for shape in turned]
        + [pl.BlockSpec((rows, shape[1]), lambda i: (2 * n + i, 0)) for shape in whole],
        out_shape=[jax.ShapeDtypeStruct(shape, BF16) for shape in upright + turned + whole],
        input_output_aliases={6 + k: k for k in range(len(so_far))},
        compiler_params=pltpu.CompilerParams(vmem_limit_bytes=VMEM_LIMIT),
        cost_estimate=pl.CostEstimate(
            flops=flops,
            bytes_accessed=16 * rows * depth + 24 * rows * units + 6 * depth * units,
            transcendentals=2 * rows * units,
        ),
        name="hidden_step",
    )(*[array for array, _ in pieces], weights, w_down, *so_far)


def rows_kernel(me_ref, left_ref, right_ref, result_ref, *, right_dim):
    result_ref[...] = dot(left_ref[...], right_ref[...], 1, right_dim).astype(BF16)


def rows_product(me, left, right, right_dim, block_rows, name):
    count, width = left.shape
    return pl.pallas_call(
        functools.partial(rows_kernel, right_dim=right_dim),
        grid_spec=pltpu.PrefetchScalarGridSpec(
            num_scalar_prefetch=1,
            grid=(count // block_rows,),
            in_specs=[
                pl.BlockSpec((block_rows, width), lambda i, me_ref: (i, 0)),
                pl.BlockSpec(
                    right.shape, lambda i, me_ref: (0, 0), pipeline_mode=pl.Buffered(1)
                ),
            ],
            out_specs=pl.BlockSpec((block_rows, D), lambda i, me_ref: (me_ref[0] ^ i, 0)),
        ),
        out_shape=jax.ShapeDtypeStruct((count, D), BF16),
        compiler_params=pltpu.CompilerParams(vmem_limit_bytes=VMEM_LIMIT),
        cost_estimate=pl.CostEstimate(
            flops=2 * count * D * width,
            bytes_accessed=2 * (count * width + count * D + D * width),
            transcendentals=0,
        ),
        name=name,
    )(me, left, right)


def grad_kernel(grads_ref, weight_ref, own_ref, other_ref):
    result = dot(grads_ref[...], weight_ref[...], 1, 1).astype(BF16)

    @pl.when(pl.program_id(0) == 0)
    def _():
        own_ref[...] = result

    @pl.when(pl.program_id(0) == 1)
    def _():
        other_ref[...] = result


def grad_step(n, grads, weights, rows):
    depth, width = weights.shape
    part = pl.BlockSpec((rows, depth), lambda i: (0, 0))
    return pl.pallas_call(
        grad_kernel,
        grid=(2,),
        in_specs=[
            pl.BlockSpec((rows, width), lambda i: (2 * n + i, 0)),
            pl.BlockSpec((depth, width), lambda i: (0, 0), pipeline_mode=pl.Buffered(1)),
        ],
        out_specs=[part, part],
        out_shape=[jax.ShapeDtypeStruct((rows, depth), BF16)] * 2,
        compiler_params=pltpu.CompilerParams(vmem_limit_bytes=VMEM_LIMIT),
        cost_estimate=pl.CostEstimate(
            flops=4 * rows * depth * width,
            bytes_accessed=4 * rows * (width + depth) + 2 * depth * width,
            transcendentals=0,
        ),
        name="grad_ffn_normed",
    )(grads, weights)


def weight_kernel(left_ref, right_ref, *result_refs, parts):
    total = dot(left_ref[...], right_ref[...], 1, 0)
    half = total.shape[0] // HALVES
    for h, result_ref in enumerate(result_refs):
        piece = total[h * half : (h + 1) * half]
        if parts == 0:
            result_ref[0] = piece.astype(BF16)
            continue
        wide = piece.shape[1] // parts
        for p in range(parts):
            result_ref[p] = piece[:, p * wide : (p + 1) * wide].astype(BF16).T


def weight_product(left, right, first, units, wide, name):
    depth = left.shape[1]
    half = units // HALVES
    column = min(512, D)
    parts = column // wide if wide else 0
    block = first // units
    if wide:
        out_spec = pl.BlockSpec((parts, wide, half), lambda j: (j, 0, 0))
        out_shape = jax.ShapeDtypeStruct((D // wide, wide, half), BF16)
    else:
        out_spec = pl.BlockSpec((1, half, column), lambda j: (j, 0, 0))
        out_shape = jax.ShapeDtypeStruct((D // column, half, column), BF16)
    return pl.pallas_call(
        functools.partial(weight_kernel, parts=parts),
        grid=(D // column,),
        in_specs=[
            pl.BlockSpec((units, depth), lambda j: (block, 0), pipeline_mode=pl.Buffered(1)),
            pl.BlockSpec((depth, column), lambda j: (0, j)),
        ],
        out_specs=[out_spec] * HALVES,
        out_shape=[out_shape] * HALVES,
        compiler_params=pltpu.CompilerParams(vmem_limit_bytes=VMEM_LIMIT),
        cost_estimate=pl.CostEstimate(
            flops=2 * units * depth * D,
            bytes_accessed=2 * depth * (units + D) + 2 * units * D,
            transcendentals=0,
        ),
        name=name,
    )(left, right)


def merge_kernel(even_ref, *refs):
    result_ref = refs[-1]
    piece = result_ref.shape[1] // (2 * SWAPS)
    for h in range(SWAPS):
        mine, theirs = refs[h][...], refs[SWAPS + h][...]
        gate = jnp.where(even_ref[0] > 0, mine, theirs)
        up = jnp.where(even_ref[0] > 0, theirs, mine)
        result_ref[:, h * piece : (h + 1) * piece] = gate
        result_ref[:, (SWAPS + h) * piece : (SWAPS + h + 1) * piece] = up


def merge_columns(even, mine, theirs):
    rows, piece = mine[0].shape
    tile = min(256, rows)
    return pl.pallas_call(
        merge_kernel,
        grid=(rows // tile,),
        in_specs=[pl.BlockSpec(memory_space=pltpu.SMEM)]
        + [pl.BlockSpec((tile, piece), lambda i: (i, 0))] * (2 * SWAPS),
        out_specs=pl.BlockSpec((tile, 2 * SWAPS * piece), lambda i: (i, 0)),
        out_shape=jax.ShapeDtypeStruct((rows, 2 * SWAPS * piece), BF16),
        compiler_params=pltpu.CompilerParams(vmem_limit_bytes=VMEM_LIMIT),
        cost_estimate=pl.CostEstimate(
            flops=0, bytes_accessed=8 * rows * SWAPS * piece, transcendentals=0
        ),
        name="merge_columns",
    )(even.astype(jnp.int32).reshape(1), *mine, *theirs)


def pack_kernel(even_ref, first_ref, second_ref, result_ref):
    chosen = jnp.where(even_ref[0] > 0, first_ref[...], second_ref[...])
    width = result_ref.shape[-1]
    for h in range(SWAPS):
        result_ref[0, h] = chosen[:, h * width : (h + 1) * width]


def pack_columns(even, first, second, parts):
    rows, columns = first.shape
    width = columns // parts
    block = pl.BlockSpec((rows, width), lambda i: (0, i))
    piece = width // SWAPS
    return pl.pallas_call(
        pack_kernel,
        grid=(parts,),
        in_specs=[pl.BlockSpec(memory_space=pltpu.SMEM), block, block],
        out_specs=pl.BlockSpec((1, SWAPS, rows, piece), lambda i: (i, 0, 0, 0)),
        out_shape=jax.ShapeDtypeStruct((parts, SWAPS, rows, piece), BF16),
        compiler_params=pltpu.CompilerParams(vmem_limit_bytes=VMEM_LIMIT),
        cost_estimate=pl.CostEstimate(
            flops=0, bytes_accessed=6 * rows * columns, transcendentals=0
        ),
        name="pack_columns",
    )(even.astype(jnp.int32).reshape(1), first, second)


def unpack_kernel(stacked_ref, result_ref):
    width = stacked_ref.shape[-1]
    for h in range(HALVES):
        result_ref[:, h * width : (h + 1) * width] = stacked_ref[0, h].astype(F32)


def unpack_columns(stacked):
    parts, _, rows, half = stacked.shape
    return pl.pallas_call(
        unpack_kernel,
        grid=(parts,),
        in_specs=[pl.BlockSpec((1, HALVES, rows, half), lambda i: (i, 0, 0, 0))],
        out_specs=pl.BlockSpec((rows, HALVES * half), lambda i: (0, i)),
        out_shape=jax.ShapeDtypeStruct((rows, parts * HALVES * half), F32),
        compiler_params=pltpu.CompilerParams(vmem_limit_bytes=VMEM_LIMIT),
        cost_estimate=pl.CostEstimate(
            flops=0, bytes_accessed=6 * parts * rows * HALVES * half, transcendentals=0
        ),
        name="unpack_columns",
    )(stacked)


def unpack_rows_kernel(*refs):
    result_ref = refs[-1]
    height = refs[0].shape[1]
    for h in range(HALVES):
        result_ref[h * height : (h + 1) * height, :] = refs[h][0].astype(F32)


def unpack_rows(pieces):
    blocks, half, column = pieces[0].shape
    return pl.pallas_call(
        unpack_rows_kernel,
        grid=(blocks,),
        in_specs=[pl.BlockSpec((1, half, column), lambda i: (i, 0, 0))] * HALVES,
        out_specs=pl.BlockSpec((HALVES * half, column), lambda i: (0, i)),
        out_shape=jax.ShapeDtypeStruct((HALVES * half, blocks * column), F32),
        compiler_params=pltpu.CompilerParams(vmem_limit_bytes=VMEM_LIMIT),
        cost_estimate=pl.CostEstimate(
            flops=0, bytes_accessed=6 * blocks * HALVES * half * column, transcendentals=0
        ),
        name="unpack_rows",
    )(*pieces)


class Layout:
    def __init__(self, fsdp_devices, seq_devices, rows_dev):
        self.fsdp = fsdp_devices
        self.seq = seq_devices
        self.chips = fsdp_devices // 2
        self.share = 2 * seq_devices // (2 * MICRO)
        self.near = self.share // 2
        self.piece_rows = rows_dev // self.share
        self.step_rows = rows_dev
        self.rows = LENGTH // self.share

    def flat(self, f, z):
        return f * self.seq + z

    def moved(self, r):
        pairs = []
        for f in range(self.fsdp):
            for z in range(self.seq):
                slot = z ^ r
                micro, j = slot // self.share, slot % self.share
                target_f = (f // 2) * 2 + j % 2
                target_z = (2 * micro + f % 2) * self.near + j // 2
                pairs.append((self.flat(f, z), self.flat(target_f, target_z)))
        return pairs

    def other(self, k):
        return [
            (self.flat(f, z), self.flat(f ^ k, z))
            for f in range(self.fsdp)
            for z in range(self.seq)
        ]

    def across(self, k):
        pairs = []
        for f in range(self.fsdp):
            for z in range(self.seq):
                pairs.append((self.flat(f, z), self.flat(f ^ (k & 1), z ^ (k >> 1))))
        return pairs


def permute(value, pairs):
    return lax.ppermute(value, ("fsdp", "seq"), pairs)


def scatter_rows(layout, values, z, slot):
    parts = values.reshape(layout.seq, layout.piece_rows, values.shape[-1])
    result = jnp.zeros_like(parts)
    for r in range(layout.seq):
        sent = lax.dynamic_index_in_dim(parts, z ^ r, 0, keepdims=False)
        got = permute(sent, layout.moved(r))
        result = lax.dynamic_update_index_in_dim(result, got, slot ^ r, 0)
    return result.reshape(layout.rows, values.shape[-1])


def return_rows(layout, values, z, slot):
    parts = values.reshape(layout.seq, layout.piece_rows, values.shape[-1])
    result = jnp.zeros_like(parts)
    for r in range(layout.seq):
        sent = lax.dynamic_index_in_dim(parts, slot ^ r, 0, keepdims=False)
        got = permute(sent, [(b, a) for a, b in layout.moved(r)])
        result = lax.dynamic_update_index_in_dim(result, got, z ^ r, 0)
    return result.reshape(MICRO, layout.step_rows, values.shape[-1])


def seq_sum(value, z, seq_devices):
    share = value.shape[1] // seq_devices

    def exchange(piece, k):
        return lax.ppermute(piece, "seq", [(i, i ^ k) for i in range(seq_devices)])

    def piece_of(k):
        return lax.dynamic_slice_in_dim(value, (z ^ k) * share, share, 1)

    total = piece_of(0).astype(F32)
    for k in range(1, seq_devices):
        total = total + exchange(piece_of(k), k).astype(F32)
    total = total.astype(BF16)
    result = lax.dynamic_update_slice_in_dim(jnp.zeros_like(value), total, z * share, 1)
    for k in range(1, seq_devices):
        result = lax.dynamic_update_slice_in_dim(
            result, exchange(total, k), (z ^ k) * share, 1
        )
    return result


class RowGather:
    def __init__(self, layout, own):
        self.layout = layout
        self.own = {0: own}
        self.sibling = {0: self.move(own, 1)}
        chips = layout.chips
        for n in range(1, 3 if chips == 4 else chips):
            self.own[n] = self.move(own, 2 * n)

    def move(self, value, k):
        return permute(value, self.layout.other(k))

    def pass_on(self):
        if self.layout.chips == 4:
            cut = self.own[0].shape[0] // 2
            far = [self.move(self.own[2][:cut], 2), self.move(self.own[1][cut:], 4)]
            self.own[3] = jnp.concatenate(far)
        for m in self.own:
            if m not in self.sibling:
                self.sibling[m] = self.move(self.own[m], 1)

    def after(self, n, *values):
        chips = self.layout.chips
        if n + 1 < chips:
            waiting = {m: value for m, value in self.own.items() if m > n}
            siblings = {m: value for m, value in self.sibling.items() if m > n}
            waiting, siblings, values = lax.optimization_barrier((waiting, siblings, values))
            self.own.update(waiting)
            self.sibling.update(siblings)
            if chips == 4 and n == 0:
                cut = self.own[0].shape[0] // 2
                self.far = [self.move(self.own[2][:cut], 2), self.move(self.own[1][cut:], 4)]
            if chips == 4 and n == 1:
                self.far = lax.optimization_barrier((self.far, values))[0]
                self.own[3] = jnp.concatenate(self.far)
            for m in (n + 1, n + 2):
                if m in self.own and m not in self.sibling:
                    self.sibling[m] = self.move(self.own[m], 1)
        return values


def gather_small(layout, f, own):
    held = own[None]
    k = 1
    while k < layout.fsdp:
        got = permute(held, layout.other(k))
        upper = (f & k) > 0
        held = jnp.concatenate(
            [jnp.where(upper, got, held), jnp.where(upper, held, got)], axis=0
        )
        k *= 2
    return held


def sum_small(layout, value):
    k = 1
    while k < layout.fsdp:
        value = value + permute(value, layout.other(k))
        k *= 2
    return value


class LinePipe:
    def __init__(self, z, seq_devices):
        self.seq = seq_devices
        self.z = z
        self.outer = (z == 0) | (z == seq_devices - 1)
        self.flying = []
        self.results = {}

    def send(self, stage, value):
        half, last = self.seq // 2, self.seq - 1
        if stage < half - 1:
            pairs = [(stage, stage + 1), (last - stage, last - stage - 1)]
        elif stage == half - 1:
            pairs = [(half - 1, half), (half, half - 1)]
        else:
            s = last - 1 - stage
            pairs = [(s + 1, s), (last - s - 1, last - s)]
        return lax.ppermute(value, "seq", pairs)

    def join(self, stage, value, got):
        if stage < self.seq // 2:
            return value + got
        s = self.seq - 2 - stage
        return jnp.where((self.z == s) | (self.z == self.seq - 1 - s), got, value)

    def step(self, name=None, value=None, others=()):
        arrived = [entry[3] for entry in self.flying]
        arrived, self.results, value, others = lax.optimization_barrier(
            (arrived, self.results, value, others)
        )
        flying = []
        if name is not None:
            flying.append((name, 0, value, self.send(0, value)))
        for (key, stage, held, _), got in zip(self.flying, arrived):
            if stage == self.seq - 2:
                self.results[key] = jnp.where(self.outer, got, held)
                continue
            held = self.join(stage, held, got)
            flying.append((key, stage + 1, held, self.send(stage + 1, held)))
        self.flying = flying
        return others


class PairPipe:
    def __init__(self, z):
        self.outer = (z == 0) | (z == 3)
        self.entered = self.halved = self.summed = None
        self.side = self.across = None
        self.results = {}

    @property
    def flying(self):
        return self.entered or self.halved or self.summed

    def step(self, name=None, value=None, others=()):
        side, across, self.results, value, others = lax.optimization_barrier(
            (self.side, self.across, self.results, value, others)
        )
        entered, halved, summed = self.entered, self.halved, self.summed
        total = halved[1] + across if halved else None
        inward, outward = [(0, 1), (3, 2)], [(1, 0), (2, 3)]
        self.side = self.across = None
        self.entered = self.halved = self.summed = None
        sent = value if total is None else total
        pairs = inward if total is None else outward
        if value is not None and total is not None:
            sent = jnp.where(self.outer, value, total)
            pairs = inward + outward
        if sent is not None:
            self.side = lax.ppermute(sent, "seq", pairs)
        if entered:
            joined = entered[1] + side
            self.across = lax.ppermute(joined, "seq", [(1, 2), (2, 1)])
            self.halved = (entered[0], joined)
        if summed:
            self.results[summed[0]] = jnp.where(self.outer, side, summed[1])
        if halved:
            self.summed = (halved[0], sent)
        if name is not None:
            self.entered = (name, value)
        return others


def body(
    tokens,
    cotangent,
    attn_gain,
    query_gain,
    key_gain,
    w_query,
    w_key,
    w_value,
    w_out,
    ffn_gain,
    w_gate,
    w_up,
    w_down,
):
    fsdp_devices = lax.axis_size("fsdp")
    seq_devices = lax.axis_size("seq")
    layout = Layout(fsdp_devices, seq_devices, tokens.shape[2])
    f = lax.axis_index("fsdp")
    z = lax.axis_index("seq")
    rows = layout.rows
    share = layout.share
    member = (z % layout.near) * 2 + f % 2
    slot = (z // layout.near // 2) * share + member

    w_attn = lax.all_gather(
        jnp.concatenate([w_query, w_key, w_value], axis=1), "fsdp", axis=0, tiled=True
    )
    gains = gather_small(
        layout, f, jnp.concatenate([attn_gain, ffn_gain, query_gain, key_gain])
    ).astype(F32)
    wide, narrow = attn_gain.shape[0], query_gain.shape[0]
    even = z % 2 == 0
    hidden_dev = w_down.shape[0]
    gains, gate_rows, up_rows = lax.optimization_barrier((gains, w_gate, w_up))
    fetched = lax.all_to_all(
        pack_columns(even, gate_rows, up_rows, fsdp_devices),
        "fsdp",
        split_axis=0,
        concat_axis=0,
        tiled=True,
    )
    full_attn_gain = gains[:, :wide].reshape(D)
    full_ffn_gain = gains[:, wide : 2 * wide].reshape(D)
    full_query_gain = gains[:, 2 * wide : 2 * wide + narrow].reshape(HD)
    full_key_gain = gains[:, 2 * wide + narrow :].reshape(HD)
    inputs_low = scatter_rows(layout, tokens[:, 0], z, slot)
    grad_out_low = scatter_rows(layout, cotangent[:, 0], z, slot)
    full_out = lax.all_gather(w_out, "fsdp", axis=0, tiled=True)

    row = jnp.arange(rows, dtype=jnp.int32)
    position = (
        (row // layout.piece_rows) * layout.step_rows
        + member * layout.piece_rows
        + row % layout.piece_rows
    ).astype(F32)
    frequency = THETA ** (-(jnp.arange(HD // 2).astype(F32) * 2.0 / HD))
    angles = frequency[:, None] * position[None, :]
    cosine_table, sine_table = jnp.cos(angles)[None], jnp.sin(angles)[None]
    head_gains = jnp.concatenate(
        [
            jnp.broadcast_to(full_query_gain[None, :, None], (HQ, HD, 1)),
            jnp.broadcast_to(full_key_gain[None, :, None], (KVH, HD, 1)),
        ]
    )

    inputs = inputs_low.astype(F32)
    normed, normed_unit, normed_inverse = rms_fwd(inputs, full_attn_gain)
    fetched = [fetched[:, h].reshape(D, hidden_dev // SWAPS) for h in range(SWAPS)]
    swapped = [
        lax.ppermute(piece, "seq", [(i, i ^ 1) for i in range(seq_devices)]) for piece in fetched
    ]
    normed_low, grad_out_low, w_attn = lax.optimization_barrier(
        (normed.astype(BF16), grad_out_low, w_attn)
    )
    grad_out_gather = RowGather(layout, grad_out_low)
    raw = dot(w_attn, normed_low, 0, 1)
    pair_width = KVH * HD
    turned = HQ + KVH
    head_raw = raw[: turned * HD].reshape(turned, HD, rows)
    head_normed, head_unit, head_inverse = head_rms_fwd(head_raw, head_gains)
    heads_low = rotate(head_normed, cosine_table, sine_table).astype(BF16).reshape(turned * HD, rows)
    queries = heads_low[: HQ * HD]
    own_pair = jnp.concatenate([heads_low[HQ * HD :], raw[turned * HD :].astype(BF16)], axis=0)
    pair_pieces = [own_pair] + [permute(own_pair, layout.across(k)) for k in range(1, share)]
    keys = jnp.concatenate([piece[:pair_width] for piece in pair_pieces], axis=1)
    values = jnp.concatenate([piece[pair_width:] for piece in pair_pieces], axis=1)
    index = member.astype(jnp.int32).reshape(1)
    attended, log_totals = attend(
        index, queries, keys, values, share, layout.piece_rows, layout.step_rows
    )
    attended, swapped[0], grad_out_gather.own = lax.optimization_barrier(
        (attended, swapped[0], grad_out_gather.own)
    )
    grad_out_gather.pass_on()
    middle = inputs + dot(attended, full_out, 0, 0)
    ffn_normed, ffn_unit, ffn_inverse = rms_fwd(middle, full_ffn_gain)
    ffn_low = ffn_normed.astype(BF16)

    ffn_gather = RowGather(layout, ffn_low)
    line = PairPipe(z) if seq_devices == 4 else LinePipe(z, seq_devices)
    weights = merge_columns(even, fetched, swapped)
    worked = ()
    grad_ffn_parts = []
    me = f.astype(jnp.int32).reshape(1)
    for n in range(layout.chips):
        pieces = [
            (side[n], 0)
            for side in (
                ffn_gather.own,
                grad_out_gather.own,
                ffn_gather.sibling,
                grad_out_gather.sibling,
            )
        ]
        worked = hidden_step(n, fsdp_devices * rows, rows, pieces, weights, w_down, worked)
        own_grad, other_grad = grad_step(n, worked[1], weights, rows)
        worked, own_grad, other_grad = lax.optimization_barrier((worked, own_grad, other_grad))
        worked = ffn_gather.after(n, *worked)
        if grad_ffn_parts:
            worked, grad_ffn_parts[-1] = lax.optimization_barrier((worked, grad_ffn_parts[-1]))
            if n > 1:
                grad_ffn_parts[-1] = permute(grad_ffn_parts[-1], layout.other(2 * n - 2))
        grad_ffn_parts.append(own_grad + permute(other_grad, layout.other(1)))
    worked, grad_ffn_parts[-1] = lax.optimization_barrier((worked, grad_ffn_parts[-1]))
    grad_ffn_parts[-1] = permute(grad_ffn_parts[-1], layout.other(2 * layout.chips - 2))
    hidden, grads, hidden_t, grads_t, ffn_rows, grad_out_rows = worked

    waiting = {}
    finished = {}
    names = {}
    tied = []

    def to_owners(name):
        terms = [
            line.results[f"{name}{h}"].reshape(fsdp_devices, wide, -1) for h in range(HALVES)
        ]
        return lax.all_to_all(
            jnp.stack(terms, axis=1), "fsdp", split_axis=0, concat_axis=0, tiled=True
        )

    def advance(name=None, value=None, others=()):
        if name is not None:
            names[name] = value.shape
            value = value.reshape(-1, value.shape[-1])
        ties = {key: finished[key] for key in tied}
        ties, others = line.step(name, value, (ties, others))
        finished.update(ties)
        tied.clear()
        for key in ("gate", "up"):
            if key not in finished and all(f"{key}{h}" in line.results for h in range(HALVES)):
                waiting.setdefault(key, functools.partial(to_owners, key))
        if waiting:
            key = next(iter(waiting))
            finished[key] = waiting.pop(key)()
            tied.append(key)
        return others

    gate_term = weight_product(grads_t, ffn_rows, 0, hidden_dev, wide, "w_gate_grad")
    grads_t, hidden, grad_ffn_parts[:-1] = advance(
        "gate0", gate_term[0], (grads_t, hidden, grad_ffn_parts[:-1])
    )
    up_term = weight_product(grads_t, ffn_rows, hidden_dev, hidden_dev, wide, "w_up_grad")
    out_part = rows_product(me, hidden, w_down, 0, rows, "block_out")
    out_sum = lax.psum_scatter(out_part, "fsdp", scatter_dimension=0, tiled=True)
    up_term, out_part, grad_ffn_parts = lax.optimization_barrier(
        (up_term, out_part, grad_ffn_parts)
    )
    grad_ffn_normed = sum(part.astype(F32) for part in grad_ffn_parts)

    grad_middle_norm, ffn_gain_term = rms_back(
        grad_ffn_normed, ffn_unit, ffn_inverse, full_ffn_gain
    )
    grad_middle = grad_out_low.astype(F32) + grad_middle_norm
    grad_branch_low = grad_middle.astype(BF16)
    (grad_branch_low,) = advance("gate1", gate_term[1], (grad_branch_low,))
    grad_attended = dot(full_out, grad_branch_low, 1, 1).astype(BF16)
    grad_queries, grad_keys, grad_values = attend_back(
        index,
        queries,
        keys,
        values,
        attended,
        log_totals,
        grad_attended,
        share,
        layout.piece_rows,
        layout.step_rows,
    )
    grad_queries, grad_keys, grad_values, grad_branch_low = advance(
        "up0", up_term[0], (grad_queries, grad_keys, grad_values, grad_branch_low)
    )
    grad_pair = jnp.concatenate([grad_keys[:, :rows], grad_values[:, :rows]], axis=0)
    for k in range(1, share):
        columns = slice(k * rows, (k + 1) * rows)
        sent = jnp.concatenate([grad_keys[:, columns], grad_values[:, columns]], axis=0)
        grad_pair = grad_pair + permute(sent.astype(BF16), layout.across(k)).astype(F32)
    grad_pair_low = grad_pair.astype(BF16)
    grad_turned = (
        jnp.concatenate([grad_queries, grad_pair_low[:pair_width]], axis=0)
        .astype(F32)
        .reshape(turned, HD, rows)
    )
    grad_head_normed = rotate(grad_turned, cosine_table, -sine_table)
    scaled = grad_head_normed * head_gains
    grad_head_raw = head_inverse * (
        scaled - head_unit * jnp.mean(scaled * head_unit, axis=1, keepdims=True)
    )
    head_gain_terms = jnp.sum(grad_head_normed * head_unit, axis=2)
    grad_raw = jnp.concatenate(
        [grad_head_raw.astype(BF16).reshape(turned * HD, rows), grad_pair_low[pair_width:]], axis=0
    )
    projection_term = dot(normed_low, grad_raw, 0, 1).astype(BF16)
    projection_term, grad_branch_low, grad_raw = lax.optimization_barrier(
        (projection_term, grad_branch_low, grad_raw)
    )
    projection_rows = lax.psum_scatter(
        projection_term, "fsdp", scatter_dimension=0, tiled=True
    )
    out_term = dot(attended, grad_branch_low, 1, 0).astype(BF16)
    out_rows = lax.psum_scatter(out_term, "fsdp", scatter_dimension=0, tiled=True)
    grad_raw, out_sum, hidden_t = advance("up1", up_term[1], (grad_raw, out_sum, hidden_t))
    down_term = weight_product(hidden_t, grad_out_rows, 0, hidden_dev, 0, "w_down_grad")
    block_out = return_rows(layout, (middle + out_sum.astype(F32)).astype(BF16), z, slot)
    grad_normed = dot(grad_raw, w_attn, 0, 1)
    grad_input_norm, attn_gain_term = rms_back(
        grad_normed, normed_unit, normed_inverse, full_attn_gain
    )

    tokens_grad_low = (grad_middle + grad_input_norm).astype(BF16)
    gain_terms = sum_small(
        layout,
        jnp.concatenate(
            [
                attn_gain_term,
                ffn_gain_term,
                jnp.sum(head_gain_terms[:HQ], axis=0),
                jnp.sum(head_gain_terms[HQ:], axis=0),
            ]
        )[None],
    )[0]

    def own_share(first, count):
        share_of = count // fsdp_devices
        vector = lax.dynamic_slice_in_dim(gain_terms, first + f * share_of, share_of, 0)
        return jnp.pad(vector, (0, wide - share_of))

    gain_columns = jnp.stack(
        [own_share(0, D), own_share(D, D), own_share(2 * D, HD), own_share(2 * D + HD, HD)],
        axis=1,
    )
    gain_columns = jnp.pad(gain_columns, ((0, 0), (0, 512 - gain_columns.shape[1]))).astype(BF16)

    tokens_grad_low, gain_columns = advance(
        "down0", down_term[0], (tokens_grad_low, gain_columns)
    )
    tokens_grad = return_rows(layout, tokens_grad_low, z, slot)
    block_out, projection_rows = advance("down1", down_term[1], (block_out, projection_rows))
    attn_rows = seq_sum(projection_rows, z, seq_devices)
    tokens_grad, out_rows, attn_rows = advance(others=(tokens_grad, out_rows, attn_rows))
    out_rows = seq_sum(jnp.concatenate([out_rows, gain_columns], axis=1), z, seq_devices)
    while line.flying or waiting:
        advance()

    w_gate_grad = unpack_columns(finished["gate"])
    w_up_grad = unpack_columns(finished["up"])
    w_down_grad = unpack_rows(
        [line.results[f"down{h}"].reshape(names[f"down{h}"]) for h in range(HALVES)]
    )
    attn_rows = attn_rows.astype(F32)
    out_rows = out_rows.astype(F32)
    w_out_grad, gain_rows = out_rows[:, :D], out_rows[:, D:]
    query_width = HQ * HD

    return (
        block_out[:, None],
        tokens_grad[:, None],
        gain_rows[:, 0],
        gain_rows[:narrow, 2],
        gain_rows[:narrow, 3],
        attn_rows[:, :query_width],
        attn_rows[:, query_width : query_width + pair_width],
        attn_rows[:, query_width + pair_width : query_width + 2 * pair_width],
        w_out_grad,
        gain_rows[:, 1],
        w_gate_grad,
        w_up_grad,
        w_down_grad,
    )


def solution(mesh):
    activations = P(None, "fsdp", "seq", None)
    vector = P("fsdp")
    matrix = P("fsdp", None)
    specs = (
        (activations, activations)
        + (vector,) * 3
        + (matrix,) * 4
        + (vector,)
        + (matrix,) * 3
    )
    return jax.shard_map(body, mesh=mesh, in_specs=specs, out_specs=specs, check_vma=False)
```

```python
import functools
import math

import jax
import jax.numpy as jnp
from jax import lax
from jax.experimental import pallas as pl
from jax.experimental.pallas import tpu as pltpu
from jax.sharding import PartitionSpec as P

D = 2048
HQ = 32
KVH = 8
HD = 64
FF = 8192
LENGTH = 1024
MICRO = 2
HALVES = 2
SWAPS = 2

EPSILON = 1e-05
THETA = 1000000.0
GROUP = HQ // KVH
BLOCK = 128
SCALE = 1.0 / math.sqrt(HD)
LOG2E = math.log2(math.e)
VMEM_LIMIT = 56 * 1024 * 1024

F32 = jnp.float32
BF16 = jnp.bfloat16


def dot(left_side, right_side, left_dim, right_dim):
    return lax.dot_general(
        left_side,
        right_side,
        (((left_dim,), (right_dim,)), ((), ())),
        preferred_element_type=F32,
    )


def rms_fwd(values, row_gain):
    inverse = lax.rsqrt(jnp.mean(values * values, axis=-1, keepdims=True) + EPSILON)
    unit_rows = values * inverse
    return (unit_rows * row_gain, unit_rows, inverse)


def rms_back(grad_outputs, unit_rows, inverse, row_gain):
    scaled = grad_outputs * row_gain
    grad_inputs = inverse * (
        scaled - unit_rows * jnp.mean(scaled * unit_rows, axis=-1, keepdims=True)
    )
    grad_gain = jnp.sum(grad_outputs * unit_rows, axis=0)
    return (grad_inputs, grad_gain)


def head_rms_fwd(values, gains):
    inverse = lax.rsqrt(jnp.mean(values * values, axis=1, keepdims=True) + EPSILON)
    unit = values * inverse
    return (unit * gains, unit, inverse)


def rotate(values, cosine_table, sine_table):
    half_width = values.shape[1] // 2
    front_half = values[:, :half_width]
    back_half = values[:, half_width:]
    return jnp.concatenate(
        [
            front_half * cosine_table - back_half * sine_table,
            back_half * cosine_table + front_half * sine_table,
        ],
        axis=1,
    )


def block_masks(index, pieces, piece_rows, step_rows):
    key = lax.broadcasted_iota(jnp.int32, (BLOCK, GROUP * BLOCK), 0)
    query = lax.broadcasted_iota(jnp.int32, (BLOCK, GROUP * BLOCK), 1) & (BLOCK - 1)

    def place(row, piece):
        return (row // piece_rows) * step_rows + piece * piece_rows + (row & (piece_rows - 1))

    return [place(key, index ^ k) <= place(query, index) for k in range(pieces)]


def heads_beside(block, first, count):
    return jnp.concatenate(
        [block[h * HD : (h + 1) * HD, first : first + count] for h in range(GROUP)], axis=1
    )


def mask_tail(values, mask, first):
    tail = jnp.where(mask, values[first:], 0.0)
    if first == 0:
        return tail
    return jnp.concatenate([values[:first], tail], axis=0)


def attend_kernel(index_ref, q_ref, k_ref, v_ref, out_ref, lse_ref, *, pieces, piece_rows, step_rows):
    rows = q_ref.shape[1]
    masks = block_masks(index_ref[0], pieces, piece_rows, step_rows)
    queries = q_ref[...]
    for first in range(0, rows, BLOCK):
        count = first + BLOCK
        query_block = heads_beside(queries, first, BLOCK)
        total = None
        result = None
        for k in range(pieces):
            spot = pl.ds(k * rows, count)
            scores = dot(k_ref[:, spot], query_block, 0, 0)
            weights = mask_tail(jnp.exp2(scores * (SCALE * LOG2E)), masks[k], first)
            part = jnp.sum(weights, axis=0, keepdims=True)
            value = dot(v_ref[:, spot], weights.astype(BF16), 1, 0)
            total = part if total is None else total + part
            result = value if result is None else result + value
        result = result * (1.0 / total)
        log_total = jnp.log2(total)
        for h in range(GROUP):
            columns = slice(h * BLOCK, (h + 1) * BLOCK)
            out_ref[h * HD : (h + 1) * HD, first : first + BLOCK] = result[:, columns].astype(BF16)
            lse_ref[0, h : h + 1, first : first + BLOCK] = log_total[:, columns]


def attend_back_kernel(
    index_ref, q_ref, k_ref, v_ref, out_ref, lse_ref, grad_ref, dq_ref, dk_ref, dv_ref,
    *, pieces, piece_rows, step_rows
):
    rows = q_ref.shape[1]
    masks = block_masks(index_ref[0], pieces, piece_rows, step_rows)
    queries = q_ref[...]
    grads = grad_ref[...]
    results = out_ref[...]
    dk_ref[...] = jnp.zeros_like(dk_ref)
    dv_ref[...] = jnp.zeros_like(dv_ref)
    for first in range(0, rows, BLOCK):
        count = first + BLOCK
        query_block = heads_beside(queries, first, BLOCK)
        grad_block = heads_beside(grads, first, BLOCK)
        result_block = heads_beside(results, first, BLOCK)
        centre = jnp.sum(
            grad_block.astype(F32) * result_block.astype(F32), axis=0, keepdims=True
        )
        log_total = jnp.concatenate(
            [lse_ref[0, h : h + 1, first : first + BLOCK] for h in range(GROUP)], axis=1
        )
        dq = None
        for k in range(pieces):
            spot = pl.ds(k * rows, count)
            keys = k_ref[:, spot]
            scores = dot(keys, query_block, 0, 0)
            weights = mask_tail(
                jnp.exp2(scores * (SCALE * LOG2E) - log_total), masks[k], first
            )
            grad_weights = dot(v_ref[:, spot], grad_block, 0, 0)
            grad_scores = (weights * (grad_weights - centre)).astype(BF16)
            part = dot(keys, grad_scores, 1, 0)
            dq = part if dq is None else dq + part
            dk_ref[:, spot] += dot(query_block, grad_scores, 1, 1) * SCALE
            dv_ref[:, spot] += dot(grad_block, weights.astype(BF16), 1, 1)
        dq = (dq * SCALE).astype(BF16)
        for h in range(GROUP):
            columns = slice(h * BLOCK, (h + 1) * BLOCK)
            dq_ref[h * HD : (h + 1) * HD, first : first + BLOCK] = dq[:, columns]


def attention_specs(rows, total_rows):
    group_spec = pl.BlockSpec((GROUP * HD, rows), lambda i: (i, 0))
    pair_spec = pl.BlockSpec((HD, total_rows), lambda i: (i, 0))
    lse_spec = pl.BlockSpec((1, GROUP, rows), lambda i: (i, 0, 0))
    return group_spec, pair_spec, lse_spec


def attend(index, queries, keys, values, pieces, piece_rows, step_rows):
    rows, total_rows = queries.shape[1], keys.shape[1]
    group_spec, pair_spec, lse_spec = attention_specs(rows, total_rows)
    return pl.pallas_call(
        functools.partial(
            attend_kernel, pieces=pieces, piece_rows=piece_rows, step_rows=step_rows
        ),
        grid=(KVH,),
        in_specs=[pl.BlockSpec(memory_space=pltpu.SMEM), group_spec, pair_spec, pair_spec],
        out_specs=[group_spec, lse_spec],
        out_shape=[
            jax.ShapeDtypeStruct((HQ * HD, rows), BF16),
            jax.ShapeDtypeStruct((KVH, GROUP, rows), F32),
        ],
        compiler_params=pltpu.CompilerParams(vmem_limit_bytes=VMEM_LIMIT),
        cost_estimate=pl.CostEstimate(
            flops=4 * HQ * HD * rows * total_rows,
            bytes_accessed=8 * HQ * HD * rows,
            transcendentals=HQ * rows * total_rows,
        ),
        name="attend",
    )(index, queries, keys, values)


def attend_back(index, queries, keys, values, results, lse, grads, pieces, piece_rows, step_rows):
    rows, total_rows = queries.shape[1], keys.shape[1]
    group_spec, pair_spec, lse_spec = attention_specs(rows, total_rows)
    return pl.pallas_call(
        functools.partial(
            attend_back_kernel, pieces=pieces, piece_rows=piece_rows, step_rows=step_rows
        ),
        grid=(KVH,),
        in_specs=[
            pl.BlockSpec(memory_space=pltpu.SMEM),
            group_spec,
            pair_spec,
            pair_spec,
            group_spec,
            lse_spec,
            group_spec,
        ],
        out_specs=[group_spec, pair_spec, pair_spec],
        out_shape=[
            jax.ShapeDtypeStruct((HQ * HD, rows), BF16),
            jax.ShapeDtypeStruct((KVH * HD, total_rows), F32),
            jax.ShapeDtypeStruct((KVH * HD, total_rows), F32),
        ],
        compiler_params=pltpu.CompilerParams(vmem_limit_bytes=VMEM_LIMIT),
        cost_estimate=pl.CostEstimate(
            flops=10 * HQ * HD * rows * total_rows,
            bytes_accessed=16 * HQ * HD * rows,
            transcendentals=HQ * rows * total_rows,
        ),
        name="attend_back",
    )(index, queries, keys, values, results, lse, grads)


def hidden_kernel(own_x_ref, own_c_ref, other_x_ref, other_c_ref, weight_ref, down_ref, *refs):
    hidden_ref, grads_ref, hidden_t_ref, grads_t_ref, all_x_ref, all_c_ref = refs[-6:]
    units = down_ref.shape[0]
    half = units // HALVES

    def work(x_ref, c_ref):
        x = x_ref[...]
        c = c_ref[...]
        all_x_ref[...] = x
        all_c_ref[...] = c
        for h in range(HALVES):
            part = slice(h * half, (h + 1) * half)
            up_part = slice(units + h * half, units + (h + 1) * half)
            gate = dot(x, weight_ref[:, part], 1, 0)
            up = dot(x, weight_ref[:, up_part], 1, 0)
            grad_hidden = dot(c, down_ref[part, :], 1, 1)
            sigmoid = 0.5 * jnp.tanh(0.5 * gate) + 0.5
            silu = gate * sigmoid
            hidden = (silu * up).astype(BF16)
            grad_up = (grad_hidden * silu).astype(BF16)
            grad_gate = (grad_hidden * up * (sigmoid + silu * (1.0 - sigmoid))).astype(BF16)
            hidden_ref[:, part] = hidden
            grads_ref[:, part] = grad_gate
            grads_ref[:, up_part] = grad_up
            hidden_t_ref[part, :] = hidden.T
            grads_t_ref[part, :] = grad_gate.T
            grads_t_ref[up_part, :] = grad_up.T

    pl.when(pl.program_id(0) == 0)(lambda: work(own_x_ref, own_c_ref))
    pl.when(pl.program_id(0) == 1)(lambda: work(other_x_ref, other_c_ref))


def hidden_step(n, count, rows, pieces, weights, w_down, so_far):
    depth = w_down.shape[1]
    units = w_down.shape[0]
    once = pl.Buffered(1)
    read = [
        pl.BlockSpec((rows, depth), lambda i, block=block: (block, 0), pipeline_mode=once)
        for _, block in pieces
    ]
    widths = (units, 2 * units)
    upright = [(count, width) for width in widths]
    turned = [(width, count) for width in widths]
    whole = [(count, depth)] * 2
    flops = 12 * rows * depth * units
    return pl.pallas_call(
        hidden_kernel,
        grid=(2,),
        in_specs=read
        + [
            pl.BlockSpec((depth, 2 * units), lambda i: (0, 0), pipeline_mode=once),
            pl.BlockSpec((units, depth), lambda i: (0, 0), pipeline_mode=once),
        ]
        + [pl.BlockSpec(memory_space=pl.ANY)] * len(so_far),
        out_specs=[pl.BlockSpec((rows, shape[1]), lambda i: (2 * n + i, 0)) for shape in upright]
        + [pl.BlockSpec((shape[0], rows), lambda i: (0, 2 * n + i)) for shape in turned]
        + [pl.BlockSpec((rows, shape[1]), lambda i: (2 * n + i, 0)) for shape in whole],
        out_shape=[jax.ShapeDtypeStruct(shape, BF16) for shape in upright + turned + whole],
        input_output_aliases={6 + k: k for k in range(len(so_far))},
        compiler_params=pltpu.CompilerParams(vmem_limit_bytes=VMEM_LIMIT),
        cost_estimate=pl.CostEstimate(
            flops=flops,
            bytes_accessed=16 * rows * depth + 24 * rows * units + 6 * depth * units,
            transcendentals=2 * rows * units,
        ),
        name="hidden_step",
    )(*[array for array, _ in pieces], weights, w_down, *so_far)


def rows_kernel(me_ref, left_ref, right_ref, result_ref, *, right_dim):
    result_ref[...] = dot(left_ref[...], right_ref[...], 1, right_dim).astype(BF16)


def rows_product(me, left, right, right_dim, block_rows, name):
    count, width = left.shape
    return pl.pallas_call(
        functools.partial(rows_kernel, right_dim=right_dim),
        grid_spec=pltpu.PrefetchScalarGridSpec(
            num_scalar_prefetch=1,
            grid=(count // block_rows,),
            in_specs=[
                pl.BlockSpec((block_rows, width), lambda i, me_ref: (i, 0)),
                pl.BlockSpec(
                    right.shape, lambda i, me_ref: (0, 0), pipeline_mode=pl.Buffered(1)
                ),
            ],
            out_specs=pl.BlockSpec((block_rows, D), lambda i, me_ref: (me_ref[0] ^ i, 0)),
        ),
        out_shape=jax.ShapeDtypeStruct((count, D), BF16),
        compiler_params=pltpu.CompilerParams(vmem_limit_bytes=VMEM_LIMIT),
        cost_estimate=pl.CostEstimate(
            flops=2 * count * D * width,
            bytes_accessed=2 * (count * width + count * D + D * width),
            transcendentals=0,
        ),
        name=name,
    )(me, left, right)


def weight_kernel(left_ref, right_ref, *result_refs, parts):
    total = dot(left_ref[...], right_ref[...], 1, 0)
    half = total.shape[0] // HALVES
    for h, result_ref in enumerate(result_refs):
        piece = total[h * half : (h + 1) * half]
        if parts == 0:
            result_ref[0] = piece.astype(BF16)
            continue
        wide = piece.shape[1] // parts
        for p in range(parts):
            result_ref[p] = piece[:, p * wide : (p + 1) * wide].astype(BF16).T


def weight_product(left, right, first, units, wide, name):
    depth = left.shape[1]
    half = units // HALVES
    column = min(512, D)
    parts = column // wide if wide else 0
    block = first // units
    if wide:
        out_spec = pl.BlockSpec((parts, wide, half), lambda j: (j, 0, 0))
        out_shape = jax.ShapeDtypeStruct((D // wide, wide, half), BF16)
    else:
        out_spec = pl.BlockSpec((1, half, column), lambda j: (j, 0, 0))
        out_shape = jax.ShapeDtypeStruct((D // column, half, column), BF16)
    return pl.pallas_call(
        functools.partial(weight_kernel, parts=parts),
        grid=(D // column,),
        in_specs=[
            pl.BlockSpec((units, depth), lambda j: (block, 0), pipeline_mode=pl.Buffered(1)),
            pl.BlockSpec((depth, column), lambda j: (0, j)),
        ],
        out_specs=[out_spec] * HALVES,
        out_shape=[out_shape] * HALVES,
        compiler_params=pltpu.CompilerParams(vmem_limit_bytes=VMEM_LIMIT),
        cost_estimate=pl.CostEstimate(
            flops=2 * units * depth * D,
            bytes_accessed=2 * depth * (units + D) + 2 * units * D,
            transcendentals=0,
        ),
        name=name,
    )(left, right)


def merge_kernel(even_ref, *refs):
    result_ref = refs[-1]
    piece = result_ref.shape[1] // (2 * SWAPS)
    for h in range(SWAPS):
        mine, theirs = refs[h][...], refs[SWAPS + h][...]
        gate = jnp.where(even_ref[0] > 0, mine, theirs)
        up = jnp.where(even_ref[0] > 0, theirs, mine)
        result_ref[:, h * piece : (h + 1) * piece] = gate
        result_ref[:, (SWAPS + h) * piece : (SWAPS + h + 1) * piece] = up


def merge_columns(even, mine, theirs):
    rows, piece = mine[0].shape
    tile = min(256, rows)
    return pl.pallas_call(
        merge_kernel,
        grid=(rows // tile,),
        in_specs=[pl.BlockSpec(memory_space=pltpu.SMEM)]
        + [pl.BlockSpec((tile, piece), lambda i: (i, 0))] * (2 * SWAPS),
        out_specs=pl.BlockSpec((tile, 2 * SWAPS * piece), lambda i: (i, 0)),
        out_shape=jax.ShapeDtypeStruct((rows, 2 * SWAPS * piece), BF16),
        compiler_params=pltpu.CompilerParams(vmem_limit_bytes=VMEM_LIMIT),
        cost_estimate=pl.CostEstimate(
            flops=0, bytes_accessed=8 * rows * SWAPS * piece, transcendentals=0
        ),
        name="merge_columns",
    )(even.astype(jnp.int32).reshape(1), *mine, *theirs)


def pack_kernel(even_ref, first_ref, second_ref, result_ref):
    chosen = jnp.where(even_ref[0] > 0, first_ref[...], second_ref[...])
    width = result_ref.shape[-1]
    for h in range(SWAPS):
        result_ref[0, h] = chosen[:, h * width : (h + 1) * width]


def pack_columns(even, first, second, parts):
    rows, columns = first.shape
    width = columns // parts
    block = pl.BlockSpec((rows, width), lambda i: (0, i))
    piece = width // SWAPS
    return pl.pallas_call(
        pack_kernel,
        grid=(parts,),
        in_specs=[pl.BlockSpec(memory_space=pltpu.SMEM), block, block],
        out_specs=pl.BlockSpec((1, SWAPS, rows, piece), lambda i: (i, 0, 0, 0)),
        out_shape=jax.ShapeDtypeStruct((parts, SWAPS, rows, piece), BF16),
        compiler_params=pltpu.CompilerParams(vmem_limit_bytes=VMEM_LIMIT),
        cost_estimate=pl.CostEstimate(
            flops=0, bytes_accessed=6 * rows * columns, transcendentals=0
        ),
        name="pack_columns",
    )(even.astype(jnp.int32).reshape(1), first, second)


def unpack_kernel(stacked_ref, result_ref):
    width = stacked_ref.shape[-1]
    for h in range(HALVES):
        result_ref[:, h * width : (h + 1) * width] = stacked_ref[0, h].astype(F32)


def unpack_columns(stacked):
    parts, _, rows, half = stacked.shape
    return pl.pallas_call(
        unpack_kernel,
        grid=(parts,),
        in_specs=[pl.BlockSpec((1, HALVES, rows, half), lambda i: (i, 0, 0, 0))],
        out_specs=pl.BlockSpec((rows, HALVES * half), lambda i: (0, i)),
        out_shape=jax.ShapeDtypeStruct((rows, parts * HALVES * half), F32),
        compiler_params=pltpu.CompilerParams(vmem_limit_bytes=VMEM_LIMIT),
        cost_estimate=pl.CostEstimate(
            flops=0, bytes_accessed=6 * parts * rows * HALVES * half, transcendentals=0
        ),
        name="unpack_columns",
    )(stacked)


def unpack_rows_kernel(*refs):
    result_ref = refs[-1]
    height = refs[0].shape[1]
    for h in range(HALVES):
        result_ref[h * height : (h + 1) * height, :] = refs[h][0].astype(F32)


def unpack_rows(pieces):
    blocks, half, column = pieces[0].shape
    return pl.pallas_call(
        unpack_rows_kernel,
        grid=(blocks,),
        in_specs=[pl.BlockSpec((1, half, column), lambda i: (i, 0, 0))] * HALVES,
        out_specs=pl.BlockSpec((HALVES * half, column), lambda i: (0, i)),
        out_shape=jax.ShapeDtypeStruct((HALVES * half, blocks * column), F32),
        compiler_params=pltpu.CompilerParams(vmem_limit_bytes=VMEM_LIMIT),
        cost_estimate=pl.CostEstimate(
            flops=0, bytes_accessed=6 * blocks * HALVES * half * column, transcendentals=0
        ),
        name="unpack_rows",
    )(*pieces)


class Layout:
    def __init__(self, fsdp_devices, seq_devices, rows_dev):
        self.fsdp = fsdp_devices
        self.seq = seq_devices
        self.chips = fsdp_devices // 2
        self.share = 2 * seq_devices // (2 * MICRO)
        self.near = self.share // 2
        self.piece_rows = rows_dev // self.share
        self.step_rows = rows_dev
        self.rows = LENGTH // self.share

    def flat(self, f, z):
        return f * self.seq + z

    def moved(self, r):
        pairs = []
        for f in range(self.fsdp):
            for z in range(self.seq):
                slot = z ^ r
                micro, j = slot // self.share, slot % self.share
                target_f = (f // 2) * 2 + j % 2
                target_z = (2 * micro + f % 2) * self.near + j // 2
                pairs.append((self.flat(f, z), self.flat(target_f, target_z)))
        return pairs

    def other(self, k):
        return [
            (self.flat(f, z), self.flat(f ^ k, z))
            for f in range(self.fsdp)
            for z in range(self.seq)
        ]

    def across(self, k):
        pairs = []
        for f in range(self.fsdp):
            for z in range(self.seq):
                pairs.append((self.flat(f, z), self.flat(f ^ (k & 1), z ^ (k >> 1))))
        return pairs


def permute(value, pairs):
    return lax.ppermute(value, ("fsdp", "seq"), pairs)


def scatter_rows(layout, values, z, slot):
    parts = values.reshape(layout.seq, layout.piece_rows, values.shape[-1])
    result = jnp.zeros_like(parts)
    for r in range(layout.seq):
        sent = lax.dynamic_index_in_dim(parts, z ^ r, 0, keepdims=False)
        got = permute(sent, layout.moved(r))
        result = lax.dynamic_update_index_in_dim(result, got, slot ^ r, 0)
    return result.reshape(layout.rows, values.shape[-1])


def return_rows(layout, values, f):
    width = values.shape[-1]
    parts = values.reshape(layout.seq, layout.piece_rows, width)
    parts = lax.all_to_all(parts, "seq", split_axis=0, concat_axis=0, tiled=True)
    parts = parts.reshape(MICRO, 2, layout.near, layout.piece_rows, width)
    core = f % 2
    kept = lax.dynamic_index_in_dim(parts, core, 1, keepdims=False)
    sent = lax.dynamic_index_in_dim(parts, 1 - core, 1, keepdims=False)
    got = permute(sent, layout.other(1))
    both = jnp.stack(
        [jnp.where(core == 0, kept, got), jnp.where(core == 0, got, kept)], axis=2
    )
    return both.reshape(MICRO, layout.step_rows, width)


class RowGather:
    def __init__(self, layout, own):
        self.layout = layout
        self.own = {0: own}
        self.sibling = {0: self.move(own, 1)}
        chips = layout.chips
        for n in range(1, 3 if chips == 4 else chips):
            self.own[n] = self.move(own, 2 * n)

    def move(self, value, k):
        return permute(value, self.layout.other(k))

    def after(self, n, *values):
        chips = self.layout.chips
        if n + 1 < chips:
            waiting = {m: value for m, value in self.own.items() if m > n}
            siblings = {m: value for m, value in self.sibling.items() if m > n}
            waiting, siblings, values = lax.optimization_barrier((waiting, siblings, values))
            self.own.update(waiting)
            self.sibling.update(siblings)
            if chips == 4 and n == 0:
                cut = self.own[0].shape[0] // 2
                self.far = [self.move(self.own[2][:cut], 2), self.move(self.own[1][cut:], 4)]
            if chips == 4 and n == 1:
                self.far = lax.optimization_barrier((self.far, values))[0]
                self.own[3] = jnp.concatenate(self.far)
            for m in (n + 1, n + 2):
                if m in self.own and m not in self.sibling:
                    self.sibling[m] = self.move(self.own[m], 1)
        return values


def gather_small(layout, f, own):
    held = own[None]
    k = 1
    while k < layout.fsdp:
        got = permute(held, layout.other(k))
        upper = (f & k) > 0
        held = jnp.concatenate(
            [jnp.where(upper, got, held), jnp.where(upper, held, got)], axis=0
        )
        k *= 2
    return held


def sum_small(layout, value):
    k = 1
    while k < layout.fsdp:
        value = value + permute(value, layout.other(k))
        k *= 2
    return value


class LinePipe:
    def __init__(self, z, seq_devices):
        self.seq = seq_devices
        self.z = z
        self.outer = (z == 0) | (z == seq_devices - 1)
        self.flying = []
        self.results = {}

    def send(self, stage, value):
        half, last = self.seq // 2, self.seq - 1
        if stage < half - 1:
            pairs = [(stage, stage + 1), (last - stage, last - stage - 1)]
        elif stage == half - 1:
            pairs = [(half - 1, half), (half, half - 1)]
        else:
            s = last - 1 - stage
            pairs = [(s + 1, s), (last - s - 1, last - s)]
        return lax.ppermute(value, "seq", pairs)

    def join(self, stage, value, got):
        if stage < self.seq // 2:
            return value + got
        s = self.seq - 2 - stage
        return jnp.where((self.z == s) | (self.z == self.seq - 1 - s), got, value)

    def step(self, name=None, value=None, others=()):
        arrived = [entry[3] for entry in self.flying]
        arrived, self.results, value, others = lax.optimization_barrier(
            (arrived, self.results, value, others)
        )
        flying = []
        if name is not None:
            flying.append((name, 0, value, self.send(0, value)))
        for (key, stage, held, _), got in zip(self.flying, arrived):
            if stage == self.seq - 2:
                self.results[key] = jnp.where(self.outer, got, held)
                continue
            held = self.join(stage, held, got)
            flying.append((key, stage + 1, held, self.send(stage + 1, held)))
        self.flying = flying
        return others


class PairPipe:
    def __init__(self, z):
        self.outer = (z == 0) | (z == 3)
        self.entered = self.halved = self.summed = None
        self.side = self.across = None
        self.results = {}

    @property
    def flying(self):
        return self.entered or self.halved or self.summed

    def step(self, name=None, value=None, others=()):
        side, across, self.results, value, others = lax.optimization_barrier(
            (self.side, self.across, self.results, value, others)
        )
        entered, halved, summed = self.entered, self.halved, self.summed
        total = halved[1] + across if halved else None
        inward, outward = [(0, 1), (3, 2)], [(1, 0), (2, 3)]
        self.side = self.across = None
        self.entered = self.halved = self.summed = None
        sent = value if total is None else total
        pairs = inward if total is None else outward
        if value is not None and total is not None:
            sent = jnp.where(self.outer, value, total)
            pairs = inward + outward
        if sent is not None:
            self.side = lax.ppermute(sent, "seq", pairs)
        if entered:
            joined = entered[1] + side
            self.across = lax.ppermute(joined, "seq", [(1, 2), (2, 1)])
            self.halved = (entered[0], joined)
        if summed:
            self.results[summed[0]] = jnp.where(self.outer, side, summed[1])
        if halved:
            self.summed = (halved[0], sent)
        if name is not None:
            self.entered = (name, value)
        return others


def body(
    tokens,
    cotangent,
    attn_gain,
    query_gain,
    key_gain,
    w_query,
    w_key,
    w_value,
    w_out,
    ffn_gain,
    w_gate,
    w_up,
    w_down,
):
    fsdp_devices = lax.axis_size("fsdp")
    seq_devices = lax.axis_size("seq")
    layout = Layout(fsdp_devices, seq_devices, tokens.shape[2])
    f = lax.axis_index("fsdp")
    z = lax.axis_index("seq")
    rows = layout.rows
    share = layout.share
    member = (z % layout.near) * 2 + f % 2
    slot = (z // layout.near // 2) * share + member

    w_attn = lax.all_gather(
        jnp.concatenate([w_query, w_key, w_value], axis=1), "fsdp", axis=0, tiled=True
    )
    gains = gather_small(
        layout, f, jnp.concatenate([attn_gain, ffn_gain, query_gain, key_gain])
    ).astype(F32)
    wide, narrow = attn_gain.shape[0], query_gain.shape[0]
    even = z % 2 == 0
    hidden_dev = w_down.shape[0]
    gains, gate_rows, up_rows = lax.optimization_barrier((gains, w_gate, w_up))
    fetched = lax.all_to_all(
        pack_columns(even, gate_rows, up_rows, fsdp_devices),
        "fsdp",
        split_axis=0,
        concat_axis=0,
        tiled=True,
    )
    full_attn_gain = gains[:, :wide].reshape(D)
    full_ffn_gain = gains[:, wide : 2 * wide].reshape(D)
    full_query_gain = gains[:, 2 * wide : 2 * wide + narrow].reshape(HD)
    full_key_gain = gains[:, 2 * wide + narrow :].reshape(HD)
    inputs_low = scatter_rows(layout, tokens[:, 0], z, slot)
    grad_out_low = scatter_rows(layout, cotangent[:, 0], z, slot)
    full_out = lax.all_gather(w_out, "fsdp", axis=0, tiled=True)

    row = jnp.arange(rows, dtype=jnp.int32)
    position = (
        (row // layout.piece_rows) * layout.step_rows
        + member * layout.piece_rows
        + row % layout.piece_rows
    ).astype(F32)
    frequency = THETA ** (-(jnp.arange(HD // 2).astype(F32) * 2.0 / HD))
    angles = frequency[:, None] * position[None, :]
    cosine_table, sine_table = jnp.cos(angles)[None], jnp.sin(angles)[None]
    head_gains = jnp.concatenate(
        [
            jnp.broadcast_to(full_query_gain[None, :, None], (HQ, HD, 1)),
            jnp.broadcast_to(full_key_gain[None, :, None], (KVH, HD, 1)),
        ]
    )

    inputs = inputs_low.astype(F32)
    normed, normed_unit, normed_inverse = rms_fwd(inputs, full_attn_gain)
    fetched = [fetched[:, h].reshape(D, hidden_dev // SWAPS) for h in range(SWAPS)]
    swapped = [
        lax.ppermute(piece, "seq", [(i, i ^ 1) for i in range(seq_devices)]) for piece in fetched
    ]
    normed_low, grad_out_low, w_attn = lax.optimization_barrier(
        (normed.astype(BF16), grad_out_low, w_attn)
    )
    grad_out_gather = RowGather(layout, grad_out_low)
    raw = dot(w_attn, normed_low, 0, 1)
    pair_width = KVH * HD
    turned = HQ + KVH
    head_raw = raw[: turned * HD].reshape(turned, HD, rows)
    head_normed, head_unit, head_inverse = head_rms_fwd(head_raw, head_gains)
    heads_low = rotate(head_normed, cosine_table, sine_table).astype(BF16).reshape(turned * HD, rows)
    queries = heads_low[: HQ * HD]
    own_pair = jnp.concatenate([heads_low[HQ * HD :], raw[turned * HD :].astype(BF16)], axis=0)
    pair_pieces = [own_pair] + [permute(own_pair, layout.across(k)) for k in range(1, share)]
    keys = jnp.concatenate([piece[:pair_width] for piece in pair_pieces], axis=1)
    values = jnp.concatenate([piece[pair_width:] for piece in pair_pieces], axis=1)
    index = member.astype(jnp.int32).reshape(1)
    attended, log_totals = attend(
        index, queries, keys, values, share, layout.piece_rows, layout.step_rows
    )
    attended, swapped[0], grad_out_gather.own = lax.optimization_barrier(
        (attended, swapped[0], grad_out_gather.own)
    )
    middle = inputs + dot(attended, full_out, 0, 0)
    ffn_normed, ffn_unit, ffn_inverse = rms_fwd(middle, full_ffn_gain)
    ffn_low = ffn_normed.astype(BF16)

    ffn_gather = RowGather(layout, ffn_low)
    weights = merge_columns(even, fetched, swapped)
    worked = ()
    for n in range(layout.chips):
        pieces = [
            (side[n], 0)
            for side in (
                ffn_gather.own,
                grad_out_gather.own,
                ffn_gather.sibling,
                grad_out_gather.sibling,
            )
        ]
        worked = hidden_step(n, fsdp_devices * rows, rows, pieces, weights, w_down, worked)
        worked = ffn_gather.after(n, *worked)
        worked = grad_out_gather.after(n, *worked)
    hidden, grads, hidden_t, grads_t, ffn_rows, grad_out_rows = worked
    me = f.astype(jnp.int32).reshape(1)

    def pipe():
        return PairPipe(z) if seq_devices == 4 else LinePipe(z, seq_devices)

    line = pipe()
    late = [pipe() for _ in range(3)]
    waiting = {}
    finished = {}
    tied = []

    def to_owners(name):
        terms = [
            line.results[f"{name}{h}"].reshape(fsdp_devices, wide, -1) for h in range(HALVES)
        ]
        return lax.all_to_all(
            jnp.stack(terms, axis=1), "fsdp", split_axis=0, concat_axis=0, tiled=True
        )

    def advance(name=None, value=None, others=()):
        ties = {key: finished[key] for key in tied}
        ties, others = line.step(name, value, (ties, others))
        finished.update(ties)
        tied.clear()
        for key in ("gate", "up"):
            if key not in finished and all(f"{key}{h}" in line.results for h in range(HALVES)):
                waiting.setdefault(key, functools.partial(to_owners, key))
        if waiting:
            key = next(iter(waiting))
            finished[key] = waiting.pop(key)()
            tied.append(key)
        return others

    def flat(term):
        return term.reshape(-1, term.shape[-1])

    gate_term = weight_product(grads_t, ffn_rows, 0, hidden_dev, wide, "w_gate_grad")
    (grads,) = advance("gate0", flat(gate_term[0]), (grads,))
    grad_ffn_part = rows_product(me, grads, weights, 1, rows, "grad_ffn_normed")
    grad_ffn_part, grads_t, hidden = advance(
        "gate1", flat(gate_term[1]), (grad_ffn_part, grads_t, hidden)
    )
    grad_ffn_normed = lax.psum_scatter(
        grad_ffn_part, "fsdp", scatter_dimension=0, tiled=True
    )
    up_term = weight_product(grads_t, ffn_rows, hidden_dev, hidden_dev, wide, "w_up_grad")
    out_part = rows_product(me, hidden, w_down, 0, rows, "block_out")
    out_part, hidden_t = advance("up0", flat(up_term[0]), (out_part, hidden_t))
    down_term = weight_product(hidden_t, grad_out_rows, 0, hidden_dev, 0, "w_down_grad")
    down_shape = down_term[0].shape
    down_term, grad_ffn_normed = advance(
        "up1", flat(up_term[1]), (down_term, grad_ffn_normed)
    )
    grad_ffn_normed = grad_ffn_normed.astype(F32)

    grad_middle_norm, ffn_gain_term = rms_back(
        grad_ffn_normed, ffn_unit, ffn_inverse, full_ffn_gain
    )
    grad_middle = grad_out_low.astype(F32) + grad_middle_norm
    grad_branch_low = grad_middle.astype(BF16)
    grad_attended = dot(full_out, grad_branch_low, 1, 1).astype(BF16)
    out_term = dot(attended, grad_branch_low, 1, 0).astype(BF16)
    out_rows = lax.psum_scatter(out_term, "fsdp", scatter_dimension=0, tiled=True)
    grad_queries, grad_keys, grad_values = attend_back(
        index,
        queries,
        keys,
        values,
        attended,
        log_totals,
        grad_attended,
        share,
        layout.piece_rows,
        layout.step_rows,
    )
    grad_queries, grad_keys, grad_values, grad_branch_low, out_part = advance(
        "down0",
        flat(down_term[0]),
        (grad_queries, grad_keys, grad_values, grad_branch_low, out_part),
    )
    grad_pair = jnp.concatenate([grad_keys[:, :rows], grad_values[:, :rows]], axis=0)
    for k in range(1, share):
        columns = slice(k * rows, (k + 1) * rows)
        sent = jnp.concatenate([grad_keys[:, columns], grad_values[:, columns]], axis=0)
        grad_pair = grad_pair + permute(sent.astype(BF16), layout.across(k)).astype(F32)
    grad_pair_low = grad_pair.astype(BF16)
    grad_turned = (
        jnp.concatenate([grad_queries, grad_pair_low[:pair_width]], axis=0)
        .astype(F32)
        .reshape(turned, HD, rows)
    )
    grad_head_normed = rotate(grad_turned, cosine_table, -sine_table)
    scaled = grad_head_normed * head_gains
    grad_head_raw = head_inverse * (
        scaled - head_unit * jnp.mean(scaled * head_unit, axis=1, keepdims=True)
    )
    head_gain_terms = jnp.sum(grad_head_normed * head_unit, axis=2)
    grad_raw = jnp.concatenate(
        [grad_head_raw.astype(BF16).reshape(turned * HD, rows), grad_pair_low[pair_width:]], axis=0
    )
    projection_term = dot(normed_low, grad_raw, 0, 1).astype(BF16)
    projection_term, out_part, grad_raw = lax.optimization_barrier(
        (projection_term, out_part, grad_raw)
    )
    projection_rows = lax.psum_scatter(
        projection_term, "fsdp", scatter_dimension=0, tiled=True
    )
    out_sum = lax.psum_scatter(out_part, "fsdp", scatter_dimension=0, tiled=True)
    grad_raw, out_rows = advance("down1", flat(down_term[1]), (grad_raw, out_rows))
    grad_normed = dot(grad_raw, w_attn, 0, 1)
    grad_input_norm, attn_gain_term = rms_back(
        grad_normed, normed_unit, normed_inverse, full_attn_gain
    )

    tokens_grad_low = (grad_middle + grad_input_norm).astype(BF16)
    gain_terms = sum_small(
        layout,
        jnp.concatenate(
            [
                attn_gain_term,
                ffn_gain_term,
                jnp.sum(head_gain_terms[:HQ], axis=0),
                jnp.sum(head_gain_terms[HQ:], axis=0),
            ]
        )[None],
    )[0]

    def own_share(first, count):
        share_of = count // fsdp_devices
        vector = lax.dynamic_slice_in_dim(gain_terms, first + f * share_of, share_of, 0)
        return jnp.pad(vector, (0, wide - share_of))

    gain_columns = jnp.stack(
        [own_share(0, D), own_share(D, D), own_share(2 * D, HD), own_share(2 * D + HD, HD)],
        axis=1,
    )
    gain_columns = jnp.pad(gain_columns, ((0, 0), (0, 128 - gain_columns.shape[1]))).astype(BF16)

    waiting["tokens_grad"] = lambda: return_rows(layout, tokens_grad_low, f)

    tokens_grad_low, gain_columns = advance(others=(tokens_grad_low, gain_columns))
    late[0].step("out", jnp.concatenate([out_rows, gain_columns], axis=1))
    while "gate" not in finished:
        advance()
    w_gate_grad = unpack_columns(finished["gate"])
    projection_rows, w_gate_grad = advance(others=(projection_rows, w_gate_grad))
    late[0].step()
    cut = projection_rows.shape[1] // 256 * 128
    late[1].step("first", projection_rows[:, :cut])
    late[2].step("second", projection_rows[:, cut:])
    (out_sum,) = advance(others=(out_sum,))
    waiting["block_out"] = lambda: return_rows(
        layout, (middle + out_sum.astype(F32)).astype(BF16), f
    )
    while line.flying or waiting or any(pipe.flying for pipe in late):
        for side in late:
            if side.flying:
                side.step()
        advance()
    w_up_grad = unpack_columns(finished["up"])
    w_down_grad = unpack_rows(
        [line.results[f"down{h}"].reshape(down_shape) for h in range(HALVES)]
    )
    block_out, tokens_grad = finished["block_out"], finished["tokens_grad"]

    out_rows = late[0].results["out"]
    attn_rows = jnp.concatenate([late[1].results["first"], late[2].results["second"]], axis=1)
    attn_rows = attn_rows.astype(F32)
    out_rows = out_rows.astype(F32)
    w_out_grad, gain_rows = out_rows[:, :D], out_rows[:, D:]
    query_width = HQ * HD

    return (
        block_out[:, None],
        tokens_grad[:, None],
        gain_rows[:, 0],
        gain_rows[:narrow, 2],
        gain_rows[:narrow, 3],
        attn_rows[:, :query_width],
        attn_rows[:, query_width : query_width + pair_width],
        attn_rows[:, query_width + pair_width : query_width + 2 * pair_width],
        w_out_grad,
        gain_rows[:, 1],
        w_gate_grad,
        w_up_grad,
        w_down_grad,
    )


def solution(mesh):
    activations = P(None, "fsdp", "seq", None)
    vector = P("fsdp")
    matrix = P("fsdp", None)
    specs = (
        (activations, activations)
        + (vector,) * 3
        + (matrix,) * 4
        + (vector,)
        + (matrix,) * 3
    )
    return jax.shard_map(body, mesh=mesh, in_specs=specs, out_specs=specs, check_vma=False)
```

```python
import functools
import math

import jax
import jax.numpy as jnp
from jax import lax
from jax.experimental import pallas as pl
from jax.experimental.pallas import tpu as pltpu
from jax.sharding import PartitionSpec as P

D = 2048
HQ = 32
KVH = 8
HD = 64
FF = 8192
LENGTH = 1024
MICRO = 2
HALVES = 2
SWAPS = 2

EPSILON = 1e-05
THETA = 1000000.0
GROUP = HQ // KVH
BLOCK = 128
SCALE = 1.0 / math.sqrt(HD)
LOG2E = math.log2(math.e)
VMEM_LIMIT = 56 * 1024 * 1024

F32 = jnp.float32
BF16 = jnp.bfloat16


def dot(left_side, right_side, left_dim, right_dim):
    return lax.dot_general(
        left_side,
        right_side,
        (((left_dim,), (right_dim,)), ((), ())),
        preferred_element_type=F32,
    )


def rms_fwd(values, row_gain):
    inverse = lax.rsqrt(jnp.mean(values * values, axis=-1, keepdims=True) + EPSILON)
    unit_rows = values * inverse
    return (unit_rows * row_gain, unit_rows, inverse)


def rms_back(grad_outputs, unit_rows, inverse, row_gain):
    scaled = grad_outputs * row_gain
    grad_inputs = inverse * (
        scaled - unit_rows * jnp.mean(scaled * unit_rows, axis=-1, keepdims=True)
    )
    grad_gain = jnp.sum(grad_outputs * unit_rows, axis=0)
    return (grad_inputs, grad_gain)


def head_rms_fwd(values, gains):
    inverse = lax.rsqrt(jnp.mean(values * values, axis=1, keepdims=True) + EPSILON)
    unit = values * inverse
    return (unit * gains, unit, inverse)


def rotate(values, cosine_table, sine_table):
    half_width = values.shape[1] // 2
    front_half = values[:, :half_width]
    back_half = values[:, half_width:]
    return jnp.concatenate(
        [
            front_half * cosine_table - back_half * sine_table,
            back_half * cosine_table + front_half * sine_table,
        ],
        axis=1,
    )


def block_masks(index, pieces, piece_rows, step_rows):
    key = lax.broadcasted_iota(jnp.int32, (BLOCK, GROUP * BLOCK), 0)
    query = lax.broadcasted_iota(jnp.int32, (BLOCK, GROUP * BLOCK), 1) & (BLOCK - 1)

    def place(row, piece):
        return (row // piece_rows) * step_rows + piece * piece_rows + (row & (piece_rows - 1))

    return [place(key, index ^ k) <= place(query, index) for k in range(pieces)]


def heads_beside(block, first, count):
    return jnp.concatenate(
        [block[h * HD : (h + 1) * HD, first : first + count] for h in range(GROUP)], axis=1
    )


def mask_tail(values, mask, first):
    tail = jnp.where(mask, values[first:], 0.0)
    if first == 0:
        return tail
    return jnp.concatenate([values[:first], tail], axis=0)


def attend_kernel(index_ref, q_ref, k_ref, v_ref, out_ref, lse_ref, *, pieces, piece_rows, step_rows):
    rows = q_ref.shape[1]
    masks = block_masks(index_ref[0], pieces, piece_rows, step_rows)
    queries = q_ref[...]
    for first in range(0, rows, BLOCK):
        count = first + BLOCK
        query_block = heads_beside(queries, first, BLOCK)
        total = None
        result = None
        for k in range(pieces):
            spot = pl.ds(k * rows, count)
            scores = dot(k_ref[:, spot], query_block, 0, 0)
            weights = mask_tail(jnp.exp2(scores * (SCALE * LOG2E)), masks[k], first)
            part = jnp.sum(weights, axis=0, keepdims=True)
            value = dot(v_ref[:, spot], weights.astype(BF16), 1, 0)
            total = part if total is None else total + part
            result = value if result is None else result + value
        result = result * (1.0 / total)
        log_total = jnp.log2(total)
        for h in range(GROUP):
            columns = slice(h * BLOCK, (h + 1) * BLOCK)
            out_ref[h * HD : (h + 1) * HD, first : first + BLOCK] = result[:, columns].astype(BF16)
            lse_ref[0, h : h + 1, first : first + BLOCK] = log_total[:, columns]


def attend_back_kernel(
    index_ref, q_ref, k_ref, v_ref, out_ref, lse_ref, grad_ref, dq_ref, dk_ref, dv_ref,
    *, pieces, piece_rows, step_rows
):
    rows = q_ref.shape[1]
    masks = block_masks(index_ref[0], pieces, piece_rows, step_rows)
    queries = q_ref[...]
    grads = grad_ref[...]
    results = out_ref[...]
    dk_ref[...] = jnp.zeros_like(dk_ref)
    dv_ref[...] = jnp.zeros_like(dv_ref)
    for first in range(0, rows, BLOCK):
        count = first + BLOCK
        query_block = heads_beside(queries, first, BLOCK)
        grad_block = heads_beside(grads, first, BLOCK)
        result_block = heads_beside(results, first, BLOCK)
        centre = jnp.sum(
            grad_block.astype(F32) * result_block.astype(F32), axis=0, keepdims=True
        )
        log_total = jnp.concatenate(
            [lse_ref[0, h : h + 1, first : first + BLOCK] for h in range(GROUP)], axis=1
        )
        dq = None
        for k in range(pieces):
            spot = pl.ds(k * rows, count)
            keys = k_ref[:, spot]
            scores = dot(keys, query_block, 0, 0)
            weights = mask_tail(
                jnp.exp2(scores * (SCALE * LOG2E) - log_total), masks[k], first
            )
            grad_weights = dot(v_ref[:, spot], grad_block, 0, 0)
            grad_scores = (weights * (grad_weights - centre)).astype(BF16)
            part = dot(keys, grad_scores, 1, 0)
            dq = part if dq is None else dq + part
            dk_ref[:, spot] += dot(query_block, grad_scores, 1, 1) * SCALE
            dv_ref[:, spot] += dot(grad_block, weights.astype(BF16), 1, 1)
        dq = (dq * SCALE).astype(BF16)
        for h in range(GROUP):
            columns = slice(h * BLOCK, (h + 1) * BLOCK)
            dq_ref[h * HD : (h + 1) * HD, first : first + BLOCK] = dq[:, columns]


def attention_specs(rows, total_rows):
    group_spec = pl.BlockSpec((GROUP * HD, rows), lambda i: (i, 0))
    pair_spec = pl.BlockSpec((HD, total_rows), lambda i: (i, 0))
    lse_spec = pl.BlockSpec((1, GROUP, rows), lambda i: (i, 0, 0))
    return group_spec, pair_spec, lse_spec


def attend(index, queries, keys, values, pieces, piece_rows, step_rows):
    rows, total_rows = queries.shape[1], keys.shape[1]
    group_spec, pair_spec, lse_spec = attention_specs(rows, total_rows)
    return pl.pallas_call(
        functools.partial(
            attend_kernel, pieces=pieces, piece_rows=piece_rows, step_rows=step_rows
        ),
        grid=(KVH,),
        in_specs=[pl.BlockSpec(memory_space=pltpu.SMEM), group_spec, pair_spec, pair_spec],
        out_specs=[group_spec, lse_spec],
        out_shape=[
            jax.ShapeDtypeStruct((HQ * HD, rows), BF16),
            jax.ShapeDtypeStruct((KVH, GROUP, rows), F32),
        ],
        compiler_params=pltpu.CompilerParams(vmem_limit_bytes=VMEM_LIMIT),
        cost_estimate=pl.CostEstimate(
            flops=4 * HQ * HD * rows * total_rows,
            bytes_accessed=8 * HQ * HD * rows,
            transcendentals=HQ * rows * total_rows,
        ),
        name="attend",
    )(index, queries, keys, values)


def attend_back(index, queries, keys, values, results, lse, grads, pieces, piece_rows, step_rows):
    rows, total_rows = queries.shape[1], keys.shape[1]
    group_spec, pair_spec, lse_spec = attention_specs(rows, total_rows)
    return pl.pallas_call(
        functools.partial(
            attend_back_kernel, pieces=pieces, piece_rows=piece_rows, step_rows=step_rows
        ),
        grid=(KVH,),
        in_specs=[
            pl.BlockSpec(memory_space=pltpu.SMEM),
            group_spec,
            pair_spec,
            pair_spec,
            group_spec,
            lse_spec,
            group_spec,
        ],
        out_specs=[group_spec, pair_spec, pair_spec],
        out_shape=[
            jax.ShapeDtypeStruct((HQ * HD, rows), BF16),
            jax.ShapeDtypeStruct((KVH * HD, total_rows), F32),
            jax.ShapeDtypeStruct((KVH * HD, total_rows), F32),
        ],
        compiler_params=pltpu.CompilerParams(vmem_limit_bytes=VMEM_LIMIT),
        cost_estimate=pl.CostEstimate(
            flops=10 * HQ * HD * rows * total_rows,
            bytes_accessed=16 * HQ * HD * rows,
            transcendentals=HQ * rows * total_rows,
        ),
        name="attend_back",
    )(index, queries, keys, values, results, lse, grads)


def hidden_kernel(own_x_ref, own_c_ref, other_x_ref, other_c_ref, weight_ref, down_ref, *refs):
    hidden_ref, grads_ref, hidden_t_ref, grads_t_ref, all_x_ref, all_c_ref = refs[-6:]
    units = down_ref.shape[0]
    half = units // HALVES

    def work(x_ref, c_ref):
        x = x_ref[...]
        c = c_ref[...]
        all_x_ref[...] = x
        all_c_ref[...] = c
        for h in range(HALVES):
            part = slice(h * half, (h + 1) * half)
            up_part = slice(units + h * half, units + (h + 1) * half)
            gate = dot(x, weight_ref[:, part], 1, 0)
            up = dot(x, weight_ref[:, up_part], 1, 0)
            grad_hidden = dot(c, down_ref[part, :], 1, 1)
            sigmoid = 0.5 * jnp.tanh(0.5 * gate) + 0.5
            silu = gate * sigmoid
            hidden = (silu * up).astype(BF16)
            grad_up = (grad_hidden * silu).astype(BF16)
            grad_gate = (grad_hidden * up * (sigmoid + silu * (1.0 - sigmoid))).astype(BF16)
            hidden_ref[:, part] = hidden
            grads_ref[:, part] = grad_gate
            grads_ref[:, up_part] = grad_up
            hidden_t_ref[part, :] = hidden.T
            grads_t_ref[part, :] = grad_gate.T
            grads_t_ref[up_part, :] = grad_up.T

    pl.when(pl.program_id(0) == 0)(lambda: work(own_x_ref, own_c_ref))
    pl.when(pl.program_id(0) == 1)(lambda: work(other_x_ref, other_c_ref))


def hidden_step(n, count, rows, pieces, weights, w_down, so_far):
    depth = w_down.shape[1]
    units = w_down.shape[0]
    once = pl.Buffered(1)
    read = [
        pl.BlockSpec((rows, depth), lambda i, block=block: (block, 0), pipeline_mode=once)
        for _, block in pieces
    ]
    widths = (units, 2 * units)
    upright = [(count, width) for width in widths]
    turned = [(width, count) for width in widths]
    whole = [(count, depth)] * 2
    flops = 12 * rows * depth * units
    return pl.pallas_call(
        hidden_kernel,
        grid=(2,),
        in_specs=read
        + [
            pl.BlockSpec((depth, 2 * units), lambda i: (0, 0), pipeline_mode=once),
            pl.BlockSpec((units, depth), lambda i: (0, 0), pipeline_mode=once),
        ]
        + [pl.BlockSpec(memory_space=pl.ANY)] * len(so_far),
        out_specs=[pl.BlockSpec((rows, shape[1]), lambda i: (2 * n + i, 0)) for shape in upright]
        + [pl.BlockSpec((shape[0], rows), lambda i: (0, 2 * n + i)) for shape in turned]
        + [pl.BlockSpec((rows, shape[1]), lambda i: (2 * n + i, 0)) for shape in whole],
        out_shape=[jax.ShapeDtypeStruct(shape, BF16) for shape in upright + turned + whole],
        input_output_aliases={6 + k: k for k in range(len(so_far))},
        compiler_params=pltpu.CompilerParams(vmem_limit_bytes=VMEM_LIMIT),
        cost_estimate=pl.CostEstimate(
            flops=flops,
            bytes_accessed=16 * rows * depth + 24 * rows * units + 6 * depth * units,
            transcendentals=2 * rows * units,
        ),
        name="hidden_step",
    )(*[array for array, _ in pieces], weights, w_down, *so_far)


def rows_kernel(me_ref, left_ref, right_ref, result_ref, *, right_dim):
    result_ref[...] = dot(left_ref[...], right_ref[...], 1, right_dim).astype(BF16)


def rows_product(me, left, right, right_dim, block_rows, name):
    count, width = left.shape
    return pl.pallas_call(
        functools.partial(rows_kernel, right_dim=right_dim),
        grid_spec=pltpu.PrefetchScalarGridSpec(
            num_scalar_prefetch=1,
            grid=(count // block_rows,),
            in_specs=[
                pl.BlockSpec((block_rows, width), lambda i, me_ref: (i, 0)),
                pl.BlockSpec(
                    right.shape, lambda i, me_ref: (0, 0), pipeline_mode=pl.Buffered(1)
                ),
            ],
            out_specs=pl.BlockSpec((block_rows, D), lambda i, me_ref: (me_ref[0] ^ i, 0)),
        ),
        out_shape=jax.ShapeDtypeStruct((count, D), BF16),
        compiler_params=pltpu.CompilerParams(vmem_limit_bytes=VMEM_LIMIT),
        cost_estimate=pl.CostEstimate(
            flops=2 * count * D * width,
            bytes_accessed=2 * (count * width + count * D + D * width),
            transcendentals=0,
        ),
        name=name,
    )(me, left, right)


def weight_kernel(left_ref, right_ref, *result_refs, parts):
    total = dot(left_ref[...], right_ref[...], 1, 0)
    half = total.shape[0] // HALVES
    for h, result_ref in enumerate(result_refs):
        piece = total[h * half : (h + 1) * half]
        if parts == 0:
            result_ref[0] = piece.astype(BF16)
            continue
        wide = piece.shape[1] // parts
        for p in range(parts):
            result_ref[p] = piece[:, p * wide : (p + 1) * wide].astype(BF16).T


def weight_product(left, right, first, units, wide, name):
    depth = left.shape[1]
    half = units // HALVES
    column = min(512, D)
    parts = column // wide if wide else 0
    block = first // units
    if wide:
        out_spec = pl.BlockSpec((parts, wide, half), lambda j: (j, 0, 0))
        out_shape = jax.ShapeDtypeStruct((D // wide, wide, half), BF16)
    else:
        out_spec = pl.BlockSpec((1, half, column), lambda j: (j, 0, 0))
        out_shape = jax.ShapeDtypeStruct((D // column, half, column), BF16)
    return pl.pallas_call(
        functools.partial(weight_kernel, parts=parts),
        grid=(D // column,),
        in_specs=[
            pl.BlockSpec((units, depth), lambda j: (block, 0), pipeline_mode=pl.Buffered(1)),
            pl.BlockSpec((depth, column), lambda j: (0, j)),
        ],
        out_specs=[out_spec] * HALVES,
        out_shape=[out_shape] * HALVES,
        compiler_params=pltpu.CompilerParams(vmem_limit_bytes=VMEM_LIMIT),
        cost_estimate=pl.CostEstimate(
            flops=2 * units * depth * D,
            bytes_accessed=2 * depth * (units + D) + 2 * units * D,
            transcendentals=0,
        ),
        name=name,
    )(left, right)


def merge_kernel(even_ref, *refs):
    result_ref = refs[-1]
    piece = result_ref.shape[1] // (2 * SWAPS)
    for h in range(SWAPS):
        mine, theirs = refs[h][...], refs[SWAPS + h][...]
        gate = jnp.where(even_ref[0] > 0, mine, theirs)
        up = jnp.where(even_ref[0] > 0, theirs, mine)
        result_ref[:, h * piece : (h + 1) * piece] = gate
        result_ref[:, (SWAPS + h) * piece : (SWAPS + h + 1) * piece] = up


def merge_columns(even, mine, theirs):
    rows, piece = mine[0].shape
    tile = min(256, rows)
    return pl.pallas_call(
        merge_kernel,
        grid=(rows // tile,),
        in_specs=[pl.BlockSpec(memory_space=pltpu.SMEM)]
        + [pl.BlockSpec((tile, piece), lambda i: (i, 0))] * (2 * SWAPS),
        out_specs=pl.BlockSpec((tile, 2 * SWAPS * piece), lambda i: (i, 0)),
        out_shape=jax.ShapeDtypeStruct((rows, 2 * SWAPS * piece), BF16),
        compiler_params=pltpu.CompilerParams(vmem_limit_bytes=VMEM_LIMIT),
        cost_estimate=pl.CostEstimate(
            flops=0, bytes_accessed=8 * rows * SWAPS * piece, transcendentals=0
        ),
        name="merge_columns",
    )(even.astype(jnp.int32).reshape(1), *mine, *theirs)


def pack_kernel(even_ref, first_ref, second_ref, result_ref):
    chosen = jnp.where(even_ref[0] > 0, first_ref[...], second_ref[...])
    width = result_ref.shape[-1]
    for h in range(SWAPS):
        result_ref[0, h] = chosen[:, h * width : (h + 1) * width]


def pack_columns(even, first, second, parts):
    rows, columns = first.shape
    width = columns // parts
    block = pl.BlockSpec((rows, width), lambda i: (0, i))
    piece = width // SWAPS
    return pl.pallas_call(
        pack_kernel,
        grid=(parts,),
        in_specs=[pl.BlockSpec(memory_space=pltpu.SMEM), block, block],
        out_specs=pl.BlockSpec((1, SWAPS, rows, piece), lambda i: (i, 0, 0, 0)),
        out_shape=jax.ShapeDtypeStruct((parts, SWAPS, rows, piece), BF16),
        compiler_params=pltpu.CompilerParams(vmem_limit_bytes=VMEM_LIMIT),
        cost_estimate=pl.CostEstimate(
            flops=0, bytes_accessed=6 * rows * columns, transcendentals=0
        ),
        name="pack_columns",
    )(even.astype(jnp.int32).reshape(1), first, second)


def unpack_kernel(stacked_ref, result_ref):
    width = stacked_ref.shape[-1]
    for h in range(HALVES):
        result_ref[:, h * width : (h + 1) * width] = stacked_ref[0, h].astype(F32)


def unpack_columns(stacked):
    parts, _, rows, half = stacked.shape
    return pl.pallas_call(
        unpack_kernel,
        grid=(parts,),
        in_specs=[pl.BlockSpec((1, HALVES, rows, half), lambda i: (i, 0, 0, 0))],
        out_specs=pl.BlockSpec((rows, HALVES * half), lambda i: (0, i)),
        out_shape=jax.ShapeDtypeStruct((rows, parts * HALVES * half), F32),
        compiler_params=pltpu.CompilerParams(vmem_limit_bytes=VMEM_LIMIT),
        cost_estimate=pl.CostEstimate(
            flops=0, bytes_accessed=6 * parts * rows * HALVES * half, transcendentals=0
        ),
        name="unpack_columns",
    )(stacked)


def unpack_rows_kernel(*refs):
    result_ref = refs[-1]
    height = refs[0].shape[1]
    for h in range(HALVES):
        result_ref[h * height : (h + 1) * height, :] = refs[h][0].astype(F32)


def unpack_rows(pieces):
    blocks, half, column = pieces[0].shape
    return pl.pallas_call(
        unpack_rows_kernel,
        grid=(blocks,),
        in_specs=[pl.BlockSpec((1, half, column), lambda i: (i, 0, 0))] * HALVES,
        out_specs=pl.BlockSpec((HALVES * half, column), lambda i: (0, i)),
        out_shape=jax.ShapeDtypeStruct((HALVES * half, blocks * column), F32),
        compiler_params=pltpu.CompilerParams(vmem_limit_bytes=VMEM_LIMIT),
        cost_estimate=pl.CostEstimate(
            flops=0, bytes_accessed=6 * blocks * HALVES * half * column, transcendentals=0
        ),
        name="unpack_rows",
    )(*pieces)


class Layout:
    def __init__(self, fsdp_devices, seq_devices, rows_dev):
        self.fsdp = fsdp_devices
        self.seq = seq_devices
        self.chips = fsdp_devices // 2
        self.share = 2 * seq_devices // (2 * MICRO)
        self.near = self.share // 2
        self.piece_rows = rows_dev // self.share
        self.step_rows = rows_dev
        self.rows = LENGTH // self.share

    def flat(self, f, z):
        return f * self.seq + z

    def moved(self, r):
        pairs = []
        for f in range(self.fsdp):
            for z in range(self.seq):
                slot = z ^ r
                micro, j = slot // self.share, slot % self.share
                target_f = (f // 2) * 2 + j % 2
                target_z = (2 * micro + f % 2) * self.near + j // 2
                pairs.append((self.flat(f, z), self.flat(target_f, target_z)))
        return pairs

    def other(self, k):
        return [
            (self.flat(f, z), self.flat(f ^ k, z))
            for f in range(self.fsdp)
            for z in range(self.seq)
        ]

    def across(self, k):
        pairs = []
        for f in range(self.fsdp):
            for z in range(self.seq):
                pairs.append((self.flat(f, z), self.flat(f ^ (k & 1), z ^ (k >> 1))))
        return pairs


def permute(value, pairs):
    return lax.ppermute(value, ("fsdp", "seq"), pairs)


def scatter_rows(layout, values, z, slot):
    parts = values.reshape(layout.seq, layout.piece_rows, values.shape[-1])
    result = jnp.zeros_like(parts)
    for r in range(layout.seq):
        sent = lax.dynamic_index_in_dim(parts, z ^ r, 0, keepdims=False)
        got = permute(sent, layout.moved(r))
        result = lax.dynamic_update_index_in_dim(result, got, slot ^ r, 0)
    return result.reshape(layout.rows, values.shape[-1])


def return_over_seq(layout, values):
    width = values.shape[-1]
    parts = values.reshape(layout.seq, layout.piece_rows, width)
    parts = lax.all_to_all(parts, "seq", split_axis=0, concat_axis=0, tiled=True)
    return parts.reshape(MICRO, 2, layout.near, layout.piece_rows, width)


def return_over_cores(layout, parts, f):
    core = f % 2
    kept = lax.dynamic_index_in_dim(parts, core, 1, keepdims=False)
    sent = lax.dynamic_index_in_dim(parts, 1 - core, 1, keepdims=False)
    got = permute(sent, layout.other(1))
    both = jnp.stack(
        [jnp.where(core == 0, kept, got), jnp.where(core == 0, got, kept)], axis=2
    )
    return both.reshape(MICRO, layout.step_rows, parts.shape[-1])


class RowGather:
    def __init__(self, layout, own):
        self.layout = layout
        self.own = {0: own}
        self.sibling = {0: self.move(own, 1)}
        chips = layout.chips
        for n in range(1, 3 if chips == 4 else chips):
            self.own[n] = self.move(own, 2 * n)

    def move(self, value, k):
        return permute(value, self.layout.other(k))

    def after(self, n, *values):
        chips = self.layout.chips
        if n + 1 < chips:
            waiting = {m: value for m, value in self.own.items() if m > n}
            siblings = {m: value for m, value in self.sibling.items() if m > n}
            waiting, siblings, values = lax.optimization_barrier((waiting, siblings, values))
            self.own.update(waiting)
            self.sibling.update(siblings)
            if chips == 4 and n == 0:
                cut = self.own[0].shape[0] // 2
                self.far = [self.move(self.own[2][:cut], 2), self.move(self.own[1][cut:], 4)]
            if chips == 4 and n == 1:
                self.far = lax.optimization_barrier((self.far, values))[0]
                self.own[3] = jnp.concatenate(self.far)
            for m in (n + 1, n + 2):
                if m in self.own and m not in self.sibling:
                    self.sibling[m] = self.move(self.own[m], 1)
        return values


def gather_small(layout, f, own):
    held = own[None]
    k = 1
    while k < layout.fsdp:
        got = permute(held, layout.other(k))
        upper = (f & k) > 0
        held = jnp.concatenate(
            [jnp.where(upper, got, held), jnp.where(upper, held, got)], axis=0
        )
        k *= 2
    return held


def sum_small(layout, value):
    k = 1
    while k < layout.fsdp:
        value = value + permute(value, layout.other(k))
        k *= 2
    return value


class LinePipe:
    def __init__(self, z, seq_devices):
        self.seq = seq_devices
        self.z = z
        self.outer = (z == 0) | (z == seq_devices - 1)
        self.flying = []
        self.results = {}

    def send(self, stage, value):
        half, last = self.seq // 2, self.seq - 1
        if stage < half - 1:
            pairs = [(stage, stage + 1), (last - stage, last - stage - 1)]
        elif stage == half - 1:
            pairs = [(half - 1, half), (half, half - 1)]
        else:
            s = last - 1 - stage
            pairs = [(s + 1, s), (last - s - 1, last - s)]
        return lax.ppermute(value, "seq", pairs)

    def join(self, stage, value, got):
        if stage < self.seq // 2:
            return value + got
        s = self.seq - 2 - stage
        return jnp.where((self.z == s) | (self.z == self.seq - 1 - s), got, value)

    def step(self, name=None, value=None, others=()):
        arrived = [entry[3] for entry in self.flying]
        arrived, self.results, value, others = lax.optimization_barrier(
            (arrived, self.results, value, others)
        )
        flying = []
        if name is not None:
            flying.append((name, 0, value, self.send(0, value)))
        for (key, stage, held, _), got in zip(self.flying, arrived):
            if stage == self.seq - 2:
                self.results[key] = jnp.where(self.outer, got, held)
                continue
            held = self.join(stage, held, got)
            flying.append((key, stage + 1, held, self.send(stage + 1, held)))
        self.flying = flying
        return others


class PairPipe:
    def __init__(self, z):
        self.outer = (z == 0) | (z == 3)
        self.entered = self.halved = self.summed = None
        self.side = self.across = None
        self.results = {}

    @property
    def flying(self):
        return self.entered or self.halved or self.summed

    def step(self, name=None, value=None, others=()):
        side, across, self.results, value, others = lax.optimization_barrier(
            (self.side, self.across, self.results, value, others)
        )
        entered, halved, summed = self.entered, self.halved, self.summed
        total = halved[1] + across if halved else None
        inward, outward = [(0, 1), (3, 2)], [(1, 0), (2, 3)]
        self.side = self.across = None
        self.entered = self.halved = self.summed = None
        sent = value if total is None else total
        pairs = inward if total is None else outward
        if value is not None and total is not None:
            sent = jnp.where(self.outer, value, total)
            pairs = inward + outward
        if sent is not None:
            self.side = lax.ppermute(sent, "seq", pairs)
        if entered:
            joined = entered[1] + side
            self.across = lax.ppermute(joined, "seq", [(1, 2), (2, 1)])
            self.halved = (entered[0], joined)
        if summed:
            self.results[summed[0]] = jnp.where(self.outer, side, summed[1])
        if halved:
            self.summed = (halved[0], sent)
        if name is not None:
            self.entered = (name, value)
        return others


def body(
    tokens,
    cotangent,
    attn_gain,
    query_gain,
    key_gain,
    w_query,
    w_key,
    w_value,
    w_out,
    ffn_gain,
    w_gate,
    w_up,
    w_down,
):
    fsdp_devices = lax.axis_size("fsdp")
    seq_devices = lax.axis_size("seq")
    layout = Layout(fsdp_devices, seq_devices, tokens.shape[2])
    f = lax.axis_index("fsdp")
    z = lax.axis_index("seq")
    rows = layout.rows
    share = layout.share
    member = (z % layout.near) * 2 + f % 2
    slot = (z // layout.near // 2) * share + member

    w_attn = lax.all_gather(
        jnp.concatenate([w_query, w_key, w_value], axis=1), "fsdp", axis=0, tiled=True
    )
    gains = gather_small(
        layout, f, jnp.concatenate([attn_gain, ffn_gain, query_gain, key_gain])
    ).astype(F32)
    wide, narrow = attn_gain.shape[0], query_gain.shape[0]
    even = z % 2 == 0
    hidden_dev = w_down.shape[0]
    gains, gate_rows, up_rows = lax.optimization_barrier((gains, w_gate, w_up))
    fetched = lax.all_to_all(
        pack_columns(even, gate_rows, up_rows, fsdp_devices),
        "fsdp",
        split_axis=0,
        concat_axis=0,
        tiled=True,
    )
    full_attn_gain = gains[:, :wide].reshape(D)
    full_ffn_gain = gains[:, wide : 2 * wide].reshape(D)
    full_query_gain = gains[:, 2 * wide : 2 * wide + narrow].reshape(HD)
    full_key_gain = gains[:, 2 * wide + narrow :].reshape(HD)
    inputs_low = scatter_rows(layout, tokens[:, 0], z, slot)
    grad_out_low = scatter_rows(layout, cotangent[:, 0], z, slot)
    full_out = lax.all_gather(w_out, "fsdp", axis=0, tiled=True)

    row = jnp.arange(rows, dtype=jnp.int32)
    position = (
        (row // layout.piece_rows) * layout.step_rows
        + member * layout.piece_rows
        + row % layout.piece_rows
    ).astype(F32)
    frequency = THETA ** (-(jnp.arange(HD // 2).astype(F32) * 2.0 / HD))
    angles = frequency[:, None] * position[None, :]
    cosine_table, sine_table = jnp.cos(angles)[None], jnp.sin(angles)[None]
    head_gains = jnp.concatenate(
        [
            jnp.broadcast_to(full_query_gain[None, :, None], (HQ, HD, 1)),
            jnp.broadcast_to(full_key_gain[None, :, None], (KVH, HD, 1)),
        ]
    )

    inputs = inputs_low.astype(F32)
    normed, normed_unit, normed_inverse = rms_fwd(inputs, full_attn_gain)
    fetched = [fetched[:, h].reshape(D, hidden_dev // SWAPS) for h in range(SWAPS)]
    swapped = [
        lax.ppermute(piece, "seq", [(i, i ^ 1) for i in range(seq_devices)]) for piece in fetched
    ]
    normed_low, grad_out_low, w_attn = lax.optimization_barrier(
        (normed.astype(BF16), grad_out_low, w_attn)
    )
    grad_out_gather = RowGather(layout, grad_out_low)
    raw = dot(w_attn, normed_low, 0, 1)
    pair_width = KVH * HD
    turned = HQ + KVH
    head_raw = raw[: turned * HD].reshape(turned, HD, rows)
    head_normed, head_unit, head_inverse = head_rms_fwd(head_raw, head_gains)
    heads_low = rotate(head_normed, cosine_table, sine_table).astype(BF16).reshape(turned * HD, rows)
    queries = heads_low[: HQ * HD]
    own_pair = jnp.concatenate([heads_low[HQ * HD :], raw[turned * HD :].astype(BF16)], axis=0)
    pair_pieces = [own_pair] + [permute(own_pair, layout.across(k)) for k in range(1, share)]
    keys = jnp.concatenate([piece[:pair_width] for piece in pair_pieces], axis=1)
    values = jnp.concatenate([piece[pair_width:] for piece in pair_pieces], axis=1)
    index = member.astype(jnp.int32).reshape(1)
    attended, log_totals = attend(
        index, queries, keys, values, share, layout.piece_rows, layout.step_rows
    )
    attended, swapped[0], grad_out_gather.own = lax.optimization_barrier(
        (attended, swapped[0], grad_out_gather.own)
    )
    middle = inputs + dot(attended, full_out, 0, 0)
    ffn_normed, ffn_unit, ffn_inverse = rms_fwd(middle, full_ffn_gain)
    ffn_low = ffn_normed.astype(BF16)

    ffn_gather = RowGather(layout, ffn_low)
    weights = merge_columns(even, fetched, swapped)
    worked = ()
    for n in range(layout.chips):
        pieces = [
            (side[n], 0)
            for side in (
                ffn_gather.own,
                grad_out_gather.own,
                ffn_gather.sibling,
                grad_out_gather.sibling,
            )
        ]
        worked = hidden_step(n, fsdp_devices * rows, rows, pieces, weights, w_down, worked)
        worked = ffn_gather.after(n, *worked)
        worked = grad_out_gather.after(n, *worked)
    hidden, grads, hidden_t, grads_t, ffn_rows, grad_out_rows = worked
    me = f.astype(jnp.int32).reshape(1)

    def pipe():
        return PairPipe(z) if seq_devices == 4 else LinePipe(z, seq_devices)

    line = pipe()
    late = [pipe() for _ in range(3)]

    def to_owners(name):
        terms = [
            line.results[f"{name}{h}"].reshape(fsdp_devices, wide, -1) for h in range(HALVES)
        ]
        return lax.all_to_all(
            jnp.stack(terms, axis=1), "fsdp", split_axis=0, concat_axis=0, tiled=True
        )

    def advance(name=None, value=None, others=()):
        flights = [getattr(side, "side", None) for side in late]
        flights += [getattr(side, "across", None) for side in late]
        flights, others = line.step(name, value, (flights, others))
        for k, side in enumerate(late):
            if isinstance(side, PairPipe):
                side.side, side.across = flights[k], flights[len(late) + k]
        return others

    def until(name):
        while any(f"{name}{h}" not in line.results for h in range(HALVES)):
            advance()

    def flat(term):
        return term.reshape(-1, term.shape[-1])

    gate_term = weight_product(grads_t, ffn_rows, 0, hidden_dev, wide, "w_gate_grad")
    (grads,) = advance("gate0", flat(gate_term[0]), (grads,))
    grad_ffn_part = rows_product(me, grads, weights, 1, rows, "grad_ffn_normed")
    grad_ffn_part, grads_t, hidden = advance(
        "gate1", flat(gate_term[1]), (grad_ffn_part, grads_t, hidden)
    )
    grad_ffn_normed = lax.psum_scatter(
        grad_ffn_part, "fsdp", scatter_dimension=0, tiled=True
    )
    up_term = weight_product(grads_t, ffn_rows, hidden_dev, hidden_dev, wide, "w_up_grad")
    out_part = rows_product(me, hidden, w_down, 0, rows, "block_out")
    out_part, hidden_t = advance("up0", flat(up_term[0]), (out_part, hidden_t))
    down_term = weight_product(hidden_t, grad_out_rows, 0, hidden_dev, 0, "w_down_grad")
    down_shape = down_term[0].shape
    down_term, grad_ffn_normed = advance(
        "up1", flat(up_term[1]), (down_term, grad_ffn_normed)
    )
    grad_ffn_normed = grad_ffn_normed.astype(F32)

    grad_middle_norm, ffn_gain_term = rms_back(
        grad_ffn_normed, ffn_unit, ffn_inverse, full_ffn_gain
    )
    grad_middle = grad_out_low.astype(F32) + grad_middle_norm
    grad_branch_low = grad_middle.astype(BF16)
    grad_attended = dot(full_out, grad_branch_low, 1, 1).astype(BF16)
    out_term = dot(attended, grad_branch_low, 1, 0).astype(BF16)
    out_rows = lax.psum_scatter(out_term, "fsdp", scatter_dimension=0, tiled=True)
    grad_queries, grad_keys, grad_values = attend_back(
        index,
        queries,
        keys,
        values,
        attended,
        log_totals,
        grad_attended,
        share,
        layout.piece_rows,
        layout.step_rows,
    )
    grad_queries, grad_keys, grad_values, grad_branch_low, out_part = advance(
        "down0",
        flat(down_term[0]),
        (grad_queries, grad_keys, grad_values, grad_branch_low, out_part),
    )
    grad_pair = jnp.concatenate([grad_keys[:, :rows], grad_values[:, :rows]], axis=0)
    for k in range(1, share):
        columns = slice(k * rows, (k + 1) * rows)
        sent = jnp.concatenate([grad_keys[:, columns], grad_values[:, columns]], axis=0)
        grad_pair = grad_pair + permute(sent.astype(BF16), layout.across(k)).astype(F32)
    grad_pair_low = grad_pair.astype(BF16)
    grad_turned = (
        jnp.concatenate([grad_queries, grad_pair_low[:pair_width]], axis=0)
        .astype(F32)
        .reshape(turned, HD, rows)
    )
    grad_head_normed = rotate(grad_turned, cosine_table, -sine_table)
    scaled = grad_head_normed * head_gains
    grad_head_raw = head_inverse * (
        scaled - head_unit * jnp.mean(scaled * head_unit, axis=1, keepdims=True)
    )
    head_gain_terms = jnp.sum(grad_head_normed * head_unit, axis=2)
    grad_raw = jnp.concatenate(
        [grad_head_raw.astype(BF16).reshape(turned * HD, rows), grad_pair_low[pair_width:]], axis=0
    )
    projection_term = dot(normed_low, grad_raw, 0, 1).astype(BF16)
    projection_term, out_part, grad_raw = lax.optimization_barrier(
        (projection_term, out_part, grad_raw)
    )
    projection_rows = lax.psum_scatter(
        projection_term, "fsdp", scatter_dimension=0, tiled=True
    )
    out_sum = lax.psum_scatter(out_part, "fsdp", scatter_dimension=0, tiled=True)
    until("gate")
    gate_all = to_owners("gate")
    grad_raw, out_rows = advance("down1", flat(down_term[1]), (grad_raw, out_rows))
    late[0].step("out", out_rows)
    grad_normed = dot(grad_raw, w_attn, 0, 1)
    grad_input_norm, attn_gain_term = rms_back(
        grad_normed, normed_unit, normed_inverse, full_attn_gain
    )

    tokens_grad_low = (grad_middle + grad_input_norm).astype(BF16)
    gain_terms = sum_small(
        layout,
        jnp.concatenate(
            [
                attn_gain_term,
                ffn_gain_term,
                jnp.sum(head_gain_terms[:HQ], axis=0),
                jnp.sum(head_gain_terms[HQ:], axis=0),
            ]
        )[None],
    )[0]

    def own_share(first, count):
        share_of = count // fsdp_devices
        vector = lax.dynamic_slice_in_dim(gain_terms, first + f * share_of, share_of, 0)
        return jnp.pad(vector, (0, wide - share_of))

    gain_columns = jnp.stack(
        [own_share(0, D), own_share(D, D), own_share(2 * D, HD), own_share(2 * D + HD, HD)],
        axis=1,
    )
    gain_columns = jnp.pad(gain_columns, ((0, 0), (0, 128 - gain_columns.shape[1]))).astype(BF16)


    gate_all, gain_columns = advance(others=(gate_all, gain_columns))
    late[0].step()
    until("up")
    up_all = to_owners("up")
    w_gate_grad = unpack_columns(gate_all)
    projection_rows, w_gate_grad, tokens_grad_low = advance(
        others=(projection_rows, w_gate_grad, tokens_grad_low)
    )
    cut = projection_rows.shape[1] // 256 * 128
    late[1].step("first", projection_rows[:, :cut])
    late[2].step("second", jnp.concatenate([projection_rows[:, cut:], gain_columns], axis=1))
    late[0].step()
    tokens_grad = return_over_seq(layout, tokens_grad_low)
    up_all, tokens_grad = advance(others=(up_all, tokens_grad))
    for side in late:
        side.step()
    tokens_grad = return_over_cores(layout, tokens_grad, f)
    w_up_grad = unpack_columns(up_all)
    until("down")
    w_down_grad = unpack_rows(
        [line.results[f"down{h}"].reshape(down_shape) for h in range(HALVES)]
    )
    tokens_grad, w_up_grad, w_down_grad, middle = advance(
        others=(tokens_grad, w_up_grad, w_down_grad, middle)
    )
    for side in late:
        side.step()
    block_out = return_over_seq(layout, (middle + out_sum.astype(F32)).astype(BF16))
    while any(side.flying for side in late):
        (block_out,) = advance(others=(block_out,))
        for side in late:
            side.step()
    block_out = return_over_cores(layout, block_out, f)

    out_rows = late[0].results["out"]
    attn_rows = jnp.concatenate([late[1].results["first"], late[2].results["second"]], axis=1)
    attn_rows = attn_rows.astype(F32)
    w_out_grad = out_rows.astype(F32)
    gain_rows = attn_rows[:, attn_rows.shape[1] - 128 :]
    query_width = HQ * HD

    return (
        block_out[:, None],
        tokens_grad[:, None],
        gain_rows[:, 0],
        gain_rows[:narrow, 2],
        gain_rows[:narrow, 3],
        attn_rows[:, :query_width],
        attn_rows[:, query_width : query_width + pair_width],
        attn_rows[:, query_width + pair_width : query_width + 2 * pair_width],
        w_out_grad,
        gain_rows[:, 1],
        w_gate_grad,
        w_up_grad,
        w_down_grad,
    )


def solution(mesh):
    activations = P(None, "fsdp", "seq", None)
    vector = P("fsdp")
    matrix = P("fsdp", None)
    specs = (
        (activations, activations)
        + (vector,) * 3
        + (matrix,) * 4
        + (vector,)
        + (matrix,) * 3
    )
    return jax.shard_map(body, mesh=mesh, in_specs=specs, out_specs=specs, check_vma=False)
```

```python
import functools
import math

import jax
import jax.numpy as jnp
from jax import lax
from jax.experimental import pallas as pl
from jax.experimental.pallas import tpu as pltpu
from jax.sharding import PartitionSpec as P

D = 2048
HQ = 32
KVH = 8
HD = 64
FF = 8192
LENGTH = 1024
MICRO = 2
HALVES = 2
SWAPS = 2

EPSILON = 1e-05
THETA = 1000000.0
GROUP = HQ // KVH
BLOCK = 128
SCALE = 1.0 / math.sqrt(HD)
LOG2E = math.log2(math.e)
VMEM_LIMIT = 56 * 1024 * 1024

F32 = jnp.float32
BF16 = jnp.bfloat16


def dot(left_side, right_side, left_dim, right_dim):
    return lax.dot_general(
        left_side,
        right_side,
        (((left_dim,), (right_dim,)), ((), ())),
        preferred_element_type=F32,
    )


def rms_fwd(values, row_gain):
    inverse = lax.rsqrt(jnp.mean(values * values, axis=-1, keepdims=True) + EPSILON)
    unit_rows = values * inverse
    return (unit_rows * row_gain, unit_rows, inverse)


def rms_back(grad_outputs, unit_rows, inverse, row_gain):
    scaled = grad_outputs * row_gain
    grad_inputs = inverse * (
        scaled - unit_rows * jnp.mean(scaled * unit_rows, axis=-1, keepdims=True)
    )
    grad_gain = jnp.sum(grad_outputs * unit_rows, axis=0)
    return (grad_inputs, grad_gain)


def head_rms_fwd(values, gains):
    inverse = lax.rsqrt(jnp.mean(values * values, axis=1, keepdims=True) + EPSILON)
    unit = values * inverse
    return (unit * gains, unit, inverse)


def rotate(values, cosine_table, sine_table):
    half_width = values.shape[1] // 2
    front_half = values[:, :half_width]
    back_half = values[:, half_width:]
    return jnp.concatenate(
        [
            front_half * cosine_table - back_half * sine_table,
            back_half * cosine_table + front_half * sine_table,
        ],
        axis=1,
    )


def block_masks(index, pieces, piece_rows, step_rows):
    key = lax.broadcasted_iota(jnp.int32, (BLOCK, GROUP * BLOCK), 0)
    query = lax.broadcasted_iota(jnp.int32, (BLOCK, GROUP * BLOCK), 1) & (BLOCK - 1)

    def place(row, piece):
        return (row // piece_rows) * step_rows + piece * piece_rows + (row & (piece_rows - 1))

    return [place(key, index ^ k) <= place(query, index) for k in range(pieces)]


def heads_beside(block, first, count):
    return jnp.concatenate(
        [block[h * HD : (h + 1) * HD, first : first + count] for h in range(GROUP)], axis=1
    )


def mask_tail(values, mask, first):
    tail = jnp.where(mask, values[first:], 0.0)
    if first == 0:
        return tail
    return jnp.concatenate([values[:first], tail], axis=0)


def attend_kernel(index_ref, q_ref, k_ref, v_ref, out_ref, lse_ref, *, pieces, piece_rows, step_rows):
    rows = q_ref.shape[1]
    masks = block_masks(index_ref[0], pieces, piece_rows, step_rows)
    queries = q_ref[...]
    for first in range(0, rows, BLOCK):
        count = first + BLOCK
        query_block = heads_beside(queries, first, BLOCK)
        total = None
        result = None
        for k in range(pieces):
            spot = pl.ds(k * rows, count)
            scores = dot(k_ref[:, spot], query_block, 0, 0)
            weights = mask_tail(jnp.exp2(scores * (SCALE * LOG2E)), masks[k], first)
            part = jnp.sum(weights, axis=0, keepdims=True)
            value = dot(v_ref[:, spot], weights.astype(BF16), 1, 0)
            total = part if total is None else total + part
            result = value if result is None else result + value
        result = result * (1.0 / total)
        log_total = jnp.log2(total)
        for h in range(GROUP):
            columns = slice(h * BLOCK, (h + 1) * BLOCK)
            out_ref[h * HD : (h + 1) * HD, first : first + BLOCK] = result[:, columns].astype(BF16)
            lse_ref[0, h : h + 1, first : first + BLOCK] = log_total[:, columns]


def attend_back_kernel(
    index_ref, q_ref, k_ref, v_ref, out_ref, lse_ref, grad_ref, dq_ref, dk_ref, dv_ref,
    *, pieces, piece_rows, step_rows
):
    rows = q_ref.shape[1]
    masks = block_masks(index_ref[0], pieces, piece_rows, step_rows)
    queries = q_ref[...]
    grads = grad_ref[...]
    results = out_ref[...]
    dk_ref[...] = jnp.zeros_like(dk_ref)
    dv_ref[...] = jnp.zeros_like(dv_ref)
    for first in range(0, rows, BLOCK):
        count = first + BLOCK
        query_block = heads_beside(queries, first, BLOCK)
        grad_block = heads_beside(grads, first, BLOCK)
        result_block = heads_beside(results, first, BLOCK)
        centre = jnp.sum(
            grad_block.astype(F32) * result_block.astype(F32), axis=0, keepdims=True
        )
        log_total = jnp.concatenate(
            [lse_ref[0, h : h + 1, first : first + BLOCK] for h in range(GROUP)], axis=1
        )
        dq = None
        for k in range(pieces):
            spot = pl.ds(k * rows, count)
            keys = k_ref[:, spot]
            scores = dot(keys, query_block, 0, 0)
            weights = mask_tail(
                jnp.exp2(scores * (SCALE * LOG2E) - log_total), masks[k], first
            )
            grad_weights = dot(v_ref[:, spot], grad_block, 0, 0)
            grad_scores = (weights * (grad_weights - centre)).astype(BF16)
            part = dot(keys, grad_scores, 1, 0)
            dq = part if dq is None else dq + part
            dk_ref[:, spot] += dot(query_block, grad_scores, 1, 1) * SCALE
            dv_ref[:, spot] += dot(grad_block, weights.astype(BF16), 1, 1)
        dq = (dq * SCALE).astype(BF16)
        for h in range(GROUP):
            columns = slice(h * BLOCK, (h + 1) * BLOCK)
            dq_ref[h * HD : (h + 1) * HD, first : first + BLOCK] = dq[:, columns]


def attention_specs(rows, total_rows):
    group_spec = pl.BlockSpec((GROUP * HD, rows), lambda i: (i, 0))
    pair_spec = pl.BlockSpec((HD, total_rows), lambda i: (i, 0))
    lse_spec = pl.BlockSpec((1, GROUP, rows), lambda i: (i, 0, 0))
    return group_spec, pair_spec, lse_spec


def attend(index, queries, keys, values, pieces, piece_rows, step_rows):
    rows, total_rows = queries.shape[1], keys.shape[1]
    group_spec, pair_spec, lse_spec = attention_specs(rows, total_rows)
    return pl.pallas_call(
        functools.partial(
            attend_kernel, pieces=pieces, piece_rows=piece_rows, step_rows=step_rows
        ),
        grid=(KVH,),
        in_specs=[pl.BlockSpec(memory_space=pltpu.SMEM), group_spec, pair_spec, pair_spec],
        out_specs=[group_spec, lse_spec],
        out_shape=[
            jax.ShapeDtypeStruct((HQ * HD, rows), BF16),
            jax.ShapeDtypeStruct((KVH, GROUP, rows), F32),
        ],
        compiler_params=pltpu.CompilerParams(vmem_limit_bytes=VMEM_LIMIT),
        cost_estimate=pl.CostEstimate(
            flops=4 * HQ * HD * rows * total_rows,
            bytes_accessed=8 * HQ * HD * rows,
            transcendentals=HQ * rows * total_rows,
        ),
        name="attend",
    )(index, queries, keys, values)


def attend_back(index, queries, keys, values, results, lse, grads, pieces, piece_rows, step_rows):
    rows, total_rows = queries.shape[1], keys.shape[1]
    group_spec, pair_spec, lse_spec = attention_specs(rows, total_rows)
    return pl.pallas_call(
        functools.partial(
            attend_back_kernel, pieces=pieces, piece_rows=piece_rows, step_rows=step_rows
        ),
        grid=(KVH,),
        in_specs=[
            pl.BlockSpec(memory_space=pltpu.SMEM),
            group_spec,
            pair_spec,
            pair_spec,
            group_spec,
            lse_spec,
            group_spec,
        ],
        out_specs=[group_spec, pair_spec, pair_spec],
        out_shape=[
            jax.ShapeDtypeStruct((HQ * HD, rows), BF16),
            jax.ShapeDtypeStruct((KVH * HD, total_rows), F32),
            jax.ShapeDtypeStruct((KVH * HD, total_rows), F32),
        ],
        compiler_params=pltpu.CompilerParams(vmem_limit_bytes=VMEM_LIMIT),
        cost_estimate=pl.CostEstimate(
            flops=10 * HQ * HD * rows * total_rows,
            bytes_accessed=16 * HQ * HD * rows,
            transcendentals=HQ * rows * total_rows,
        ),
        name="attend_back",
    )(index, queries, keys, values, results, lse, grads)


def hidden_kernel(own_x_ref, own_c_ref, other_x_ref, other_c_ref, weight_ref, down_ref, *refs):
    hidden_ref, grads_ref, hidden_t_ref, grads_t_ref, all_x_ref, all_c_ref = refs[-6:]
    units = down_ref.shape[0]
    half = units // HALVES

    def work(x_ref, c_ref):
        x = x_ref[...]
        c = c_ref[...]
        all_x_ref[...] = x
        all_c_ref[...] = c
        for h in range(HALVES):
            part = slice(h * half, (h + 1) * half)
            up_part = slice(units + h * half, units + (h + 1) * half)
            gate = dot(x, weight_ref[:, part], 1, 0)
            up = dot(x, weight_ref[:, up_part], 1, 0)
            grad_hidden = dot(c, down_ref[part, :], 1, 1)
            sigmoid = 0.5 * jnp.tanh(0.5 * gate) + 0.5
            silu = gate * sigmoid
            hidden = (silu * up).astype(BF16)
            grad_up = (grad_hidden * silu).astype(BF16)
            grad_gate = (grad_hidden * up * (sigmoid + silu * (1.0 - sigmoid))).astype(BF16)
            hidden_ref[:, part] = hidden
            grads_ref[:, part] = grad_gate
            grads_ref[:, up_part] = grad_up
            hidden_t_ref[part, :] = hidden.T
            grads_t_ref[part, :] = grad_gate.T
            grads_t_ref[up_part, :] = grad_up.T

    pl.when(pl.program_id(0) == 0)(lambda: work(own_x_ref, own_c_ref))
    pl.when(pl.program_id(0) == 1)(lambda: work(other_x_ref, other_c_ref))


def hidden_step(n, count, rows, pieces, weights, w_down, so_far):
    depth = w_down.shape[1]
    units = w_down.shape[0]
    once = pl.Buffered(1)
    read = [
        pl.BlockSpec((rows, depth), lambda i, block=block: (block, 0), pipeline_mode=once)
        for _, block in pieces
    ]
    widths = (units, 2 * units)
    upright = [(count, width) for width in widths]
    turned = [(width, count) for width in widths]
    whole = [(count, depth)] * 2
    flops = 12 * rows * depth * units
    return pl.pallas_call(
        hidden_kernel,
        grid=(2,),
        in_specs=read
        + [
            pl.BlockSpec((depth, 2 * units), lambda i: (0, 0), pipeline_mode=once),
            pl.BlockSpec((units, depth), lambda i: (0, 0), pipeline_mode=once),
        ]
        + [pl.BlockSpec(memory_space=pl.ANY)] * len(so_far),
        out_specs=[pl.BlockSpec((rows, shape[1]), lambda i: (2 * n + i, 0)) for shape in upright]
        + [pl.BlockSpec((shape[0], rows), lambda i: (0, 2 * n + i)) for shape in turned]
        + [pl.BlockSpec((rows, shape[1]), lambda i: (2 * n + i, 0)) for shape in whole],
        out_shape=[jax.ShapeDtypeStruct(shape, BF16) for shape in upright + turned + whole],
        input_output_aliases={6 + k: k for k in range(len(so_far))},
        compiler_params=pltpu.CompilerParams(vmem_limit_bytes=VMEM_LIMIT),
        cost_estimate=pl.CostEstimate(
            flops=flops,
            bytes_accessed=16 * rows * depth + 24 * rows * units + 6 * depth * units,
            transcendentals=2 * rows * units,
        ),
        name="hidden_step",
    )(*[array for array, _ in pieces], weights, w_down, *so_far)


def rows_kernel(me_ref, left_ref, right_ref, result_ref, *, right_dim):
    result_ref[...] = dot(left_ref[...], right_ref[...], 1, right_dim).astype(BF16)


def rows_product(me, left, right, right_dim, block_rows, name):
    count, width = left.shape
    return pl.pallas_call(
        functools.partial(rows_kernel, right_dim=right_dim),
        grid_spec=pltpu.PrefetchScalarGridSpec(
            num_scalar_prefetch=1,
            grid=(count // block_rows,),
            in_specs=[
                pl.BlockSpec((block_rows, width), lambda i, me_ref: (i, 0)),
                pl.BlockSpec(
                    right.shape, lambda i, me_ref: (0, 0), pipeline_mode=pl.Buffered(1)
                ),
            ],
            out_specs=pl.BlockSpec((block_rows, D), lambda i, me_ref: (me_ref[0] ^ i, 0)),
        ),
        out_shape=jax.ShapeDtypeStruct((count, D), BF16),
        compiler_params=pltpu.CompilerParams(vmem_limit_bytes=VMEM_LIMIT),
        cost_estimate=pl.CostEstimate(
            flops=2 * count * D * width,
            bytes_accessed=2 * (count * width + count * D + D * width),
            transcendentals=0,
        ),
        name=name,
    )(me, left, right)


def weight_kernel(left_ref, right_ref, *result_refs, parts):
    total = dot(left_ref[...], right_ref[...], 1, 0)
    half = total.shape[0] // HALVES
    for h, result_ref in enumerate(result_refs):
        piece = total[h * half : (h + 1) * half]
        if parts == 0:
            result_ref[0] = piece.astype(BF16)
            continue
        wide = piece.shape[1] // parts
        for p in range(parts):
            result_ref[p] = piece[:, p * wide : (p + 1) * wide].astype(BF16).T


def weight_product(left, right, first, units, wide, name):
    depth = left.shape[1]
    half = units // HALVES
    column = min(512, D)
    parts = column // wide if wide else 0
    block = first // units
    if wide:
        out_spec = pl.BlockSpec((parts, wide, half), lambda j: (j, 0, 0))
        out_shape = jax.ShapeDtypeStruct((D // wide, wide, half), BF16)
    else:
        out_spec = pl.BlockSpec((1, half, column), lambda j: (j, 0, 0))
        out_shape = jax.ShapeDtypeStruct((D // column, half, column), BF16)
    return pl.pallas_call(
        functools.partial(weight_kernel, parts=parts),
        grid=(D // column,),
        in_specs=[
            pl.BlockSpec((units, depth), lambda j: (block, 0), pipeline_mode=pl.Buffered(1)),
            pl.BlockSpec((depth, column), lambda j: (0, j)),
        ],
        out_specs=[out_spec] * HALVES,
        out_shape=[out_shape] * HALVES,
        compiler_params=pltpu.CompilerParams(vmem_limit_bytes=VMEM_LIMIT),
        cost_estimate=pl.CostEstimate(
            flops=2 * units * depth * D,
            bytes_accessed=2 * depth * (units + D) + 2 * units * D,
            transcendentals=0,
        ),
        name=name,
    )(left, right)


def merge_kernel(even_ref, *refs):
    result_ref = refs[-1]
    piece = result_ref.shape[1] // (2 * SWAPS)
    for h in range(SWAPS):
        mine, theirs = refs[h][...], refs[SWAPS + h][...]
        gate = jnp.where(even_ref[0] > 0, mine, theirs)
        up = jnp.where(even_ref[0] > 0, theirs, mine)
        result_ref[:, h * piece : (h + 1) * piece] = gate
        result_ref[:, (SWAPS + h) * piece : (SWAPS + h + 1) * piece] = up


def merge_columns(even, mine, theirs):
    rows, piece = mine[0].shape
    tile = min(256, rows)
    return pl.pallas_call(
        merge_kernel,
        grid=(rows // tile,),
        in_specs=[pl.BlockSpec(memory_space=pltpu.SMEM)]
        + [pl.BlockSpec((tile, piece), lambda i: (i, 0))] * (2 * SWAPS),
        out_specs=pl.BlockSpec((tile, 2 * SWAPS * piece), lambda i: (i, 0)),
        out_shape=jax.ShapeDtypeStruct((rows, 2 * SWAPS * piece), BF16),
        compiler_params=pltpu.CompilerParams(vmem_limit_bytes=VMEM_LIMIT),
        cost_estimate=pl.CostEstimate(
            flops=0, bytes_accessed=8 * rows * SWAPS * piece, transcendentals=0
        ),
        name="merge_columns",
    )(even.astype(jnp.int32).reshape(1), *mine, *theirs)


def pack_kernel(even_ref, first_ref, second_ref, result_ref):
    chosen = jnp.where(even_ref[0] > 0, first_ref[...], second_ref[...])
    width = result_ref.shape[-1]
    for h in range(SWAPS):
        result_ref[0, h] = chosen[:, h * width : (h + 1) * width]


def pack_columns(even, first, second, parts):
    rows, columns = first.shape
    width = columns // parts
    block = pl.BlockSpec((rows, width), lambda i: (0, i))
    piece = width // SWAPS
    return pl.pallas_call(
        pack_kernel,
        grid=(parts,),
        in_specs=[pl.BlockSpec(memory_space=pltpu.SMEM), block, block],
        out_specs=pl.BlockSpec((1, SWAPS, rows, piece), lambda i: (i, 0, 0, 0)),
        out_shape=jax.ShapeDtypeStruct((parts, SWAPS, rows, piece), BF16),
        compiler_params=pltpu.CompilerParams(vmem_limit_bytes=VMEM_LIMIT),
        cost_estimate=pl.CostEstimate(
            flops=0, bytes_accessed=6 * rows * columns, transcendentals=0
        ),
        name="pack_columns",
    )(even.astype(jnp.int32).reshape(1), first, second)


def unpack_kernel(stacked_ref, result_ref):
    width = stacked_ref.shape[-1]
    for h in range(HALVES):
        result_ref[:, h * width : (h + 1) * width] = stacked_ref[0, h].astype(F32)


def unpack_columns(stacked):
    parts, _, rows, half = stacked.shape
    return pl.pallas_call(
        unpack_kernel,
        grid=(parts,),
        in_specs=[pl.BlockSpec((1, HALVES, rows, half), lambda i: (i, 0, 0, 0))],
        out_specs=pl.BlockSpec((rows, HALVES * half), lambda i: (0, i)),
        out_shape=jax.ShapeDtypeStruct((rows, parts * HALVES * half), F32),
        compiler_params=pltpu.CompilerParams(vmem_limit_bytes=VMEM_LIMIT),
        cost_estimate=pl.CostEstimate(
            flops=0, bytes_accessed=6 * parts * rows * HALVES * half, transcendentals=0
        ),
        name="unpack_columns",
    )(stacked)


def unpack_rows_kernel(*refs):
    result_ref = refs[-1]
    height = refs[0].shape[1]
    for h in range(HALVES):
        result_ref[h * height : (h + 1) * height, :] = refs[h][0].astype(F32)


def unpack_rows(pieces):
    blocks, half, column = pieces[0].shape
    return pl.pallas_call(
        unpack_rows_kernel,
        grid=(blocks,),
        in_specs=[pl.BlockSpec((1, half, column), lambda i: (i, 0, 0))] * HALVES,
        out_specs=pl.BlockSpec((HALVES * half, column), lambda i: (0, i)),
        out_shape=jax.ShapeDtypeStruct((HALVES * half, blocks * column), F32),
        compiler_params=pltpu.CompilerParams(vmem_limit_bytes=VMEM_LIMIT),
        cost_estimate=pl.CostEstimate(
            flops=0, bytes_accessed=6 * blocks * HALVES * half * column, transcendentals=0
        ),
        name="unpack_rows",
    )(*pieces)


class Layout:
    def __init__(self, fsdp_devices, seq_devices, rows_dev):
        self.fsdp = fsdp_devices
        self.seq = seq_devices
        self.chips = fsdp_devices // 2
        self.share = 2 * seq_devices // (2 * MICRO)
        self.near = self.share // 2
        self.piece_rows = rows_dev // self.share
        self.step_rows = rows_dev
        self.rows = LENGTH // self.share

    def flat(self, f, z):
        return f * self.seq + z

    def moved(self, r):
        pairs = []
        for f in range(self.fsdp):
            for z in range(self.seq):
                slot = z ^ r
                micro, j = slot // self.share, slot % self.share
                target_f = (f // 2) * 2 + j % 2
                target_z = (2 * micro + f % 2) * self.near + j // 2
                pairs.append((self.flat(f, z), self.flat(target_f, target_z)))
        return pairs

    def other(self, k):
        return [
            (self.flat(f, z), self.flat(f ^ k, z))
            for f in range(self.fsdp)
            for z in range(self.seq)
        ]

    def across(self, k):
        pairs = []
        for f in range(self.fsdp):
            for z in range(self.seq):
                pairs.append((self.flat(f, z), self.flat(f ^ (k & 1), z ^ (k >> 1))))
        return pairs


def permute(value, pairs):
    return lax.ppermute(value, ("fsdp", "seq"), pairs)


def scatter_rows(layout, values, z, slot):
    parts = values.reshape(layout.seq, layout.piece_rows, values.shape[-1])
    result = jnp.zeros_like(parts)
    for r in range(layout.seq):
        sent = lax.dynamic_index_in_dim(parts, z ^ r, 0, keepdims=False)
        got = permute(sent, layout.moved(r))
        result = lax.dynamic_update_index_in_dim(result, got, slot ^ r, 0)
    return result.reshape(layout.rows, values.shape[-1])


def return_over_seq(layout, values):
    width = values.shape[-1]
    parts = values.reshape(layout.seq, layout.piece_rows, width)
    parts = lax.all_to_all(parts, "seq", split_axis=0, concat_axis=0, tiled=True)
    return parts.reshape(MICRO, 2, layout.near, layout.piece_rows, width)


def return_over_cores(layout, parts, f):
    core = f % 2
    kept = lax.dynamic_index_in_dim(parts, core, 1, keepdims=False)
    sent = lax.dynamic_index_in_dim(parts, 1 - core, 1, keepdims=False)
    got = permute(sent, layout.other(1))
    both = jnp.stack(
        [jnp.where(core == 0, kept, got), jnp.where(core == 0, got, kept)], axis=2
    )
    return both.reshape(MICRO, layout.step_rows, parts.shape[-1])


class RowGather:
    def __init__(self, layout, own):
        self.layout = layout
        self.own = {0: own}
        self.sibling = {0: self.move(own, 1)}
        chips = layout.chips
        for n in range(1, 3 if chips == 4 else chips):
            self.own[n] = self.move(own, 2 * n)

    def move(self, value, k):
        return permute(value, self.layout.other(k))

    def after(self, n, *values):
        chips = self.layout.chips
        if n + 1 < chips:
            waiting = {m: value for m, value in self.own.items() if m > n}
            siblings = {m: value for m, value in self.sibling.items() if m > n}
            waiting, siblings, values = lax.optimization_barrier((waiting, siblings, values))
            self.own.update(waiting)
            self.sibling.update(siblings)
            if chips == 4 and n == 0:
                cut = self.own[0].shape[0] // 2
                self.far = [self.move(self.own[2][:cut], 2), self.move(self.own[1][cut:], 4)]
            if chips == 4 and n == 1:
                self.far = lax.optimization_barrier((self.far, values))[0]
                self.own[3] = jnp.concatenate(self.far)
            for m in (n + 1, n + 2):
                if m in self.own and m not in self.sibling:
                    self.sibling[m] = self.move(self.own[m], 1)
        return values


def gather_small(layout, f, own):
    held = own[None]
    k = 1
    while k < layout.fsdp:
        got = permute(held, layout.other(k))
        upper = (f & k) > 0
        held = jnp.concatenate(
            [jnp.where(upper, got, held), jnp.where(upper, held, got)], axis=0
        )
        k *= 2
    return held


def sum_small(layout, value):
    k = 1
    while k < layout.fsdp:
        value = value + permute(value, layout.other(k))
        k *= 2
    return value


class LinePipe:
    def __init__(self, z, seq_devices):
        self.seq = seq_devices
        self.z = z
        self.outer = (z == 0) | (z == seq_devices - 1)
        self.flying = []
        self.results = {}

    def send(self, stage, value):
        half, last = self.seq // 2, self.seq - 1
        if stage < half - 1:
            pairs = [(stage, stage + 1), (last - stage, last - stage - 1)]
        elif stage == half - 1:
            pairs = [(half - 1, half), (half, half - 1)]
        else:
            s = last - 1 - stage
            pairs = [(s + 1, s), (last - s - 1, last - s)]
        return lax.ppermute(value, "seq", pairs)

    def join(self, stage, value, got):
        if stage < self.seq // 2:
            return value + got
        s = self.seq - 2 - stage
        return jnp.where((self.z == s) | (self.z == self.seq - 1 - s), got, value)

    def step(self, name=None, value=None, others=()):
        arrived = [entry[3] for entry in self.flying]
        arrived, self.results, value, others = lax.optimization_barrier(
            (arrived, self.results, value, others)
        )
        flying = []
        if name is not None:
            flying.append((name, 0, value, self.send(0, value)))
        for (key, stage, held, _), got in zip(self.flying, arrived):
            if stage == self.seq - 2:
                self.results[key] = jnp.where(self.outer, got, held)
                continue
            held = self.join(stage, held, got)
            flying.append((key, stage + 1, held, self.send(stage + 1, held)))
        self.flying = flying
        return others


class PairPipe:
    def __init__(self, z):
        self.outer = (z == 0) | (z == 3)
        self.entered = self.halved = self.summed = None
        self.side = self.across = None
        self.results = {}

    @property
    def flying(self):
        return self.entered or self.halved or self.summed

    def step(self, name=None, value=None, others=()):
        side, across, self.results, value, others = lax.optimization_barrier(
            (self.side, self.across, self.results, value, others)
        )
        entered, halved, summed = self.entered, self.halved, self.summed
        total = halved[1] + across if halved else None
        inward, outward = [(0, 1), (3, 2)], [(1, 0), (2, 3)]
        self.side = self.across = None
        self.entered = self.halved = self.summed = None
        sent = value if total is None else total
        pairs = inward if total is None else outward
        if value is not None and total is not None:
            sent = jnp.where(self.outer, value, total)
            pairs = inward + outward
        if sent is not None:
            self.side = lax.ppermute(sent, "seq", pairs)
        if entered:
            joined = entered[1] + side
            self.across = lax.ppermute(joined, "seq", [(1, 2), (2, 1)])
            self.halved = (entered[0], joined)
        if summed:
            self.results[summed[0]] = jnp.where(self.outer, side, summed[1])
        if halved:
            self.summed = (halved[0], sent)
        if name is not None:
            self.entered = (name, value)
        return others


def body(
    tokens,
    cotangent,
    attn_gain,
    query_gain,
    key_gain,
    w_query,
    w_key,
    w_value,
    w_out,
    ffn_gain,
    w_gate,
    w_up,
    w_down,
):
    fsdp_devices = lax.axis_size("fsdp")
    seq_devices = lax.axis_size("seq")
    layout = Layout(fsdp_devices, seq_devices, tokens.shape[2])
    f = lax.axis_index("fsdp")
    z = lax.axis_index("seq")
    rows = layout.rows
    share = layout.share
    member = (z % layout.near) * 2 + f % 2
    slot = (z // layout.near // 2) * share + member

    w_attn = lax.all_gather(
        jnp.concatenate([w_query, w_key, w_value], axis=1), "fsdp", axis=0, tiled=True
    )
    gains = gather_small(
        layout, f, jnp.concatenate([attn_gain, ffn_gain, query_gain, key_gain])
    ).astype(F32)
    wide, narrow = attn_gain.shape[0], query_gain.shape[0]
    even = z % 2 == 0
    hidden_dev = w_down.shape[0]
    gains, gate_rows, up_rows = lax.optimization_barrier((gains, w_gate, w_up))
    fetched = lax.all_to_all(
        pack_columns(even, gate_rows, up_rows, fsdp_devices),
        "fsdp",
        split_axis=0,
        concat_axis=0,
        tiled=True,
    )
    full_attn_gain = gains[:, :wide].reshape(D)
    full_ffn_gain = gains[:, wide : 2 * wide].reshape(D)
    full_query_gain = gains[:, 2 * wide : 2 * wide + narrow].reshape(HD)
    full_key_gain = gains[:, 2 * wide + narrow :].reshape(HD)
    inputs_low = scatter_rows(layout, tokens[:, 0], z, slot)
    grad_out_low = scatter_rows(layout, cotangent[:, 0], z, slot)
    full_out = lax.all_gather(w_out, "fsdp", axis=0, tiled=True)

    row = jnp.arange(rows, dtype=jnp.int32)
    position = (
        (row // layout.piece_rows) * layout.step_rows
        + member * layout.piece_rows
        + row % layout.piece_rows
    ).astype(F32)
    frequency = THETA ** (-(jnp.arange(HD // 2).astype(F32) * 2.0 / HD))
    angles = frequency[:, None] * position[None, :]
    cosine_table, sine_table = jnp.cos(angles)[None], jnp.sin(angles)[None]
    head_gains = jnp.concatenate(
        [
            jnp.broadcast_to(full_query_gain[None, :, None], (HQ, HD, 1)),
            jnp.broadcast_to(full_key_gain[None, :, None], (KVH, HD, 1)),
        ]
    )

    inputs = inputs_low.astype(F32)
    normed, normed_unit, normed_inverse = rms_fwd(inputs, full_attn_gain)
    fetched = [fetched[:, h].reshape(D, hidden_dev // SWAPS) for h in range(SWAPS)]
    swapped = [
        lax.ppermute(piece, "seq", [(i, i ^ 1) for i in range(seq_devices)]) for piece in fetched
    ]
    normed_low, grad_out_low, w_attn = lax.optimization_barrier(
        (normed.astype(BF16), grad_out_low, w_attn)
    )
    grad_out_gather = RowGather(layout, grad_out_low)
    raw = dot(w_attn, normed_low, 0, 1)
    pair_width = KVH * HD
    turned = HQ + KVH
    head_raw = raw[: turned * HD].reshape(turned, HD, rows)
    head_normed, head_unit, head_inverse = head_rms_fwd(head_raw, head_gains)
    heads_low = rotate(head_normed, cosine_table, sine_table).astype(BF16).reshape(turned * HD, rows)
    queries = heads_low[: HQ * HD]
    own_pair = jnp.concatenate([heads_low[HQ * HD :], raw[turned * HD :].astype(BF16)], axis=0)
    pair_pieces = [own_pair] + [permute(own_pair, layout.across(k)) for k in range(1, share)]
    keys = jnp.concatenate([piece[:pair_width] for piece in pair_pieces], axis=1)
    values = jnp.concatenate([piece[pair_width:] for piece in pair_pieces], axis=1)
    index = member.astype(jnp.int32).reshape(1)
    attended, log_totals = attend(
        index, queries, keys, values, share, layout.piece_rows, layout.step_rows
    )
    attended, swapped[0], grad_out_gather.own = lax.optimization_barrier(
        (attended, swapped[0], grad_out_gather.own)
    )
    middle = inputs + dot(attended, full_out, 0, 0)
    ffn_normed, ffn_unit, ffn_inverse = rms_fwd(middle, full_ffn_gain)
    ffn_low = ffn_normed.astype(BF16)

    ffn_gather = RowGather(layout, ffn_low)
    weights = merge_columns(even, fetched, swapped)
    worked = ()
    for n in range(layout.chips):
        pieces = [
            (side[n], 0)
            for side in (
                ffn_gather.own,
                grad_out_gather.own,
                ffn_gather.sibling,
                grad_out_gather.sibling,
            )
        ]
        worked = hidden_step(n, fsdp_devices * rows, rows, pieces, weights, w_down, worked)
        worked = ffn_gather.after(n, *worked)
        worked = grad_out_gather.after(n, *worked)
    hidden, grads, hidden_t, grads_t, ffn_rows, grad_out_rows = worked
    me = f.astype(jnp.int32).reshape(1)

    def pipe():
        return PairPipe(z) if seq_devices == 4 else LinePipe(z, seq_devices)

    line = pipe()
    late = [pipe() for _ in range(4)]

    def to_owners(name):
        terms = [
            line.results[f"{name}{h}"].reshape(fsdp_devices, wide, -1) for h in range(HALVES)
        ]
        return lax.all_to_all(
            jnp.stack(terms, axis=1), "fsdp", split_axis=0, concat_axis=0, tiled=True
        )

    def advance(name=None, value=None, others=()):
        flights = [getattr(side, "side", None) for side in late]
        flights += [getattr(side, "across", None) for side in late]
        flights, others = line.step(name, value, (flights, others))
        for k, side in enumerate(late):
            if isinstance(side, PairPipe):
                side.side, side.across = flights[k], flights[len(late) + k]
        return others

    def until(name):
        while any(f"{name}{h}" not in line.results for h in range(HALVES)):
            advance()

    def flat(term):
        return term.reshape(-1, term.shape[-1])

    gate_term = weight_product(grads_t, ffn_rows, 0, hidden_dev, wide, "w_gate_grad")
    (grads,) = advance("gate0", flat(gate_term[0]), (grads,))
    grad_ffn_part = rows_product(me, grads, weights, 1, rows, "grad_ffn_normed")
    grad_ffn_part, grads_t, hidden = advance(
        "gate1", flat(gate_term[1]), (grad_ffn_part, grads_t, hidden)
    )
    grad_ffn_normed = lax.psum_scatter(
        grad_ffn_part, "fsdp", scatter_dimension=0, tiled=True
    )
    up_term = weight_product(grads_t, ffn_rows, hidden_dev, hidden_dev, wide, "w_up_grad")
    out_part = rows_product(me, hidden, w_down, 0, rows, "block_out")
    out_part, hidden_t = advance("up0", flat(up_term[0]), (out_part, hidden_t))
    down_term = weight_product(hidden_t, grad_out_rows, 0, hidden_dev, 0, "w_down_grad")
    down_shape = down_term[0].shape
    down_term, grad_ffn_normed = advance(
        "up1", flat(up_term[1]), (down_term, grad_ffn_normed)
    )
    grad_ffn_normed = grad_ffn_normed.astype(F32)

    grad_middle_norm, ffn_gain_term = rms_back(
        grad_ffn_normed, ffn_unit, ffn_inverse, full_ffn_gain
    )
    grad_middle = grad_out_low.astype(F32) + grad_middle_norm
    grad_branch_low = grad_middle.astype(BF16)
    grad_attended = dot(full_out, grad_branch_low, 1, 1).astype(BF16)
    out_term = dot(attended, grad_branch_low, 1, 0).astype(BF16)
    out_rows = lax.psum_scatter(out_term, "fsdp", scatter_dimension=0, tiled=True)
    grad_queries, grad_keys, grad_values = attend_back(
        index,
        queries,
        keys,
        values,
        attended,
        log_totals,
        grad_attended,
        share,
        layout.piece_rows,
        layout.step_rows,
    )
    grad_queries, grad_keys, grad_values, grad_branch_low, out_part = advance(
        "down0",
        flat(down_term[0]),
        (grad_queries, grad_keys, grad_values, grad_branch_low, out_part),
    )
    grad_pair = jnp.concatenate([grad_keys[:, :rows], grad_values[:, :rows]], axis=0)
    for k in range(1, share):
        columns = slice(k * rows, (k + 1) * rows)
        sent = jnp.concatenate([grad_keys[:, columns], grad_values[:, columns]], axis=0)
        grad_pair = grad_pair + permute(sent.astype(BF16), layout.across(k)).astype(F32)
    grad_pair_low = grad_pair.astype(BF16)
    grad_turned = (
        jnp.concatenate([grad_queries, grad_pair_low[:pair_width]], axis=0)
        .astype(F32)
        .reshape(turned, HD, rows)
    )
    grad_head_normed = rotate(grad_turned, cosine_table, -sine_table)
    scaled = grad_head_normed * head_gains
    grad_head_raw = head_inverse * (
        scaled - head_unit * jnp.mean(scaled * head_unit, axis=1, keepdims=True)
    )
    head_gain_terms = jnp.sum(grad_head_normed * head_unit, axis=2)
    grad_raw = jnp.concatenate(
        [grad_head_raw.astype(BF16).reshape(turned * HD, rows), grad_pair_low[pair_width:]], axis=0
    )
    projection_term = dot(normed_low, grad_raw, 0, 1).astype(BF16)
    projection_term, out_part, grad_raw = lax.optimization_barrier(
        (projection_term, out_part, grad_raw)
    )
    projection_rows = lax.psum_scatter(
        projection_term, "fsdp", scatter_dimension=0, tiled=True
    )
    out_sum = lax.psum_scatter(out_part, "fsdp", scatter_dimension=0, tiled=True)
    until("gate")
    gate_all = to_owners("gate")
    grad_normed = dot(grad_raw, w_attn, 0, 1)
    grad_input_norm, attn_gain_term = rms_back(
        grad_normed, normed_unit, normed_inverse, full_attn_gain
    )

    tokens_grad_low = (grad_middle + grad_input_norm).astype(BF16)
    gain_terms = sum_small(
        layout,
        jnp.concatenate(
            [
                attn_gain_term,
                ffn_gain_term,
                jnp.sum(head_gain_terms[:HQ], axis=0),
                jnp.sum(head_gain_terms[HQ:], axis=0),
            ]
        )[None],
    )[0]

    def own_share(first, count):
        share_of = count // fsdp_devices
        vector = lax.dynamic_slice_in_dim(gain_terms, first + f * share_of, share_of, 0)
        return jnp.pad(vector, (0, wide - share_of))

    gain_columns = jnp.stack(
        [own_share(0, D), own_share(D, D), own_share(2 * D, HD), own_share(2 * D + HD, HD)],
        axis=1,
    )
    gain_columns = jnp.pad(gain_columns, ((0, 0), (0, 128 - gain_columns.shape[1]))).astype(BF16)


    out_rows, gain_columns, tokens_grad_low = advance(
        "down1", flat(down_term[1]), (out_rows, gain_columns, tokens_grad_low)
    )
    late[0].step("out", out_rows)
    (projection_rows,) = advance(others=(projection_rows,))
    cut = projection_rows.shape[1] // 256 * 128
    late[0].step()
    late[1].step("first", projection_rows[:, :cut])
    late[2].step("second", projection_rows[:, cut:])
    late[3].step("gain", gain_columns)
    until("up")
    up_all = to_owners("up")
    gate_all, tokens_grad_low = advance(others=(gate_all, tokens_grad_low))
    for side in late:
        side.step()
    w_gate_grad = unpack_columns(gate_all)
    tokens_grad = return_over_seq(layout, tokens_grad_low)
    up_all, w_gate_grad, tokens_grad, middle = advance(
        others=(up_all, w_gate_grad, tokens_grad, middle)
    )
    for side in late:
        side.step()
    w_up_grad = unpack_columns(up_all)
    tokens_grad = return_over_cores(layout, tokens_grad, f)
    until("down")
    w_down_grad = unpack_rows(
        [line.results[f"down{h}"].reshape(down_shape) for h in range(HALVES)]
    )
    block_out = return_over_seq(layout, (middle + out_sum.astype(F32)).astype(BF16))
    tokens_grad, w_up_grad, w_down_grad = advance(others=(tokens_grad, w_up_grad, w_down_grad))
    for side in late:
        side.step()
    while any(side.flying for side in late):
        (block_out,) = advance(others=(block_out,))
        for side in late:
            side.step()
    block_out = return_over_cores(layout, block_out, f)

    out_rows = late[0].results["out"]
    attn_rows = jnp.concatenate([late[1].results["first"], late[2].results["second"]], axis=1)
    attn_rows = attn_rows.astype(F32)
    w_out_grad = out_rows.astype(F32)
    gain_rows = late[3].results["gain"].astype(F32)
    query_width = HQ * HD

    return (
        block_out[:, None],
        tokens_grad[:, None],
        gain_rows[:, 0],
        gain_rows[:narrow, 2],
        gain_rows[:narrow, 3],
        attn_rows[:, :query_width],
        attn_rows[:, query_width : query_width + pair_width],
        attn_rows[:, query_width + pair_width : query_width + 2 * pair_width],
        w_out_grad,
        gain_rows[:, 1],
        w_gate_grad,
        w_up_grad,
        w_down_grad,
    )


def solution(mesh):
    activations = P(None, "fsdp", "seq", None)
    vector = P("fsdp")
    matrix = P("fsdp", None)
    specs = (
        (activations, activations)
        + (vector,) * 3
        + (matrix,) * 4
        + (vector,)
        + (matrix,) * 3
    )
    return jax.shard_map(body, mesh=mesh, in_specs=specs, out_specs=specs, check_vma=False)
```

```python
import functools
import math

import jax
import jax.numpy as jnp
from jax import lax
from jax.experimental import pallas as pl
from jax.experimental.pallas import tpu as pltpu
from jax.sharding import PartitionSpec as P

D = 2048
HQ = 32
KVH = 8
HD = 64
FF = 8192
LENGTH = 1024
MICRO = 2
HALVES = 2
SWAPS = 2

EPSILON = 1e-05
THETA = 1000000.0
GROUP = HQ // KVH
BLOCK = 128
SCALE = 1.0 / math.sqrt(HD)
LOG2E = math.log2(math.e)
VMEM_LIMIT = 56 * 1024 * 1024

F32 = jnp.float32
BF16 = jnp.bfloat16


def dot(left_side, right_side, left_dim, right_dim):
    return lax.dot_general(
        left_side,
        right_side,
        (((left_dim,), (right_dim,)), ((), ())),
        preferred_element_type=F32,
    )


def rms_fwd(values, row_gain):
    inverse = lax.rsqrt(jnp.mean(values * values, axis=-1, keepdims=True) + EPSILON)
    unit_rows = values * inverse
    return (unit_rows * row_gain, unit_rows, inverse)


def rms_back(grad_outputs, unit_rows, inverse, row_gain):
    scaled = grad_outputs * row_gain
    grad_inputs = inverse * (
        scaled - unit_rows * jnp.mean(scaled * unit_rows, axis=-1, keepdims=True)
    )
    grad_gain = jnp.sum(grad_outputs * unit_rows, axis=0)
    return (grad_inputs, grad_gain)


def head_rms_fwd(values, gains):
    inverse = lax.rsqrt(jnp.mean(values * values, axis=1, keepdims=True) + EPSILON)
    unit = values * inverse
    return (unit * gains, unit, inverse)


def rotate(values, cosine_table, sine_table):
    half_width = values.shape[1] // 2
    front_half = values[:, :half_width]
    back_half = values[:, half_width:]
    return jnp.concatenate(
        [
            front_half * cosine_table - back_half * sine_table,
            back_half * cosine_table + front_half * sine_table,
        ],
        axis=1,
    )


def block_masks(index, pieces, piece_rows, step_rows):
    key = lax.broadcasted_iota(jnp.int32, (BLOCK, GROUP * BLOCK), 0)
    query = lax.broadcasted_iota(jnp.int32, (BLOCK, GROUP * BLOCK), 1) & (BLOCK - 1)

    def place(row, piece):
        return (row // piece_rows) * step_rows + piece * piece_rows + (row & (piece_rows - 1))

    return [place(key, index ^ k) <= place(query, index) for k in range(pieces)]


def heads_beside(block, first, count):
    return jnp.concatenate(
        [block[h * HD : (h + 1) * HD, first : first + count] for h in range(GROUP)], axis=1
    )


def mask_tail(values, mask, first):
    tail = jnp.where(mask, values[first:], 0.0)
    if first == 0:
        return tail
    return jnp.concatenate([values[:first], tail], axis=0)


def attend_kernel(index_ref, q_ref, k_ref, v_ref, out_ref, lse_ref, *, pieces, piece_rows, step_rows):
    rows = q_ref.shape[1]
    masks = block_masks(index_ref[0], pieces, piece_rows, step_rows)
    queries = q_ref[...]
    for first in range(0, rows, BLOCK):
        count = first + BLOCK
        query_block = heads_beside(queries, first, BLOCK)
        total = None
        result = None
        for k in range(pieces):
            spot = pl.ds(k * rows, count)
            scores = dot(k_ref[:, spot], query_block, 0, 0)
            weights = mask_tail(jnp.exp2(scores * (SCALE * LOG2E)), masks[k], first)
            part = jnp.sum(weights, axis=0, keepdims=True)
            value = dot(v_ref[:, spot], weights.astype(BF16), 1, 0)
            total = part if total is None else total + part
            result = value if result is None else result + value
        result = result * (1.0 / total)
        log_total = jnp.log2(total)
        for h in range(GROUP):
            columns = slice(h * BLOCK, (h + 1) * BLOCK)
            out_ref[h * HD : (h + 1) * HD, first : first + BLOCK] = result[:, columns].astype(BF16)
            lse_ref[0, h : h + 1, first : first + BLOCK] = log_total[:, columns]


def attend_back_kernel(
    index_ref, q_ref, k_ref, v_ref, out_ref, lse_ref, grad_ref, dq_ref, dk_ref, dv_ref,
    *, pieces, piece_rows, step_rows
):
    rows = q_ref.shape[1]
    masks = block_masks(index_ref[0], pieces, piece_rows, step_rows)
    queries = q_ref[...]
    grads = grad_ref[...]
    results = out_ref[...]
    dk_ref[...] = jnp.zeros_like(dk_ref)
    dv_ref[...] = jnp.zeros_like(dv_ref)
    for first in range(0, rows, BLOCK):
        count = first + BLOCK
        query_block = heads_beside(queries, first, BLOCK)
        grad_block = heads_beside(grads, first, BLOCK)
        result_block = heads_beside(results, first, BLOCK)
        centre = jnp.sum(
            grad_block.astype(F32) * result_block.astype(F32), axis=0, keepdims=True
        )
        log_total = jnp.concatenate(
            [lse_ref[0, h : h + 1, first : first + BLOCK] for h in range(GROUP)], axis=1
        )
        dq = None
        for k in range(pieces):
            spot = pl.ds(k * rows, count)
            keys = k_ref[:, spot]
            scores = dot(keys, query_block, 0, 0)
            weights = mask_tail(
                jnp.exp2(scores * (SCALE * LOG2E) - log_total), masks[k], first
            )
            grad_weights = dot(v_ref[:, spot], grad_block, 0, 0)
            grad_scores = (weights * (grad_weights - centre)).astype(BF16)
            part = dot(keys, grad_scores, 1, 0)
            dq = part if dq is None else dq + part
            dk_ref[:, spot] += dot(query_block, grad_scores, 1, 1) * SCALE
            dv_ref[:, spot] += dot(grad_block, weights.astype(BF16), 1, 1)
        dq = (dq * SCALE).astype(BF16)
        for h in range(GROUP):
            columns = slice(h * BLOCK, (h + 1) * BLOCK)
            dq_ref[h * HD : (h + 1) * HD, first : first + BLOCK] = dq[:, columns]


def attention_specs(rows, total_rows):
    group_spec = pl.BlockSpec((GROUP * HD, rows), lambda i: (i, 0))
    pair_spec = pl.BlockSpec((HD, total_rows), lambda i: (i, 0))
    lse_spec = pl.BlockSpec((1, GROUP, rows), lambda i: (i, 0, 0))
    return group_spec, pair_spec, lse_spec


def attend(index, queries, keys, values, pieces, piece_rows, step_rows):
    rows, total_rows = queries.shape[1], keys.shape[1]
    group_spec, pair_spec, lse_spec = attention_specs(rows, total_rows)
    return pl.pallas_call(
        functools.partial(
            attend_kernel, pieces=pieces, piece_rows=piece_rows, step_rows=step_rows
        ),
        grid=(KVH,),
        in_specs=[pl.BlockSpec(memory_space=pltpu.SMEM), group_spec, pair_spec, pair_spec],
        out_specs=[group_spec, lse_spec],
        out_shape=[
            jax.ShapeDtypeStruct((HQ * HD, rows), BF16),
            jax.ShapeDtypeStruct((KVH, GROUP, rows), F32),
        ],
        compiler_params=pltpu.CompilerParams(vmem_limit_bytes=VMEM_LIMIT),
        cost_estimate=pl.CostEstimate(
            flops=4 * HQ * HD * rows * total_rows,
            bytes_accessed=8 * HQ * HD * rows,
            transcendentals=HQ * rows * total_rows,
        ),
        name="attend",
    )(index, queries, keys, values)


def attend_back(index, queries, keys, values, results, lse, grads, pieces, piece_rows, step_rows):
    rows, total_rows = queries.shape[1], keys.shape[1]
    group_spec, pair_spec, lse_spec = attention_specs(rows, total_rows)
    return pl.pallas_call(
        functools.partial(
            attend_back_kernel, pieces=pieces, piece_rows=piece_rows, step_rows=step_rows
        ),
        grid=(KVH,),
        in_specs=[
            pl.BlockSpec(memory_space=pltpu.SMEM),
            group_spec,
            pair_spec,
            pair_spec,
            group_spec,
            lse_spec,
            group_spec,
        ],
        out_specs=[group_spec, pair_spec, pair_spec],
        out_shape=[
            jax.ShapeDtypeStruct((HQ * HD, rows), BF16),
            jax.ShapeDtypeStruct((KVH * HD, total_rows), F32),
            jax.ShapeDtypeStruct((KVH * HD, total_rows), F32),
        ],
        compiler_params=pltpu.CompilerParams(vmem_limit_bytes=VMEM_LIMIT),
        cost_estimate=pl.CostEstimate(
            flops=10 * HQ * HD * rows * total_rows,
            bytes_accessed=16 * HQ * HD * rows,
            transcendentals=HQ * rows * total_rows,
        ),
        name="attend_back",
    )(index, queries, keys, values, results, lse, grads)


def hidden_kernel(own_x_ref, own_c_ref, other_x_ref, other_c_ref, weight_ref, down_ref, *refs):
    hidden_ref, grads_ref, hidden_t_ref, grads_t_ref, all_x_ref, all_c_ref = refs[-6:]
    units = down_ref.shape[0]
    half = units // HALVES

    def work(x_ref, c_ref):
        x = x_ref[...]
        c = c_ref[...]
        all_x_ref[...] = x
        all_c_ref[...] = c
        for h in range(HALVES):
            part = slice(h * half, (h + 1) * half)
            up_part = slice(units + h * half, units + (h + 1) * half)
            gate = dot(x, weight_ref[:, part], 1, 0)
            up = dot(x, weight_ref[:, up_part], 1, 0)
            grad_hidden = dot(c, down_ref[part, :], 1, 1)
            sigmoid = 0.5 * jnp.tanh(0.5 * gate) + 0.5
            silu = gate * sigmoid
            hidden = (silu * up).astype(BF16)
            grad_up = (grad_hidden * silu).astype(BF16)
            grad_gate = (grad_hidden * up * (sigmoid + silu * (1.0 - sigmoid))).astype(BF16)
            hidden_ref[:, part] = hidden
            grads_ref[:, part] = grad_gate
            grads_ref[:, up_part] = grad_up
            hidden_t_ref[part, :] = hidden.T
            grads_t_ref[part, :] = grad_gate.T
            grads_t_ref[up_part, :] = grad_up.T

    pl.when(pl.program_id(0) == 0)(lambda: work(own_x_ref, own_c_ref))
    pl.when(pl.program_id(0) == 1)(lambda: work(other_x_ref, other_c_ref))


def hidden_step(n, count, rows, pieces, weights, w_down, so_far):
    depth = w_down.shape[1]
    units = w_down.shape[0]
    once = pl.Buffered(1)
    read = [
        pl.BlockSpec((rows, depth), lambda i, block=block: (block, 0), pipeline_mode=once)
        for _, block in pieces
    ]
    widths = (units, 2 * units)
    upright = [(count, width) for width in widths]
    turned = [(width, count) for width in widths]
    whole = [(count, depth)] * 2
    flops = 12 * rows * depth * units
    return pl.pallas_call(
        hidden_kernel,
        grid=(2,),
        in_specs=read
        + [
            pl.BlockSpec((depth, 2 * units), lambda i: (0, 0), pipeline_mode=once),
            pl.BlockSpec((units, depth), lambda i: (0, 0), pipeline_mode=once),
        ]
        + [pl.BlockSpec(memory_space=pl.ANY)] * len(so_far),
        out_specs=[pl.BlockSpec((rows, shape[1]), lambda i: (2 * n + i, 0)) for shape in upright]
        + [pl.BlockSpec((shape[0], rows), lambda i: (0, 2 * n + i)) for shape in turned]
        + [pl.BlockSpec((rows, shape[1]), lambda i: (2 * n + i, 0)) for shape in whole],
        out_shape=[jax.ShapeDtypeStruct(shape, BF16) for shape in upright + turned + whole],
        input_output_aliases={6 + k: k for k in range(len(so_far))},
        compiler_params=pltpu.CompilerParams(vmem_limit_bytes=VMEM_LIMIT),
        cost_estimate=pl.CostEstimate(
            flops=flops,
            bytes_accessed=16 * rows * depth + 24 * rows * units + 6 * depth * units,
            transcendentals=2 * rows * units,
        ),
        name="hidden_step",
    )(*[array for array, _ in pieces], weights, w_down, *so_far)


def rows_kernel(me_ref, left_ref, right_ref, result_ref, *, right_dim):
    result_ref[...] = dot(left_ref[...], right_ref[...], 1, right_dim).astype(BF16)


def rows_product(me, left, right, right_dim, block_rows, name):
    count, width = left.shape
    return pl.pallas_call(
        functools.partial(rows_kernel, right_dim=right_dim),
        grid_spec=pltpu.PrefetchScalarGridSpec(
            num_scalar_prefetch=1,
            grid=(count // block_rows,),
            in_specs=[
                pl.BlockSpec((block_rows, width), lambda i, me_ref: (i, 0)),
                pl.BlockSpec(
                    right.shape, lambda i, me_ref: (0, 0), pipeline_mode=pl.Buffered(1)
                ),
            ],
            out_specs=pl.BlockSpec((block_rows, D), lambda i, me_ref: (me_ref[0] ^ i, 0)),
        ),
        out_shape=jax.ShapeDtypeStruct((count, D), BF16),
        compiler_params=pltpu.CompilerParams(vmem_limit_bytes=VMEM_LIMIT),
        cost_estimate=pl.CostEstimate(
            flops=2 * count * D * width,
            bytes_accessed=2 * (count * width + count * D + D * width),
            transcendentals=0,
        ),
        name=name,
    )(me, left, right)


def weight_kernel(left_ref, right_ref, *result_refs, parts):
    total = dot(left_ref[...], right_ref[...], 1, 0)
    half = total.shape[0] // HALVES
    for h, result_ref in enumerate(result_refs):
        piece = total[h * half : (h + 1) * half]
        if parts == 0:
            result_ref[0] = piece.astype(BF16)
            continue
        wide = piece.shape[1] // parts
        for p in range(parts):
            result_ref[p] = piece[:, p * wide : (p + 1) * wide].astype(BF16).T


def weight_product(left, right, first, units, wide, name):
    depth = left.shape[1]
    half = units // HALVES
    column = min(512, D)
    parts = column // wide if wide else 0
    block = first // units
    if wide:
        out_spec = pl.BlockSpec((parts, wide, half), lambda j: (j, 0, 0))
        out_shape = jax.ShapeDtypeStruct((D // wide, wide, half), BF16)
    else:
        out_spec = pl.BlockSpec((1, half, column), lambda j: (j, 0, 0))
        out_shape = jax.ShapeDtypeStruct((D // column, half, column), BF16)
    return pl.pallas_call(
        functools.partial(weight_kernel, parts=parts),
        grid=(D // column,),
        in_specs=[
            pl.BlockSpec((units, depth), lambda j: (block, 0), pipeline_mode=pl.Buffered(1)),
            pl.BlockSpec((depth, column), lambda j: (0, j)),
        ],
        out_specs=[out_spec] * HALVES,
        out_shape=[out_shape] * HALVES,
        compiler_params=pltpu.CompilerParams(vmem_limit_bytes=VMEM_LIMIT),
        cost_estimate=pl.CostEstimate(
            flops=2 * units * depth * D,
            bytes_accessed=2 * depth * (units + D) + 2 * units * D,
            transcendentals=0,
        ),
        name=name,
    )(left, right)


def merge_kernel(even_ref, *refs):
    result_ref = refs[-1]
    piece = result_ref.shape[1] // (2 * SWAPS)
    for h in range(SWAPS):
        mine, theirs = refs[h][...], refs[SWAPS + h][...]
        gate = jnp.where(even_ref[0] > 0, mine, theirs)
        up = jnp.where(even_ref[0] > 0, theirs, mine)
        result_ref[:, h * piece : (h + 1) * piece] = gate
        result_ref[:, (SWAPS + h) * piece : (SWAPS + h + 1) * piece] = up


def merge_columns(even, mine, theirs):
    rows, piece = mine[0].shape
    tile = min(256, rows)
    return pl.pallas_call(
        merge_kernel,
        grid=(rows // tile,),
        in_specs=[pl.BlockSpec(memory_space=pltpu.SMEM)]
        + [pl.BlockSpec((tile, piece), lambda i: (i, 0))] * (2 * SWAPS),
        out_specs=pl.BlockSpec((tile, 2 * SWAPS * piece), lambda i: (i, 0)),
        out_shape=jax.ShapeDtypeStruct((rows, 2 * SWAPS * piece), BF16),
        compiler_params=pltpu.CompilerParams(vmem_limit_bytes=VMEM_LIMIT),
        cost_estimate=pl.CostEstimate(
            flops=0, bytes_accessed=8 * rows * SWAPS * piece, transcendentals=0
        ),
        name="merge_columns",
    )(even.astype(jnp.int32).reshape(1), *mine, *theirs)


def pack_kernel(even_ref, first_ref, second_ref, result_ref):
    chosen = jnp.where(even_ref[0] > 0, first_ref[...], second_ref[...])
    width = result_ref.shape[-1]
    for h in range(SWAPS):
        result_ref[0, h] = chosen[:, h * width : (h + 1) * width]


def pack_columns(even, first, second, parts):
    rows, columns = first.shape
    width = columns // parts
    block = pl.BlockSpec((rows, width), lambda i: (0, i))
    piece = width // SWAPS
    return pl.pallas_call(
        pack_kernel,
        grid=(parts,),
        in_specs=[pl.BlockSpec(memory_space=pltpu.SMEM), block, block],
        out_specs=pl.BlockSpec((1, SWAPS, rows, piece), lambda i: (i, 0, 0, 0)),
        out_shape=jax.ShapeDtypeStruct((parts, SWAPS, rows, piece), BF16),
        compiler_params=pltpu.CompilerParams(vmem_limit_bytes=VMEM_LIMIT),
        cost_estimate=pl.CostEstimate(
            flops=0, bytes_accessed=6 * rows * columns, transcendentals=0
        ),
        name="pack_columns",
    )(even.astype(jnp.int32).reshape(1), first, second)


def unpack_kernel(stacked_ref, result_ref):
    width = stacked_ref.shape[-1]
    for h in range(HALVES):
        result_ref[:, h * width : (h + 1) * width] = stacked_ref[0, h].astype(F32)


def unpack_columns(stacked):
    parts, _, rows, half = stacked.shape
    return pl.pallas_call(
        unpack_kernel,
        grid=(parts,),
        in_specs=[pl.BlockSpec((1, HALVES, rows, half), lambda i: (i, 0, 0, 0))],
        out_specs=pl.BlockSpec((rows, HALVES * half), lambda i: (0, i)),
        out_shape=jax.ShapeDtypeStruct((rows, parts * HALVES * half), F32),
        compiler_params=pltpu.CompilerParams(vmem_limit_bytes=VMEM_LIMIT),
        cost_estimate=pl.CostEstimate(
            flops=0, bytes_accessed=6 * parts * rows * HALVES * half, transcendentals=0
        ),
        name="unpack_columns",
    )(stacked)


def unpack_rows_kernel(*refs):
    result_ref = refs[-1]
    height = refs[0].shape[1]
    for h in range(HALVES):
        result_ref[h * height : (h + 1) * height, :] = refs[h][0].astype(F32)


def unpack_rows(pieces):
    blocks, half, column = pieces[0].shape
    return pl.pallas_call(
        unpack_rows_kernel,
        grid=(blocks,),
        in_specs=[pl.BlockSpec((1, half, column), lambda i: (i, 0, 0))] * HALVES,
        out_specs=pl.BlockSpec((HALVES * half, column), lambda i: (0, i)),
        out_shape=jax.ShapeDtypeStruct((HALVES * half, blocks * column), F32),
        compiler_params=pltpu.CompilerParams(vmem_limit_bytes=VMEM_LIMIT),
        cost_estimate=pl.CostEstimate(
            flops=0, bytes_accessed=6 * blocks * HALVES * half * column, transcendentals=0
        ),
        name="unpack_rows",
    )(*pieces)


class Layout:
    def __init__(self, fsdp_devices, seq_devices, rows_dev):
        self.fsdp = fsdp_devices
        self.seq = seq_devices
        self.chips = fsdp_devices // 2
        self.share = 2 * seq_devices // (2 * MICRO)
        self.near = self.share // 2
        self.piece_rows = rows_dev // self.share
        self.step_rows = rows_dev
        self.rows = LENGTH // self.share

    def flat(self, f, z):
        return f * self.seq + z

    def moved(self, r):
        pairs = []
        for f in range(self.fsdp):
            for z in range(self.seq):
                slot = z ^ r
                micro, j = slot // self.share, slot % self.share
                target_f = (f // 2) * 2 + j % 2
                target_z = (2 * micro + f % 2) * self.near + j // 2
                pairs.append((self.flat(f, z), self.flat(target_f, target_z)))
        return pairs

    def other(self, k):
        return [
            (self.flat(f, z), self.flat(f ^ k, z))
            for f in range(self.fsdp)
            for z in range(self.seq)
        ]

    def across(self, k):
        pairs = []
        for f in range(self.fsdp):
            for z in range(self.seq):
                pairs.append((self.flat(f, z), self.flat(f ^ (k & 1), z ^ (k >> 1))))
        return pairs


def permute(value, pairs):
    return lax.ppermute(value, ("fsdp", "seq"), pairs)


def scatter_rows(layout, values, z, slot):
    parts = values.reshape(layout.seq, layout.piece_rows, values.shape[-1])
    result = jnp.zeros_like(parts)
    for r in range(layout.seq):
        sent = lax.dynamic_index_in_dim(parts, z ^ r, 0, keepdims=False)
        got = permute(sent, layout.moved(r))
        result = lax.dynamic_update_index_in_dim(result, got, slot ^ r, 0)
    return result.reshape(layout.rows, values.shape[-1])


def return_over_seq(layout, values):
    width = values.shape[-1]
    parts = values.reshape(layout.seq, layout.piece_rows, width)
    parts = lax.all_to_all(parts, "seq", split_axis=0, concat_axis=0, tiled=True)
    return parts.reshape(MICRO, 2, layout.near, layout.piece_rows, width)


def return_over_cores(layout, parts, f):
    core = f % 2
    kept = lax.dynamic_index_in_dim(parts, core, 1, keepdims=False)
    sent = lax.dynamic_index_in_dim(parts, 1 - core, 1, keepdims=False)
    got = permute(sent, layout.other(1))
    both = jnp.stack(
        [jnp.where(core == 0, kept, got), jnp.where(core == 0, got, kept)], axis=2
    )
    return both.reshape(MICRO, layout.step_rows, parts.shape[-1])


class RowGather:
    def __init__(self, layout, own):
        self.layout = layout
        self.own = {0: own}
        self.sibling = {0: self.move(own, 1)}
        chips = layout.chips
        for n in range(1, 3 if chips == 4 else chips):
            self.own[n] = self.move(own, 2 * n)

    def move(self, value, k):
        return permute(value, self.layout.other(k))

    def after(self, n, *values):
        chips = self.layout.chips
        if n + 1 < chips:
            waiting = {m: value for m, value in self.own.items() if m > n}
            siblings = {m: value for m, value in self.sibling.items() if m > n}
            waiting, siblings, values = lax.optimization_barrier((waiting, siblings, values))
            self.own.update(waiting)
            self.sibling.update(siblings)
            if chips == 4 and n == 0:
                cut = self.own[0].shape[0] // 2
                self.far = [self.move(self.own[2][:cut], 2), self.move(self.own[1][cut:], 4)]
            if chips == 4 and n == 1:
                self.far = lax.optimization_barrier((self.far, values))[0]
                self.own[3] = jnp.concatenate(self.far)
            for m in (n + 1, n + 2):
                if m in self.own and m not in self.sibling:
                    self.sibling[m] = self.move(self.own[m], 1)
        return values


def gather_small(layout, f, own):
    held = own[None]
    k = 1
    while k < layout.fsdp:
        got = permute(held, layout.other(k))
        upper = (f & k) > 0
        held = jnp.concatenate(
            [jnp.where(upper, got, held), jnp.where(upper, held, got)], axis=0
        )
        k *= 2
    return held


def sum_small(layout, value):
    k = 1
    while k < layout.fsdp:
        value = value + permute(value, layout.other(k))
        k *= 2
    return value


class LinePipe:
    def __init__(self, z, seq_devices):
        self.seq = seq_devices
        self.z = z
        self.outer = (z == 0) | (z == seq_devices - 1)
        self.flying = []
        self.results = {}

    def send(self, stage, value):
        half, last = self.seq // 2, self.seq - 1
        if stage < half - 1:
            pairs = [(stage, stage + 1), (last - stage, last - stage - 1)]
        elif stage == half - 1:
            pairs = [(half - 1, half), (half, half - 1)]
        else:
            s = last - 1 - stage
            pairs = [(s + 1, s), (last - s - 1, last - s)]
        return lax.ppermute(value, "seq", pairs)

    def join(self, stage, value, got):
        if stage < self.seq // 2:
            return value + got
        s = self.seq - 2 - stage
        return jnp.where((self.z == s) | (self.z == self.seq - 1 - s), got, value)

    def step(self, name=None, value=None, others=()):
        arrived = [entry[3] for entry in self.flying]
        arrived, self.results, value, others = lax.optimization_barrier(
            (arrived, self.results, value, others)
        )
        flying = []
        if name is not None:
            flying.append((name, 0, value, self.send(0, value)))
        for (key, stage, held, _), got in zip(self.flying, arrived):
            if stage == self.seq - 2:
                self.results[key] = jnp.where(self.outer, got, held)
                continue
            held = self.join(stage, held, got)
            flying.append((key, stage + 1, held, self.send(stage + 1, held)))
        self.flying = flying
        return others


class PairPipe:
    def __init__(self, z):
        self.outer = (z == 0) | (z == 3)
        self.entered = self.halved = self.summed = None
        self.side = self.across = None
        self.results = {}

    @property
    def flying(self):
        return self.entered or self.halved or self.summed

    def step(self, name=None, value=None, others=()):
        side, across, self.results, value, others = lax.optimization_barrier(
            (self.side, self.across, self.results, value, others)
        )
        entered, halved, summed = self.entered, self.halved, self.summed
        total = halved[1] + across if halved else None
        inward, outward = [(0, 1), (3, 2)], [(1, 0), (2, 3)]
        self.side = self.across = None
        self.entered = self.halved = self.summed = None
        sent = value if total is None else total
        pairs = inward if total is None else outward
        if value is not None and total is not None:
            sent = jnp.where(self.outer, value, total)
            pairs = inward + outward
        if sent is not None:
            self.side = lax.ppermute(sent, "seq", pairs)
        if entered:
            joined = entered[1] + side
            self.across = lax.ppermute(joined, "seq", [(1, 2), (2, 1)])
            self.halved = (entered[0], joined)
        if summed:
            self.results[summed[0]] = jnp.where(self.outer, side, summed[1])
        if halved:
            self.summed = (halved[0], sent)
        if name is not None:
            self.entered = (name, value)
        return others


def body(
    tokens,
    cotangent,
    attn_gain,
    query_gain,
    key_gain,
    w_query,
    w_key,
    w_value,
    w_out,
    ffn_gain,
    w_gate,
    w_up,
    w_down,
):
    fsdp_devices = lax.axis_size("fsdp")
    seq_devices = lax.axis_size("seq")
    layout = Layout(fsdp_devices, seq_devices, tokens.shape[2])
    f = lax.axis_index("fsdp")
    z = lax.axis_index("seq")
    rows = layout.rows
    share = layout.share
    member = (z % layout.near) * 2 + f % 2
    slot = (z // layout.near // 2) * share + member

    w_attn = lax.all_gather(
        jnp.concatenate([w_query, w_key, w_value], axis=1), "fsdp", axis=0, tiled=True
    )
    gains = gather_small(
        layout, f, jnp.concatenate([attn_gain, ffn_gain, query_gain, key_gain])
    ).astype(F32)
    wide, narrow = attn_gain.shape[0], query_gain.shape[0]
    even = z % 2 == 0
    hidden_dev = w_down.shape[0]
    gains, gate_rows, up_rows = lax.optimization_barrier((gains, w_gate, w_up))
    fetched = lax.all_to_all(
        pack_columns(even, gate_rows, up_rows, fsdp_devices),
        "fsdp",
        split_axis=0,
        concat_axis=0,
        tiled=True,
    )
    full_attn_gain = gains[:, :wide].reshape(D)
    full_ffn_gain = gains[:, wide : 2 * wide].reshape(D)
    full_query_gain = gains[:, 2 * wide : 2 * wide + narrow].reshape(HD)
    full_key_gain = gains[:, 2 * wide + narrow :].reshape(HD)
    inputs_low = scatter_rows(layout, tokens[:, 0], z, slot)
    grad_out_low = scatter_rows(layout, cotangent[:, 0], z, slot)
    full_out = lax.all_gather(w_out, "fsdp", axis=0, tiled=True)

    row = jnp.arange(rows, dtype=jnp.int32)
    position = (
        (row // layout.piece_rows) * layout.step_rows
        + member * layout.piece_rows
        + row % layout.piece_rows
    ).astype(F32)
    frequency = THETA ** (-(jnp.arange(HD // 2).astype(F32) * 2.0 / HD))
    angles = frequency[:, None] * position[None, :]
    cosine_table, sine_table = jnp.cos(angles)[None], jnp.sin(angles)[None]
    head_gains = jnp.concatenate(
        [
            jnp.broadcast_to(full_query_gain[None, :, None], (HQ, HD, 1)),
            jnp.broadcast_to(full_key_gain[None, :, None], (KVH, HD, 1)),
        ]
    )

    inputs = inputs_low.astype(F32)
    normed, normed_unit, normed_inverse = rms_fwd(inputs, full_attn_gain)
    fetched = [fetched[:, h].reshape(D, hidden_dev // SWAPS) for h in range(SWAPS)]
    swapped = [
        lax.ppermute(piece, "seq", [(i, i ^ 1) for i in range(seq_devices)]) for piece in fetched
    ]
    normed_low, grad_out_low, w_attn = lax.optimization_barrier(
        (normed.astype(BF16), grad_out_low, w_attn)
    )
    grad_out_gather = RowGather(layout, grad_out_low)
    raw = dot(w_attn, normed_low, 0, 1)
    pair_width = KVH * HD
    turned = HQ + KVH
    head_raw = raw[: turned * HD].reshape(turned, HD, rows)
    head_normed, head_unit, head_inverse = head_rms_fwd(head_raw, head_gains)
    heads_low = rotate(head_normed, cosine_table, sine_table).astype(BF16).reshape(turned * HD, rows)
    queries = heads_low[: HQ * HD]
    own_pair = jnp.concatenate([heads_low[HQ * HD :], raw[turned * HD :].astype(BF16)], axis=0)
    pair_pieces = [own_pair] + [permute(own_pair, layout.across(k)) for k in range(1, share)]
    keys = jnp.concatenate([piece[:pair_width] for piece in pair_pieces], axis=1)
    values = jnp.concatenate([piece[pair_width:] for piece in pair_pieces], axis=1)
    index = member.astype(jnp.int32).reshape(1)
    attended, log_totals = attend(
        index, queries, keys, values, share, layout.piece_rows, layout.step_rows
    )
    attended, swapped[0], grad_out_gather.own = lax.optimization_barrier(
        (attended, swapped[0], grad_out_gather.own)
    )
    middle = inputs + dot(attended, full_out, 0, 0)
    ffn_normed, ffn_unit, ffn_inverse = rms_fwd(middle, full_ffn_gain)
    ffn_low = ffn_normed.astype(BF16)

    ffn_gather = RowGather(layout, ffn_low)
    weights = merge_columns(even, fetched, swapped)
    worked = ()
    for n in range(layout.chips):
        pieces = [
            (side[n], 0)
            for side in (
                ffn_gather.own,
                grad_out_gather.own,
                ffn_gather.sibling,
                grad_out_gather.sibling,
            )
        ]
        worked = hidden_step(n, fsdp_devices * rows, rows, pieces, weights, w_down, worked)
        worked = ffn_gather.after(n, *worked)
        worked = grad_out_gather.after(n, *worked)
    hidden, grads, hidden_t, grads_t, ffn_rows, grad_out_rows = worked
    me = f.astype(jnp.int32).reshape(1)

    def pipe():
        return PairPipe(z) if seq_devices == 4 else LinePipe(z, seq_devices)

    line = pipe()
    late = [pipe() for _ in range(4)]

    def to_owners(name):
        terms = [
            line.results[f"{name}{h}"].reshape(fsdp_devices, wide, -1) for h in range(HALVES)
        ]
        return lax.all_to_all(
            jnp.stack(terms, axis=1), "fsdp", split_axis=0, concat_axis=0, tiled=True
        )

    def advance(name=None, value=None, others=()):
        flights = [getattr(side, "side", None) for side in late]
        flights += [getattr(side, "across", None) for side in late]
        flights, others = line.step(name, value, (flights, others))
        for k, side in enumerate(late):
            if isinstance(side, PairPipe):
                side.side, side.across = flights[k], flights[len(late) + k]
        return others

    def until(name):
        while any(f"{name}{h}" not in line.results for h in range(HALVES)):
            advance()

    def flat(term):
        return term.reshape(-1, term.shape[-1])

    gate_term = weight_product(grads_t, ffn_rows, 0, hidden_dev, wide, "w_gate_grad")
    (grads,) = advance("gate0", flat(gate_term[0]), (grads,))
    grad_ffn_part = rows_product(me, grads, weights, 1, rows, "grad_ffn_normed")
    grad_ffn_part, grads_t, hidden = advance(
        "gate1", flat(gate_term[1]), (grad_ffn_part, grads_t, hidden)
    )
    grad_ffn_normed = lax.psum_scatter(
        grad_ffn_part, "fsdp", scatter_dimension=0, tiled=True
    )
    up_term = weight_product(grads_t, ffn_rows, hidden_dev, hidden_dev, wide, "w_up_grad")
    out_part = rows_product(me, hidden, w_down, 0, rows, "block_out")
    out_part, hidden_t = advance("up0", flat(up_term[0]), (out_part, hidden_t))
    down_term = weight_product(hidden_t, grad_out_rows, 0, hidden_dev, 0, "w_down_grad")
    down_shape = down_term[0].shape
    down_term, grad_ffn_normed = advance(
        "up1", flat(up_term[1]), (down_term, grad_ffn_normed)
    )
    grad_ffn_normed = grad_ffn_normed.astype(F32)

    grad_middle_norm, ffn_gain_term = rms_back(
        grad_ffn_normed, ffn_unit, ffn_inverse, full_ffn_gain
    )
    grad_middle = grad_out_low.astype(F32) + grad_middle_norm
    grad_branch_low = grad_middle.astype(BF16)
    grad_attended = dot(full_out, grad_branch_low, 1, 1).astype(BF16)
    out_term = dot(attended, grad_branch_low, 1, 0).astype(BF16)
    out_rows = lax.psum_scatter(out_term, "fsdp", scatter_dimension=0, tiled=True)
    grad_queries, grad_keys, grad_values = attend_back(
        index,
        queries,
        keys,
        values,
        attended,
        log_totals,
        grad_attended,
        share,
        layout.piece_rows,
        layout.step_rows,
    )
    grad_queries, grad_keys, grad_values, grad_branch_low, out_part = advance(
        "down0",
        flat(down_term[0]),
        (grad_queries, grad_keys, grad_values, grad_branch_low, out_part),
    )
    grad_pair = jnp.concatenate([grad_keys[:, :rows], grad_values[:, :rows]], axis=0)
    for k in range(1, share):
        columns = slice(k * rows, (k + 1) * rows)
        sent = jnp.concatenate([grad_keys[:, columns], grad_values[:, columns]], axis=0)
        grad_pair = grad_pair + permute(sent.astype(BF16), layout.across(k)).astype(F32)
    grad_pair_low = grad_pair.astype(BF16)
    grad_turned = (
        jnp.concatenate([grad_queries, grad_pair_low[:pair_width]], axis=0)
        .astype(F32)
        .reshape(turned, HD, rows)
    )
    grad_head_normed = rotate(grad_turned, cosine_table, -sine_table)
    scaled = grad_head_normed * head_gains
    grad_head_raw = head_inverse * (
        scaled - head_unit * jnp.mean(scaled * head_unit, axis=1, keepdims=True)
    )
    head_gain_terms = jnp.sum(grad_head_normed * head_unit, axis=2)
    grad_raw = jnp.concatenate(
        [grad_head_raw.astype(BF16).reshape(turned * HD, rows), grad_pair_low[pair_width:]], axis=0
    )
    projection_term = dot(normed_low, grad_raw, 0, 1).astype(BF16)
    projection_term, out_part, grad_raw = lax.optimization_barrier(
        (projection_term, out_part, grad_raw)
    )
    projection_rows = lax.psum_scatter(
        projection_term, "fsdp", scatter_dimension=0, tiled=True
    )
    out_sum = lax.psum_scatter(out_part, "fsdp", scatter_dimension=0, tiled=True)
    until("gate")
    grad_normed = dot(grad_raw, w_attn, 0, 1)
    grad_input_norm, attn_gain_term = rms_back(
        grad_normed, normed_unit, normed_inverse, full_attn_gain
    )

    tokens_grad_low = (grad_middle + grad_input_norm).astype(BF16)
    gain_terms = sum_small(
        layout,
        jnp.concatenate(
            [
                attn_gain_term,
                ffn_gain_term,
                jnp.sum(head_gain_terms[:HQ], axis=0),
                jnp.sum(head_gain_terms[HQ:], axis=0),
            ]
        )[None],
    )[0]

    def own_share(first, count):
        share_of = count // fsdp_devices
        vector = lax.dynamic_slice_in_dim(gain_terms, first + f * share_of, share_of, 0)
        return jnp.pad(vector, (0, wide - share_of))

    gain_columns = jnp.stack(
        [own_share(0, D), own_share(D, D), own_share(2 * D, HD), own_share(2 * D + HD, HD)],
        axis=1,
    )
    gain_columns = jnp.pad(gain_columns, ((0, 0), (0, 128 - gain_columns.shape[1]))).astype(BF16)


    line.results, gain_columns = lax.optimization_barrier((line.results, gain_columns))
    gate_all = to_owners("gate")

    out_rows, gain_columns, tokens_grad_low = advance(
        "down1", flat(down_term[1]), (out_rows, gain_columns, tokens_grad_low)
    )
    late[0].step("out", out_rows)
    (projection_rows,) = advance(others=(projection_rows,))
    cut = projection_rows.shape[1] // 256 * 128
    late[0].step()
    late[1].step("first", projection_rows[:, :cut])
    late[2].step("second", projection_rows[:, cut:])
    late[3].step("gain", gain_columns)
    until("up")
    up_all = to_owners("up")
    gate_all, tokens_grad_low = advance(others=(gate_all, tokens_grad_low))
    for side in late:
        side.step()
    w_gate_grad = unpack_columns(gate_all)
    tokens_grad = return_over_seq(layout, tokens_grad_low)
    up_all, w_gate_grad, tokens_grad, middle = advance(
        others=(up_all, w_gate_grad, tokens_grad, middle)
    )
    for side in late:
        side.step()
    w_up_grad = unpack_columns(up_all)
    tokens_grad = return_over_cores(layout, tokens_grad, f)
    until("down")
    w_down_grad = unpack_rows(
        [line.results[f"down{h}"].reshape(down_shape) for h in range(HALVES)]
    )
    block_out = return_over_seq(layout, (middle + out_sum.astype(F32)).astype(BF16))
    tokens_grad, w_up_grad, w_down_grad = advance(others=(tokens_grad, w_up_grad, w_down_grad))
    for side in late:
        side.step()
    while any(side.flying for side in late):
        (block_out,) = advance(others=(block_out,))
        for side in late:
            side.step()
    block_out = return_over_cores(layout, block_out, f)

    out_rows = late[0].results["out"]
    attn_rows = jnp.concatenate([late[1].results["first"], late[2].results["second"]], axis=1)
    attn_rows = attn_rows.astype(F32)
    w_out_grad = out_rows.astype(F32)
    gain_rows = late[3].results["gain"].astype(F32)
    query_width = HQ * HD

    return (
        block_out[:, None],
        tokens_grad[:, None],
        gain_rows[:, 0],
        gain_rows[:narrow, 2],
        gain_rows[:narrow, 3],
        attn_rows[:, :query_width],
        attn_rows[:, query_width : query_width + pair_width],
        attn_rows[:, query_width + pair_width : query_width + 2 * pair_width],
        w_out_grad,
        gain_rows[:, 1],
        w_gate_grad,
        w_up_grad,
        w_down_grad,
    )


def solution(mesh):
    activations = P(None, "fsdp", "seq", None)
    vector = P("fsdp")
    matrix = P("fsdp", None)
    specs = (
        (activations, activations)
        + (vector,) * 3
        + (matrix,) * 4
        + (vector,)
        + (matrix,) * 3
    )
    return jax.shard_map(body, mesh=mesh, in_specs=specs, out_specs=specs, check_vma=False)
```

```python
import functools
import math

import jax
import jax.numpy as jnp
from jax import lax
from jax.experimental import pallas as pl
from jax.experimental.pallas import tpu as pltpu
from jax.sharding import PartitionSpec as P

D = 2048
HQ = 32
KVH = 8
HD = 64
FF = 8192
LENGTH = 1024
MICRO = 2
HALVES = 2
SWAPS = 2

EPSILON = 1e-05
THETA = 1000000.0
GROUP = HQ // KVH
BLOCK = 128
SCALE = 1.0 / math.sqrt(HD)
LOG2E = math.log2(math.e)
VMEM_LIMIT = 56 * 1024 * 1024

F32 = jnp.float32
BF16 = jnp.bfloat16


def dot(left_side, right_side, left_dim, right_dim):
    return lax.dot_general(
        left_side,
        right_side,
        (((left_dim,), (right_dim,)), ((), ())),
        preferred_element_type=F32,
    )


def rms_fwd(values, row_gain):
    inverse = lax.rsqrt(jnp.mean(values * values, axis=-1, keepdims=True) + EPSILON)
    unit_rows = values * inverse
    return (unit_rows * row_gain, unit_rows, inverse)


def rms_back(grad_outputs, unit_rows, inverse, row_gain):
    scaled = grad_outputs * row_gain
    grad_inputs = inverse * (
        scaled - unit_rows * jnp.mean(scaled * unit_rows, axis=-1, keepdims=True)
    )
    grad_gain = jnp.sum(grad_outputs * unit_rows, axis=0)
    return (grad_inputs, grad_gain)


def head_rms_fwd(values, gains):
    inverse = lax.rsqrt(jnp.mean(values * values, axis=1, keepdims=True) + EPSILON)
    unit = values * inverse
    return (unit * gains, unit, inverse)


def rotate(values, cosine_table, sine_table):
    half_width = values.shape[1] // 2
    front_half = values[:, :half_width]
    back_half = values[:, half_width:]
    return jnp.concatenate(
        [
            front_half * cosine_table - back_half * sine_table,
            back_half * cosine_table + front_half * sine_table,
        ],
        axis=1,
    )


def block_masks(index, pieces, piece_rows, step_rows):
    key = lax.broadcasted_iota(jnp.int32, (BLOCK, GROUP * BLOCK), 0)
    query = lax.broadcasted_iota(jnp.int32, (BLOCK, GROUP * BLOCK), 1) & (BLOCK - 1)

    def place(row, piece):
        return (row // piece_rows) * step_rows + piece * piece_rows + (row & (piece_rows - 1))

    return [place(key, index ^ k) <= place(query, index) for k in range(pieces)]


def heads_beside(block, first, count):
    return jnp.concatenate(
        [block[h * HD : (h + 1) * HD, first : first + count] for h in range(GROUP)], axis=1
    )


def mask_tail(values, mask, first):
    tail = jnp.where(mask, values[first:], 0.0)
    if first == 0:
        return tail
    return jnp.concatenate([values[:first], tail], axis=0)


def attend_kernel(index_ref, q_ref, k_ref, v_ref, out_ref, lse_ref, *, pieces, piece_rows, step_rows):
    rows = q_ref.shape[1]
    masks = block_masks(index_ref[0], pieces, piece_rows, step_rows)
    queries = q_ref[...]
    for first in range(0, rows, BLOCK):
        count = first + BLOCK
        query_block = heads_beside(queries, first, BLOCK)
        total = None
        result = None
        for k in range(pieces):
            spot = pl.ds(k * rows, count)
            scores = dot(k_ref[:, spot], query_block, 0, 0)
            weights = mask_tail(jnp.exp2(scores * (SCALE * LOG2E)), masks[k], first)
            part = jnp.sum(weights, axis=0, keepdims=True)
            value = dot(v_ref[:, spot], weights.astype(BF16), 1, 0)
            total = part if total is None else total + part
            result = value if result is None else result + value
        result = result * (1.0 / total)
        log_total = jnp.log2(total)
        for h in range(GROUP):
            columns = slice(h * BLOCK, (h + 1) * BLOCK)
            out_ref[h * HD : (h + 1) * HD, first : first + BLOCK] = result[:, columns].astype(BF16)
            lse_ref[0, h : h + 1, first : first + BLOCK] = log_total[:, columns]


def attend_back_kernel(
    index_ref, q_ref, k_ref, v_ref, out_ref, lse_ref, grad_ref, dq_ref, dk_ref, dv_ref,
    *, pieces, piece_rows, step_rows
):
    rows = q_ref.shape[1]
    masks = block_masks(index_ref[0], pieces, piece_rows, step_rows)
    queries = q_ref[...]
    grads = grad_ref[...]
    results = out_ref[...]
    dk_ref[...] = jnp.zeros_like(dk_ref)
    dv_ref[...] = jnp.zeros_like(dv_ref)
    for first in range(0, rows, BLOCK):
        count = first + BLOCK
        query_block = heads_beside(queries, first, BLOCK)
        grad_block = heads_beside(grads, first, BLOCK)
        result_block = heads_beside(results, first, BLOCK)
        centre = jnp.sum(
            grad_block.astype(F32) * result_block.astype(F32), axis=0, keepdims=True
        )
        log_total = jnp.concatenate(
            [lse_ref[0, h : h + 1, first : first + BLOCK] for h in range(GROUP)], axis=1
        )
        dq = None
        for k in range(pieces):
            spot = pl.ds(k * rows, count)
            keys = k_ref[:, spot]
            scores = dot(keys, query_block, 0, 0)
            weights = mask_tail(
                jnp.exp2(scores * (SCALE * LOG2E) - log_total), masks[k], first
            )
            grad_weights = dot(v_ref[:, spot], grad_block, 0, 0)
            grad_scores = (weights * (grad_weights - centre)).astype(BF16)
            part = dot(keys, grad_scores, 1, 0)
            dq = part if dq is None else dq + part
            dk_ref[:, spot] += dot(query_block, grad_scores, 1, 1) * SCALE
            dv_ref[:, spot] += dot(grad_block, weights.astype(BF16), 1, 1)
        dq = (dq * SCALE).astype(BF16)
        for h in range(GROUP):
            columns = slice(h * BLOCK, (h + 1) * BLOCK)
            dq_ref[h * HD : (h + 1) * HD, first : first + BLOCK] = dq[:, columns]


def attention_specs(rows, total_rows):
    group_spec = pl.BlockSpec((GROUP * HD, rows), lambda i: (i, 0))
    pair_spec = pl.BlockSpec((HD, total_rows), lambda i: (i, 0))
    lse_spec = pl.BlockSpec((1, GROUP, rows), lambda i: (i, 0, 0))
    return group_spec, pair_spec, lse_spec


def attend(index, queries, keys, values, pieces, piece_rows, step_rows):
    rows, total_rows = queries.shape[1], keys.shape[1]
    group_spec, pair_spec, lse_spec = attention_specs(rows, total_rows)
    return pl.pallas_call(
        functools.partial(
            attend_kernel, pieces=pieces, piece_rows=piece_rows, step_rows=step_rows
        ),
        grid=(KVH,),
        in_specs=[pl.BlockSpec(memory_space=pltpu.SMEM), group_spec, pair_spec, pair_spec],
        out_specs=[group_spec, lse_spec],
        out_shape=[
            jax.ShapeDtypeStruct((HQ * HD, rows), BF16),
            jax.ShapeDtypeStruct((KVH, GROUP, rows), F32),
        ],
        compiler_params=pltpu.CompilerParams(vmem_limit_bytes=VMEM_LIMIT),
        cost_estimate=pl.CostEstimate(
            flops=4 * HQ * HD * rows * total_rows,
            bytes_accessed=8 * HQ * HD * rows,
            transcendentals=HQ * rows * total_rows,
        ),
        name="attend",
    )(index, queries, keys, values)


def attend_back(index, queries, keys, values, results, lse, grads, pieces, piece_rows, step_rows):
    rows, total_rows = queries.shape[1], keys.shape[1]
    group_spec, pair_spec, lse_spec = attention_specs(rows, total_rows)
    return pl.pallas_call(
        functools.partial(
            attend_back_kernel, pieces=pieces, piece_rows=piece_rows, step_rows=step_rows
        ),
        grid=(KVH,),
        in_specs=[
            pl.BlockSpec(memory_space=pltpu.SMEM),
            group_spec,
            pair_spec,
            pair_spec,
            group_spec,
            lse_spec,
            group_spec,
        ],
        out_specs=[group_spec, pair_spec, pair_spec],
        out_shape=[
            jax.ShapeDtypeStruct((HQ * HD, rows), BF16),
            jax.ShapeDtypeStruct((KVH * HD, total_rows), F32),
            jax.ShapeDtypeStruct((KVH * HD, total_rows), F32),
        ],
        compiler_params=pltpu.CompilerParams(vmem_limit_bytes=VMEM_LIMIT),
        cost_estimate=pl.CostEstimate(
            flops=10 * HQ * HD * rows * total_rows,
            bytes_accessed=16 * HQ * HD * rows,
            transcendentals=HQ * rows * total_rows,
        ),
        name="attend_back",
    )(index, queries, keys, values, results, lse, grads)


def hidden_kernel(own_x_ref, own_c_ref, other_x_ref, other_c_ref, weight_ref, down_ref, *refs):
    hidden_ref, grads_ref, hidden_t_ref, grads_t_ref, all_x_ref, all_c_ref = refs[-6:]
    units = down_ref.shape[0]
    half = units // HALVES

    def work(x_ref, c_ref):
        x = x_ref[...]
        c = c_ref[...]
        all_x_ref[...] = x
        all_c_ref[...] = c
        for h in range(HALVES):
            part = slice(h * half, (h + 1) * half)
            up_part = slice(units + h * half, units + (h + 1) * half)
            gate = dot(x, weight_ref[:, part], 1, 0)
            up = dot(x, weight_ref[:, up_part], 1, 0)
            grad_hidden = dot(c, down_ref[part, :], 1, 1)
            sigmoid = 0.5 * jnp.tanh(0.5 * gate) + 0.5
            silu = gate * sigmoid
            hidden = (silu * up).astype(BF16)
            grad_up = (grad_hidden * silu).astype(BF16)
            grad_gate = (grad_hidden * up * (sigmoid + silu * (1.0 - sigmoid))).astype(BF16)
            hidden_ref[:, part] = hidden
            grads_ref[:, part] = grad_gate
            grads_ref[:, up_part] = grad_up
            hidden_t_ref[part, :] = hidden.T
            grads_t_ref[part, :] = grad_gate.T
            grads_t_ref[up_part, :] = grad_up.T

    pl.when(pl.program_id(0) == 0)(lambda: work(own_x_ref, own_c_ref))
    pl.when(pl.program_id(0) == 1)(lambda: work(other_x_ref, other_c_ref))


def hidden_step(n, count, rows, pieces, weights, w_down, so_far):
    depth = w_down.shape[1]
    units = w_down.shape[0]
    once = pl.Buffered(1)
    read = [
        pl.BlockSpec((rows, depth), lambda i, block=block: (block, 0), pipeline_mode=once)
        for _, block in pieces
    ]
    widths = (units, 2 * units)
    upright = [(count, width) for width in widths]
    turned = [(width, count) for width in widths]
    whole = [(count, depth)] * 2
    flops = 12 * rows * depth * units
    return pl.pallas_call(
        hidden_kernel,
        grid=(2,),
        in_specs=read
        + [
            pl.BlockSpec((depth, 2 * units), lambda i: (0, 0), pipeline_mode=once),
            pl.BlockSpec((units, depth), lambda i: (0, 0), pipeline_mode=once),
        ]
        + [pl.BlockSpec(memory_space=pl.ANY)] * len(so_far),
        out_specs=[pl.BlockSpec((rows, shape[1]), lambda i: (2 * n + i, 0)) for shape in upright]
        + [pl.BlockSpec((shape[0], rows), lambda i: (0, 2 * n + i)) for shape in turned]
        + [pl.BlockSpec((rows, shape[1]), lambda i: (2 * n + i, 0)) for shape in whole],
        out_shape=[jax.ShapeDtypeStruct(shape, BF16) for shape in upright + turned + whole],
        input_output_aliases={6 + k: k for k in range(len(so_far))},
        compiler_params=pltpu.CompilerParams(vmem_limit_bytes=VMEM_LIMIT),
        cost_estimate=pl.CostEstimate(
            flops=flops,
            bytes_accessed=16 * rows * depth + 24 * rows * units + 6 * depth * units,
            transcendentals=2 * rows * units,
        ),
        name="hidden_step",
    )(*[array for array, _ in pieces], weights, w_down, *so_far)


def rows_kernel(me_ref, left_ref, right_ref, result_ref, *, right_dim):
    result_ref[...] = dot(left_ref[...], right_ref[...], 1, right_dim).astype(BF16)


def rows_product(me, left, right, right_dim, block_rows, name):
    count, width = left.shape
    return pl.pallas_call(
        functools.partial(rows_kernel, right_dim=right_dim),
        grid_spec=pltpu.PrefetchScalarGridSpec(
            num_scalar_prefetch=1,
            grid=(count // block_rows,),
            in_specs=[
                pl.BlockSpec((block_rows, width), lambda i, me_ref: (i, 0)),
                pl.BlockSpec(
                    right.shape, lambda i, me_ref: (0, 0), pipeline_mode=pl.Buffered(1)
                ),
            ],
            out_specs=pl.BlockSpec((block_rows, D), lambda i, me_ref: (me_ref[0] ^ i, 0)),
        ),
        out_shape=jax.ShapeDtypeStruct((count, D), BF16),
        compiler_params=pltpu.CompilerParams(vmem_limit_bytes=VMEM_LIMIT),
        cost_estimate=pl.CostEstimate(
            flops=2 * count * D * width,
            bytes_accessed=2 * (count * width + count * D + D * width),
            transcendentals=0,
        ),
        name=name,
    )(me, left, right)


def weight_kernel(left_ref, right_ref, *result_refs, parts):
    total = dot(left_ref[...], right_ref[...], 1, 0)
    half = total.shape[0] // HALVES
    for h, result_ref in enumerate(result_refs):
        piece = total[h * half : (h + 1) * half]
        if parts == 0:
            result_ref[0] = piece.astype(BF16)
            continue
        wide = piece.shape[1] // parts
        for p in range(parts):
            result_ref[p] = piece[:, p * wide : (p + 1) * wide].astype(BF16).T


def weight_product(left, right, first, units, wide, name):
    depth = left.shape[1]
    half = units // HALVES
    column = min(512, D)
    parts = column // wide if wide else 0
    block = first // units
    if wide:
        out_spec = pl.BlockSpec((parts, wide, half), lambda j: (j, 0, 0))
        out_shape = jax.ShapeDtypeStruct((D // wide, wide, half), BF16)
    else:
        out_spec = pl.BlockSpec((1, half, column), lambda j: (j, 0, 0))
        out_shape = jax.ShapeDtypeStruct((D // column, half, column), BF16)
    return pl.pallas_call(
        functools.partial(weight_kernel, parts=parts),
        grid=(D // column,),
        in_specs=[
            pl.BlockSpec((units, depth), lambda j: (block, 0), pipeline_mode=pl.Buffered(1)),
            pl.BlockSpec((depth, column), lambda j: (0, j)),
        ],
        out_specs=[out_spec] * HALVES,
        out_shape=[out_shape] * HALVES,
        compiler_params=pltpu.CompilerParams(vmem_limit_bytes=VMEM_LIMIT),
        cost_estimate=pl.CostEstimate(
            flops=2 * units * depth * D,
            bytes_accessed=2 * depth * (units + D) + 2 * units * D,
            transcendentals=0,
        ),
        name=name,
    )(left, right)


def merge_kernel(even_ref, *refs):
    result_ref = refs[-1]
    piece = result_ref.shape[1] // (2 * SWAPS)
    for h in range(SWAPS):
        mine, theirs = refs[h][...], refs[SWAPS + h][...]
        gate = jnp.where(even_ref[0] > 0, mine, theirs)
        up = jnp.where(even_ref[0] > 0, theirs, mine)
        result_ref[:, h * piece : (h + 1) * piece] = gate
        result_ref[:, (SWAPS + h) * piece : (SWAPS + h + 1) * piece] = up


def merge_columns(even, mine, theirs):
    rows, piece = mine[0].shape
    tile = min(256, rows)
    return pl.pallas_call(
        merge_kernel,
        grid=(rows // tile,),
        in_specs=[pl.BlockSpec(memory_space=pltpu.SMEM)]
        + [pl.BlockSpec((tile, piece), lambda i: (i, 0))] * (2 * SWAPS),
        out_specs=pl.BlockSpec((tile, 2 * SWAPS * piece), lambda i: (i, 0)),
        out_shape=jax.ShapeDtypeStruct((rows, 2 * SWAPS * piece), BF16),
        compiler_params=pltpu.CompilerParams(vmem_limit_bytes=VMEM_LIMIT),
        cost_estimate=pl.CostEstimate(
            flops=0, bytes_accessed=8 * rows * SWAPS * piece, transcendentals=0
        ),
        name="merge_columns",
    )(even.astype(jnp.int32).reshape(1), *mine, *theirs)


def pack_kernel(even_ref, first_ref, second_ref, result_ref):
    chosen = jnp.where(even_ref[0] > 0, first_ref[...], second_ref[...])
    width = result_ref.shape[-1]
    for h in range(SWAPS):
        result_ref[0, h] = chosen[:, h * width : (h + 1) * width]


def pack_columns(even, first, second, parts):
    rows, columns = first.shape
    width = columns // parts
    block = pl.BlockSpec((rows, width), lambda i: (0, i))
    piece = width // SWAPS
    return pl.pallas_call(
        pack_kernel,
        grid=(parts,),
        in_specs=[pl.BlockSpec(memory_space=pltpu.SMEM), block, block],
        out_specs=pl.BlockSpec((1, SWAPS, rows, piece), lambda i: (i, 0, 0, 0)),
        out_shape=jax.ShapeDtypeStruct((parts, SWAPS, rows, piece), BF16),
        compiler_params=pltpu.CompilerParams(vmem_limit_bytes=VMEM_LIMIT),
        cost_estimate=pl.CostEstimate(
            flops=0, bytes_accessed=6 * rows * columns, transcendentals=0
        ),
        name="pack_columns",
    )(even.astype(jnp.int32).reshape(1), first, second)


def unpack_kernel(stacked_ref, result_ref):
    width = stacked_ref.shape[-1]
    for h in range(HALVES):
        result_ref[:, h * width : (h + 1) * width] = stacked_ref[0, h].astype(F32)


def unpack_columns(stacked):
    parts, _, rows, half = stacked.shape
    return pl.pallas_call(
        unpack_kernel,
        grid=(parts,),
        in_specs=[pl.BlockSpec((1, HALVES, rows, half), lambda i: (i, 0, 0, 0))],
        out_specs=pl.BlockSpec((rows, HALVES * half), lambda i: (0, i)),
        out_shape=jax.ShapeDtypeStruct((rows, parts * HALVES * half), F32),
        compiler_params=pltpu.CompilerParams(vmem_limit_bytes=VMEM_LIMIT),
        cost_estimate=pl.CostEstimate(
            flops=0, bytes_accessed=6 * parts * rows * HALVES * half, transcendentals=0
        ),
        name="unpack_columns",
    )(stacked)


def unpack_rows_kernel(*refs):
    result_ref = refs[-1]
    height = refs[0].shape[1]
    for h in range(HALVES):
        result_ref[h * height : (h + 1) * height, :] = refs[h][0].astype(F32)


def unpack_rows(pieces):
    blocks, half, column = pieces[0].shape
    return pl.pallas_call(
        unpack_rows_kernel,
        grid=(blocks,),
        in_specs=[pl.BlockSpec((1, half, column), lambda i: (i, 0, 0))] * HALVES,
        out_specs=pl.BlockSpec((HALVES * half, column), lambda i: (0, i)),
        out_shape=jax.ShapeDtypeStruct((HALVES * half, blocks * column), F32),
        compiler_params=pltpu.CompilerParams(vmem_limit_bytes=VMEM_LIMIT),
        cost_estimate=pl.CostEstimate(
            flops=0, bytes_accessed=6 * blocks * HALVES * half * column, transcendentals=0
        ),
        name="unpack_rows",
    )(*pieces)


class Layout:
    def __init__(self, fsdp_devices, seq_devices, rows_dev):
        self.fsdp = fsdp_devices
        self.seq = seq_devices
        self.chips = fsdp_devices // 2
        self.share = 2 * seq_devices // (2 * MICRO)
        self.near = self.share // 2
        self.piece_rows = rows_dev // self.share
        self.step_rows = rows_dev
        self.rows = LENGTH // self.share

    def flat(self, f, z):
        return f * self.seq + z

    def moved(self, r):
        pairs = []
        for f in range(self.fsdp):
            for z in range(self.seq):
                slot = z ^ r
                micro, j = slot // self.share, slot % self.share
                target_f = (f // 2) * 2 + j % 2
                target_z = (2 * micro + f % 2) * self.near + j // 2
                pairs.append((self.flat(f, z), self.flat(target_f, target_z)))
        return pairs

    def other(self, k):
        return [
            (self.flat(f, z), self.flat(f ^ k, z))
            for f in range(self.fsdp)
            for z in range(self.seq)
        ]

    def across(self, k):
        pairs = []
        for f in range(self.fsdp):
            for z in range(self.seq):
                pairs.append((self.flat(f, z), self.flat(f ^ (k & 1), z ^ (k >> 1))))
        return pairs


def permute(value, pairs):
    return lax.ppermute(value, ("fsdp", "seq"), pairs)


def scatter_rows(layout, values, z, slot):
    parts = values.reshape(layout.seq, layout.piece_rows, values.shape[-1])
    result = jnp.zeros_like(parts)
    for r in range(layout.seq):
        sent = lax.dynamic_index_in_dim(parts, z ^ r, 0, keepdims=False)
        got = permute(sent, layout.moved(r))
        result = lax.dynamic_update_index_in_dim(result, got, slot ^ r, 0)
    return result.reshape(layout.rows, values.shape[-1])


def return_over_seq(layout, values):
    width = values.shape[-1]
    parts = values.reshape(layout.seq, layout.piece_rows, width)
    parts = lax.all_to_all(parts, "seq", split_axis=0, concat_axis=0, tiled=True)
    return parts.reshape(MICRO, 2, layout.near, layout.piece_rows, width)


def return_over_cores(layout, parts, f):
    core = f % 2
    kept = lax.dynamic_index_in_dim(parts, core, 1, keepdims=False)
    sent = lax.dynamic_index_in_dim(parts, 1 - core, 1, keepdims=False)
    got = permute(sent, layout.other(1))
    both = jnp.stack(
        [jnp.where(core == 0, kept, got), jnp.where(core == 0, got, kept)], axis=2
    )
    return both.reshape(MICRO, layout.step_rows, parts.shape[-1])


class RowGather:
    def __init__(self, layout, own):
        self.layout = layout
        self.own = {0: own}
        self.sibling = {0: self.move(own, 1)}
        chips = layout.chips
        for n in range(1, 3 if chips == 4 else chips):
            self.own[n] = self.move(own, 2 * n)

    def move(self, value, k):
        return permute(value, self.layout.other(k))

    def after(self, n, *values):
        chips = self.layout.chips
        if n + 1 < chips:
            waiting = {m: value for m, value in self.own.items() if m > n}
            siblings = {m: value for m, value in self.sibling.items() if m > n}
            waiting, siblings, values = lax.optimization_barrier((waiting, siblings, values))
            self.own.update(waiting)
            self.sibling.update(siblings)
            if chips == 4 and n == 0:
                cut = self.own[0].shape[0] // 2
                self.far = [self.move(self.own[2][:cut], 2), self.move(self.own[1][cut:], 4)]
            if chips == 4 and n == 1:
                self.far = lax.optimization_barrier((self.far, values))[0]
                self.own[3] = jnp.concatenate(self.far)
            for m in (n + 1, n + 2):
                if m in self.own and m not in self.sibling:
                    self.sibling[m] = self.move(self.own[m], 1)
        return values


def gather_small(layout, f, own):
    held = own[None]
    k = 1
    while k < layout.fsdp:
        got = permute(held, layout.other(k))
        upper = (f & k) > 0
        held = jnp.concatenate(
            [jnp.where(upper, got, held), jnp.where(upper, held, got)], axis=0
        )
        k *= 2
    return held


def sum_small(layout, value):
    k = 1
    while k < layout.fsdp:
        value = value + permute(value, layout.other(k))
        k *= 2
    return value


class LinePipe:
    def __init__(self, z, seq_devices):
        self.seq = seq_devices
        self.z = z
        self.outer = (z == 0) | (z == seq_devices - 1)
        self.flying = []
        self.results = {}

    def send(self, stage, value):
        half, last = self.seq // 2, self.seq - 1
        if stage < half - 1:
            pairs = [(stage, stage + 1), (last - stage, last - stage - 1)]
        elif stage == half - 1:
            pairs = [(half - 1, half), (half, half - 1)]
        else:
            s = last - 1 - stage
            pairs = [(s + 1, s), (last - s - 1, last - s)]
        return lax.ppermute(value, "seq", pairs)

    def join(self, stage, value, got):
        if stage < self.seq // 2:
            return value + got
        s = self.seq - 2 - stage
        return jnp.where((self.z == s) | (self.z == self.seq - 1 - s), got, value)

    def step(self, name=None, value=None, others=()):
        arrived = [entry[3] for entry in self.flying]
        arrived, self.results, value, others = lax.optimization_barrier(
            (arrived, self.results, value, others)
        )
        flying = []
        if name is not None:
            flying.append((name, 0, value, self.send(0, value)))
        for (key, stage, held, _), got in zip(self.flying, arrived):
            if stage == self.seq - 2:
                self.results[key] = jnp.where(self.outer, got, held)
                continue
            held = self.join(stage, held, got)
            flying.append((key, stage + 1, held, self.send(stage + 1, held)))
        self.flying = flying
        return others


class PairPipe:
    def __init__(self, z):
        self.outer = (z == 0) | (z == 3)
        self.entered = self.halved = self.summed = None
        self.side = self.across = None
        self.results = {}

    @property
    def flying(self):
        return self.entered or self.halved or self.summed

    def step(self, name=None, value=None, others=()):
        side, across, self.results, value, others = lax.optimization_barrier(
            (self.side, self.across, self.results, value, others)
        )
        entered, halved, summed = self.entered, self.halved, self.summed
        total = halved[1] + across if halved else None
        inward, outward = [(0, 1), (3, 2)], [(1, 0), (2, 3)]
        self.side = self.across = None
        self.entered = self.halved = self.summed = None
        sent = value if total is None else total
        pairs = inward if total is None else outward
        if value is not None and total is not None:
            sent = jnp.where(self.outer, value, total)
            pairs = inward + outward
        if sent is not None:
            self.side = lax.ppermute(sent, "seq", pairs)
        if entered:
            joined = entered[1] + side
            self.across = lax.ppermute(joined, "seq", [(1, 2), (2, 1)])
            self.halved = (entered[0], joined)
        if summed:
            self.results[summed[0]] = jnp.where(self.outer, side, summed[1])
        if halved:
            self.summed = (halved[0], sent)
        if name is not None:
            self.entered = (name, value)
        return others


def body(
    tokens,
    cotangent,
    attn_gain,
    query_gain,
    key_gain,
    w_query,
    w_key,
    w_value,
    w_out,
    ffn_gain,
    w_gate,
    w_up,
    w_down,
):
    fsdp_devices = lax.axis_size("fsdp")
    seq_devices = lax.axis_size("seq")
    layout = Layout(fsdp_devices, seq_devices, tokens.shape[2])
    f = lax.axis_index("fsdp")
    z = lax.axis_index("seq")
    rows = layout.rows
    share = layout.share
    member = (z % layout.near) * 2 + f % 2
    slot = (z // layout.near // 2) * share + member

    w_attn = lax.all_gather(
        jnp.concatenate([w_query, w_key, w_value], axis=1), "fsdp", axis=0, tiled=True
    )
    gains = gather_small(
        layout, f, jnp.concatenate([attn_gain, ffn_gain, query_gain, key_gain])
    ).astype(F32)
    wide, narrow = attn_gain.shape[0], query_gain.shape[0]
    even = z % 2 == 0
    hidden_dev = w_down.shape[0]
    gains, gate_rows, up_rows = lax.optimization_barrier((gains, w_gate, w_up))
    fetched = lax.all_to_all(
        pack_columns(even, gate_rows, up_rows, fsdp_devices),
        "fsdp",
        split_axis=0,
        concat_axis=0,
        tiled=True,
    )
    full_attn_gain = gains[:, :wide].reshape(D)
    full_ffn_gain = gains[:, wide : 2 * wide].reshape(D)
    full_query_gain = gains[:, 2 * wide : 2 * wide + narrow].reshape(HD)
    full_key_gain = gains[:, 2 * wide + narrow :].reshape(HD)
    inputs_low = scatter_rows(layout, tokens[:, 0], z, slot)
    grad_out_low = scatter_rows(layout, cotangent[:, 0], z, slot)
    full_out = lax.all_gather(w_out, "fsdp", axis=0, tiled=True)

    row = jnp.arange(rows, dtype=jnp.int32)
    position = (
        (row // layout.piece_rows) * layout.step_rows
        + member * layout.piece_rows
        + row % layout.piece_rows
    ).astype(F32)
    frequency = THETA ** (-(jnp.arange(HD // 2).astype(F32) * 2.0 / HD))
    angles = frequency[:, None] * position[None, :]
    cosine_table, sine_table = jnp.cos(angles)[None], jnp.sin(angles)[None]
    head_gains = jnp.concatenate(
        [
            jnp.broadcast_to(full_query_gain[None, :, None], (HQ, HD, 1)),
            jnp.broadcast_to(full_key_gain[None, :, None], (KVH, HD, 1)),
        ]
    )

    inputs = inputs_low.astype(F32)
    normed, normed_unit, normed_inverse = rms_fwd(inputs, full_attn_gain)
    fetched = [fetched[:, h].reshape(D, hidden_dev // SWAPS) for h in range(SWAPS)]
    swapped = [
        lax.ppermute(piece, "seq", [(i, i ^ 1) for i in range(seq_devices)]) for piece in fetched
    ]
    normed_low, grad_out_low, w_attn = lax.optimization_barrier(
        (normed.astype(BF16), grad_out_low, w_attn)
    )
    grad_out_gather = RowGather(layout, grad_out_low)
    raw = dot(w_attn, normed_low, 0, 1)
    pair_width = KVH * HD
    turned = HQ + KVH
    head_raw = raw[: turned * HD].reshape(turned, HD, rows)
    head_normed, head_unit, head_inverse = head_rms_fwd(head_raw, head_gains)
    heads_low = rotate(head_normed, cosine_table, sine_table).astype(BF16).reshape(turned * HD, rows)
    queries = heads_low[: HQ * HD]
    own_pair = jnp.concatenate([heads_low[HQ * HD :], raw[turned * HD :].astype(BF16)], axis=0)
    pair_pieces = [own_pair] + [permute(own_pair, layout.across(k)) for k in range(1, share)]
    keys = jnp.concatenate([piece[:pair_width] for piece in pair_pieces], axis=1)
    values = jnp.concatenate([piece[pair_width:] for piece in pair_pieces], axis=1)
    index = member.astype(jnp.int32).reshape(1)
    attended, log_totals = attend(
        index, queries, keys, values, share, layout.piece_rows, layout.step_rows
    )
    attended, swapped[0], grad_out_gather.own = lax.optimization_barrier(
        (attended, swapped[0], grad_out_gather.own)
    )
    middle = inputs + dot(attended, full_out, 0, 0)
    ffn_normed, ffn_unit, ffn_inverse = rms_fwd(middle, full_ffn_gain)
    ffn_low = ffn_normed.astype(BF16)

    ffn_gather = RowGather(layout, ffn_low)
    weights = merge_columns(even, fetched, swapped)
    worked = ()
    for n in range(layout.chips):
        pieces = [
            (side[n], 0)
            for side in (
                ffn_gather.own,
                grad_out_gather.own,
                ffn_gather.sibling,
                grad_out_gather.sibling,
            )
        ]
        worked = hidden_step(n, fsdp_devices * rows, rows, pieces, weights, w_down, worked)
        worked = ffn_gather.after(n, *worked)
        worked = grad_out_gather.after(n, *worked)
    hidden, grads, hidden_t, grads_t, ffn_rows, grad_out_rows = worked
    me = f.astype(jnp.int32).reshape(1)

    def pipe():
        return PairPipe(z) if seq_devices == 4 else LinePipe(z, seq_devices)

    line = pipe()
    late = [pipe() for _ in range(4)]

    def to_owners(name):
        terms = [
            line.results[f"{name}{h}"].reshape(fsdp_devices, wide, -1) for h in range(HALVES)
        ]
        return lax.all_to_all(
            jnp.stack(terms, axis=1), "fsdp", split_axis=0, concat_axis=0, tiled=True
        )

    def advance(name=None, value=None, others=()):
        flights = [getattr(side, "side", None) for side in late]
        flights += [getattr(side, "across", None) for side in late]
        flights, others = line.step(name, value, (flights, others))
        for k, side in enumerate(late):
            if isinstance(side, PairPipe):
                side.side, side.across = flights[k], flights[len(late) + k]
        return others

    def until(name):
        while any(f"{name}{h}" not in line.results for h in range(HALVES)):
            advance()

    def flat(term):
        return term.reshape(-1, term.shape[-1])

    gate_term = weight_product(grads_t, ffn_rows, 0, hidden_dev, wide, "w_gate_grad")
    (grads,) = advance("gate0", flat(gate_term[0]), (grads,))
    grad_ffn_part = rows_product(me, grads, weights, 1, rows, "grad_ffn_normed")
    grad_ffn_part, grads_t, hidden = advance(
        "gate1", flat(gate_term[1]), (grad_ffn_part, grads_t, hidden)
    )
    grad_ffn_normed = lax.psum_scatter(
        grad_ffn_part, "fsdp", scatter_dimension=0, tiled=True
    )
    up_term = weight_product(grads_t, ffn_rows, hidden_dev, hidden_dev, wide, "w_up_grad")
    out_part = rows_product(me, hidden, w_down, 0, rows, "block_out")
    out_part, hidden_t = advance("up0", flat(up_term[0]), (out_part, hidden_t))
    down_term = weight_product(hidden_t, grad_out_rows, 0, hidden_dev, 0, "w_down_grad")
    down_shape = down_term[0].shape
    down_term, grad_ffn_normed = advance(
        "up1", flat(up_term[1]), (down_term, grad_ffn_normed)
    )
    grad_ffn_normed = grad_ffn_normed.astype(F32)

    grad_middle_norm, ffn_gain_term = rms_back(
        grad_ffn_normed, ffn_unit, ffn_inverse, full_ffn_gain
    )
    grad_middle = grad_out_low.astype(F32) + grad_middle_norm
    grad_branch_low = grad_middle.astype(BF16)
    grad_attended = dot(full_out, grad_branch_low, 1, 1).astype(BF16)
    out_term = dot(attended, grad_branch_low, 1, 0).astype(BF16)
    out_rows = lax.psum_scatter(out_term, "fsdp", scatter_dimension=0, tiled=True)
    grad_queries, grad_keys, grad_values = attend_back(
        index,
        queries,
        keys,
        values,
        attended,
        log_totals,
        grad_attended,
        share,
        layout.piece_rows,
        layout.step_rows,
    )
    grad_queries, grad_keys, grad_values, grad_branch_low, out_part = advance(
        "down0",
        flat(down_term[0]),
        (grad_queries, grad_keys, grad_values, grad_branch_low, out_part),
    )
    grad_pair = jnp.concatenate([grad_keys[:, :rows], grad_values[:, :rows]], axis=0)
    for k in range(1, share):
        columns = slice(k * rows, (k + 1) * rows)
        sent = jnp.concatenate([grad_keys[:, columns], grad_values[:, columns]], axis=0)
        grad_pair = grad_pair + permute(sent.astype(BF16), layout.across(k)).astype(F32)
    grad_pair_low = grad_pair.astype(BF16)
    grad_turned = (
        jnp.concatenate([grad_queries, grad_pair_low[:pair_width]], axis=0)
        .astype(F32)
        .reshape(turned, HD, rows)
    )
    grad_head_normed = rotate(grad_turned, cosine_table, -sine_table)
    scaled = grad_head_normed * head_gains
    grad_head_raw = head_inverse * (
        scaled - head_unit * jnp.mean(scaled * head_unit, axis=1, keepdims=True)
    )
    head_gain_terms = jnp.sum(grad_head_normed * head_unit, axis=2)
    grad_raw = jnp.concatenate(
        [grad_head_raw.astype(BF16).reshape(turned * HD, rows), grad_pair_low[pair_width:]], axis=0
    )
    projection_term = dot(normed_low, grad_raw, 0, 1).astype(BF16)
    projection_term, out_part, grad_raw, out_rows = lax.optimization_barrier(
        (projection_term, out_part, grad_raw, out_rows)
    )
    late[0].step("out", out_rows)
    projection_rows = lax.psum_scatter(
        projection_term, "fsdp", scatter_dimension=0, tiled=True
    )
    out_sum = lax.psum_scatter(out_part, "fsdp", scatter_dimension=0, tiled=True)
    until("gate")
    grad_normed = dot(grad_raw, w_attn, 0, 1)
    grad_input_norm, attn_gain_term = rms_back(
        grad_normed, normed_unit, normed_inverse, full_attn_gain
    )

    tokens_grad_low = (grad_middle + grad_input_norm).astype(BF16)
    gain_terms = sum_small(
        layout,
        jnp.concatenate(
            [
                attn_gain_term,
                ffn_gain_term,
                jnp.sum(head_gain_terms[:HQ], axis=0),
                jnp.sum(head_gain_terms[HQ:], axis=0),
            ]
        )[None],
    )[0]

    def own_share(first, count):
        share_of = count // fsdp_devices
        vector = lax.dynamic_slice_in_dim(gain_terms, first + f * share_of, share_of, 0)
        return jnp.pad(vector, (0, wide - share_of))

    gain_columns = jnp.stack(
        [own_share(0, D), own_share(D, D), own_share(2 * D, HD), own_share(2 * D + HD, HD)],
        axis=1,
    )
    gain_columns = jnp.pad(gain_columns, ((0, 0), (0, 128 - gain_columns.shape[1]))).astype(BF16)


    line.results, gain_columns = lax.optimization_barrier((line.results, gain_columns))
    gate_all = to_owners("gate")

    gain_columns, tokens_grad_low = advance(
        "down1", flat(down_term[1]), (gain_columns, tokens_grad_low)
    )
    late[0].step()
    (projection_rows,) = advance(others=(projection_rows,))
    cut = projection_rows.shape[1] // 256 * 128
    late[0].step()
    late[1].step("first", projection_rows[:, :cut])
    late[2].step("second", projection_rows[:, cut:])
    late[3].step("gain", gain_columns)
    until("up")
    up_all = to_owners("up")
    gate_all, tokens_grad_low = advance(others=(gate_all, tokens_grad_low))
    for side in late:
        side.step()
    w_gate_grad = unpack_columns(gate_all)
    tokens_grad = return_over_seq(layout, tokens_grad_low)
    up_all, w_gate_grad, tokens_grad, middle = advance(
        others=(up_all, w_gate_grad, tokens_grad, middle)
    )
    for side in late:
        side.step()
    w_up_grad = unpack_columns(up_all)
    tokens_grad = return_over_cores(layout, tokens_grad, f)
    until("down")
    w_down_grad = unpack_rows(
        [line.results[f"down{h}"].reshape(down_shape) for h in range(HALVES)]
    )
    block_out = return_over_seq(layout, (middle + out_sum.astype(F32)).astype(BF16))
    tokens_grad, w_up_grad, w_down_grad = advance(others=(tokens_grad, w_up_grad, w_down_grad))
    for side in late:
        side.step()
    while any(side.flying for side in late):
        (block_out,) = advance(others=(block_out,))
        for side in late:
            side.step()
    block_out = return_over_cores(layout, block_out, f)

    out_rows = late[0].results["out"]
    attn_rows = jnp.concatenate([late[1].results["first"], late[2].results["second"]], axis=1)
    attn_rows = attn_rows.astype(F32)
    w_out_grad = out_rows.astype(F32)
    gain_rows = late[3].results["gain"].astype(F32)
    query_width = HQ * HD

    return (
        block_out[:, None],
        tokens_grad[:, None],
        gain_rows[:, 0],
        gain_rows[:narrow, 2],
        gain_rows[:narrow, 3],
        attn_rows[:, :query_width],
        attn_rows[:, query_width : query_width + pair_width],
        attn_rows[:, query_width + pair_width : query_width + 2 * pair_width],
        w_out_grad,
        gain_rows[:, 1],
        w_gate_grad,
        w_up_grad,
        w_down_grad,
    )


def solution(mesh):
    activations = P(None, "fsdp", "seq", None)
    vector = P("fsdp")
    matrix = P("fsdp", None)
    specs = (
        (activations, activations)
        + (vector,) * 3
        + (matrix,) * 4
        + (vector,)
        + (matrix,) * 3
    )
    return jax.shard_map(body, mesh=mesh, in_specs=specs, out_specs=specs, check_vma=False)
```

```python
import functools
import math

import jax
import jax.numpy as jnp
from jax import lax
from jax.experimental import pallas as pl
from jax.experimental.pallas import tpu as pltpu
from jax.sharding import PartitionSpec as P

D = 2048
HQ = 32
KVH = 8
HD = 64
FF = 8192
LENGTH = 1024
MICRO = 2
HALVES = 2
SWAPS = 2

EPSILON = 1e-05
THETA = 1000000.0
GROUP = HQ // KVH
BLOCK = 128
SCALE = 1.0 / math.sqrt(HD)
LOG2E = math.log2(math.e)
VMEM_LIMIT = 56 * 1024 * 1024

F32 = jnp.float32
BF16 = jnp.bfloat16


def dot(left_side, right_side, left_dim, right_dim):
    return lax.dot_general(
        left_side,
        right_side,
        (((left_dim,), (right_dim,)), ((), ())),
        preferred_element_type=F32,
    )


def rms_fwd(values, row_gain):
    inverse = lax.rsqrt(jnp.mean(values * values, axis=-1, keepdims=True) + EPSILON)
    unit_rows = values * inverse
    return (unit_rows * row_gain, unit_rows, inverse)


def rms_back(grad_outputs, unit_rows, inverse, row_gain):
    scaled = grad_outputs * row_gain
    grad_inputs = inverse * (
        scaled - unit_rows * jnp.mean(scaled * unit_rows, axis=-1, keepdims=True)
    )
    grad_gain = jnp.sum(grad_outputs * unit_rows, axis=0)
    return (grad_inputs, grad_gain)


def head_rms_fwd(values, gains):
    inverse = lax.rsqrt(jnp.mean(values * values, axis=1, keepdims=True) + EPSILON)
    unit = values * inverse
    return (unit * gains, unit, inverse)


def rotate(values, cosine_table, sine_table):
    half_width = values.shape[1] // 2
    front_half = values[:, :half_width]
    back_half = values[:, half_width:]
    return jnp.concatenate(
        [
            front_half * cosine_table - back_half * sine_table,
            back_half * cosine_table + front_half * sine_table,
        ],
        axis=1,
    )


def block_masks(index, pieces, piece_rows, step_rows):
    key = lax.broadcasted_iota(jnp.int32, (BLOCK, GROUP * BLOCK), 0)
    query = lax.broadcasted_iota(jnp.int32, (BLOCK, GROUP * BLOCK), 1) & (BLOCK - 1)

    def place(row, piece):
        return (row // piece_rows) * step_rows + piece * piece_rows + (row & (piece_rows - 1))

    return [place(key, index ^ k) <= place(query, index) for k in range(pieces)]


def heads_beside(block, first, count):
    return jnp.concatenate(
        [block[h * HD : (h + 1) * HD, first : first + count] for h in range(GROUP)], axis=1
    )


def mask_tail(values, mask, first):
    tail = jnp.where(mask, values[first:], 0.0)
    if first == 0:
        return tail
    return jnp.concatenate([values[:first], tail], axis=0)


def attend_kernel(index_ref, q_ref, k_ref, v_ref, out_ref, lse_ref, *, pieces, piece_rows, step_rows):
    rows = q_ref.shape[1]
    masks = block_masks(index_ref[0], pieces, piece_rows, step_rows)
    queries = q_ref[...]
    for first in range(0, rows, BLOCK):
        count = first + BLOCK
        query_block = heads_beside(queries, first, BLOCK)
        total = None
        result = None
        for k in range(pieces):
            spot = pl.ds(k * rows, count)
            scores = dot(k_ref[:, spot], query_block, 0, 0)
            weights = mask_tail(jnp.exp2(scores * (SCALE * LOG2E)), masks[k], first)
            part = jnp.sum(weights, axis=0, keepdims=True)
            value = dot(v_ref[:, spot], weights.astype(BF16), 1, 0)
            total = part if total is None else total + part
            result = value if result is None else result + value
        result = result * (1.0 / total)
        log_total = jnp.log2(total)
        for h in range(GROUP):
            columns = slice(h * BLOCK, (h + 1) * BLOCK)
            out_ref[h * HD : (h + 1) * HD, first : first + BLOCK] = result[:, columns].astype(BF16)
            lse_ref[0, h : h + 1, first : first + BLOCK] = log_total[:, columns]


def attend_back_kernel(
    index_ref, q_ref, k_ref, v_ref, out_ref, lse_ref, grad_ref, dq_ref, dk_ref, dv_ref,
    *, pieces, piece_rows, step_rows
):
    rows = q_ref.shape[1]
    masks = block_masks(index_ref[0], pieces, piece_rows, step_rows)
    queries = q_ref[...]
    grads = grad_ref[...]
    results = out_ref[...]
    dk_ref[...] = jnp.zeros_like(dk_ref)
    dv_ref[...] = jnp.zeros_like(dv_ref)
    for first in range(0, rows, BLOCK):
        count = first + BLOCK
        query_block = heads_beside(queries, first, BLOCK)
        grad_block = heads_beside(grads, first, BLOCK)
        result_block = heads_beside(results, first, BLOCK)
        centre = jnp.sum(
            grad_block.astype(F32) * result_block.astype(F32), axis=0, keepdims=True
        )
        log_total = jnp.concatenate(
            [lse_ref[0, h : h + 1, first : first + BLOCK] for h in range(GROUP)], axis=1
        )
        dq = None
        for k in range(pieces):
            spot = pl.ds(k * rows, count)
            keys = k_ref[:, spot]
            scores = dot(keys, query_block, 0, 0)
            weights = mask_tail(
                jnp.exp2(scores * (SCALE * LOG2E) - log_total), masks[k], first
            )
            grad_weights = dot(v_ref[:, spot], grad_block, 0, 0)
            grad_scores = (weights * (grad_weights - centre)).astype(BF16)
            part = dot(keys, grad_scores, 1, 0)
            dq = part if dq is None else dq + part
            dk_ref[:, spot] += dot(query_block, grad_scores, 1, 1) * SCALE
            dv_ref[:, spot] += dot(grad_block, weights.astype(BF16), 1, 1)
        dq = (dq * SCALE).astype(BF16)
        for h in range(GROUP):
            columns = slice(h * BLOCK, (h + 1) * BLOCK)
            dq_ref[h * HD : (h + 1) * HD, first : first + BLOCK] = dq[:, columns]


def attention_specs(rows, total_rows):
    group_spec = pl.BlockSpec((GROUP * HD, rows), lambda i: (i, 0))
    pair_spec = pl.BlockSpec((HD, total_rows), lambda i: (i, 0))
    lse_spec = pl.BlockSpec((1, GROUP, rows), lambda i: (i, 0, 0))
    return group_spec, pair_spec, lse_spec


def attend(index, queries, keys, values, pieces, piece_rows, step_rows):
    rows, total_rows = queries.shape[1], keys.shape[1]
    group_spec, pair_spec, lse_spec = attention_specs(rows, total_rows)
    return pl.pallas_call(
        functools.partial(
            attend_kernel, pieces=pieces, piece_rows=piece_rows, step_rows=step_rows
        ),
        grid=(KVH,),
        in_specs=[pl.BlockSpec(memory_space=pltpu.SMEM), group_spec, pair_spec, pair_spec],
        out_specs=[group_spec, lse_spec],
        out_shape=[
            jax.ShapeDtypeStruct((HQ * HD, rows), BF16),
            jax.ShapeDtypeStruct((KVH, GROUP, rows), F32),
        ],
        compiler_params=pltpu.CompilerParams(vmem_limit_bytes=VMEM_LIMIT),
        cost_estimate=pl.CostEstimate(
            flops=4 * HQ * HD * rows * total_rows,
            bytes_accessed=8 * HQ * HD * rows,
            transcendentals=HQ * rows * total_rows,
        ),
        name="attend",
    )(index, queries, keys, values)


def attend_back(index, queries, keys, values, results, lse, grads, pieces, piece_rows, step_rows):
    rows, total_rows = queries.shape[1], keys.shape[1]
    group_spec, pair_spec, lse_spec = attention_specs(rows, total_rows)
    return pl.pallas_call(
        functools.partial(
            attend_back_kernel, pieces=pieces, piece_rows=piece_rows, step_rows=step_rows
        ),
        grid=(KVH,),
        in_specs=[
            pl.BlockSpec(memory_space=pltpu.SMEM),
            group_spec,
            pair_spec,
            pair_spec,
            group_spec,
            lse_spec,
            group_spec,
        ],
        out_specs=[group_spec, pair_spec, pair_spec],
        out_shape=[
            jax.ShapeDtypeStruct((HQ * HD, rows), BF16),
            jax.ShapeDtypeStruct((KVH * HD, total_rows), F32),
            jax.ShapeDtypeStruct((KVH * HD, total_rows), F32),
        ],
        compiler_params=pltpu.CompilerParams(vmem_limit_bytes=VMEM_LIMIT),
        cost_estimate=pl.CostEstimate(
            flops=10 * HQ * HD * rows * total_rows,
            bytes_accessed=16 * HQ * HD * rows,
            transcendentals=HQ * rows * total_rows,
        ),
        name="attend_back",
    )(index, queries, keys, values, results, lse, grads)


def hidden_kernel(own_x_ref, own_c_ref, other_x_ref, other_c_ref, weight_ref, down_ref, *refs):
    hidden_ref, grads_ref, hidden_t_ref, grads_t_ref, all_x_ref, all_c_ref = refs[-6:]
    units = down_ref.shape[0]
    half = units // HALVES

    def work(x_ref, c_ref):
        x = x_ref[...]
        c = c_ref[...]
        all_x_ref[...] = x
        all_c_ref[...] = c
        for h in range(HALVES):
            part = slice(h * half, (h + 1) * half)
            up_part = slice(units + h * half, units + (h + 1) * half)
            gate = dot(x, weight_ref[:, part], 1, 0)
            up = dot(x, weight_ref[:, up_part], 1, 0)
            grad_hidden = dot(c, down_ref[part, :], 1, 1)
            sigmoid = 0.5 * jnp.tanh(0.5 * gate) + 0.5
            silu = gate * sigmoid
            hidden = (silu * up).astype(BF16)
            grad_up = (grad_hidden * silu).astype(BF16)
            grad_gate = (grad_hidden * up * (sigmoid + silu * (1.0 - sigmoid))).astype(BF16)
            hidden_ref[:, part] = hidden
            grads_ref[:, part] = grad_gate
            grads_ref[:, up_part] = grad_up
            hidden_t_ref[part, :] = hidden.T
            grads_t_ref[part, :] = grad_gate.T
            grads_t_ref[up_part, :] = grad_up.T

    pl.when(pl.program_id(0) == 0)(lambda: work(own_x_ref, own_c_ref))
    pl.when(pl.program_id(0) == 1)(lambda: work(other_x_ref, other_c_ref))


def hidden_step(n, count, rows, pieces, weights, w_down, so_far):
    depth = w_down.shape[1]
    units = w_down.shape[0]
    once = pl.Buffered(1)
    read = [
        pl.BlockSpec((rows, depth), lambda i, block=block: (block, 0), pipeline_mode=once)
        for _, block in pieces
    ]
    widths = (units, 2 * units)
    upright = [(count, width) for width in widths]
    turned = [(width, count) for width in widths]
    whole = [(count, depth)] * 2
    flops = 12 * rows * depth * units
    return pl.pallas_call(
        hidden_kernel,
        grid=(2,),
        in_specs=read
        + [
            pl.BlockSpec((depth, 2 * units), lambda i: (0, 0), pipeline_mode=once),
            pl.BlockSpec((units, depth), lambda i: (0, 0), pipeline_mode=once),
        ]
        + [pl.BlockSpec(memory_space=pl.ANY)] * len(so_far),
        out_specs=[pl.BlockSpec((rows, shape[1]), lambda i: (2 * n + i, 0)) for shape in upright]
        + [pl.BlockSpec((shape[0], rows), lambda i: (0, 2 * n + i)) for shape in turned]
        + [pl.BlockSpec((rows, shape[1]), lambda i: (2 * n + i, 0)) for shape in whole],
        out_shape=[jax.ShapeDtypeStruct(shape, BF16) for shape in upright + turned + whole],
        input_output_aliases={6 + k: k for k in range(len(so_far))},
        compiler_params=pltpu.CompilerParams(vmem_limit_bytes=VMEM_LIMIT),
        cost_estimate=pl.CostEstimate(
            flops=flops,
            bytes_accessed=16 * rows * depth + 24 * rows * units + 6 * depth * units,
            transcendentals=2 * rows * units,
        ),
        name="hidden_step",
    )(*[array for array, _ in pieces], weights, w_down, *so_far)


def rows_kernel(me_ref, left_ref, right_ref, result_ref, *, right_dim):
    result_ref[...] = dot(left_ref[...], right_ref[...], 1, right_dim).astype(BF16)


def rows_product(me, left, right, right_dim, block_rows, name):
    count, width = left.shape
    return pl.pallas_call(
        functools.partial(rows_kernel, right_dim=right_dim),
        grid_spec=pltpu.PrefetchScalarGridSpec(
            num_scalar_prefetch=1,
            grid=(count // block_rows,),
            in_specs=[
                pl.BlockSpec((block_rows, width), lambda i, me_ref: (i, 0)),
                pl.BlockSpec(
                    right.shape, lambda i, me_ref: (0, 0), pipeline_mode=pl.Buffered(1)
                ),
            ],
            out_specs=pl.BlockSpec((block_rows, D), lambda i, me_ref: (me_ref[0] ^ i, 0)),
        ),
        out_shape=jax.ShapeDtypeStruct((count, D), BF16),
        compiler_params=pltpu.CompilerParams(vmem_limit_bytes=VMEM_LIMIT),
        cost_estimate=pl.CostEstimate(
            flops=2 * count * D * width,
            bytes_accessed=2 * (count * width + count * D + D * width),
            transcendentals=0,
        ),
        name=name,
    )(me, left, right)


def weight_kernel(left_ref, right_ref, *result_refs, parts):
    total = dot(left_ref[...], right_ref[...], 1, 0)
    half = total.shape[0] // HALVES
    for h, result_ref in enumerate(result_refs):
        piece = total[h * half : (h + 1) * half]
        if parts == 0:
            result_ref[0] = piece.astype(BF16)
            continue
        wide = piece.shape[1] // parts
        for p in range(parts):
            result_ref[p] = piece[:, p * wide : (p + 1) * wide].astype(BF16).T


def weight_product(left, right, first, units, wide, name):
    depth = left.shape[1]
    half = units // HALVES
    column = min(512, D)
    parts = column // wide if wide else 0
    block = first // units
    if wide:
        out_spec = pl.BlockSpec((parts, wide, half), lambda j: (j, 0, 0))
        out_shape = jax.ShapeDtypeStruct((D // wide, wide, half), BF16)
    else:
        out_spec = pl.BlockSpec((1, half, column), lambda j: (j, 0, 0))
        out_shape = jax.ShapeDtypeStruct((D // column, half, column), BF16)
    return pl.pallas_call(
        functools.partial(weight_kernel, parts=parts),
        grid=(D // column,),
        in_specs=[
            pl.BlockSpec((units, depth), lambda j: (block, 0), pipeline_mode=pl.Buffered(1)),
            pl.BlockSpec((depth, column), lambda j: (0, j)),
        ],
        out_specs=[out_spec] * HALVES,
        out_shape=[out_shape] * HALVES,
        compiler_params=pltpu.CompilerParams(vmem_limit_bytes=VMEM_LIMIT),
        cost_estimate=pl.CostEstimate(
            flops=2 * units * depth * D,
            bytes_accessed=2 * depth * (units + D) + 2 * units * D,
            transcendentals=0,
        ),
        name=name,
    )(left, right)


def merge_kernel(even_ref, *refs):
    result_ref = refs[-1]
    piece = result_ref.shape[1] // (2 * SWAPS)
    for h in range(SWAPS):
        mine, theirs = refs[h][...], refs[SWAPS + h][...]
        gate = jnp.where(even_ref[0] > 0, mine, theirs)
        up = jnp.where(even_ref[0] > 0, theirs, mine)
        result_ref[:, h * piece : (h + 1) * piece] = gate
        result_ref[:, (SWAPS + h) * piece : (SWAPS + h + 1) * piece] = up


def merge_columns(even, mine, theirs):
    rows, piece = mine[0].shape
    tile = min(256, rows)
    return pl.pallas_call(
        merge_kernel,
        grid=(rows // tile,),
        in_specs=[pl.BlockSpec(memory_space=pltpu.SMEM)]
        + [pl.BlockSpec((tile, piece), lambda i: (i, 0))] * (2 * SWAPS),
        out_specs=pl.BlockSpec((tile, 2 * SWAPS * piece), lambda i: (i, 0)),
        out_shape=jax.ShapeDtypeStruct((rows, 2 * SWAPS * piece), BF16),
        compiler_params=pltpu.CompilerParams(vmem_limit_bytes=VMEM_LIMIT),
        cost_estimate=pl.CostEstimate(
            flops=0, bytes_accessed=8 * rows * SWAPS * piece, transcendentals=0
        ),
        name="merge_columns",
    )(even.astype(jnp.int32).reshape(1), *mine, *theirs)


def pack_kernel(even_ref, first_ref, second_ref, result_ref):
    chosen = jnp.where(even_ref[0] > 0, first_ref[...], second_ref[...])
    width = result_ref.shape[-1]
    for h in range(SWAPS):
        result_ref[0, h] = chosen[:, h * width : (h + 1) * width]


def pack_columns(even, first, second, parts):
    rows, columns = first.shape
    width = columns // parts
    block = pl.BlockSpec((rows, width), lambda i: (0, i))
    piece = width // SWAPS
    return pl.pallas_call(
        pack_kernel,
        grid=(parts,),
        in_specs=[pl.BlockSpec(memory_space=pltpu.SMEM), block, block],
        out_specs=pl.BlockSpec((1, SWAPS, rows, piece), lambda i: (i, 0, 0, 0)),
        out_shape=jax.ShapeDtypeStruct((parts, SWAPS, rows, piece), BF16),
        compiler_params=pltpu.CompilerParams(vmem_limit_bytes=VMEM_LIMIT),
        cost_estimate=pl.CostEstimate(
            flops=0, bytes_accessed=6 * rows * columns, transcendentals=0
        ),
        name="pack_columns",
    )(even.astype(jnp.int32).reshape(1), first, second)


def unpack_kernel(stacked_ref, result_ref):
    width = stacked_ref.shape[-1]
    for h in range(HALVES):
        result_ref[:, h * width : (h + 1) * width] = stacked_ref[0, h].astype(F32)


def unpack_columns(stacked):
    parts, _, rows, half = stacked.shape
    return pl.pallas_call(
        unpack_kernel,
        grid=(parts,),
        in_specs=[pl.BlockSpec((1, HALVES, rows, half), lambda i: (i, 0, 0, 0))],
        out_specs=pl.BlockSpec((rows, HALVES * half), lambda i: (0, i)),
        out_shape=jax.ShapeDtypeStruct((rows, parts * HALVES * half), F32),
        compiler_params=pltpu.CompilerParams(vmem_limit_bytes=VMEM_LIMIT),
        cost_estimate=pl.CostEstimate(
            flops=0, bytes_accessed=6 * parts * rows * HALVES * half, transcendentals=0
        ),
        name="unpack_columns",
    )(stacked)


def unpack_rows_kernel(*refs):
    result_ref = refs[-1]
    height = refs[0].shape[1]
    for h in range(HALVES):
        result_ref[h * height : (h + 1) * height, :] = refs[h][0].astype(F32)


def unpack_rows(pieces):
    blocks, half, column = pieces[0].shape
    return pl.pallas_call(
        unpack_rows_kernel,
        grid=(blocks,),
        in_specs=[pl.BlockSpec((1, half, column), lambda i: (i, 0, 0))] * HALVES,
        out_specs=pl.BlockSpec((HALVES * half, column), lambda i: (0, i)),
        out_shape=jax.ShapeDtypeStruct((HALVES * half, blocks * column), F32),
        compiler_params=pltpu.CompilerParams(vmem_limit_bytes=VMEM_LIMIT),
        cost_estimate=pl.CostEstimate(
            flops=0, bytes_accessed=6 * blocks * HALVES * half * column, transcendentals=0
        ),
        name="unpack_rows",
    )(*pieces)


class Layout:
    def __init__(self, fsdp_devices, seq_devices, rows_dev):
        self.fsdp = fsdp_devices
        self.seq = seq_devices
        self.chips = fsdp_devices // 2
        self.share = 2 * seq_devices // (2 * MICRO)
        self.near = self.share // 2
        self.piece_rows = rows_dev // self.share
        self.step_rows = rows_dev
        self.rows = LENGTH // self.share

    def flat(self, f, z):
        return f * self.seq + z

    def moved(self, r):
        pairs = []
        for f in range(self.fsdp):
            for z in range(self.seq):
                slot = z ^ r
                micro, j = slot // self.share, slot % self.share
                target_f = (f // 2) * 2 + j % 2
                target_z = (2 * micro + f % 2) * self.near + j // 2
                pairs.append((self.flat(f, z), self.flat(target_f, target_z)))
        return pairs

    def other(self, k):
        return [
            (self.flat(f, z), self.flat(f ^ k, z))
            for f in range(self.fsdp)
            for z in range(self.seq)
        ]

    def across(self, k):
        pairs = []
        for f in range(self.fsdp):
            for z in range(self.seq):
                pairs.append((self.flat(f, z), self.flat(f ^ (k & 1), z ^ (k >> 1))))
        return pairs


def permute(value, pairs):
    return lax.ppermute(value, ("fsdp", "seq"), pairs)


def scatter_rows(layout, values, z, slot):
    parts = values.reshape(layout.seq, layout.piece_rows, values.shape[-1])
    result = jnp.zeros_like(parts)
    for r in range(layout.seq):
        sent = lax.dynamic_index_in_dim(parts, z ^ r, 0, keepdims=False)
        got = permute(sent, layout.moved(r))
        result = lax.dynamic_update_index_in_dim(result, got, slot ^ r, 0)
    return result.reshape(layout.rows, values.shape[-1])


def return_over_seq(layout, values):
    width = values.shape[-1]
    parts = values.reshape(layout.seq, layout.piece_rows, width)
    parts = lax.all_to_all(parts, "seq", split_axis=0, concat_axis=0, tiled=True)
    return parts.reshape(MICRO, 2, layout.near, layout.piece_rows, width)


def return_over_cores(layout, parts, f):
    core = f % 2
    kept = lax.dynamic_index_in_dim(parts, core, 1, keepdims=False)
    sent = lax.dynamic_index_in_dim(parts, 1 - core, 1, keepdims=False)
    got = permute(sent, layout.other(1))
    both = jnp.stack(
        [jnp.where(core == 0, kept, got), jnp.where(core == 0, got, kept)], axis=2
    )
    return both.reshape(MICRO, layout.step_rows, parts.shape[-1])


class RowGather:
    def __init__(self, layout, own):
        self.layout = layout
        self.own = {0: own}
        self.sibling = {0: self.move(own, 1)}
        chips = layout.chips
        for n in range(1, 3 if chips == 4 else chips):
            self.own[n] = self.move(own, 2 * n)

    def move(self, value, k):
        return permute(value, self.layout.other(k))

    def after(self, n, *values):
        chips = self.layout.chips
        if n + 1 < chips:
            waiting = {m: value for m, value in self.own.items() if m > n}
            siblings = {m: value for m, value in self.sibling.items() if m > n}
            waiting, siblings, values = lax.optimization_barrier((waiting, siblings, values))
            self.own.update(waiting)
            self.sibling.update(siblings)
            if chips == 4 and n == 0:
                cut = self.own[0].shape[0] // 2
                self.far = [self.move(self.own[2][:cut], 2), self.move(self.own[1][cut:], 4)]
            if chips == 4 and n == 1:
                self.far = lax.optimization_barrier((self.far, values))[0]
                self.own[3] = jnp.concatenate(self.far)
            for m in (n + 1, n + 2):
                if m in self.own and m not in self.sibling:
                    self.sibling[m] = self.move(self.own[m], 1)
        return values


def gather_small(layout, f, own):
    held = own[None]
    k = 1
    while k < layout.fsdp:
        got = permute(held, layout.other(k))
        upper = (f & k) > 0
        held = jnp.concatenate(
            [jnp.where(upper, got, held), jnp.where(upper, held, got)], axis=0
        )
        k *= 2
    return held


def sum_small(layout, value):
    k = 1
    while k < layout.fsdp:
        value = value + permute(value, layout.other(k))
        k *= 2
    return value


class LinePipe:
    def __init__(self, z, seq_devices):
        self.seq = seq_devices
        self.z = z
        self.outer = (z == 0) | (z == seq_devices - 1)
        self.flying = []
        self.results = {}

    def send(self, stage, value):
        half, last = self.seq // 2, self.seq - 1
        if stage < half - 1:
            pairs = [(stage, stage + 1), (last - stage, last - stage - 1)]
        elif stage == half - 1:
            pairs = [(half - 1, half), (half, half - 1)]
        else:
            s = last - 1 - stage
            pairs = [(s + 1, s), (last - s - 1, last - s)]
        return lax.ppermute(value, "seq", pairs)

    def join(self, stage, value, got):
        if stage < self.seq // 2:
            return value + got
        s = self.seq - 2 - stage
        return jnp.where((self.z == s) | (self.z == self.seq - 1 - s), got, value)

    def step(self, name=None, value=None, others=()):
        arrived = [entry[3] for entry in self.flying]
        arrived, self.results, value, others = lax.optimization_barrier(
            (arrived, self.results, value, others)
        )
        flying = []
        if name is not None:
            flying.append((name, 0, value, self.send(0, value)))
        for (key, stage, held, _), got in zip(self.flying, arrived):
            if stage == self.seq - 2:
                self.results[key] = jnp.where(self.outer, got, held)
                continue
            held = self.join(stage, held, got)
            flying.append((key, stage + 1, held, self.send(stage + 1, held)))
        self.flying = flying
        return others


class PairPipe:
    def __init__(self, z):
        self.outer = (z == 0) | (z == 3)
        self.entered = self.halved = self.summed = None
        self.side = self.across = None
        self.results = {}

    @property
    def flying(self):
        return self.entered or self.halved or self.summed

    def step(self, name=None, value=None, others=()):
        side, across, self.results, value, others = lax.optimization_barrier(
            (self.side, self.across, self.results, value, others)
        )
        entered, halved, summed = self.entered, self.halved, self.summed
        total = halved[1] + across if halved else None
        inward, outward = [(0, 1), (3, 2)], [(1, 0), (2, 3)]
        self.side = self.across = None
        self.entered = self.halved = self.summed = None
        sent = value if total is None else total
        pairs = inward if total is None else outward
        if value is not None and total is not None:
            sent = jnp.where(self.outer, value, total)
            pairs = inward + outward
        if sent is not None:
            self.side = lax.ppermute(sent, "seq", pairs)
        if entered:
            joined = entered[1] + side
            self.across = lax.ppermute(joined, "seq", [(1, 2), (2, 1)])
            self.halved = (entered[0], joined)
        if summed:
            self.results[summed[0]] = jnp.where(self.outer, side, summed[1])
        if halved:
            self.summed = (halved[0], sent)
        if name is not None:
            self.entered = (name, value)
        return others


def body(
    tokens,
    cotangent,
    attn_gain,
    query_gain,
    key_gain,
    w_query,
    w_key,
    w_value,
    w_out,
    ffn_gain,
    w_gate,
    w_up,
    w_down,
):
    fsdp_devices = lax.axis_size("fsdp")
    seq_devices = lax.axis_size("seq")
    layout = Layout(fsdp_devices, seq_devices, tokens.shape[2])
    f = lax.axis_index("fsdp")
    z = lax.axis_index("seq")
    rows = layout.rows
    share = layout.share
    member = (z % layout.near) * 2 + f % 2
    slot = (z // layout.near // 2) * share + member

    w_attn = lax.all_gather(
        jnp.concatenate([w_query, w_key, w_value], axis=1), "fsdp", axis=0, tiled=True
    )
    gains = gather_small(
        layout, f, jnp.concatenate([attn_gain, ffn_gain, query_gain, key_gain])
    ).astype(F32)
    wide, narrow = attn_gain.shape[0], query_gain.shape[0]
    even = z % 2 == 0
    hidden_dev = w_down.shape[0]
    gains, gate_rows, up_rows = lax.optimization_barrier((gains, w_gate, w_up))
    fetched = lax.all_to_all(
        pack_columns(even, gate_rows, up_rows, fsdp_devices),
        "fsdp",
        split_axis=0,
        concat_axis=0,
        tiled=True,
    )
    full_attn_gain = gains[:, :wide].reshape(D)
    full_ffn_gain = gains[:, wide : 2 * wide].reshape(D)
    full_query_gain = gains[:, 2 * wide : 2 * wide + narrow].reshape(HD)
    full_key_gain = gains[:, 2 * wide + narrow :].reshape(HD)
    inputs_low = scatter_rows(layout, tokens[:, 0], z, slot)
    grad_out_low = scatter_rows(layout, cotangent[:, 0], z, slot)
    full_out = lax.all_gather(w_out, "fsdp", axis=0, tiled=True)

    row = jnp.arange(rows, dtype=jnp.int32)
    position = (
        (row // layout.piece_rows) * layout.step_rows
        + member * layout.piece_rows
        + row % layout.piece_rows
    ).astype(F32)
    frequency = THETA ** (-(jnp.arange(HD // 2).astype(F32) * 2.0 / HD))
    angles = frequency[:, None] * position[None, :]
    cosine_table, sine_table = jnp.cos(angles)[None], jnp.sin(angles)[None]
    head_gains = jnp.concatenate(
        [
            jnp.broadcast_to(full_query_gain[None, :, None], (HQ, HD, 1)),
            jnp.broadcast_to(full_key_gain[None, :, None], (KVH, HD, 1)),
        ]
    )

    inputs = inputs_low.astype(F32)
    normed, normed_unit, normed_inverse = rms_fwd(inputs, full_attn_gain)
    fetched = [fetched[:, h].reshape(D, hidden_dev // SWAPS) for h in range(SWAPS)]
    swapped = [
        lax.ppermute(piece, "seq", [(i, i ^ 1) for i in range(seq_devices)]) for piece in fetched
    ]
    normed_low, grad_out_low, w_attn = lax.optimization_barrier(
        (normed.astype(BF16), grad_out_low, w_attn)
    )
    grad_out_gather = RowGather(layout, grad_out_low)
    raw = dot(w_attn, normed_low, 0, 1)
    pair_width = KVH * HD
    turned = HQ + KVH
    head_raw = raw[: turned * HD].reshape(turned, HD, rows)
    head_normed, head_unit, head_inverse = head_rms_fwd(head_raw, head_gains)
    heads_low = rotate(head_normed, cosine_table, sine_table).astype(BF16).reshape(turned * HD, rows)
    queries = heads_low[: HQ * HD]
    own_pair = jnp.concatenate([heads_low[HQ * HD :], raw[turned * HD :].astype(BF16)], axis=0)
    pair_pieces = [own_pair] + [permute(own_pair, layout.across(k)) for k in range(1, share)]
    keys = jnp.concatenate([piece[:pair_width] for piece in pair_pieces], axis=1)
    values = jnp.concatenate([piece[pair_width:] for piece in pair_pieces], axis=1)
    index = member.astype(jnp.int32).reshape(1)
    attended, log_totals = attend(
        index, queries, keys, values, share, layout.piece_rows, layout.step_rows
    )
    attended, swapped[0], grad_out_gather.own = lax.optimization_barrier(
        (attended, swapped[0], grad_out_gather.own)
    )
    middle = inputs + dot(attended, full_out, 0, 0)
    ffn_normed, ffn_unit, ffn_inverse = rms_fwd(middle, full_ffn_gain)
    ffn_low = ffn_normed.astype(BF16)

    ffn_gather = RowGather(layout, ffn_low)
    weights = merge_columns(even, fetched, swapped)
    worked = ()
    for n in range(layout.chips):
        pieces = [
            (side[n], 0)
            for side in (
                ffn_gather.own,
                grad_out_gather.own,
                ffn_gather.sibling,
                grad_out_gather.sibling,
            )
        ]
        worked = hidden_step(n, fsdp_devices * rows, rows, pieces, weights, w_down, worked)
        worked = ffn_gather.after(n, *worked)
        worked = grad_out_gather.after(n, *worked)
    hidden, grads, hidden_t, grads_t, ffn_rows, grad_out_rows = worked
    me = f.astype(jnp.int32).reshape(1)

    def pipe():
        return PairPipe(z) if seq_devices == 4 else LinePipe(z, seq_devices)

    line = pipe()
    late = [pipe() for _ in range(4)]

    def to_owners(name):
        terms = [
            line.results[f"{name}{h}"].reshape(fsdp_devices, wide, -1) for h in range(HALVES)
        ]
        return lax.all_to_all(
            jnp.stack(terms, axis=1), "fsdp", split_axis=0, concat_axis=0, tiled=True
        )

    def advance(name=None, value=None, others=()):
        flights = [getattr(side, "side", None) for side in late]
        flights += [getattr(side, "across", None) for side in late]
        flights, others = line.step(name, value, (flights, others))
        for k, side in enumerate(late):
            if isinstance(side, PairPipe):
                side.side, side.across = flights[k], flights[len(late) + k]
        return others

    def until(name):
        while any(f"{name}{h}" not in line.results for h in range(HALVES)):
            advance()

    def flat(term):
        return term.reshape(-1, term.shape[-1])

    gate_term = weight_product(grads_t, ffn_rows, 0, hidden_dev, wide, "w_gate_grad")
    (grads,) = advance("gate0", flat(gate_term[0]), (grads,))
    grad_ffn_part = rows_product(me, grads, weights, 1, rows, "grad_ffn_normed")
    grad_ffn_part, grads_t, hidden = advance(
        "gate1", flat(gate_term[1]), (grad_ffn_part, grads_t, hidden)
    )
    grad_ffn_normed = lax.psum_scatter(
        grad_ffn_part, "fsdp", scatter_dimension=0, tiled=True
    )
    up_term = weight_product(grads_t, ffn_rows, hidden_dev, hidden_dev, wide, "w_up_grad")
    out_part = rows_product(me, hidden, w_down, 0, rows, "block_out")
    out_part, hidden_t = advance("up0", flat(up_term[0]), (out_part, hidden_t))
    down_term = weight_product(hidden_t, grad_out_rows, 0, hidden_dev, 0, "w_down_grad")
    down_shape = down_term[0].shape
    down_term, grad_ffn_normed = advance(
        "up1", flat(up_term[1]), (down_term, grad_ffn_normed)
    )
    grad_ffn_normed = grad_ffn_normed.astype(F32)

    grad_middle_norm, ffn_gain_term = rms_back(
        grad_ffn_normed, ffn_unit, ffn_inverse, full_ffn_gain
    )
    grad_middle = grad_out_low.astype(F32) + grad_middle_norm
    grad_branch_low = grad_middle.astype(BF16)
    grad_attended = dot(full_out, grad_branch_low, 1, 1).astype(BF16)
    out_term = dot(attended, grad_branch_low, 1, 0).astype(BF16)
    out_rows = lax.psum_scatter(out_term, "fsdp", scatter_dimension=0, tiled=True)
    grad_queries, grad_keys, grad_values = attend_back(
        index,
        queries,
        keys,
        values,
        attended,
        log_totals,
        grad_attended,
        share,
        layout.piece_rows,
        layout.step_rows,
    )
    grad_queries, grad_keys, grad_values, grad_branch_low, out_part = advance(
        "down0",
        flat(down_term[0]),
        (grad_queries, grad_keys, grad_values, grad_branch_low, out_part),
    )
    grad_pair = jnp.concatenate([grad_keys[:, :rows], grad_values[:, :rows]], axis=0)
    for k in range(1, share):
        columns = slice(k * rows, (k + 1) * rows)
        sent = jnp.concatenate([grad_keys[:, columns], grad_values[:, columns]], axis=0)
        grad_pair = grad_pair + permute(sent.astype(BF16), layout.across(k)).astype(F32)
    grad_pair_low = grad_pair.astype(BF16)
    grad_turned = (
        jnp.concatenate([grad_queries, grad_pair_low[:pair_width]], axis=0)
        .astype(F32)
        .reshape(turned, HD, rows)
    )
    grad_head_normed = rotate(grad_turned, cosine_table, -sine_table)
    scaled = grad_head_normed * head_gains
    grad_head_raw = head_inverse * (
        scaled - head_unit * jnp.mean(scaled * head_unit, axis=1, keepdims=True)
    )
    head_gain_terms = jnp.sum(grad_head_normed * head_unit, axis=2)
    grad_raw = jnp.concatenate(
        [grad_head_raw.astype(BF16).reshape(turned * HD, rows), grad_pair_low[pair_width:]], axis=0
    )
    projection_term = dot(normed_low, grad_raw, 0, 1).astype(BF16)
    projection_term, out_part, grad_raw, out_rows = lax.optimization_barrier(
        (projection_term, out_part, grad_raw, out_rows)
    )
    late[0].step("out", out_rows)
    projection_rows = lax.psum_scatter(
        projection_term, "fsdp", scatter_dimension=0, tiled=True
    )
    out_sum = lax.psum_scatter(out_part, "fsdp", scatter_dimension=0, tiled=True)
    until("gate")
    grad_normed = dot(grad_raw, w_attn, 0, 1)
    grad_input_norm, attn_gain_term = rms_back(
        grad_normed, normed_unit, normed_inverse, full_attn_gain
    )

    tokens_grad_low = (grad_middle + grad_input_norm).astype(BF16)
    gain_terms = sum_small(
        layout,
        jnp.concatenate(
            [
                attn_gain_term,
                ffn_gain_term,
                jnp.sum(head_gain_terms[:HQ], axis=0),
                jnp.sum(head_gain_terms[HQ:], axis=0),
            ]
        )[None],
    )[0]

    def own_share(first, count):
        share_of = count // fsdp_devices
        vector = lax.dynamic_slice_in_dim(gain_terms, first + f * share_of, share_of, 0)
        return jnp.pad(vector, (0, wide - share_of))

    gain_columns = jnp.stack(
        [own_share(0, D), own_share(D, D), own_share(2 * D, HD), own_share(2 * D + HD, HD)],
        axis=1,
    )
    gain_columns = jnp.pad(gain_columns, ((0, 0), (0, 128 - gain_columns.shape[1]))).astype(BF16)


    line.results, gain_columns = lax.optimization_barrier((line.results, gain_columns))
    gate_all = to_owners("gate")

    gain_columns, tokens_grad_low = advance(
        "down1", flat(down_term[1]), (gain_columns, tokens_grad_low)
    )
    late[0].step()
    late[3].step("gain", gain_columns)
    (projection_rows,) = advance(others=(projection_rows,))
    cut = projection_rows.shape[1] // 256 * 128
    late[0].step()
    late[1].step("first", projection_rows[:, :cut])
    late[2].step("second", projection_rows[:, cut:])
    late[3].step()
    until("up")
    up_all = to_owners("up")
    gate_all, tokens_grad_low = advance(others=(gate_all, tokens_grad_low))
    for side in late:
        side.step()
    w_gate_grad = unpack_columns(gate_all)
    tokens_grad = return_over_seq(layout, tokens_grad_low)
    up_all, w_gate_grad, tokens_grad, middle = advance(
        others=(up_all, w_gate_grad, tokens_grad, middle)
    )
    for side in late:
        side.step()
    w_up_grad = unpack_columns(up_all)
    tokens_grad = return_over_cores(layout, tokens_grad, f)
    until("down")
    w_down_grad = unpack_rows(
        [line.results[f"down{h}"].reshape(down_shape) for h in range(HALVES)]
    )
    block_out = return_over_seq(layout, (middle + out_sum.astype(F32)).astype(BF16))
    tokens_grad, w_up_grad, w_down_grad = advance(others=(tokens_grad, w_up_grad, w_down_grad))
    for side in late:
        side.step()
    while any(side.flying for side in late):
        (block_out,) = advance(others=(block_out,))
        for side in late:
            side.step()
    block_out = return_over_cores(layout, block_out, f)

    out_rows = late[0].results["out"]
    attn_rows = jnp.concatenate([late[1].results["first"], late[2].results["second"]], axis=1)
    attn_rows = attn_rows.astype(F32)
    w_out_grad = out_rows.astype(F32)
    gain_rows = late[3].results["gain"].astype(F32)
    query_width = HQ * HD

    return (
        block_out[:, None],
        tokens_grad[:, None],
        gain_rows[:, 0],
        gain_rows[:narrow, 2],
        gain_rows[:narrow, 3],
        attn_rows[:, :query_width],
        attn_rows[:, query_width : query_width + pair_width],
        attn_rows[:, query_width + pair_width : query_width + 2 * pair_width],
        w_out_grad,
        gain_rows[:, 1],
        w_gate_grad,
        w_up_grad,
        w_down_grad,
    )


def solution(mesh):
    activations = P(None, "fsdp", "seq", None)
    vector = P("fsdp")
    matrix = P("fsdp", None)
    specs = (
        (activations, activations)
        + (vector,) * 3
        + (matrix,) * 4
        + (vector,)
        + (matrix,) * 3
    )
    return jax.shard_map(body, mesh=mesh, in_specs=specs, out_specs=specs, check_vma=False)
```
